32 devices in a mesh: ctx: 8 (over y, x, core), tp: 4 (over z).
Axes of the slice: x: 2, y: 2, z: 4, core: 2. Of those that a mesh axis runs over, the one named last changes fastest.
Arguments:
- streams: bfloat16 [3, 4096, 1024], P(None, 'tp', 'ctx'), may hold values from -6 to 6
- conv_weight: float32 [3, 7, 4096], P(None, None, 'tp'), may hold values from -2 to 2
- rates: float32 [512, 16], P('tp'), may hold values from 0.0001953125 to 0.05
- residues: float32 [512, 16], P('tp'), may hold values from -4 to 4
- skip: float32 [4096], P('tp'), may hold values from -4 to 4
- out_weight: bfloat16 [4096, 4096], P('ctx', 'tp'), may hold values from -0.09375 to 0.09375
Outputs:
- result: bfloat16 [1024, 4096], P('ctx', 'tp')
The draws below stay inside these ranges and needn't reach their ends.
All inputs are finite; a program needn't handle non-finite values.
Results may differ from the reference program's by a relative error of at most 0.014.
Values may be sent and summed in bfloat16 or wider, within the bound.
No kernel may reach another device: no remote copies, remote signals or barrier semaphores. Data moves between devices by JAX's collectives and lax.ppermute only.
A program may use at most 128 MiB of HBM per device.

```python
import math
import jax
import jax.numpy as jnp
from jax import lax

D = 4096
TAPS = 7
POLES = 16
FILTER_GROUPS = 512
TOKENS = 1024


def draw_rates(key, part):
    flag_key, slow_key, fast_key = jax.random.split(key, 3)
    slow_share = 0.5
    grid_shape = (FILTER_GROUPS, POLES)
    slow_rate = jnp.exp(jax.random.uniform(slow_key, grid_shape, jnp.float32, math.log(0.2 / TOKENS), math.log(2.0 / TOKENS)))
    fast_rate = jnp.exp(jax.random.uniform(fast_key, grid_shape, jnp.float32, math.log(0.02), math.log(0.05)))
    slow_pick = jax.random.uniform(flag_key, grid_shape, jnp.float32) < slow_share
    return jnp.where(slow_pick, slow_rate, fast_rate).astype(jnp.float32)


def level_of(rng, extent, cuts, smallest, top_value):
    level, own = 1.0, jax.random.fold_in(rng, 6)
    for axis_at, blocks in cuts:
        draws = jnp.exp(jax.random.uniform(jax.random.fold_in(own, axis_at), (blocks,), jnp.float32, smallest / len(cuts), top_value / len(cuts)))
        level = level * jnp.repeat(draws, extent[axis_at] // blocks).reshape([-1 if axis == axis_at else 1 for axis in range(len(extent))])
    return level


def gaussian(key, dims, deviation, bound, shards=(), kind=jnp.bfloat16):
    gain = level_of(key, dims, shards, -0.22, 0.18) if shards else 1.0
    drawn = jax.random.normal(key, dims, jnp.float32) * deviation * gain
    return jnp.minimum(jnp.maximum(drawn, -bound), bound).astype(kind)


def setup_inputs(seed: int = 0) -> dict:
    keys = jax.random.split(jax.random.key(seed), 7)
    streams = gaussian(keys[0], (3, D, TOKENS), 1.0, 6.0, ((1, 4), (2, 8)))
    conv_weight = gaussian(keys[1], (3, TAPS, D), TAPS ** -0.5, 2.0, ((2, 4),), jnp.float32)
    rates = draw_rates(jax.random.fold_in(keys[6], 71), 0)
    residues = gaussian(keys[3], (FILTER_GROUPS, POLES), 1.0, 4.0, ((0, 4),), jnp.float32)
    skip = gaussian(keys[4], (D,), 1.0, 4.0, ((0, 4),), jnp.float32)
    out_weight = gaussian(keys[5], (D, D), D ** -0.5, 0.09375, ((0, 8), (1, 4)))
    return {"streams": streams, "conv_weight": conv_weight, "rates": rates, "residues": residues, "skip": skip, "out_weight": out_weight}


def reference(streams, conv_weight, rates, residues, skip, out_weight):
    tap_count = conv_weight.shape[1]
    rim_width = tap_count - 1
    coefficient = residues * jnp.sqrt(2.0 * rates) / math.sqrt(POLES)
    group_width = D // FILTER_GROUPS
    block_chans = 256
    block_groups = block_chans // group_width

    def channel_block(block_index):
        first_chan = (block_index * block_chans).astype(jnp.int32)
        signal = lax.dynamic_slice_in_dim(streams, first_chan, block_chans, 1).astype(jnp.float32)
        taps_here = lax.dynamic_slice_in_dim(conv_weight, first_chan, block_chans, 2)
        padded = jnp.pad(signal, ((0, 0), (0, 0), (rim_width, 0)))
        filtered = jnp.zeros_like(signal)
        for shift_by in range(tap_count):
            filtered = filtered + taps_here[:, shift_by, :, None] * padded[:, :, rim_width - shift_by:rim_width - shift_by + TOKENS]
        queries = filtered[0]
        gated_in = (filtered[1] * filtered[2]).astype(jnp.bfloat16).astype(jnp.float32)
        first_group = (first_chan // group_width).astype(jnp.int32)
        coef_here = lax.dynamic_slice_in_dim(coefficient, first_group, block_groups, 0)
        rate_here = lax.dynamic_slice_in_dim(rates, first_group, block_groups, 0)
        position = jnp.arange(TOKENS, dtype=jnp.float32)
        kernel = jnp.einsum('gn,gnt->gt', coef_here, jnp.exp(-rate_here[:, :, None] * position), precision=lax.Precision.HIGHEST)
        kernel = jnp.repeat(kernel, group_width, axis=0)
        padded_len = 2 * TOKENS
        spectrum = jnp.fft.rfft(gated_in, n=padded_len, axis=1) * jnp.fft.rfft(kernel, n=padded_len, axis=1)
        longconv = jnp.fft.irfft(spectrum, n=padded_len, axis=1)[:, :TOKENS]
        skip_here = lax.dynamic_slice_in_dim(skip, first_chan, block_chans, 0)
        return (queries * (longconv + skip_here[:, None] * gated_in)).astype(jnp.bfloat16)
    mixed = lax.map(channel_block, jnp.arange(D // block_chans, dtype=jnp.int32))
    mixed = mixed.reshape(D, TOKENS)
    result = lax.dot_general(mixed, out_weight, (((0,), (0,)), ((), ())), preferred_element_type=jnp.float32)
    return result.astype(jnp.bfloat16)
```

```python
import math

import jax
import jax.numpy as jnp
from jax import lax
from jax.sharding import PartitionSpec as P


def from_behind(value, axis, steps):
    count = lax.axis_size(axis)
    leading, last = (max(0, -steps), min(count, count - steps))
    return lax.ppermute(value, axis, [(source, source + steps) for source in range(leading, last)])


def block_parts(signal, coefficient, rates):
    groups = coefficient.shape[0]
    channels, length = signal.shape
    group_width = channels // groups
    block_len = 128
    block_count = length // block_len
    blocks = signal.reshape(groups, group_width, block_count, block_len)
    position = jnp.arange(block_len, dtype=jnp.float32)
    centre = (block_len - 1.0) * 0.5
    left_factor = coefficient[:, :, None] * jnp.exp(-rates[:, :, None] * (position - centre))
    right_factor = jnp.exp(rates[:, :, None] * (position - centre))
    causal = (position[:, None] >= position[None, :]).astype(jnp.float32)
    toeplitz = (
        jnp.einsum("gni,gnj->gij", left_factor, right_factor, precision=lax.Precision.HIGHEST)
        * causal
    )
    inside = jnp.einsum("gij,gcbj->gcbi", toeplitz, blocks, precision=lax.Precision.HIGHEST)
    tail_decay = jnp.exp(-rates[:, :, None] * (block_len - 1.0 - position))
    block_ends = jnp.einsum("gnj,gcbj->gcbn", tail_decay, blocks, precision=lax.Precision.HIGHEST)
    block_index = jnp.arange(block_count, dtype=jnp.float32)
    lag = block_index[:, None] - block_index[None, :]
    earlier_mask = (lag >= 1.0).astype(jnp.float32)
    steps_back = jnp.maximum(lag - 1.0, 0.0)
    carry_matrix = jnp.exp(-rates[:, :, None, None] * block_len * steps_back) * earlier_mask
    entering = jnp.einsum(
        "gnab,gcbn->gcan", carry_matrix, block_ends, precision=lax.Precision.HIGHEST
    )
    last_decay = jnp.exp(-rates[:, :, None] * block_len * (block_count - 1.0 - block_index))
    segment_end = jnp.einsum(
        "gnb,gcbn->gcn", last_decay, block_ends, precision=lax.Precision.HIGHEST
    )
    return (inside, entering, segment_end)


def finish_conv(inside, entering, coefficient, rates):
    groups, group_width, block_count, block_len = inside.shape
    position = jnp.arange(block_len, dtype=jnp.float32)
    lift_out = coefficient[:, :, None] * jnp.exp(-rates[:, :, None] * (position + 1.0))
    total = inside + jnp.einsum(
        "gni,gcbn->gcbi", lift_out, entering, precision=lax.Precision.HIGHEST
    )
    return total.reshape(groups * group_width, block_count * block_len)


def local(streams, conv_weight, rates, residues, skip, out_weight):
    tap_count = conv_weight.shape[1]
    rim_width = tap_count - 1
    length = streams.shape[2]
    tail_rows = jnp.swapaxes(streams[:, :, length - rim_width :], 1, 2)
    before = from_behind(tail_rows, "ctx", 1)
    extended = jnp.concatenate([jnp.swapaxes(before, 1, 2), streams], axis=2)
    filtered = conv_weight[:, 0, :, None] * extended[:, :, rim_width:].astype(jnp.float32)
    for shift_by in range(1, tap_count):
        filtered = filtered + conv_weight[:, shift_by, :, None] * extended[
            :, :, rim_width - shift_by : rim_width - shift_by + length
        ].astype(jnp.float32)
    queries = filtered[0]
    gated_in = (filtered[1] * filtered[2]).astype(jnp.bfloat16)
    gated_wide = gated_in.astype(jnp.float32)
    coefficient = residues * jnp.sqrt(2.0 * rates) / math.sqrt(rates.shape[1])
    by_channel = lax.all_to_all(gated_in, "ctx", split_axis=0, concat_axis=1, tiled=True)
    per_device = rates.shape[0] // lax.axis_size("ctx")
    first_group = lax.axis_index("ctx") * per_device
    coef_mine = lax.dynamic_slice_in_dim(coefficient, first_group, per_device, 0)
    rates_mine = lax.dynamic_slice_in_dim(rates, first_group, per_device, 0)
    inside, entering, segment_end = block_parts(
        by_channel.astype(jnp.float32), coef_mine, rates_mine
    )
    filtered_all = finish_conv(inside, entering, coef_mine, rates_mine)
    conv_out = lax.all_to_all(filtered_all, "ctx", split_axis=1, concat_axis=0, tiled=True)
    mixed_out = (queries * (conv_out + skip[:, None] * gated_wide)).astype(jnp.bfloat16)
    layers = lax.axis_size("tp")
    copies = jnp.broadcast_to(mixed_out[None], (layers,) + mixed_out.shape)
    features = lax.all_to_all(copies, "tp", split_axis=0, concat_axis=0, tiled=True)
    features = features.reshape(layers * mixed_out.shape[0], length)
    summed = lax.dot_general(
        features,
        lax.all_gather(out_weight, "ctx", axis=0, tiled=True),
        (((0,), (0,)), ((), ())),
        preferred_element_type=jnp.float32,
    )
    return summed.astype(jnp.bfloat16)


def solution(mesh):
    return jax.shard_map(
        local,
        mesh=mesh,
        in_specs=(
            P(None, "tp", "ctx"),
            P(None, None, "tp"),
            P("tp", None),
            P("tp", None),
            P("tp"),
            P("ctx", "tp"),
        ),
        out_specs=P("ctx", "tp"),
        check_vma=False,
    )
```

```python
import math

import jax
import jax.numpy as jnp
from jax import lax
from jax.experimental import pallas as pl
from jax.experimental.pallas import tpu as pltpu
from jax.sharding import PartitionSpec as P

F32 = jnp.float32
BF16 = jnp.bfloat16
ROWS = 8
TILE = 128
VMEM_LIMIT = 40 * 1024 * 1024
CONTRACT_LANES = (((1,), (1,)), ((), ()))
CONTRACT_ROWS = (((0,), (0,)), ((), ()))


def from_behind(value, axis, steps):
    count = lax.axis_size(axis)
    leading, last = (max(0, -steps), min(count, count - steps))
    return lax.ppermute(value, axis, [(source, source + steps) for source in range(leading, last)])


def dot(left, right, dims=(((1,), (0,)), ((), ()))):
    return lax.dot_general(left, right, dims, preferred_element_type=F32)


def halves(value):
    high = value.astype(BF16)
    return high, (value - high.astype(F32)).astype(BF16)


def whole(count):
    return [pl.BlockSpec(memory_space=pltpu.VMEM)] * count


def call(kernel, outs, name, *operands, specs=None, scratch=()):
    return pl.pallas_call(
        kernel,
        out_shape=outs,
        in_specs=whole(len(operands)) if specs is None else specs,
        out_specs=tuple(whole(len(outs))),
        scratch_shapes=scratch,
        compiler_params=pltpu.CompilerParams(vmem_limit_bytes=VMEM_LIMIT),
        name=name,
    )(*operands)


def tails_kernel(streams_ref, tails_ref):
    length = streams_ref.shape[2]
    row = lax.broadcasted_iota(jnp.int32, (2 * ROWS, length), 0)
    lane = lax.broadcasted_iota(jnp.int32, (2 * ROWS, length), 1)
    pick = (lane == row + (length - ROWS)).astype(BF16)
    for stream in range(streams_ref.shape[0]):
        rows = dot(pick, streams_ref[stream], CONTRACT_LANES)
        tails_ref[stream] = rows[:ROWS].astype(BF16)


def filtered_tile(stream, chans, lane, columns, streams_ref, taps_ref, mine_ref, before_ref):
    taps = taps_ref.shape[1]
    signal = streams_ref[stream, chans, :].astype(F32)
    first = stream * taps
    total = columns[:, first : first + 1] * signal
    for shift in range(1, taps):
        total = total + columns[:, first + shift : first + shift + 1] * pltpu.roll(signal, shift, 1)
    change = before_ref[stream, :, chans].astype(F32) - mine_ref[stream, :, chans].astype(F32)
    row = lax.broadcasted_iota(jnp.int32, change.shape, 0)
    head = jnp.zeros_like(change)
    for shift in range(1, taps):
        moved = pltpu.roll(change, shift, 0)
        head = head + jnp.where(row < shift, taps_ref[stream, shift : shift + 1, chans] * moved, 0.0)
    wide = jnp.concatenate([head, jnp.zeros((TILE - ROWS, TILE), F32)], axis=0)
    return total + wide.T


def tap_columns(chans, taps_ref):
    streams, taps = taps_ref.shape[:2]
    rows = [taps_ref[stream, :, chans] for stream in range(streams)]
    rows.append(jnp.zeros((TILE - streams * taps, TILE), F32))
    return jnp.concatenate(rows, axis=0).T


def gate_kernel(streams_ref, taps_ref, mine_ref, before_ref, rates_ref, gated_ref, ends_ref):
    channels, length = gated_ref.shape
    poles, groups = rates_ref.shape
    width = channels // groups
    in_tile = TILE // width
    lane = lax.broadcasted_iota(jnp.int32, (TILE, length), 1)
    lag = (length - 1) - lax.broadcasted_iota(jnp.int32, (poles, length), 1).astype(F32)
    owner = lax.broadcasted_iota(jnp.int32, (poles, TILE), 1) // width

    def tile(index, carry):
        chans = pl.ds(pl.multiple_of(index * TILE, TILE), TILE)
        columns = tap_columns(chans, taps_ref)
        left = filtered_tile(1, chans, lane, columns, streams_ref, taps_ref, mine_ref, before_ref)
        right = filtered_tile(2, chans, lane, columns, streams_ref, taps_ref, mine_ref, before_ref)
        gated = (left * right).astype(BF16)
        gated_ref[chans, :] = gated
        here = pltpu.roll(rates_ref[...], groups - index * in_tile, 1)
        decay = jnp.concatenate(
            [jnp.exp(-here[:, g : g + 1] * lag) for g in range(in_tile)], axis=0
        )
        high, low = halves(decay)
        every = dot(high, gated, CONTRACT_LANES) + dot(low, gated, CONTRACT_LANES)
        ends = jnp.zeros((poles, TILE), F32)
        for g in range(in_tile):
            ends = jnp.where(owner == g, every[g * poles : (g + 1) * poles], ends)
        ends_ref[:, chans] = ends.astype(ends_ref.dtype)
        return carry

    lax.fori_loop(0, channels // TILE, tile, 0)


def inside_kernel(streams_ref, taps_ref, mine_ref, before_ref, rates_ref, coef_ref, skip_ref, gated_ref, query_ref, base_ref):
    channels, length = gated_ref.shape
    poles, groups = rates_ref.shape
    width = channels // groups
    in_tile = TILE // width
    lane = lax.broadcasted_iota(jnp.int32, (TILE, length), 1)
    time = lax.broadcasted_iota(jnp.int32, (poles, length), 1).astype(F32)
    causal = lax.broadcasted_iota(jnp.int32, (length, length), 1) >= lax.broadcasted_iota(
        jnp.int32, (length, length), 0
    )

    def tile(index, carry):
        chans = pl.ds(pl.multiple_of(index * TILE, TILE), TILE)
        columns = tap_columns(chans, taps_ref)
        query_ref[chans, :] = filtered_tile(
            0, chans, lane, columns, streams_ref, taps_ref, mine_ref, before_ref
        )
        skip = jnp.concatenate(
            [skip_ref[:, chans], jnp.zeros((TILE - 1, TILE), F32)], axis=0
        ).T[:, 0:1]
        gated = gated_ref[chans, :]
        here = pltpu.roll(rates_ref[...], groups - index * in_tile, 1)
        coef = pltpu.roll(coef_ref[...], groups - index * in_tile, 1)
        parts = []
        for g in range(in_tile):
            terms = coef[:, g : g + 1] * jnp.exp(-here[:, g : g + 1] * time)
            impulse = jnp.sum(terms, axis=0, keepdims=True)
            spread = jnp.broadcast_to(impulse, (length, length))
            shifted = pltpu.roll(spread, 0, 1, stride=1, stride_axis=0)
            toeplitz = jnp.where(causal, shifted, 0.0).astype(BF16)
            parts.append(dot(gated[g * width : (g + 1) * width], toeplitz))
        base_ref[chans, :] = jnp.concatenate(parts, axis=0) + skip * gated.astype(F32)
        return carry

    lax.fori_loop(0, channels // TILE, tile, 0)


def finish_kernel(me_ref, ends_ref, wide_ref, rates_ref, coef_ref, query_ref, base_ref, mixed_ref):
    channels, length = mixed_ref.shape
    poles, groups = rates_ref.shape
    width = channels // groups
    in_tile = TILE // width
    blocks = ends_ref.shape[0]
    me = me_ref[0]
    step_decay = jnp.exp(-wide_ref[...] * length)

    def earlier(block, state):
        return jnp.where(block < me, step_decay * state + ends_ref[block].astype(F32), state)

    state = lax.fori_loop(0, blocks - 1, earlier, jnp.zeros((poles, channels), F32))
    wide_ref[...] = state
    time = 1.0 + lax.broadcasted_iota(jnp.int32, (poles, length), 1).astype(F32)
    owner = lax.broadcasted_iota(jnp.int32, (poles, TILE), 1) // width

    def tile(index, carry):
        chans = pl.ds(pl.multiple_of(index * TILE, TILE), TILE)
        here = pltpu.roll(rates_ref[...], groups - index * in_tile, 1)
        coef = pltpu.roll(coef_ref[...], groups - index * in_tile, 1)
        entering = wide_ref[:, chans]
        lift = jnp.concatenate(
            [coef[:, g : g + 1] * jnp.exp(-here[:, g : g + 1] * time) for g in range(in_tile)], axis=0
        )
        apart = jnp.concatenate(
            [jnp.where(owner == g, entering, 0.0) for g in range(in_tile)], axis=0
        )
        lift_high, lift_low = halves(lift)
        high, low = halves(apart)
        carried = (
            dot(high, lift_high, CONTRACT_ROWS)
            + dot(low, lift_high, CONTRACT_ROWS)
            + dot(high, lift_low, CONTRACT_ROWS)
        )
        mixed_ref[chans, :] = (query_ref[chans, :] * (base_ref[chans, :] + carried)).astype(BF16)
        return carry

    lax.fori_loop(0, channels // TILE, tile, 0)


def broadcast_exchange(value, axis):
    count = lax.axis_size(axis)
    copies = jnp.broadcast_to(value[None], (count,) + value.shape)
    return lax.all_to_all(copies, axis, split_axis=0, concat_axis=0, tiled=True)


def local(streams, conv_weight, rates, residues, skip, out_weight):
    channels, length = streams.shape[1:]
    groups, poles = rates.shape
    layers = lax.axis_size("tp")
    weight = lax.all_gather(out_weight, "ctx", axis=0, tiled=True)

    rates_t = rates.T
    coef_t = residues.T * jnp.sqrt(2.0 * rates_t) / math.sqrt(poles)
    rates_wide = jnp.repeat(rates_t, channels // groups, axis=1)
    skip_row = skip[None, :]

    shape = jax.ShapeDtypeStruct
    (mine,) = call(tails_kernel, (shape((3, ROWS, channels), BF16),), "tails", streams)
    before = from_behind(mine, "ctx", 1)
    gated, ends = call(
        gate_kernel,
        (shape((channels, length), BF16), shape((poles, channels), BF16)),
        "gate",
        streams, conv_weight, mine, before, rates_t,
    )
    all_ends = broadcast_exchange(ends, "ctx")
    query, base = call(
        inside_kernel,
        (shape((channels, length), F32), shape((channels, length), F32)),
        "inside",
        streams, conv_weight, mine, before, rates_t, coef_t, skip_row, gated,
    )
    me = lax.axis_index("ctx").astype(jnp.int32)[None]
    (mixed,) = call(
        finish_kernel_with_scratch,
        (shape((channels, length), BF16),),
        "finish",
        me, all_ends, rates_wide, rates_t, coef_t, query, base,
        specs=[pl.BlockSpec(memory_space=pltpu.SMEM)] + whole(6),
        scratch=[pltpu.VMEM((poles, channels), F32)],
    )
    features = broadcast_exchange(mixed, "tp").reshape(layers * channels, length)
    summed = lax.dot_general(features, weight, CONTRACT_ROWS, preferred_element_type=F32)
    return summed.astype(BF16)


def finish_kernel_with_scratch(me_ref, ends_ref, wide_ref, rates_ref, coef_ref, query_ref, base_ref, mixed_ref, state_ref):
    state_ref[...] = wide_ref[...]
    finish_kernel(me_ref, ends_ref, state_ref, rates_ref, coef_ref, query_ref, base_ref, mixed_ref)


def solution(mesh):
    return jax.shard_map(
        local,
        mesh=mesh,
        in_specs=(
            P(None, "tp", "ctx"),
            P(None, None, "tp"),
            P("tp", None),
            P("tp", None),
            P("tp"),
            P("ctx", "tp"),
        ),
        out_specs=P("ctx", "tp"),
        check_vma=False,
    )
```

```python
import math

import jax
import jax.numpy as jnp
from jax import lax
from jax.experimental import pallas as pl
from jax.experimental.pallas import tpu as pltpu
from jax.sharding import PartitionSpec as P

F32 = jnp.float32
BF16 = jnp.bfloat16
ROWS = 8
TILE = 128
CORES = 2
VMEM_LIMIT = 24 * 1024 * 1024
PLAIN = (((1,), (0,)), ((), ()))
CONTRACT_LANES = (((1,), (1,)), ((), ()))


def from_behind(value, axis, steps):
    count = lax.axis_size(axis)
    leading, last = (max(0, -steps), min(count, count - steps))
    return lax.ppermute(value, axis, [(source, source + steps) for source in range(leading, last)])


def dot(left, right, dims=PLAIN):
    return lax.dot_general(left, right, dims, preferred_element_type=F32)


def halves(value):
    high = value.astype(BF16)
    return high, (value - high.astype(F32)).astype(BF16)


def iota(shape, axis):
    return lax.broadcasted_iota(jnp.int32, shape, axis)


def identity(size):
    return (iota((size, size), 0) == iota((size, size), 1)).astype(BF16)


def turned(value, unit):
    return dot(unit, value, CONTRACT_LANES)


def whole(count):
    return [pl.BlockSpec(memory_space=pltpu.VMEM)] * count


def call(kernel, outs, name, *operands, specs=None, scratch=(), flops=10**8):
    return pl.pallas_call(
        kernel,
        out_shape=tuple(jax.ShapeDtypeStruct(*out) for out in outs),
        in_specs=whole(len(operands)) if specs is None else specs,
        out_specs=tuple(whole(len(outs))),
        scratch_shapes=scratch,
        compiler_params=pltpu.CompilerParams(vmem_limit_bytes=VMEM_LIMIT),
        cost_estimate=pl.CostEstimate(flops=flops, bytes_accessed=10**6, transcendentals=0),
        name=name,
    )(*operands)


def tile_of(index, size=TILE):
    return pl.ds(pl.multiple_of(index * size, size), size)


def tails_kernel(streams_ref, tails_ref):
    length = streams_ref.shape[2]
    pick = (iota((2 * ROWS, length), 1) == iota((2 * ROWS, length), 0) + (length - ROWS)).astype(BF16)
    for stream in range(streams_ref.shape[0]):
        rows = dot(pick, streams_ref[stream], CONTRACT_LANES)
        tails_ref[stream] = rows[:ROWS].astype(BF16)


def short_conv(stream, chans, rows, padded_ref, taps_ref):
    total = None
    for shift in range(taps_ref.shape[1]):
        term = taps_ref[stream, shift : shift + 1, chans] * padded_ref[stream, pl.ds(ROWS - shift, rows), :]
        total = term if total is None else total + term
    return total


def prepare_kernel(
    streams_ref, taps_ref, rates_ref, residues_ref,
    heads_ref, query_ref, gated_ref, decay_ref, lift_ref, toeplitz_ref, step_ref, padded_ref,
):
    channels, length = streams_ref.shape[1:]
    poles, groups = rates_ref.shape
    width = channels // groups
    in_tile = TILE // width
    unit = identity(length)
    time = iota((poles, length), 1).astype(F32)
    owner = iota((poles, TILE), 1) // width
    member = (iota((in_tile, in_tile * poles), 1) // poles == iota((in_tile, in_tile * poles), 0)).astype(BF16)
    causal = iota((length, length), 1) >= iota((length, length), 0)
    for stream in range(3):
        padded_ref[stream, :ROWS, :] = jnp.zeros((ROWS, TILE), F32)

    def tile(index, carry):
        chans = tile_of(index)
        for stream in range(3):
            padded_ref[stream, ROWS:, :] = turned(streams_ref[stream, chans, :], unit)
            heads_ref[stream, :, chans] = padded_ref[stream, ROWS : 2 * ROWS, :]
        query_ref[:, chans] = short_conv(0, chans, length, padded_ref, taps_ref)
        left = short_conv(1, chans, length, padded_ref, taps_ref)
        gated_ref[:, chans] = left * short_conv(2, chans, length, padded_ref, taps_ref)

        shift = groups - index * in_tile
        rates = pltpu.roll(rates_ref[...], shift, 1)
        coef = pltpu.roll(residues_ref[...], shift, 1) * jnp.sqrt(2.0 * rates) / math.sqrt(poles)
        decay, impulse, lift = [], [], []
        wide = jnp.zeros((poles, TILE), F32)
        for g in range(in_tile):
            rate = jnp.broadcast_to(rates[:, g : g + 1], (poles, length))
            scale = jnp.broadcast_to(coef[:, g : g + 1], (poles, length))
            decay.append(jnp.exp(-rate * ((length - 1) - time)))
            impulse.append(scale * jnp.exp(-rate * time))
            lift.append(scale * jnp.exp(-rate * (time + 1.0)))
            wide = jnp.where(owner == g, rate[:, :TILE], wide)
        step_ref[:, chans] = jnp.exp(-wide * length)
        states = tile_of(index, in_tile * poles)
        for part, value in enumerate(halves(jnp.concatenate(decay, axis=0))):
            decay_ref[part, states, :] = value
        for part, value in enumerate(halves(jnp.concatenate(lift, axis=0))):
            lift_ref[part, :, states] = turned(value, unit).astype(BF16)
        high, low = halves(jnp.concatenate(impulse, axis=0))
        response = dot(member, high) + dot(member, low)
        for g in range(in_tile):
            spread = jnp.broadcast_to(response[g : g + 1], (length, length))
            shifted = pltpu.roll(spread, 0, 1, stride=1, stride_axis=0)
            block = jnp.where(causal, shifted, 0.0).astype(BF16)
            toeplitz_ref[index * (in_tile // 2) + g // 2, :, (g % 2) * length : (g % 2 + 1) * length] = block
        return carry

    lax.fori_loop(0, channels // TILE, tile, 0)


def states_kernel(before_ref, heads_ref, taps_ref, gated_ref, decay_ref, ends_ref, final_ref, first_ref, padded_ref):
    length, channels = gated_ref.shape
    poles = ends_ref.shape[1]
    in_tile = decay_ref.shape[1] // poles * TILE // channels
    owner = iota((poles, TILE), 1) // (TILE // in_tile)

    def tile(index, carry):
        chans = tile_of(index)
        for stream in range(3):
            padded_ref[stream, :ROWS, :] = before_ref[stream, :, chans].astype(F32)
            padded_ref[stream, ROWS:, :] = heads_ref[stream, :, chans]
        first_ref[:, chans] = short_conv(0, chans, ROWS, padded_ref, taps_ref)
        head = short_conv(1, chans, ROWS, padded_ref, taps_ref) * short_conv(2, chans, ROWS, padded_ref, taps_ref)
        gated = jnp.concatenate([head, gated_ref[ROWS:, chans]], axis=0).astype(BF16)
        final_ref[:, chans] = gated
        states = tile_of(index, in_tile * poles)
        every = dot(decay_ref[0, states, :], gated) + dot(decay_ref[1, states, :], gated)
        ends = jnp.zeros((poles, TILE), F32)
        for g in range(in_tile):
            ends = jnp.where(owner == g, every[g * poles : (g + 1) * poles], ends)
        ends = ends.astype(BF16)
        for block in range(ends_ref.shape[0]):
            ends_ref[block, :, chans] = ends
        return carry

    lax.fori_loop(0, channels // TILE, tile, 0)


def inside_kernel(gated_ref, toeplitz_ref, skip_ref, base_ref):
    length, channels = gated_ref.shape
    pairs = toeplitz_ref.shape[0] * TILE // channels
    width = TILE // (2 * pairs)
    unit = identity(length)

    def tile(index, carry):
        chans = tile_of(index)
        gated = gated_ref[:, chans]
        signal = turned(gated, unit).astype(BF16)
        parts = []
        for pair in range(pairs):
            both = dot(signal[pair * 2 * width : (pair + 1) * 2 * width], toeplitz_ref[index * pairs + pair])
            parts += [both[:width, :length], both[width:, length:]]
        high, low = halves(jnp.concatenate(parts, axis=0))
        base_ref[:, chans] = turned(high, unit) + turned(low, unit) + skip_ref[:, chans] * gated.astype(F32)
        return carry

    lax.fori_loop(0, channels // TILE, tile, 0)


def finish_kernel(me_ref, ends_ref, step_ref, lift_ref, query_ref, first_ref, base_ref, mixed_ref, state_ref):
    length, channels = mixed_ref.shape
    poles = step_ref.shape[0]
    in_tile = lift_ref.shape[2] // poles * TILE // channels
    me = me_ref[0]

    def earlier(block, state):
        return jnp.where(block < me, step_ref[...] * state + ends_ref[block].astype(F32), state)

    state_ref[...] = lax.fori_loop(0, ends_ref.shape[0] - 1, earlier, jnp.zeros((poles, channels), F32))
    owner = iota((poles, TILE), 1) // (TILE // in_tile)

    def tile(index, carry):
        chans = tile_of(index)
        entering = state_ref[:, chans]
        apart = jnp.concatenate([jnp.where(owner == g, entering, 0.0) for g in range(in_tile)], axis=0)
        high, low = halves(apart)
        states = tile_of(index, in_tile * poles)
        lift = lift_ref[0, :, states]
        carried = dot(lift, high) + dot(lift, low) + dot(lift_ref[1, :, states], high)
        query = jnp.concatenate([first_ref[:, chans], query_ref[ROWS:, chans]], axis=0)
        mixed_ref[:, chans] = (query * (base_ref[:, chans] + carried)).astype(BF16)
        return carry

    lax.fori_loop(0, channels // TILE, tile, 0)


def local(streams, conv_weight, rates, residues, skip, out_weight):
    channels, length = streams.shape[1:]
    groups, poles = rates.shape
    blocks, layers = lax.axis_size("ctx"), lax.axis_size("tp")
    rows, features = out_weight.shape
    core_groups = [list(range(core, blocks, CORES)) for core in range(CORES)]
    weight = lax.all_gather(out_weight, "ctx", axis=0, axis_index_groups=core_groups)

    (mine,) = call(tails_kernel, [((3, ROWS, channels), BF16)], "tails", streams)
    before = from_behind(mine, "ctx", 1)
    heads, query, gated, decay, lift, toeplitz, step = call(
        prepare_kernel,
        [
            ((3, ROWS, channels), F32),
            ((length, channels), F32),
            ((length, channels), F32),
            ((2, groups * poles, length), BF16),
            ((2, length, groups * poles), BF16),
            ((groups // 2, length, 2 * length), BF16),
            ((poles, channels), F32),
        ],
        "prepare",
        streams, conv_weight, rates.T, residues.T,
        scratch=[pltpu.VMEM((3, ROWS + length, TILE), F32)],
        flops=10**9,
    )
    ends, gated, first = call(
        states_kernel,
        [((blocks, poles, channels), BF16), ((length, channels), BF16), ((ROWS, channels), F32)],
        "states",
        before, heads, conv_weight, gated, decay,
        scratch=[pltpu.VMEM((3, 2 * ROWS, TILE), F32)],
    )
    all_ends = lax.all_to_all(ends, "ctx", split_axis=0, concat_axis=0, tiled=True)
    (base,) = call(
        inside_kernel, [((length, channels), F32)], "inside", gated, toeplitz, skip[None, :], flops=10**9
    )
    me = lax.axis_index("ctx").astype(jnp.int32)[None]
    (mixed,) = call(
        finish_kernel,
        [((length, channels), BF16)],
        "finish",
        me, all_ends, step, lift, query, first, base,
        specs=[pl.BlockSpec(memory_space=pltpu.SMEM)] + whole(6),
        scratch=[pltpu.VMEM((poles, channels), F32)],
    )
    share = channels // CORES
    by_core = mixed.reshape(length, share // rows, CORES, rows).transpose(2, 0, 1, 3)
    copies = jnp.broadcast_to(
        by_core.reshape(CORES, 1, length, share), (CORES, layers, length, share)
    ).reshape(CORES * layers, length, share)
    columns = [
        [(chip * CORES + core) * layers + layer for core in range(CORES) for layer in range(layers)]
        for chip in range(blocks // CORES)
    ]
    arrived = lax.all_to_all(
        copies, ("ctx", "tp"), split_axis=0, concat_axis=0, axis_index_groups=columns, tiled=True
    ).reshape(CORES, layers, length, share)
    summed = jnp.einsum(
        "cltk,lke->cte", arrived, weight.reshape(layers, share, features), preferred_element_type=F32
    )
    core = lax.axis_index("ctx") % CORES
    other = lax.dynamic_index_in_dim(summed, 1 - core, 0, keepdims=False).astype(BF16)
    mine = lax.dynamic_index_in_dim(summed, core, 0, keepdims=False)
    other = lax.ppermute(other, "ctx", [(source, source ^ 1) for source in range(blocks)])
    return (mine + other.astype(F32)).astype(BF16)


def solution(mesh):
    return jax.shard_map(
        local,
        mesh=mesh,
        in_specs=(
            P(None, "tp", "ctx"),
            P(None, None, "tp"),
            P("tp", None),
            P("tp", None),
            P("tp"),
            P("ctx", "tp"),
        ),
        out_specs=P("ctx", "tp"),
        check_vma=False,
    )
```

```python
import functools
import math

import jax
import jax.numpy as jnp
from jax import lax
from jax.experimental import pallas as pl
from jax.experimental.pallas import tpu as pltpu
from jax.sharding import PartitionSpec as P

F32 = jnp.float32
BF16 = jnp.bfloat16
ROWS = 8
TILE = 128
CORES = 2
VMEM_LIMIT = 24 * 1024 * 1024
FETCH_LIMIT = 58 * 1024 * 1024
PLAIN = (((1,), (0,)), ((), ()))
CONTRACT_LANES = (((1,), (1,)), ((), ()))


def from_behind(value, axis, steps):
    count = lax.axis_size(axis)
    leading, last = (max(0, -steps), min(count, count - steps))
    return lax.ppermute(value, axis, [(source, source + steps) for source in range(leading, last)])


def dot(left, right, dims=PLAIN):
    return lax.dot_general(left, right, dims, preferred_element_type=F32)


def halves(value):
    high = value.astype(BF16)
    return high, (value - high.astype(F32)).astype(BF16)


def iota(shape, axis):
    return lax.broadcasted_iota(jnp.int32, shape, axis)


def identity(size):
    return (iota((size, size), 0) == iota((size, size), 1)).astype(BF16)


def turned(value, unit):
    return dot(unit, value, CONTRACT_LANES)


def whole(count):
    return [pl.BlockSpec(memory_space=pltpu.VMEM)] * count


def call(kernel, outs, name, *operands, specs=None, scratch=(), flops=10**8, limit=VMEM_LIMIT):
    return pl.pallas_call(
        kernel,
        out_shape=tuple(jax.ShapeDtypeStruct(*out) for out in outs),
        in_specs=whole(len(operands)) if specs is None else specs,
        out_specs=tuple(whole(len(outs))),
        scratch_shapes=scratch,
        compiler_params=pltpu.CompilerParams(vmem_limit_bytes=limit),
        cost_estimate=pl.CostEstimate(flops=flops, bytes_accessed=10**6, transcendentals=0),
        name=name,
    )(*operands)


def tile_of(index, size=TILE):
    return pl.ds(pl.multiple_of(index * size, size), size)


def unrolled(count, body):
    def step(index, carry):
        body(index)
        return carry

    lax.fori_loop(0, count, step, 0, unroll=math.gcd(count, 4))


def tails_kernel(
    streams_hbm, taps_hbm, rates_hbm, residues_hbm, skip_hbm,
    tails_ref, streams_ref, taps_ref, rates_ref, residues_ref, skip_ref, sems,
):
    pairs = [
        (streams_hbm, streams_ref),
        (taps_hbm, taps_ref),
        (rates_hbm, rates_ref),
        (residues_hbm, residues_ref),
        (skip_hbm, skip_ref),
    ]
    copies = [pltpu.make_async_copy(src, dst, sems.at[at]) for at, (src, dst) in enumerate(pairs)]
    for copy in copies:
        copy.start()
    for copy in copies:
        copy.wait()
    length = streams_ref.shape[2]
    pick = (iota((2 * ROWS, length), 1) == iota((2 * ROWS, length), 0) + (length - ROWS)).astype(BF16)
    for stream in range(streams_ref.shape[0]):
        rows = dot(pick, streams_ref[stream], CONTRACT_LANES)
        tails_ref[stream] = rows[:ROWS].astype(BF16)


def short_conv(stream, chans, rows, padded, taps_ref):
    total = None
    for shift in range(taps_ref.shape[1]):
        term = taps_ref[stream, shift : shift + 1, chans] * padded[pl.ds(ROWS - shift, rows), :]
        total = term if total is None else total + term
    return total


def prepare_kernel(streams_ref, taps_ref, rates_ref, heads_ref, query_ref, gated_ref, decay_ref, step_ref, padded_ref):
    channels, length = streams_ref.shape[1:]
    poles, groups = rates_ref.shape
    width = channels // groups
    in_tile = TILE // width
    unit = identity(length)
    lag = (length - 1) - iota((poles, length), 1).astype(F32)
    owner = iota((poles, TILE), 1) // width

    def turn(index):
        chans = tile_of(index)
        for stream in range(3):
            tokens = turned(streams_ref[stream, chans, :], unit)
            padded_ref[index * 3 + stream, :ROWS, :] = jnp.zeros((ROWS, TILE), F32)
            padded_ref[index * 3 + stream, ROWS:, :] = tokens
            heads_ref[stream, :, chans] = tokens[:ROWS]

    def decays(index):
        rates = pltpu.roll(rates_ref[...], groups - index * in_tile, 1)
        decay = []
        wide = jnp.zeros((poles, TILE), F32)
        for g in range(in_tile):
            rate = jnp.broadcast_to(rates[:, g : g + 1], (poles, length))
            decay.append(jnp.exp(-rate * lag))
            wide = jnp.where(owner == g, rate[:, :TILE], wide)
        step_ref[:, tile_of(index)] = jnp.exp(-wide * length)
        for part, value in enumerate(halves(jnp.concatenate(decay, axis=0))):
            decay_ref[part, tile_of(index, in_tile * poles), :] = value

    def filters(index):
        chans = tile_of(index)
        query, left, right = (
            short_conv(stream, chans, length, padded_ref.at[index * 3 + stream], taps_ref) for stream in range(3)
        )
        query_ref[:, chans] = query
        gated_ref[:, chans] = left * right

    unrolled(channels // TILE, turn)
    unrolled(channels // TILE, decays)
    unrolled(channels // TILE, filters)


def states_kernel(before_ref, heads_ref, taps_ref, gated_ref, decay_ref, ends_ref, final_ref, first_ref, padded_ref):
    length, channels = gated_ref.shape
    poles = ends_ref.shape[1]
    in_tile = decay_ref.shape[1] // poles * TILE // channels
    owner = iota((poles, TILE), 1) // (TILE // in_tile)

    def begin(index):
        chans = tile_of(index)
        for stream in range(3):
            padded_ref[index * 3 + stream, :ROWS, :] = before_ref[stream, :, chans].astype(F32)
            padded_ref[index * 3 + stream, ROWS:, :] = heads_ref[stream, :, chans]
        query, left, right = (
            short_conv(stream, chans, ROWS, padded_ref.at[index * 3 + stream], taps_ref) for stream in range(3)
        )
        first_ref[:, chans] = query
        final_ref[:, chans] = jnp.concatenate([left * right, gated_ref[ROWS:, chans]], axis=0).astype(BF16)

    def leave(index):
        chans = tile_of(index)
        gated = final_ref[:, chans]
        states = tile_of(index, in_tile * poles)
        every = dot(decay_ref[0, states, :], gated) + dot(decay_ref[1, states, :], gated)
        ends = jnp.zeros((poles, TILE), F32)
        for g in range(in_tile):
            ends = jnp.where(owner == g, every[g * poles : (g + 1) * poles], ends)
        ends = ends.astype(BF16)
        for block in range(ends_ref.shape[0]):
            ends_ref[block, :, chans] = ends

    unrolled(channels // TILE, begin)
    unrolled(channels // TILE, leave)


def inside_kernel(gated_ref, skip_ref, rates_ref, residues_ref, lift_ref, base_ref):
    length, channels = gated_ref.shape
    poles, groups = rates_ref.shape
    width = channels // groups
    in_tile = TILE // width
    unit = identity(length)
    time = iota((poles, length), 1).astype(F32)
    member = (iota((in_tile, in_tile * poles), 1) // poles == iota((in_tile, in_tile * poles), 0)).astype(BF16)
    causal = iota((length, length), 1) >= iota((length, length), 0)

    def tile(index):
        chans = tile_of(index)
        shift = groups - index * in_tile
        rates = pltpu.roll(rates_ref[...], shift, 1)
        coef = pltpu.roll(residues_ref[...], shift, 1) * jnp.sqrt(2.0 * rates) / math.sqrt(poles)
        impulse, lift = [], []
        for g in range(in_tile):
            rate = jnp.broadcast_to(rates[:, g : g + 1], (poles, length))
            scale = jnp.broadcast_to(coef[:, g : g + 1], (poles, length))
            impulse.append(scale * jnp.exp(-rate * time))
            lift.append(scale * jnp.exp(-rate * (time + 1.0)))
        states = tile_of(index, in_tile * poles)
        for part, value in enumerate(halves(jnp.concatenate(lift, axis=0))):
            lift_ref[part, :, states] = turned(value, unit).astype(BF16)
        high, low = halves(jnp.concatenate(impulse, axis=0))
        response = dot(member, high) + dot(member, low)
        gated = gated_ref[:, chans]
        signal = turned(gated, unit).astype(BF16)
        parts = []
        for pair in range(in_tile // 2):
            blocks = []
            for g in (2 * pair, 2 * pair + 1):
                spread = jnp.broadcast_to(response[g : g + 1], (length, length))
                shifted = pltpu.roll(spread, 0, 1, stride=1, stride_axis=0)
                blocks.append(jnp.where(causal, shifted, 0.0).astype(BF16))
            both = dot(signal[pair * 2 * width : (pair + 1) * 2 * width], jnp.concatenate(blocks, axis=1))
            parts += [both[:width, :length], both[width:, length:]]
        high, low = halves(jnp.concatenate(parts, axis=0))
        base_ref[:, chans] = turned(high, unit) + turned(low, unit) + skip_ref[:, chans] * gated.astype(F32)

    unrolled(channels // TILE, tile)


def finish_kernel(at_ref, ends_ref, step_ref, lift_ref, query_ref, first_ref, base_ref, mine_ref, other_ref, mixed_ref, state_ref):
    length, channels = mixed_ref.shape
    poles = step_ref.shape[0]
    in_tile = lift_ref.shape[2] // poles * TILE // channels
    me, core = at_ref[0], at_ref[1]

    def earlier(block, state):
        return jnp.where(block < me, step_ref[...] * state + ends_ref[block].astype(F32), state)

    state_ref[...] = lax.fori_loop(0, ends_ref.shape[0] - 1, earlier, jnp.zeros((poles, channels), F32))
    owner = iota((poles, TILE), 1) // (TILE // in_tile)

    def tile(index):
        chans = tile_of(index)
        entering = state_ref[:, chans]
        apart = jnp.concatenate([jnp.where(owner == g, entering, 0.0) for g in range(in_tile)], axis=0)
        high, low = halves(apart)
        states = tile_of(index, in_tile * poles)
        lift = lift_ref[0, :, states]
        carried = dot(lift, high) + dot(lift, low) + dot(lift_ref[1, :, states], high)
        query = jnp.concatenate([first_ref[:, chans], query_ref[ROWS:, chans]], axis=0)
        mixed_ref[:, chans] = (query * (base_ref[:, chans] + carried)).astype(BF16)

    unrolled(channels // TILE, tile)
    share = channels // CORES
    mine_ref[...] = mixed_ref[:, tile_of(core, share)]
    other_ref[...] = mixed_ref[:, tile_of(1 - core, share)]


def project_kernel(place, at_ref, own_ref, below_ref, above_ref, middle_ref, far_ref, weight_hbm, mine_ref, other_ref, weight_ref, sems):
    layer = at_ref[0]
    edge = (layer == 0) | (layer == 3)
    sources = [layer, jnp.where(layer == 0, 1, layer - 1), (layer + 2) % 4, jnp.where(edge, 3 - layer, layer + 1)]
    copies = []
    for at, source in enumerate(sources):
        row = sum(jnp.where(source == index, place[index], 0) for index in range(4))
        copies.append(pltpu.make_async_copy(weight_hbm.at[row], weight_ref.at[at], sems.at[at]))
        copies[-1].start()
    blocks = [
        lambda: own_ref[...],
        lambda: jnp.where(layer == 0, above_ref[...], below_ref[...]),
        lambda: middle_ref[...],
        lambda: jnp.where(edge, far_ref[...], above_ref[...]),
    ]
    total = None
    for copy, block, rows in zip(copies, blocks, range(4)):
        copy.wait()
        term = dot(block(), weight_ref[rows])
        total = term if total is None else total + term
    length = mine_ref.shape[0]
    mine_ref[...] = total[:length]
    other_ref[...] = total[length:].astype(BF16)


def over_layers(block):
    layer = lax.axis_index("tp")
    below = lax.ppermute(block, "tp", [(0, 1), (1, 2), (2, 3)])
    above = lax.ppermute(block, "tp", [(1, 0), (2, 1), (3, 2)])
    far = lax.ppermute(block, "tp", [(0, 3), (3, 0)])
    onward = jnp.where(layer == 1, above, jnp.where(layer == 2, below, block))
    middle = lax.ppermute(onward, "tp", [(0, 2), (3, 1), (2, 3), (1, 0)])
    return below, above, middle, far


def local(streams, conv_weight, rates, residues, skip, out_weight):
    channels, length = streams.shape[1:]
    groups, poles = rates.shape
    blocks, layers = lax.axis_size("ctx"), lax.axis_size("tp")
    rows, features = out_weight.shape
    share = channels // CORES
    chips = blocks // CORES
    ring = [0, 1, 3, 2] if chips == 4 and rows == share else list(range(chips))
    core_groups = [[chip * CORES + core for chip in ring] for core in range(CORES)]
    weight = lax.all_gather(out_weight, "ctx", axis=0, axis_index_groups=core_groups)
    weight = weight.reshape(layers, share, features)
    place = ring if rows == share else list(range(layers))

    tails, streams, conv_weight, rates, residues, skip = call(
        tails_kernel,
        [
            ((3, ROWS, channels), BF16),
            (streams.shape, BF16),
            (conv_weight.shape, F32),
            ((poles, groups), F32),
            ((poles, groups), F32),
            ((1, channels), F32),
        ],
        "tails",
        streams, conv_weight, rates.T, residues.T, skip[None, :],
        specs=[pl.BlockSpec(memory_space=pltpu.HBM)] * 5,
        scratch=[pltpu.SemaphoreType.DMA((5,))],
        limit=FETCH_LIMIT,
    )
    before = from_behind(tails, "ctx", 1)
    tiles = channels // TILE
    heads, query, gated, decay, step = call(
        prepare_kernel,
        [
            ((3, ROWS, channels), F32),
            ((length, channels), F32),
            ((length, channels), F32),
            ((2, groups * poles, length), BF16),
            ((poles, channels), F32),
        ],
        "prepare",
        streams, conv_weight, rates,
        scratch=[pltpu.VMEM((3 * tiles, ROWS + length, TILE), F32)],
        flops=10**9,
    )
    ends, gated, first = call(
        states_kernel,
        [((blocks, poles, channels), BF16), ((length, channels), BF16), ((ROWS, channels), F32)],
        "states",
        before, heads, conv_weight, gated, decay,
        scratch=[pltpu.VMEM((3 * tiles, 2 * ROWS, TILE), F32)],
    )
    all_ends = lax.all_to_all(ends, "ctx", split_axis=0, concat_axis=0, tiled=True)
    lift, base = call(
        inside_kernel,
        [((2, length, groups * poles), BF16), ((length, channels), F32)],
        "inside",
        gated, skip, rates, residues,
        flops=10**9,
    )
    me = lax.axis_index("ctx").astype(jnp.int32)
    core = me % CORES
    smem = [pl.BlockSpec(memory_space=pltpu.SMEM)]
    outs = [((length, share), BF16), ((length, share), BF16), ((length, channels), BF16)]
    mine, other, mixed = call(
        finish_kernel,
        outs,
        "finish",
        jnp.stack([me, core]), all_ends, step, lift, query, first, base,
        specs=smem + whole(6),
        scratch=[pltpu.VMEM((poles, channels), F32)],
    )
    if rows != share:
        by_core = mixed.reshape(length, share // rows, CORES, rows).transpose(2, 0, 1, 3)
        by_core = by_core.reshape(CORES, length, share)
        mine = lax.dynamic_index_in_dim(by_core, core, 0, keepdims=False)
        other = lax.dynamic_index_in_dim(by_core, 1 - core, 0, keepdims=False)
    siblings = [(source, source ^ 1) for source in range(blocks)]
    block = jnp.concatenate([mine, lax.ppermute(other, "ctx", siblings)], axis=0)
    layer = lax.axis_index("tp").astype(jnp.int32)
    mine, other = call(
        functools.partial(project_kernel, place),
        [((length, features), F32), ((length, features), BF16)],
        "project",
        layer[None], block, *over_layers(block), weight,
        specs=smem + whole(5) + [pl.BlockSpec(memory_space=pltpu.HBM)],
        scratch=[pltpu.VMEM((layers, share, features), BF16), pltpu.SemaphoreType.DMA((layers,))],
        limit=FETCH_LIMIT,
    )
    other = lax.ppermute(other, "ctx", siblings)
    return (mine + other.astype(F32)).astype(BF16)


def solution(mesh):
    return jax.shard_map(
        local,
        mesh=mesh,
        in_specs=(
            P(None, "tp", "ctx"),
            P(None, None, "tp"),
            P("tp", None),
            P("tp", None),
            P("tp"),
            P("ctx", "tp"),
        ),
        out_specs=P("ctx", "tp"),
        check_vma=False,
    )
```

```python
import math

import jax
import jax.numpy as jnp
from jax import lax
from jax.experimental import pallas as pl
from jax.experimental.pallas import tpu as pltpu
from jax.sharding import PartitionSpec as P

F32 = jnp.float32
BF16 = jnp.bfloat16
ROWS = 8
TILE = 128
CORES = 2
VMEM_LIMIT = 24 * 1024 * 1024
FETCH_LIMIT = 52 * 1024 * 1024
PLAIN = (((1,), (0,)), ((), ()))
CONTRACT_LANES = (((1,), (1,)), ((), ()))


def from_behind(value, axis, steps):
    count = lax.axis_size(axis)
    leading, last = (max(0, -steps), min(count, count - steps))
    return lax.ppermute(value, axis, [(source, source + steps) for source in range(leading, last)])


def dot(left, right, dims=PLAIN):
    return lax.dot_general(left, right, dims, preferred_element_type=F32)


def halves(value):
    high = value.astype(BF16)
    return high, (value - high.astype(F32)).astype(BF16)


def iota(shape, axis):
    return lax.broadcasted_iota(jnp.int32, shape, axis)


def identity(size):
    return (iota((size, size), 0) == iota((size, size), 1)).astype(BF16)


def turned(value, unit):
    return dot(unit, value, CONTRACT_LANES)


def whole(count):
    return [pl.BlockSpec(memory_space=pltpu.VMEM)] * count


def call(kernel, outs, name, *operands, specs=None, scratch=(), flops=10**8, limit=VMEM_LIMIT):
    return pl.pallas_call(
        kernel,
        out_shape=tuple(jax.ShapeDtypeStruct(*out) for out in outs),
        in_specs=whole(len(operands)) if specs is None else specs,
        out_specs=tuple(whole(len(outs))),
        scratch_shapes=scratch,
        compiler_params=pltpu.CompilerParams(vmem_limit_bytes=limit),
        cost_estimate=pl.CostEstimate(flops=flops, bytes_accessed=10**6, transcendentals=0),
        name=name,
    )(*operands)


def tile_of(index, size=TILE):
    return pl.ds(pl.multiple_of(index * size, size), size)


def unrolled(count, body):
    def step(index, carry):
        body(index)
        return carry

    lax.fori_loop(0, count, step, 0, unroll=math.gcd(count, 4))


def tails_kernel(
    streams_hbm, taps_hbm, rates_hbm, residues_hbm, skip_hbm,
    tails_ref, streams_ref, taps_ref, rates_ref, residues_ref, skip_ref, sems,
):
    pairs = [
        (streams_hbm, streams_ref),
        (taps_hbm, taps_ref),
        (rates_hbm, rates_ref),
        (residues_hbm, residues_ref),
        (skip_hbm, skip_ref),
    ]
    copies = [pltpu.make_async_copy(src, dst, sems.at[at]) for at, (src, dst) in enumerate(pairs)]
    for copy in copies:
        copy.start()
    for copy in copies:
        copy.wait()
    length = streams_ref.shape[2]
    pick = (iota((2 * ROWS, length), 1) == iota((2 * ROWS, length), 0) + (length - ROWS)).astype(BF16)
    for stream in range(streams_ref.shape[0]):
        rows = dot(pick, streams_ref[stream], CONTRACT_LANES)
        tails_ref[stream] = rows[:ROWS].astype(BF16)


def short_conv(stream, chans, rows, padded, taps_ref):
    total = None
    for shift in range(taps_ref.shape[1]):
        term = taps_ref[stream, shift : shift + 1, chans] * padded[pl.ds(ROWS - shift, rows), :]
        total = term if total is None else total + term
    return total


def prepare_kernel(streams_ref, taps_ref, rates_ref, heads_ref, query_ref, gated_ref, decay_ref, step_ref, padded_ref):
    channels, length = streams_ref.shape[1:]
    poles, groups = rates_ref.shape
    width = channels // groups
    in_tile = TILE // width
    unit = identity(length)
    lag = (length - 1) - iota((poles, length), 1).astype(F32)
    owner = iota((poles, TILE), 1) // width

    def turn(index):
        chans = tile_of(index)
        for stream in range(3):
            tokens = turned(streams_ref[stream, chans, :], unit)
            padded_ref[index * 3 + stream, :ROWS, :] = jnp.zeros((ROWS, TILE), F32)
            padded_ref[index * 3 + stream, ROWS:, :] = tokens
            heads_ref[stream, :, chans] = tokens[:ROWS]

    def decays(index):
        rates = pltpu.roll(rates_ref[...], groups - index * in_tile, 1)
        decay = []
        wide = jnp.zeros((poles, TILE), F32)
        for g in range(in_tile):
            rate = jnp.broadcast_to(rates[:, g : g + 1], (poles, length))
            decay.append(jnp.exp(-rate * lag))
            wide = jnp.where(owner == g, rate[:, :TILE], wide)
        step_ref[:, tile_of(index)] = jnp.exp(-wide * length)
        for part, value in enumerate(halves(jnp.concatenate(decay, axis=0))):
            decay_ref[part, tile_of(index, in_tile * poles), :] = value

    def filters(index):
        chans = tile_of(index)
        query, left, right = (
            short_conv(stream, chans, length, padded_ref.at[index * 3 + stream], taps_ref) for stream in range(3)
        )
        query_ref[:, chans] = query
        gated_ref[:, chans] = left * right

    unrolled(channels // TILE, turn)
    unrolled(channels // TILE, decays)
    unrolled(channels // TILE, filters)


def states_kernel(before_ref, heads_ref, taps_ref, gated_ref, decay_ref, ends_ref, final_ref, first_ref, padded_ref):
    length, channels = gated_ref.shape
    poles = ends_ref.shape[1]
    in_tile = decay_ref.shape[1] // poles * TILE // channels
    owner = iota((poles, TILE), 1) // (TILE // in_tile)

    def begin(index):
        chans = tile_of(index)
        for stream in range(3):
            padded_ref[index * 3 + stream, :ROWS, :] = before_ref[stream, :, chans].astype(F32)
            padded_ref[index * 3 + stream, ROWS:, :] = heads_ref[stream, :, chans]
        query, left, right = (
            short_conv(stream, chans, ROWS, padded_ref.at[index * 3 + stream], taps_ref) for stream in range(3)
        )
        first_ref[:, chans] = query
        final_ref[:, chans] = jnp.concatenate([left * right, gated_ref[ROWS:, chans]], axis=0).astype(BF16)

    def leave(index):
        chans = tile_of(index)
        gated = final_ref[:, chans]
        states = tile_of(index, in_tile * poles)
        every = dot(decay_ref[0, states, :], gated) + dot(decay_ref[1, states, :], gated)
        ends = jnp.zeros((poles, TILE), F32)
        for g in range(in_tile):
            ends = jnp.where(owner == g, every[g * poles : (g + 1) * poles], ends)
        ends = ends.astype(BF16)
        for block in range(ends_ref.shape[0]):
            ends_ref[block, :, chans] = ends

    unrolled(channels // TILE, begin)
    unrolled(channels // TILE, leave)


def inside_kernel(gated_ref, skip_ref, rates_ref, residues_ref, lift_ref, base_ref):
    length, channels = gated_ref.shape
    poles, groups = rates_ref.shape
    width = channels // groups
    in_tile = TILE // width
    unit = identity(length)
    time = iota((poles, length), 1).astype(F32)
    member = (iota((in_tile, in_tile * poles), 1) // poles == iota((in_tile, in_tile * poles), 0)).astype(BF16)
    causal = iota((length, length), 1) >= iota((length, length), 0)

    def tile(index):
        chans = tile_of(index)
        shift = groups - index * in_tile
        rates = pltpu.roll(rates_ref[...], shift, 1)
        coef = pltpu.roll(residues_ref[...], shift, 1) * jnp.sqrt(2.0 * rates) / math.sqrt(poles)
        impulse, lift = [], []
        for g in range(in_tile):
            rate = jnp.broadcast_to(rates[:, g : g + 1], (poles, length))
            scale = jnp.broadcast_to(coef[:, g : g + 1], (poles, length))
            impulse.append(scale * jnp.exp(-rate * time))
            lift.append(scale * jnp.exp(-rate * (time + 1.0)))
        states = tile_of(index, in_tile * poles)
        for part, value in enumerate(halves(jnp.concatenate(lift, axis=0))):
            lift_ref[part, :, states] = turned(value, unit).astype(BF16)
        high, low = halves(jnp.concatenate(impulse, axis=0))
        response = dot(member, high) + dot(member, low)
        gated = gated_ref[:, chans]
        signal = turned(gated, unit).astype(BF16)
        parts = []
        for pair in range(in_tile // 2):
            blocks = []
            for g in (2 * pair, 2 * pair + 1):
                spread = jnp.broadcast_to(response[g : g + 1], (length, length))
                shifted = pltpu.roll(spread, 0, 1, stride=1, stride_axis=0)
                blocks.append(jnp.where(causal, shifted, 0.0).astype(BF16))
            both = dot(signal[pair * 2 * width : (pair + 1) * 2 * width], jnp.concatenate(blocks, axis=1))
            parts += [both[:width, :length], both[width:, length:]]
        high, low = halves(jnp.concatenate(parts, axis=0))
        base_ref[:, chans] = turned(high, unit) + turned(low, unit) + skip_ref[:, chans] * gated.astype(F32)

    unrolled(channels // TILE, tile)


def finish_kernel(at_ref, ends_ref, step_ref, lift_ref, query_ref, first_ref, base_ref, mine_ref, other_ref, mixed_ref, state_ref):
    length, channels = mixed_ref.shape
    poles = step_ref.shape[0]
    in_tile = lift_ref.shape[2] // poles * TILE // channels
    me, core = at_ref[0], at_ref[1]

    def earlier(block, state):
        return jnp.where(block < me, step_ref[...] * state + ends_ref[block].astype(F32), state)

    state_ref[...] = lax.fori_loop(0, ends_ref.shape[0] - 1, earlier, jnp.zeros((poles, channels), F32))
    owner = iota((poles, TILE), 1) // (TILE // in_tile)

    def tile(index):
        chans = tile_of(index)
        entering = state_ref[:, chans]
        apart = jnp.concatenate([jnp.where(owner == g, entering, 0.0) for g in range(in_tile)], axis=0)
        high, low = halves(apart)
        states = tile_of(index, in_tile * poles)
        lift = lift_ref[0, :, states]
        carried = dot(lift, high) + dot(lift, low) + dot(lift_ref[1, :, states], high)
        query = jnp.concatenate([first_ref[:, chans], query_ref[ROWS:, chans]], axis=0)
        mixed_ref[:, chans] = (query * (base_ref[:, chans] + carried)).astype(BF16)

    unrolled(channels // TILE, tile)
    share = channels // CORES
    mine_ref[...] = mixed_ref[:, tile_of(core, share)]
    other_ref[...] = mixed_ref[:, tile_of(1 - core, share)]


def project_kernel(at_ref, own_ref, below_ref, above_ref, middle_ref, far_ref, *rest):
    *weight_refs, mine_ref, other_ref, layers_ref = rest
    layer, chip = at_ref[0], at_ref[1]
    edge = (layer == 0) | (layer == 3)
    layers_ref[layer] = own_ref[...]
    layers_ref[jnp.where(layer == 0, 1, layer - 1)] = jnp.where(layer == 0, above_ref[...], below_ref[...])
    layers_ref[lax.rem(layer + 2, 4)] = middle_ref[...]
    layers_ref[jnp.where(edge, 3 - layer, layer + 1)] = jnp.where(edge, far_ref[...], above_ref[...])
    total, row = None, 0
    share = own_ref.shape[1]
    for weight_ref in weight_refs:
        start = row % share
        rows = weight_ref.shape[0]
        block = layers_ref[chip ^ (row // share), :, start : start + rows]
        term = dot(block, weight_ref[...])
        total = term if total is None else total + term
        row += rows
    length = mine_ref.shape[0]
    mine_ref[...] = total[:length]
    other_ref[...] = total[length:].astype(BF16)


def over_square(own):
    half = own.shape[0] // 2

    def swap(value, bit):
        return lax.ppermute(value, "ctx", [(source, source ^ bit) for source in range(8)])

    across, along = swap(own, 2), swap(own, 4)
    return own, across, along, swap(across[:half], 4), swap(along[half:], 2)


def over_layers(block):
    layer = lax.axis_index("tp")
    below = lax.ppermute(block, "tp", [(0, 1), (1, 2), (2, 3)])
    above = lax.ppermute(block, "tp", [(1, 0), (2, 1), (3, 2)])
    far = lax.ppermute(block, "tp", [(0, 3), (3, 0)])
    onward = jnp.where(layer == 1, above, jnp.where(layer == 2, below, block))
    middle = lax.ppermute(onward, "tp", [(0, 2), (3, 1), (2, 3), (1, 0)])
    return below, above, middle, far


def local(streams, conv_weight, rates, residues, skip, out_weight):
    channels, length = streams.shape[1:]
    groups, poles = rates.shape
    blocks, layers = lax.axis_size("ctx"), lax.axis_size("tp")
    rows, features = out_weight.shape
    share = channels // CORES
    square = blocks == 8 and rows == share
    if square:
        weight = over_square(out_weight)
    else:
        core_groups = [list(range(core, blocks, CORES)) for core in range(CORES)]
        weight = lax.all_gather(out_weight, "ctx", axis=0, axis_index_groups=core_groups)
        weight = weight.reshape(layers, share, features)

    tails, streams, conv_weight, rates, residues, skip = call(
        tails_kernel,
        [
            ((3, ROWS, channels), BF16),
            (streams.shape, BF16),
            (conv_weight.shape, F32),
            ((poles, groups), F32),
            ((poles, groups), F32),
            ((1, channels), F32),
        ],
        "tails",
        streams, conv_weight, rates.T, residues.T, skip[None, :],
        specs=[pl.BlockSpec(memory_space=pltpu.HBM)] * 5,
        scratch=[pltpu.SemaphoreType.DMA((5,))],
        limit=FETCH_LIMIT,
    )
    before = from_behind(tails, "ctx", 1)
    tiles = channels // TILE
    heads, query, gated, decay, step = call(
        prepare_kernel,
        [
            ((3, ROWS, channels), F32),
            ((length, channels), F32),
            ((length, channels), F32),
            ((2, groups * poles, length), BF16),
            ((poles, channels), F32),
        ],
        "prepare",
        streams, conv_weight, rates,
        scratch=[pltpu.VMEM((3 * tiles, ROWS + length, TILE), F32)],
        flops=10**9,
    )
    ends, gated, first = call(
        states_kernel,
        [((blocks, poles, channels), BF16), ((length, channels), BF16), ((ROWS, channels), F32)],
        "states",
        before, heads, conv_weight, gated, decay,
        scratch=[pltpu.VMEM((3 * tiles, 2 * ROWS, TILE), F32)],
    )
    all_ends = lax.all_to_all(ends, "ctx", split_axis=0, concat_axis=0, tiled=True)
    lift, base = call(
        inside_kernel,
        [((2, length, groups * poles), BF16), ((length, channels), F32)],
        "inside",
        gated, skip, rates, residues,
        flops=10**9,
    )
    me = lax.axis_index("ctx").astype(jnp.int32)
    core = me % CORES
    smem = [pl.BlockSpec(memory_space=pltpu.SMEM)]
    outs = [((length, share), BF16), ((length, share), BF16), ((length, channels), BF16)]
    mine, other, mixed = call(
        finish_kernel,
        outs,
        "finish",
        jnp.stack([me, core]), all_ends, step, lift, query, first, base,
        specs=smem + whole(6),
        scratch=[pltpu.VMEM((poles, channels), F32)],
    )
    if rows != share:
        by_core = mixed.reshape(length, share // rows, CORES, rows).transpose(2, 0, 1, 3)
        by_core = by_core.reshape(CORES, length, share)
        mine = lax.dynamic_index_in_dim(by_core, core, 0, keepdims=False)
        other = lax.dynamic_index_in_dim(by_core, 1 - core, 0, keepdims=False)
    siblings = [(source, source ^ 1) for source in range(blocks)]
    block = jnp.concatenate([mine, lax.ppermute(other, "ctx", siblings)], axis=0)
    layer = lax.axis_index("tp").astype(jnp.int32)
    if not square:
        weight = tuple(weight)
    chip = me // CORES if square else jnp.zeros_like(me)
    mine, other = call(
        project_kernel,
        [((length, features), F32), ((length, features), BF16)],
        "project",
        jnp.stack([layer, chip]), block, *over_layers(block), *weight,
        specs=smem + whole(5 + len(weight)),
        scratch=[pltpu.VMEM((layers,) + block.shape, BF16)],
    )
    other = lax.ppermute(other, "ctx", siblings)
    return (mine + other.astype(F32)).astype(BF16)


def solution(mesh):
    return jax.shard_map(
        local,
        mesh=mesh,
        in_specs=(
            P(None, "tp", "ctx"),
            P(None, None, "tp"),
            P("tp", None),
            P("tp", None),
            P("tp"),
            P("ctx", "tp"),
        ),
        out_specs=P("ctx", "tp"),
        check_vma=False,
    )
```

```python
import math

import jax
import jax.numpy as jnp
from jax import lax
from jax.experimental import pallas as pl
from jax.experimental.pallas import tpu as pltpu
from jax.sharding import PartitionSpec as P

F32 = jnp.float32
BF16 = jnp.bfloat16
ROWS = 8
TILE = 128
CORES = 2
FIRST_ROWS = 128
VMEM_LIMIT = 24 * 1024 * 1024
PLAIN = (((1,), (0,)), ((), ()))
CONTRACT_LANES = (((1,), (1,)), ((), ()))


def from_behind(value, axis, steps):
    count = lax.axis_size(axis)
    leading, last = (max(0, -steps), min(count, count - steps))
    return lax.ppermute(value, axis, [(source, source + steps) for source in range(leading, last)])


def dot(left, right, dims=PLAIN):
    return lax.dot_general(left, right, dims, preferred_element_type=F32)


def halves(value):
    high = value.astype(BF16)
    return high, (value - high.astype(F32)).astype(BF16)


def iota(shape, axis):
    return lax.broadcasted_iota(jnp.int32, shape, axis)


def identity(size):
    return (iota((size, size), 0) == iota((size, size), 1)).astype(BF16)


def turned(value, unit):
    return dot(unit, value, CONTRACT_LANES)


def whole(count):
    return [pl.BlockSpec(memory_space=pltpu.VMEM)] * count


def call(kernel, outs, name, *operands, specs=None, scratch=(), flops=10**8):
    return pl.pallas_call(
        kernel,
        out_shape=tuple(jax.ShapeDtypeStruct(*out) for out in outs),
        in_specs=whole(len(operands)) if specs is None else specs,
        out_specs=tuple(whole(len(outs))),
        scratch_shapes=scratch,
        compiler_params=pltpu.CompilerParams(vmem_limit_bytes=VMEM_LIMIT),
        cost_estimate=pl.CostEstimate(flops=flops, bytes_accessed=10**6, transcendentals=0),
        name=name,
    )(*operands)


def tile_of(index, size=TILE):
    return pl.ds(pl.multiple_of(index * size, size), size)


def unrolled(count, body):
    def step(index, carry):
        body(index)
        return carry

    lax.fori_loop(0, count, step, 0, unroll=math.gcd(count, 4))


def tails_kernel(streams_ref, tails_ref):
    length = streams_ref.shape[2]
    pick = (iota((2 * ROWS, length), 1) == iota((2 * ROWS, length), 0) + (length - ROWS)).astype(BF16)
    for stream in range(streams_ref.shape[0]):
        rows = dot(pick, streams_ref[stream], CONTRACT_LANES)
        tails_ref[stream] = rows[:ROWS].astype(BF16)


def short_conv(stream, chans, rows, padded, taps_ref):
    total = None
    for shift in range(taps_ref.shape[1]):
        term = taps_ref[stream, shift : shift + 1, chans] * padded[pl.ds(ROWS - shift, rows), :]
        total = term if total is None else total + term
    return total


def prepare_kernel(streams_ref, taps_ref, rates_ref, heads_ref, query_ref, gated_ref, decay_ref, step_ref, padded_ref):
    channels, length = streams_ref.shape[1:]
    poles, groups = rates_ref.shape
    width = channels // groups
    in_tile = TILE // width
    unit = identity(length)
    lag = (length - 1) - iota((poles, length), 1).astype(F32)
    owner = iota((poles, TILE), 1) // width

    def turn(index):
        chans = tile_of(index)
        for stream in range(3):
            tokens = turned(streams_ref[stream, chans, :], unit)
            padded_ref[index * 3 + stream, :ROWS, :] = jnp.zeros((ROWS, TILE), F32)
            padded_ref[index * 3 + stream, ROWS:, :] = tokens
            heads_ref[stream, :, chans] = tokens[:ROWS]

    def decays(index):
        rates = pltpu.roll(rates_ref[...], groups - index * in_tile, 1)
        decay = []
        wide = jnp.zeros((poles, TILE), F32)
        for g in range(in_tile):
            rate = jnp.broadcast_to(rates[:, g : g + 1], (poles, length))
            decay.append(jnp.exp(-rate * lag))
            wide = jnp.where(owner == g, rate[:, :TILE], wide)
        step_ref[:, tile_of(index)] = jnp.exp(-wide * length)
        for part, value in enumerate(halves(jnp.concatenate(decay, axis=0))):
            decay_ref[part, tile_of(index, in_tile * poles), :] = value

    def filters(index):
        chans = tile_of(index)
        query, left, right = (
            short_conv(stream, chans, length, padded_ref.at[index * 3 + stream], taps_ref) for stream in range(3)
        )
        query_ref[:, chans] = query
        gated_ref[:, chans] = left * right

    unrolled(channels // TILE, turn)
    unrolled(channels // TILE, decays)
    unrolled(channels // TILE, filters)


def states_kernel(before_ref, heads_ref, taps_ref, gated_ref, decay_ref, ends_ref, final_ref, first_ref, padded_ref):
    length, channels = gated_ref.shape
    poles = ends_ref.shape[1]
    in_tile = decay_ref.shape[1] // poles * TILE // channels
    owner = iota((poles, TILE), 1) // (TILE // in_tile)

    def begin(index):
        chans = tile_of(index)
        for stream in range(3):
            padded_ref[index * 3 + stream, :ROWS, :] = before_ref[stream, :, chans].astype(F32)
            padded_ref[index * 3 + stream, ROWS:, :] = heads_ref[stream, :, chans]
        query, left, right = (
            short_conv(stream, chans, ROWS, padded_ref.at[index * 3 + stream], taps_ref) for stream in range(3)
        )
        first_ref[:, chans] = query
        final_ref[:, chans] = jnp.concatenate([left * right, gated_ref[ROWS:, chans]], axis=0).astype(BF16)

    def leave(index):
        chans = tile_of(index)
        gated = final_ref[:, chans]
        states = tile_of(index, in_tile * poles)
        every = dot(decay_ref[0, states, :], gated) + dot(decay_ref[1, states, :], gated)
        ends = jnp.zeros((poles, TILE), F32)
        for g in range(in_tile):
            ends = jnp.where(owner == g, every[g * poles : (g + 1) * poles], ends)
        ends = ends.astype(BF16)
        for block in range(ends_ref.shape[0]):
            ends_ref[block, :, chans] = ends

    unrolled(channels // TILE, begin)
    unrolled(channels // TILE, leave)


def inside_kernel(gated_ref, skip_ref, rates_ref, residues_ref, lift_ref, base_ref):
    length, channels = gated_ref.shape
    poles, groups = rates_ref.shape
    width = channels // groups
    in_tile = TILE // width
    unit = identity(length)
    time = iota((poles, length), 1).astype(F32)
    member = (iota((in_tile, in_tile * poles), 1) // poles == iota((in_tile, in_tile * poles), 0)).astype(BF16)
    causal = iota((length, length), 1) >= iota((length, length), 0)

    def tile(index):
        chans = tile_of(index)
        shift = groups - index * in_tile
        rates = pltpu.roll(rates_ref[...], shift, 1)
        coef = pltpu.roll(residues_ref[...], shift, 1) * jnp.sqrt(2.0 * rates) / math.sqrt(poles)
        impulse, lift = [], []
        for g in range(in_tile):
            rate = jnp.broadcast_to(rates[:, g : g + 1], (poles, length))
            scale = jnp.broadcast_to(coef[:, g : g + 1], (poles, length))
            impulse.append(scale * jnp.exp(-rate * time))
            lift.append(scale * jnp.exp(-rate * (time + 1.0)))
        states = tile_of(index, in_tile * poles)
        for part, value in enumerate(halves(jnp.concatenate(lift, axis=0))):
            lift_ref[part, :, states] = turned(value, unit).astype(BF16)
        high, low = halves(jnp.concatenate(impulse, axis=0))
        response = dot(member, high) + dot(member, low)
        gated = gated_ref[:, chans]
        signal = turned(gated, unit).astype(BF16)
        parts = []
        for pair in range(in_tile // 2):
            blocks = []
            for g in (2 * pair, 2 * pair + 1):
                spread = jnp.broadcast_to(response[g : g + 1], (length, length))
                shifted = pltpu.roll(spread, 0, 1, stride=1, stride_axis=0)
                blocks.append(jnp.where(causal, shifted, 0.0).astype(BF16))
            both = dot(signal[pair * 2 * width : (pair + 1) * 2 * width], jnp.concatenate(blocks, axis=1))
            parts += [both[:width, :length], both[width:, length:]]
        high, low = halves(jnp.concatenate(parts, axis=0))
        base_ref[:, chans] = turned(high, unit) + turned(low, unit) + skip_ref[:, chans] * gated.astype(F32)

    unrolled(channels // TILE, tile)


def finish_kernel(at_ref, ends_ref, step_ref, lift_ref, query_ref, first_ref, base_ref, mine_ref, other_ref, mixed_ref, state_ref):
    length, channels = mixed_ref.shape
    poles = step_ref.shape[0]
    in_tile = lift_ref.shape[2] // poles * TILE // channels
    me, core = at_ref[0], at_ref[1]

    def earlier(block, state):
        return jnp.where(block < me, step_ref[...] * state + ends_ref[block].astype(F32), state)

    state_ref[...] = lax.fori_loop(0, ends_ref.shape[0] - 1, earlier, jnp.zeros((poles, channels), F32))
    owner = iota((poles, TILE), 1) // (TILE // in_tile)

    def tile(index):
        chans = tile_of(index)
        entering = state_ref[:, chans]
        apart = jnp.concatenate([jnp.where(owner == g, entering, 0.0) for g in range(in_tile)], axis=0)
        high, low = halves(apart)
        states = tile_of(index, in_tile * poles)
        lift = lift_ref[0, :, states]
        carried = dot(lift, high) + dot(lift, low) + dot(lift_ref[1, :, states], high)
        query = jnp.concatenate([first_ref[:, chans], query_ref[ROWS:, chans]], axis=0)
        mixed_ref[:, chans] = (query * (base_ref[:, chans] + carried)).astype(BF16)

    unrolled(channels // TILE, tile)
    share = channels // CORES
    mine_ref[...] = mixed_ref[:, tile_of(core, share)]
    other_ref[...] = mixed_ref[:, tile_of(1 - core, share)]


def project_kernel(at_ref, own_ref, below_ref, above_ref, middle_ref, far_ref, *rest):
    *weight_refs, mine_ref, other_ref, layers_ref = rest
    layer, chip = at_ref[0], at_ref[1]
    edge = (layer == 0) | (layer == 3)
    layers_ref[layer] = own_ref[...]
    layers_ref[jnp.where(layer == 0, 1, layer - 1)] = jnp.where(layer == 0, above_ref[...], below_ref[...])
    layers_ref[lax.rem(layer + 2, 4)] = middle_ref[...]
    layers_ref[jnp.where(edge, 3 - layer, layer + 1)] = jnp.where(edge, far_ref[...], above_ref[...])
    total, row = None, 0
    share = own_ref.shape[1]
    for weight_ref in weight_refs:
        start = row % share
        rows = weight_ref.shape[0]
        block = layers_ref[chip ^ (row // share), :, start : start + rows]
        term = dot(block, weight_ref[...])
        total = term if total is None else total + term
        row += rows
    length = mine_ref.shape[0]
    mine_ref[...] = total[:length]
    other_ref[...] = total[length:].astype(BF16)


def swap(value, bit):
    count = lax.axis_size("ctx")
    return lax.ppermute(value, "ctx", [(source, source ^ bit) for source in range(count)])


def after(value, earlier):
    return lax.optimization_barrier((value, earlier))[0]


def over_layers(block):
    layer = lax.axis_index("tp")
    below = lax.ppermute(block, "tp", [(0, 1), (1, 2), (2, 3)])
    above = lax.ppermute(block, "tp", [(1, 0), (2, 1), (3, 2)])
    far = lax.ppermute(block, "tp", [(0, 3), (3, 0)])
    onward = jnp.where(layer == 1, above, jnp.where(layer == 2, below, block))
    middle = lax.ppermute(onward, "tp", [(0, 2), (3, 1), (2, 3), (1, 0)])
    return below, above, middle, far


def local(streams, conv_weight, rates, residues, skip, out_weight):
    channels, length = streams.shape[1:]
    groups, poles = rates.shape
    blocks, layers = lax.axis_size("ctx"), lax.axis_size("tp")
    rows, features = out_weight.shape
    share = channels // CORES
    square = blocks == 8 and rows == share

    rates, residues, skip = rates.T, residues.T, skip[None, :]
    (tails,) = call(tails_kernel, [((3, ROWS, channels), BF16)], "tails", streams)
    before = from_behind(tails, "ctx", 1)
    piece, half = FIRST_ROWS, rows // 2
    if square:
        across_first = swap(after(out_weight, tails)[:piece], 2)
        along_first = swap(after(out_weight, tails)[rows - piece :], 4)
    tiles = channels // TILE
    heads, query, gated, decay, step = call(
        prepare_kernel,
        [
            ((3, ROWS, channels), F32),
            ((length, channels), F32),
            ((length, channels), F32),
            ((2, groups * poles, length), BF16),
            ((poles, channels), F32),
        ],
        "prepare",
        streams, conv_weight, rates,
        scratch=[pltpu.VMEM((3 * tiles, ROWS + length, TILE), F32)],
        flops=10**9,
    )
    ends, gated, first = call(
        states_kernel,
        [((blocks, poles, channels), BF16), ((length, channels), BF16), ((ROWS, channels), F32)],
        "states",
        before, heads, conv_weight, gated, decay,
        scratch=[pltpu.VMEM((3 * tiles, 2 * ROWS, TILE), F32)],
    )
    all_ends = lax.all_to_all(ends, "ctx", split_axis=0, concat_axis=0, tiled=True)
    if square:
        gated, across_first, along_first = lax.optimization_barrier((gated, across_first, along_first))
        across_rest = swap(after(out_weight, all_ends)[piece:], 2)
        along_rest = swap(after(out_weight, all_ends)[: rows - piece], 4)
    lift, base = call(
        inside_kernel,
        [((2, length, groups * poles), BF16), ((length, channels), F32)],
        "inside",
        gated, skip, rates, residues,
        flops=10**9,
    )
    me = lax.axis_index("ctx").astype(jnp.int32)
    core = me % CORES
    smem = [pl.BlockSpec(memory_space=pltpu.SMEM)]
    outs = [((length, share), BF16), ((length, share), BF16), ((length, channels), BF16)]
    mine, other, mixed = call(
        finish_kernel,
        outs,
        "finish",
        jnp.stack([me, core]), all_ends, step, lift, query, first, base,
        specs=smem + whole(6),
        scratch=[pltpu.VMEM((poles, channels), F32)],
    )
    if rows != share:
        by_core = mixed.reshape(length, share // rows, CORES, rows).transpose(2, 0, 1, 3)
        by_core = by_core.reshape(CORES, length, share)
        mine = lax.dynamic_index_in_dim(by_core, core, 0, keepdims=False)
        other = lax.dynamic_index_in_dim(by_core, 1 - core, 0, keepdims=False)
    block = jnp.concatenate([mine, swap(other, 1)], axis=0)
    layer = lax.axis_index("tp").astype(jnp.int32)
    if square:
        weight = (
            out_weight,
            across_first,
            across_rest,
            along_rest,
            along_first,
            swap(after(across_first, block), 4),
            swap(across_rest[: half - piece], 4),
            swap(along_rest[half:], 2),
            swap(after(along_first, block), 2),
        )
    else:
        core_groups = [list(range(core, blocks, CORES)) for core in range(CORES)]
        weight = lax.all_gather(out_weight, "ctx", axis=0, axis_index_groups=core_groups)
        weight = tuple(weight.reshape(layers, share, features))
    chip = me // CORES if square else jnp.zeros_like(me)
    mine, other = call(
        project_kernel,
        [((length, features), F32), ((length, features), BF16)],
        "project",
        jnp.stack([layer, chip]), block, *over_layers(block), *weight,
        specs=smem + whole(5 + len(weight)),
        scratch=[pltpu.VMEM((layers,) + block.shape, BF16)],
    )
    other = swap(other, 1)
    return (mine + other.astype(F32)).astype(BF16)


def solution(mesh):
    return jax.shard_map(
        local,
        mesh=mesh,
        in_specs=(
            P(None, "tp", "ctx"),
            P(None, None, "tp"),
            P("tp", None),
            P("tp", None),
            P("tp"),
            P("ctx", "tp"),
        ),
        out_specs=P("ctx", "tp"),
        check_vma=False,
    )
```

```python
import functools
import math

import jax
import jax.numpy as jnp
from jax import lax
from jax.experimental import pallas as pl
from jax.experimental.pallas import tpu as pltpu
from jax.sharding import PartitionSpec as P

F32 = jnp.float32
BF16 = jnp.bfloat16
ROWS = 8
TILE = 128
CORES = 2
FIRST_ROWS = 192
VMEM_LIMIT = 24 * 1024 * 1024
PLAIN = (((1,), (0,)), ((), ()))
CONTRACT_LANES = (((1,), (1,)), ((), ()))


def from_behind(value, axis, steps):
    count = lax.axis_size(axis)
    leading, last = (max(0, -steps), min(count, count - steps))
    return lax.ppermute(value, axis, [(source, source + steps) for source in range(leading, last)])


def dot(left, right, dims=PLAIN):
    return lax.dot_general(left, right, dims, preferred_element_type=F32)


def halves(value):
    high = value.astype(BF16)
    return high, (value - high.astype(F32)).astype(BF16)


def iota(shape, axis):
    return lax.broadcasted_iota(jnp.int32, shape, axis)


def identity(size):
    return (iota((size, size), 0) == iota((size, size), 1)).astype(BF16)


def turned(value, unit):
    return dot(unit, value, CONTRACT_LANES)


def whole(count):
    return [pl.BlockSpec(memory_space=pltpu.VMEM)] * count


def call(kernel, outs, name, *operands, specs=None, scratch=(), flops=10**8):
    return pl.pallas_call(
        kernel,
        out_shape=tuple(jax.ShapeDtypeStruct(*out) for out in outs),
        in_specs=whole(len(operands)) if specs is None else specs,
        out_specs=tuple(whole(len(outs))),
        scratch_shapes=scratch,
        compiler_params=pltpu.CompilerParams(vmem_limit_bytes=VMEM_LIMIT),
        cost_estimate=pl.CostEstimate(flops=flops, bytes_accessed=flops // 100, transcendentals=0),
        name=name,
    )(*operands)


def tile_of(index, size=TILE):
    return pl.ds(pl.multiple_of(index * size, size), size)


def unrolled(count, body):
    def step(index, carry):
        body(index)
        return carry

    lax.fori_loop(0, count, step, 0, unroll=math.gcd(count, 4))


def tails_kernel(streams_ref, tails_ref):
    length = streams_ref.shape[2]
    pick = (iota((2 * ROWS, length), 1) == iota((2 * ROWS, length), 0) + (length - ROWS)).astype(BF16)
    for stream in range(streams_ref.shape[0]):
        rows = dot(pick, streams_ref[stream], CONTRACT_LANES)
        tails_ref[stream] = rows[:ROWS].astype(BF16)


def short_conv(stream, chans, rows, padded, taps_ref):
    total = None
    for shift in range(taps_ref.shape[1]):
        term = taps_ref[stream, shift : shift + 1, chans] * padded[pl.ds(ROWS - shift, rows), :]
        total = term if total is None else total + term
    return total


def prepare_kernel(streams_ref, taps_ref, rates_ref, heads_ref, query_ref, gated_ref, decay_ref, step_ref, padded_ref):
    channels, length = streams_ref.shape[1:]
    poles, groups = rates_ref.shape
    width = channels // groups
    in_tile = TILE // width
    unit = identity(length)
    lag = (length - 1) - iota((poles, length), 1).astype(F32)
    owner = iota((poles, TILE), 1) // width

    def turn(index):
        chans = tile_of(index)
        for stream in range(3):
            tokens = turned(streams_ref[stream, chans, :], unit)
            padded_ref[index * 3 + stream, :ROWS, :] = jnp.zeros((ROWS, TILE), F32)
            padded_ref[index * 3 + stream, ROWS:, :] = tokens
            heads_ref[stream, :, chans] = tokens[:ROWS]

    def decays(index):
        rates = pltpu.roll(rates_ref[...], groups - index * in_tile, 1)
        decay = []
        wide = jnp.zeros((poles, TILE), F32)
        for g in range(in_tile):
            rate = jnp.broadcast_to(rates[:, g : g + 1], (poles, length))
            decay.append(jnp.exp(-rate * lag))
            wide = jnp.where(owner == g, rate[:, :TILE], wide)
        step_ref[:, tile_of(index)] = jnp.exp(-wide * length)
        for part, value in enumerate(halves(jnp.concatenate(decay, axis=0))):
            decay_ref[part, tile_of(index, in_tile * poles), :] = value

    def filters(index):
        chans = tile_of(index)
        query, left, right = (
            short_conv(stream, chans, length, padded_ref.at[index * 3 + stream], taps_ref) for stream in range(3)
        )
        query_ref[:, chans] = query
        gated_ref[:, chans] = left * right

    unrolled(channels // TILE, turn)
    unrolled(channels // TILE, decays)
    unrolled(channels // TILE, filters)


def states_kernel(before_ref, heads_ref, taps_ref, gated_ref, decay_ref, ends_ref, final_ref, first_ref, padded_ref):
    length, channels = gated_ref.shape
    poles = ends_ref.shape[1]
    in_tile = decay_ref.shape[1] // poles * TILE // channels
    owner = iota((poles, TILE), 1) // (TILE // in_tile)

    def begin(index):
        chans = tile_of(index)
        for stream in range(3):
            padded_ref[index * 3 + stream, :ROWS, :] = before_ref[stream, :, chans].astype(F32)
            padded_ref[index * 3 + stream, ROWS:, :] = heads_ref[stream, :, chans]
        query, left, right = (
            short_conv(stream, chans, ROWS, padded_ref.at[index * 3 + stream], taps_ref) for stream in range(3)
        )
        first_ref[:, chans] = query
        final_ref[:, chans] = jnp.concatenate([left * right, gated_ref[ROWS:, chans]], axis=0).astype(BF16)

    def leave(index):
        chans = tile_of(index)
        gated = final_ref[:, chans]
        states = tile_of(index, in_tile * poles)
        every = dot(decay_ref[0, states, :], gated) + dot(decay_ref[1, states, :], gated)
        ends = jnp.zeros((poles, TILE), F32)
        for g in range(in_tile):
            ends = jnp.where(owner == g, every[g * poles : (g + 1) * poles], ends)
        ends = ends.astype(BF16)
        for block in range(ends_ref.shape[0]):
            ends_ref[block, :, chans] = ends

    unrolled(channels // TILE, begin)
    unrolled(channels // TILE, leave)


def inside_kernel(gated_ref, skip_ref, rates_ref, residues_ref, lift_ref, base_ref):
    length, channels = gated_ref.shape
    poles, groups = rates_ref.shape
    width = channels // groups
    in_tile = TILE // width
    unit = identity(length)
    time = iota((poles, length), 1).astype(F32)
    member = (iota((in_tile, in_tile * poles), 1) // poles == iota((in_tile, in_tile * poles), 0)).astype(BF16)
    causal = iota((length, length), 1) >= iota((length, length), 0)

    def tile(index):
        chans = tile_of(index)
        shift = groups - index * in_tile
        rates = pltpu.roll(rates_ref[...], shift, 1)
        coef = pltpu.roll(residues_ref[...], shift, 1) * jnp.sqrt(2.0 * rates) / math.sqrt(poles)
        impulse, lift = [], []
        for g in range(in_tile):
            rate = jnp.broadcast_to(rates[:, g : g + 1], (poles, length))
            scale = jnp.broadcast_to(coef[:, g : g + 1], (poles, length))
            impulse.append(scale * jnp.exp(-rate * time))
            lift.append(scale * jnp.exp(-rate * (time + 1.0)))
        states = tile_of(index, in_tile * poles)
        lift_ref[:, states] = turned(jnp.concatenate(lift, axis=0).astype(BF16), unit).astype(BF16)
        high, low = halves(jnp.concatenate(impulse, axis=0))
        response = dot(member, high) + dot(member, low)
        gated = gated_ref[:, chans]
        signal = turned(gated, unit).astype(BF16)
        parts = []
        for pair in range(in_tile // 2):
            blocks = []
            for g in (2 * pair, 2 * pair + 1):
                spread = jnp.broadcast_to(response[g : g + 1], (length, length))
                shifted = pltpu.roll(spread, 0, 1, stride=1, stride_axis=0)
                blocks.append(jnp.where(causal, shifted, 0.0).astype(BF16))
            both = dot(signal[pair * 2 * width : (pair + 1) * 2 * width], jnp.concatenate(blocks, axis=1))
            parts += [both[:width, :length], both[width:, length:]]
        high, low = halves(jnp.concatenate(parts, axis=0))
        base_ref[:, chans] = turned(high, unit) + turned(low, unit) + skip_ref[:, chans] * gated.astype(F32)

    unrolled(channels // TILE, tile)


def finish_kernel(at_ref, ends_ref, step_ref, lift_ref, query_ref, first_ref, base_ref, mine_ref, other_ref, mixed_ref, state_ref):
    length, channels = mixed_ref.shape
    poles = step_ref.shape[0]
    in_tile = lift_ref.shape[1] // poles * TILE // channels
    me, core = at_ref[0], at_ref[1]

    def earlier(block, state):
        return jnp.where(block < me, step_ref[...] * state + ends_ref[block].astype(F32), state)

    state_ref[...] = lax.fori_loop(0, ends_ref.shape[0] - 1, earlier, jnp.zeros((poles, channels), F32))
    owner = iota((poles, TILE), 1) // (TILE // in_tile)

    def tile(index):
        chans = tile_of(index)
        entering = state_ref[:, chans]
        apart = jnp.concatenate([jnp.where(owner == g, entering, 0.0) for g in range(in_tile)], axis=0)
        high, low = halves(apart)
        states = tile_of(index, in_tile * poles)
        lift = lift_ref[:, states]
        carried = dot(lift, high) + dot(lift, low)
        query = jnp.concatenate([first_ref[:, chans], query_ref[ROWS:, chans]], axis=0)
        mixed_ref[:, chans] = (query * (base_ref[:, chans] + carried)).astype(BF16)

    unrolled(channels // TILE, tile)
    share = channels // CORES
    mine_ref[...] = mixed_ref[:, tile_of(core, share)]
    other_ref[...] = mixed_ref[:, tile_of(1 - core, share)]


def early_kernel(pieces, at_ref, own_ref, up_ref, second_ref, down_ref, *rest):
    *weight_refs, total_ref, diagonal_ref, layers_ref = rest
    layer, chip = at_ref[0], at_ref[1]
    layers_ref[layer] = own_ref[...]
    layers_ref[lax.rem(layer + 3, 4)] = up_ref[...]
    layers_ref[lax.rem(layer + 2, 4)] = second_ref[...]
    layers_ref[lax.rem(layer + 1, 4)] = down_ref[...]
    total = None
    for ref, (relation, start) in zip(weight_refs, pieces):
        term = dot(layers_ref[chip ^ relation, :, start : start + ref.shape[0]], ref[...])
        total = term if total is None else total + term
    total_ref[...] = total
    diagonal_ref[...] = layers_ref[chip ^ 3]


def late_kernel(first, pieces, total_ref, diagonal_ref, *rest):
    *weight_refs, out_ref = rest
    tokens = pl.ds(first, out_ref.shape[0])
    total = total_ref[tokens, :]
    for ref, start in zip(weight_refs, pieces):
        total = total + dot(diagonal_ref[tokens, start : start + ref.shape[0]], ref[...])
    out_ref[...] = total.astype(out_ref.dtype)


def swap(value, bit):
    count = lax.axis_size("ctx")
    return lax.ppermute(value, "ctx", [(source, source ^ bit) for source in range(count)])


def after(value, earlier):
    return lax.optimization_barrier((value, earlier))[0]


def around(value, steps):
    count = lax.axis_size("tp")
    return lax.ppermute(value, "tp", [(source, (source + steps) % count) for source in range(count)])


def local(streams, conv_weight, rates, residues, skip, out_weight):
    channels, length = streams.shape[1:]
    groups, poles = rates.shape
    blocks, layers = lax.axis_size("ctx"), lax.axis_size("tp")
    rows, features = out_weight.shape
    share = channels // CORES
    square = blocks == 8 and rows == share

    rates, residues, skip = rates.T, residues.T, skip[None, :]
    piece, half = FIRST_ROWS, rows // 2
    if square:
        upper, lower = out_weight[:piece], out_weight[rows - piece :]
        streams, upper, lower = lax.optimization_barrier((streams, upper, lower))
    (tails,) = call(tails_kernel, [((3, ROWS, channels), BF16)], "tails", streams)
    before = from_behind(tails, "ctx", 1)
    if square:
        across_first, along_first = swap(upper, 2), swap(lower, 4)
    tiles = channels // TILE
    heads, query, gated, decay, step = call(
        prepare_kernel,
        [
            ((3, ROWS, channels), F32),
            ((length, channels), F32),
            ((length, channels), F32),
            ((2, groups * poles, length), BF16),
            ((poles, channels), F32),
        ],
        "prepare",
        streams, conv_weight, rates,
        scratch=[pltpu.VMEM((3 * tiles, ROWS + length, TILE), F32)],
        flops=10**9,
    )
    ends, gated, first = call(
        states_kernel,
        [((blocks, poles, channels), BF16), ((length, channels), BF16), ((ROWS, channels), F32)],
        "states",
        before, heads, conv_weight, gated, decay,
        scratch=[pltpu.VMEM((3 * tiles, 2 * ROWS, TILE), F32)],
    )
    all_ends = lax.all_to_all(ends, "ctx", split_axis=0, concat_axis=0, tiled=True)
    if square:
        gated, across_first, along_first = lax.optimization_barrier((gated, across_first, along_first))
    lift, base = call(
        inside_kernel,
        [((length, groups * poles), BF16), ((length, channels), F32)],
        "inside",
        gated, skip, rates, residues,
        flops=10**9,
    )
    if square:
        across_rest = swap(after(after(out_weight, base)[piece:], all_ends), 2)
        along_rest = swap(after(after(out_weight, base)[: rows - piece], all_ends), 4)
    me = lax.axis_index("ctx").astype(jnp.int32)
    core = me % CORES
    smem = [pl.BlockSpec(memory_space=pltpu.SMEM)]
    outs = [((length, share), BF16), ((length, share), BF16), ((length, channels), BF16)]
    mine, other, mixed = call(
        finish_kernel,
        outs,
        "finish",
        jnp.stack([me, core]), all_ends, step, lift, query, first, base,
        specs=smem + whole(6),
        scratch=[pltpu.VMEM((poles, channels), F32)],
    )
    if rows != share:
        by_core = mixed.reshape(length, share // rows, CORES, rows).transpose(2, 0, 1, 3)
        by_core = by_core.reshape(CORES, length, share)
        mine = lax.dynamic_index_in_dim(by_core, core, 0, keepdims=False)
        other = lax.dynamic_index_in_dim(by_core, 1 - core, 0, keepdims=False)
    block = jnp.concatenate([mine, swap(other, 1)], axis=0)
    layer = lax.axis_index("tp").astype(jnp.int32)
    up, down = around(block, 1), around(block, -1)
    second = around(after(up, down), 1)
    if square:
        weight = (
            (0, 0, out_weight),
            (1, 0, across_first),
            (1, piece, across_rest),
            (2, 0, along_rest),
            (2, rows - piece, along_first),
            (3, 0, swap(after(across_first, (block, across_rest)), 4)),
            (3, rows - piece, swap(after(along_first, (block, along_rest)), 2)),
        )
        last = (
            (piece, swap(after(across_rest, block)[: half - piece], 4)),
            (half, swap(after(along_rest, block)[half:], 2)),
        )
    else:
        core_groups = [list(range(core, blocks, CORES)) for core in range(CORES)]
        weight = lax.all_gather(out_weight, "ctx", axis=0, axis_index_groups=core_groups)
        weight = tuple((index, 0, part) for index, part in enumerate(weight.reshape(layers, share, features)))
        last = ()
    chip = me // CORES if square else jnp.zeros_like(me)
    total, diagonal = call(
        functools.partial(early_kernel, [part[:2] for part in weight]),
        [((CORES * length, features), F32), (block.shape, BF16)],
        "early",
        jnp.stack([layer, chip]), block, up, second, down, *(part[2] for part in weight),
        specs=smem + whole(4 + len(weight)),
        scratch=[pltpu.VMEM((layers,) + block.shape, BF16)],
        flops=10**9,
    )
    sides = []
    for side, kind in ((1, BF16), (0, F32)):
        sides += call(
            functools.partial(late_kernel, side * length, [part[0] for part in last]),
            [((length, features), kind)],
            "late",
            total, diagonal, *(part[1] for part in last),
        )
    other, mine = sides
    other = swap(other, 1)
    return (mine + other.astype(F32)).astype(BF16)


def solution(mesh):
    return jax.shard_map(
        local,
        mesh=mesh,
        in_specs=(
            P(None, "tp", "ctx"),
            P(None, None, "tp"),
            P("tp", None),
            P("tp", None),
            P("tp"),
            P("ctx", "tp"),
        ),
        out_specs=P("ctx", "tp"),
        check_vma=False,
    )
```

```python
import functools
import math

import jax
import jax.numpy as jnp
from jax import lax
from jax.experimental import pallas as pl
from jax.experimental.pallas import tpu as pltpu
from jax.sharding import PartitionSpec as P

F32 = jnp.float32
BF16 = jnp.bfloat16
ROWS = 8
TILE = 128
CORES = 2
COLUMNS = 256
VMEM_LIMIT = 24 * 1024 * 1024
PLAIN = (((1,), (0,)), ((), ()))
CONTRACT_LANES = (((1,), (1,)), ((), ()))


def from_behind(value, axis, steps):
    count = lax.axis_size(axis)
    leading, last = (max(0, -steps), min(count, count - steps))
    return lax.ppermute(value, axis, [(source, source + steps) for source in range(leading, last)])


def dot(left, right, dims=PLAIN):
    return lax.dot_general(left, right, dims, preferred_element_type=F32)


def halves(value):
    high = value.astype(BF16)
    return high, (value - high.astype(F32)).astype(BF16)


def iota(shape, axis):
    return lax.broadcasted_iota(jnp.int32, shape, axis)


def identity(size):
    return (iota((size, size), 0) == iota((size, size), 1)).astype(BF16)


def turned(value, unit):
    return dot(unit, value, CONTRACT_LANES)


def whole(count):
    return [pl.BlockSpec(memory_space=pltpu.VMEM)] * count


def call(kernel, outs, name, *operands, specs=None, scratch=(), flops=10**8):
    return pl.pallas_call(
        kernel,
        out_shape=tuple(jax.ShapeDtypeStruct(*out) for out in outs),
        in_specs=whole(len(operands)) if specs is None else specs,
        out_specs=tuple(whole(len(outs))),
        scratch_shapes=scratch,
        compiler_params=pltpu.CompilerParams(vmem_limit_bytes=VMEM_LIMIT),
        cost_estimate=pl.CostEstimate(flops=flops, bytes_accessed=flops // 100, transcendentals=0),
        name=name,
    )(*operands)


def tile_of(index, size=TILE):
    return pl.ds(pl.multiple_of(index * size, size), size)


def unrolled(count, body):
    def step(index, carry):
        body(index)
        return carry

    lax.fori_loop(0, count, step, 0, unroll=math.gcd(count, 4))


def tails_kernel(streams_ref, tails_ref):
    length = streams_ref.shape[2]
    pick = (iota((2 * ROWS, length), 1) == iota((2 * ROWS, length), 0) + (length - ROWS)).astype(BF16)
    for stream in range(streams_ref.shape[0]):
        rows = dot(pick, streams_ref[stream], CONTRACT_LANES)
        tails_ref[stream] = rows[:ROWS].astype(BF16)


def short_conv(stream, chans, rows, padded, taps_ref):
    total = None
    for shift in range(taps_ref.shape[1]):
        term = taps_ref[stream, shift : shift + 1, chans] * padded[pl.ds(ROWS - shift, rows), :]
        total = term if total is None else total + term
    return total


def prepare_kernel(streams_ref, taps_ref, rates_ref, heads_ref, query_ref, gated_ref, decay_ref, step_ref, padded_ref):
    channels, length = streams_ref.shape[1:]
    poles, groups = rates_ref.shape
    width = channels // groups
    in_tile = TILE // width
    unit = identity(length)
    lag = (length - 1) - iota((poles, length), 1).astype(F32)
    owner = iota((poles, TILE), 1) // width

    def turn(index):
        chans = tile_of(index)
        for stream in range(3):
            tokens = turned(streams_ref[stream, chans, :], unit)
            padded_ref[index * 3 + stream, :ROWS, :] = jnp.zeros((ROWS, TILE), F32)
            padded_ref[index * 3 + stream, ROWS:, :] = tokens
            heads_ref[stream, :, chans] = tokens[:ROWS]

    def decays(index):
        rates = pltpu.roll(rates_ref[...], groups - index * in_tile, 1)
        decay = []
        wide = jnp.zeros((poles, TILE), F32)
        for g in range(in_tile):
            rate = jnp.broadcast_to(rates[:, g : g + 1], (poles, length))
            decay.append(jnp.exp(-rate * lag))
            wide = jnp.where(owner == g, rate[:, :TILE], wide)
        step_ref[:, tile_of(index)] = jnp.exp(-wide * length)
        for part, value in enumerate(halves(jnp.concatenate(decay, axis=0))):
            decay_ref[part, tile_of(index, in_tile * poles), :] = value

    def filters(index):
        chans = tile_of(index)
        query, left, right = (
            short_conv(stream, chans, length, padded_ref.at[index * 3 + stream], taps_ref) for stream in range(3)
        )
        query_ref[:, chans] = query
        gated_ref[:, chans] = left * right

    unrolled(channels // TILE, turn)
    unrolled(channels // TILE, decays)
    unrolled(channels // TILE, filters)


def states_kernel(before_ref, heads_ref, taps_ref, gated_ref, decay_ref, ends_ref, final_ref, first_ref, padded_ref):
    length, channels = gated_ref.shape
    poles = ends_ref.shape[1]
    in_tile = decay_ref.shape[1] // poles * TILE // channels
    owner = iota((poles, TILE), 1) // (TILE // in_tile)

    def begin(index):
        chans = tile_of(index)
        for stream in range(3):
            padded_ref[index * 3 + stream, :ROWS, :] = before_ref[stream, :, chans].astype(F32)
            padded_ref[index * 3 + stream, ROWS:, :] = heads_ref[stream, :, chans]
        query, left, right = (
            short_conv(stream, chans, ROWS, padded_ref.at[index * 3 + stream], taps_ref) for stream in range(3)
        )
        first_ref[:, chans] = query
        final_ref[:, chans] = jnp.concatenate([left * right, gated_ref[ROWS:, chans]], axis=0).astype(BF16)

    def leave(index):
        chans = tile_of(index)
        gated = final_ref[:, chans]
        states = tile_of(index, in_tile * poles)
        every = dot(decay_ref[0, states, :], gated) + dot(decay_ref[1, states, :], gated)
        ends = jnp.zeros((poles, TILE), F32)
        for g in range(in_tile):
            ends = jnp.where(owner == g, every[g * poles : (g + 1) * poles], ends)
        ends = ends.astype(BF16)
        for block in range(ends_ref.shape[0]):
            ends_ref[block, :, chans] = ends

    unrolled(channels // TILE, begin)
    unrolled(channels // TILE, leave)


def inside_kernel(gated_ref, skip_ref, rates_ref, residues_ref, lift_ref, base_ref):
    length, channels = gated_ref.shape
    poles, groups = rates_ref.shape
    width = channels // groups
    in_tile = TILE // width
    unit = identity(length)
    time = iota((poles, length), 1).astype(F32)
    member = (iota((in_tile, in_tile * poles), 1) // poles == iota((in_tile, in_tile * poles), 0)).astype(BF16)
    causal = iota((length, length), 1) >= iota((length, length), 0)

    def tile(index):
        chans = tile_of(index)
        shift = groups - index * in_tile
        rates = pltpu.roll(rates_ref[...], shift, 1)
        coef = pltpu.roll(residues_ref[...], shift, 1) * jnp.sqrt(2.0 * rates) / math.sqrt(poles)
        impulse, lift = [], []
        for g in range(in_tile):
            rate = jnp.broadcast_to(rates[:, g : g + 1], (poles, length))
            scale = jnp.broadcast_to(coef[:, g : g + 1], (poles, length))
            impulse.append(scale * jnp.exp(-rate * time))
            lift.append(scale * jnp.exp(-rate * (time + 1.0)))
        states = tile_of(index, in_tile * poles)
        lift_ref[:, states] = turned(jnp.concatenate(lift, axis=0).astype(BF16), unit).astype(BF16)
        high, low = halves(jnp.concatenate(impulse, axis=0))
        response = dot(member, high) + dot(member, low)
        gated = gated_ref[:, chans]
        signal = turned(gated, unit).astype(BF16)
        parts = []
        for pair in range(in_tile // 2):
            blocks = []
            for g in (2 * pair, 2 * pair + 1):
                spread = jnp.broadcast_to(response[g : g + 1], (length, length))
                shifted = pltpu.roll(spread, 0, 1, stride=1, stride_axis=0)
                blocks.append(jnp.where(causal, shifted, 0.0).astype(BF16))
            both = dot(signal[pair * 2 * width : (pair + 1) * 2 * width], jnp.concatenate(blocks, axis=1))
            parts += [both[:width, :length], both[width:, length:]]
        high, low = halves(jnp.concatenate(parts, axis=0))
        base_ref[:, chans] = turned(high, unit) + turned(low, unit) + skip_ref[:, chans] * gated.astype(F32)

    unrolled(channels // TILE, tile)


def finish_kernel(at_ref, ends_ref, step_ref, lift_ref, query_ref, first_ref, base_ref, mine_ref, other_ref, mixed_ref, state_ref):
    length, channels = mixed_ref.shape
    poles = step_ref.shape[0]
    in_tile = lift_ref.shape[1] // poles * TILE // channels
    me, core = at_ref[0], at_ref[1]

    def earlier(block, state):
        return jnp.where(block < me, step_ref[...] * state + ends_ref[block].astype(F32), state)

    state_ref[...] = lax.fori_loop(0, ends_ref.shape[0] - 1, earlier, jnp.zeros((poles, channels), F32))
    owner = iota((poles, TILE), 1) // (TILE // in_tile)

    def tile(index):
        chans = tile_of(index)
        entering = state_ref[:, chans]
        apart = jnp.concatenate([jnp.where(owner == g, entering, 0.0) for g in range(in_tile)], axis=0)
        high, low = halves(apart)
        states = tile_of(index, in_tile * poles)
        lift = lift_ref[:, states]
        carried = dot(lift, high) + dot(lift, low)
        query = jnp.concatenate([first_ref[:, chans], query_ref[ROWS:, chans]], axis=0)
        mixed_ref[:, chans] = (query * (base_ref[:, chans] + carried)).astype(BF16)

    unrolled(channels // TILE, tile)
    share = channels // CORES
    mine_ref[...] = mixed_ref[:, tile_of(core, share)]
    other_ref[...] = mixed_ref[:, tile_of(1 - core, share)]


def project_kernel(at_ref, own_ref, up_ref, second_ref, down_ref, *rest):
    *weight_refs, mine_ref, other_ref, layers_ref = rest
    layer = at_ref[0]
    layers_ref[layer] = own_ref[...]
    layers_ref[lax.rem(layer + 3, 4)] = up_ref[...]
    layers_ref[lax.rem(layer + 2, 4)] = second_ref[...]
    layers_ref[lax.rem(layer + 1, 4)] = down_ref[...]
    length, features = mine_ref.shape
    for column in range(0, features, COLUMNS):
        columns = slice(column, column + COLUMNS)
        total = None
        for at, ref in enumerate(weight_refs):
            term = dot(layers_ref[at_ref[1 + at]], ref[:, columns])
            total = term if total is None else total + term
        mine_ref[:, columns] = total[:length]
        other_ref[:, columns] = total[length:].astype(BF16)


def swap(value, *bits):
    count = lax.axis_size("ctx")
    pairs = [(source, source ^ bits[source % len(bits)]) for source in range(count)]
    return lax.ppermute(value, "ctx", pairs)


def after(value, earlier):
    return lax.optimization_barrier((value, earlier))[0]


def around(value, steps):
    count = lax.axis_size("tp")
    return lax.ppermute(value, "tp", [(source, (source + steps) % count) for source in range(count)])


def local(streams, conv_weight, rates, residues, skip, out_weight):
    channels, length = streams.shape[1:]
    groups, poles = rates.shape
    blocks, layers = lax.axis_size("ctx"), lax.axis_size("tp")
    rows, features = out_weight.shape
    share = channels // CORES
    square = blocks == 8 and rows == share

    rates, residues, skip = rates.T, residues.T, skip[None, :]
    (tails,) = call(tails_kernel, [((3, ROWS, channels), BF16)], "tails", streams)
    before = from_behind(tails, "ctx", 1)
    if square:
        near = swap(after(out_weight, tails), 2, 4)
    tiles = channels // TILE
    heads, query, gated, decay, step = call(
        prepare_kernel,
        [
            ((3, ROWS, channels), F32),
            ((length, channels), F32),
            ((length, channels), F32),
            ((2, groups * poles, length), BF16),
            ((poles, channels), F32),
        ],
        "prepare",
        streams, conv_weight, rates,
        scratch=[pltpu.VMEM((3 * tiles, ROWS + length, TILE), F32)],
        flops=10**9,
    )
    ends, gated, first = call(
        states_kernel,
        [((blocks, poles, channels), BF16), ((length, channels), BF16), ((ROWS, channels), F32)],
        "states",
        before, heads, conv_weight, gated, decay,
        scratch=[pltpu.VMEM((3 * tiles, 2 * ROWS, TILE), F32)],
    )
    all_ends = lax.all_to_all(ends, "ctx", split_axis=0, concat_axis=0, tiled=True)
    lift, base = call(
        inside_kernel,
        [((length, groups * poles), BF16), ((length, channels), F32)],
        "inside",
        gated, skip, rates, residues,
        flops=10**9,
    )
    if square:
        base, near = lax.optimization_barrier((base, near))
        other_near = swap(after(out_weight, base), 4, 2)
    me = lax.axis_index("ctx").astype(jnp.int32)
    core = me % CORES
    smem = [pl.BlockSpec(memory_space=pltpu.SMEM)]
    outs = [((length, share), BF16), ((length, share), BF16), ((length, channels), BF16)]
    mine, other, mixed = call(
        finish_kernel,
        outs,
        "finish",
        jnp.stack([me, core]), all_ends, step, lift, query, first, base,
        specs=smem + whole(6),
        scratch=[pltpu.VMEM((poles, channels), F32)],
    )
    if rows != share:
        by_core = mixed.reshape(length, share // rows, CORES, rows).transpose(2, 0, 1, 3)
        by_core = by_core.reshape(CORES, length, share)
        mine = lax.dynamic_index_in_dim(by_core, core, 0, keepdims=False)
        other = lax.dynamic_index_in_dim(by_core, 1 - core, 0, keepdims=False)
    block = jnp.concatenate([mine, swap(other, 1)], axis=0)
    layer = lax.axis_index("tp").astype(jnp.int32)
    up, down = around(block, 1), around(block, -1)
    second = around(after(up, down), 1)
    if square:
        diagonal = swap(after(near, block), 4, 2)
        weight = (out_weight, near, other_near, diagonal)
    else:
        core_groups = [list(range(core, blocks, CORES)) for core in range(CORES)]
        weight = lax.all_gather(out_weight, "ctx", axis=0, axis_index_groups=core_groups)
        weight = tuple(weight.reshape(layers, share, features))
    first_row = jnp.where(core == 0, 1, 2)
    chip = me // CORES
    place = [chip, chip ^ first_row, chip ^ (3 - first_row), chip ^ 3] if square else [jnp.full_like(me, at) for at in range(4)]
    mine, other = call(
        project_kernel,
        [((length, features), F32), ((length, features), BF16)],
        "project",
        jnp.stack([layer] + place), block, up, second, down, *weight,
        specs=smem + whole(4 + len(weight)),
        scratch=[pltpu.VMEM((layers,) + block.shape, BF16)],
        flops=10**9,
    )
    other = swap(other, 1)
    return (mine + other.astype(F32)).astype(BF16)


def solution(mesh):
    return jax.shard_map(
        local,
        mesh=mesh,
        in_specs=(
            P(None, "tp", "ctx"),
            P(None, None, "tp"),
            P("tp", None),
            P("tp", None),
            P("tp"),
            P("ctx", "tp"),
        ),
        out_specs=P("ctx", "tp"),
        check_vma=False,
    )
```

```python
import functools
import math

import jax
import jax.numpy as jnp
from jax import lax
from jax.experimental import pallas as pl
from jax.experimental.pallas import tpu as pltpu
from jax.sharding import PartitionSpec as P

F32 = jnp.float32
BF16 = jnp.bfloat16
ROWS = 8
TILE = 128
CORES = 2
COLUMNS = 256
VMEM_LIMIT = 24 * 1024 * 1024
PLAIN = (((1,), (0,)), ((), ()))
CONTRACT_LANES = (((1,), (1,)), ((), ()))


def from_behind(value, axis, steps):
    count = lax.axis_size(axis)
    leading, last = (max(0, -steps), min(count, count - steps))
    return lax.ppermute(value, axis, [(source, source + steps) for source in range(leading, last)])


def dot(left, right, dims=PLAIN):
    return lax.dot_general(left, right, dims, preferred_element_type=F32)


def halves(value):
    high = value.astype(BF16)
    return high, (value - high.astype(F32)).astype(BF16)


def iota(shape, axis):
    return lax.broadcasted_iota(jnp.int32, shape, axis)


def identity(size):
    return (iota((size, size), 0) == iota((size, size), 1)).astype(BF16)


def turned(value, unit):
    return dot(unit, value, CONTRACT_LANES)


def whole(count):
    return [pl.BlockSpec(memory_space=pltpu.VMEM)] * count


def call(kernel, outs, name, *operands, specs=None, scratch=(), flops=10**8):
    return pl.pallas_call(
        kernel,
        out_shape=tuple(jax.ShapeDtypeStruct(*out) for out in outs),
        in_specs=whole(len(operands)) if specs is None else specs,
        out_specs=tuple(whole(len(outs))),
        scratch_shapes=scratch,
        compiler_params=pltpu.CompilerParams(vmem_limit_bytes=VMEM_LIMIT),
        cost_estimate=pl.CostEstimate(flops=flops, bytes_accessed=flops // 1000, transcendentals=0),
        name=name,
    )(*operands)


def tile_of(index, size=TILE):
    return pl.ds(pl.multiple_of(index * size, size), size)


def unrolled(count, body):
    def step(index, carry):
        body(index)
        return carry

    lax.fori_loop(0, count, step, 0, unroll=math.gcd(count, 4))


def tails_kernel(streams_ref, tails_ref):
    length = streams_ref.shape[2]
    pick = (iota((2 * ROWS, length), 1) == iota((2 * ROWS, length), 0) + (length - ROWS)).astype(BF16)
    for stream in range(streams_ref.shape[0]):
        rows = dot(pick, streams_ref[stream], CONTRACT_LANES)
        tails_ref[stream] = rows[:ROWS].astype(BF16)


def short_conv(stream, chans, rows, padded, taps_ref):
    total = None
    for shift in range(taps_ref.shape[1]):
        term = taps_ref[stream, shift : shift + 1, chans] * padded[pl.ds(ROWS - shift, rows), :]
        total = term if total is None else total + term
    return total


def prepare_kernel(streams_ref, taps_ref, rates_ref, heads_ref, query_ref, gated_ref, decay_ref, step_ref, padded_ref):
    channels, length = streams_ref.shape[1:]
    poles, groups = rates_ref.shape
    width = channels // groups
    in_tile = TILE // width
    unit = identity(length)
    lag = (length - 1) - iota((poles, length), 1).astype(F32)
    owner = iota((poles, TILE), 1) // width

    def turn(index):
        chans = tile_of(index)
        for stream in range(3):
            tokens = turned(streams_ref[stream, chans, :], unit)
            padded_ref[index * 3 + stream, :ROWS, :] = jnp.zeros((ROWS, TILE), F32)
            padded_ref[index * 3 + stream, ROWS:, :] = tokens
            heads_ref[stream, :, chans] = tokens[:ROWS]

    def decays(index):
        rates = pltpu.roll(rates_ref[...], groups - index * in_tile, 1)
        decay = []
        wide = jnp.zeros((poles, TILE), F32)
        for g in range(in_tile):
            rate = jnp.broadcast_to(rates[:, g : g + 1], (poles, length))
            decay.append(jnp.exp(-rate * lag))
            wide = jnp.where(owner == g, rate[:, :TILE], wide)
        step_ref[:, tile_of(index)] = jnp.exp(-wide * length)
        for part, value in enumerate(halves(jnp.concatenate(decay, axis=0))):
            decay_ref[part, tile_of(index, in_tile * poles), :] = value

    def filters(index):
        chans = tile_of(index)
        query, left, right = (
            short_conv(stream, chans, length, padded_ref.at[index * 3 + stream], taps_ref) for stream in range(3)
        )
        query_ref[:, chans] = query.astype(BF16)
        gated_ref[:, chans] = left * right

    unrolled(channels // TILE, turn)
    unrolled(channels // TILE, decays)
    unrolled(channels // TILE, filters)


def states_kernel(before_ref, heads_ref, taps_ref, gated_ref, decay_ref, ends_ref, final_ref, first_ref, padded_ref):
    length, channels = gated_ref.shape
    poles = ends_ref.shape[1]
    in_tile = decay_ref.shape[1] // poles * TILE // channels
    owner = iota((poles, TILE), 1) // (TILE // in_tile)

    def begin(index):
        chans = tile_of(index)
        for stream in range(3):
            padded_ref[index * 3 + stream, :ROWS, :] = before_ref[stream, :, chans].astype(F32)
            padded_ref[index * 3 + stream, ROWS:, :] = heads_ref[stream, :, chans]
        query, left, right = (
            short_conv(stream, chans, ROWS, padded_ref.at[index * 3 + stream], taps_ref) for stream in range(3)
        )
        first_ref[:, chans] = query
        final_ref[:, chans] = jnp.concatenate([left * right, gated_ref[ROWS:, chans]], axis=0).astype(BF16)

    def leave(index):
        chans = tile_of(index)
        gated = final_ref[:, chans]
        states = tile_of(index, in_tile * poles)
        every = dot(decay_ref[0, states, :], gated) + dot(decay_ref[1, states, :], gated)
        ends = jnp.zeros((poles, TILE), F32)
        for g in range(in_tile):
            ends = jnp.where(owner == g, every[g * poles : (g + 1) * poles], ends)
        ends = ends.astype(BF16)
        for block in range(ends_ref.shape[0]):
            ends_ref[block, :, chans] = ends

    unrolled(channels // TILE, begin)
    unrolled(channels // TILE, leave)


def inside_kernel(gated_ref, skip_ref, rates_ref, residues_ref, lift_ref, base_ref):
    length, channels = gated_ref.shape
    poles, groups = rates_ref.shape
    width = channels // groups
    in_tile = TILE // width
    unit = identity(length)
    time = iota((poles, length), 1).astype(F32)
    member = (iota((in_tile, in_tile * poles), 1) // poles == iota((in_tile, in_tile * poles), 0)).astype(BF16)
    causal = iota((length, length), 1) >= iota((length, length), 0)

    def tile(index):
        chans = tile_of(index)
        shift = groups - index * in_tile
        rates = pltpu.roll(rates_ref[...], shift, 1)
        coef = pltpu.roll(residues_ref[...], shift, 1) * jnp.sqrt(2.0 * rates) / math.sqrt(poles)
        impulse, lift = [], []
        for g in range(in_tile):
            rate = jnp.broadcast_to(rates[:, g : g + 1], (poles, length))
            scale = jnp.broadcast_to(coef[:, g : g + 1], (poles, length))
            impulse.append(scale * jnp.exp(-rate * time))
            lift.append(scale * jnp.exp(-rate * (time + 1.0)))
        states = tile_of(index, in_tile * poles)
        lift_ref[:, states] = turned(jnp.concatenate(lift, axis=0).astype(BF16), unit).astype(BF16)
        high, low = halves(jnp.concatenate(impulse, axis=0))
        response = dot(member, high) + dot(member, low)
        gated = gated_ref[:, chans]
        signal = turned(gated, unit).astype(BF16)
        parts = []
        for pair in range(in_tile // 2):
            blocks = []
            for g in (2 * pair, 2 * pair + 1):
                spread = jnp.broadcast_to(response[g : g + 1], (length, length))
                shifted = pltpu.roll(spread, 0, 1, stride=1, stride_axis=0)
                blocks.append(jnp.where(causal, shifted, 0.0).astype(BF16))
            both = dot(signal[pair * 2 * width : (pair + 1) * 2 * width], jnp.concatenate(blocks, axis=1))
            parts += [both[:width, :length], both[width:, length:]]
        high, low = halves(jnp.concatenate(parts, axis=0))
        base_ref[:, chans] = turned(high, unit) + turned(low, unit) + skip_ref[:, chans] * gated.astype(F32)

    unrolled(channels // TILE, tile)


def finish_kernel(at_ref, ends_ref, step_ref, lift_ref, query_ref, first_ref, base_ref, mine_ref, other_ref, mixed_ref, state_ref):
    length, channels = mixed_ref.shape
    poles = step_ref.shape[0]
    in_tile = lift_ref.shape[1] // poles * TILE // channels
    me, core = at_ref[0], at_ref[1]

    def earlier(block, state):
        return jnp.where(block < me, step_ref[...] * state + ends_ref[block].astype(F32), state)

    state_ref[...] = lax.fori_loop(0, ends_ref.shape[0] - 1, earlier, jnp.zeros((poles, channels), F32))
    owner = iota((poles, TILE), 1) // (TILE // in_tile)

    def tile(index):
        chans = tile_of(index)
        entering = state_ref[:, chans]
        apart = jnp.concatenate([jnp.where(owner == g, entering, 0.0) for g in range(in_tile)], axis=0)
        high, low = halves(apart)
        states = tile_of(index, in_tile * poles)
        lift = lift_ref[:, states]
        carried = dot(lift, high) + dot(lift, low)
        query = jnp.concatenate([first_ref[:, chans], query_ref[:, chans].astype(F32)[ROWS:]], axis=0)
        mixed_ref[:, chans] = (query * (base_ref[:, chans] + carried)).astype(BF16)

    unrolled(channels // TILE, tile)
    share = channels // CORES
    mine_ref[...] = mixed_ref[:, tile_of(core, share)]
    other_ref[...] = mixed_ref[:, tile_of(1 - core, share)]


def early_kernel(at_ref, own_ref, up_ref, down_ref, *rest):
    *weight_refs, total_ref, layers_ref = rest
    layer = at_ref[0]
    layers_ref[layer] = own_ref[...]
    layers_ref[lax.rem(layer + 3, 4)] = up_ref[...]
    layers_ref[lax.rem(layer + 2, 4)] = jnp.zeros_like(own_ref)
    layers_ref[lax.rem(layer + 1, 4)] = down_ref[...]
    for column in range(0, total_ref.shape[1], COLUMNS):
        columns = slice(column, column + COLUMNS)
        total = None
        for at, ref in enumerate(weight_refs):
            term = dot(layers_ref[at_ref[1 + at]], ref[:, columns])
            total = term if total is None else total + term
        total_ref[:, columns] = total


def late_kernel(first, at_ref, second_ref, total_ref, *rest):
    *weight_refs, out_ref = rest
    tokens = pl.ds(first, out_ref.shape[0])
    last = lax.rem(at_ref[0] + 2, 4)
    for at, ref in enumerate(weight_refs):

        @pl.when(at_ref[1 + at] == last)
        def _():
            out_ref[...] = (total_ref[tokens, :] + dot(second_ref[tokens, :], ref[...])).astype(out_ref.dtype)


def swap(value, *bits):
    count = lax.axis_size("ctx")
    pairs = [(source, source ^ bits[source % len(bits)]) for source in range(count)]
    return lax.ppermute(value, "ctx", pairs)


def after(value, earlier):
    return lax.optimization_barrier((value, earlier))[0]


def around(value, steps):
    count = lax.axis_size("tp")
    return lax.ppermute(value, "tp", [(source, (source + steps) % count) for source in range(count)])


def local(streams, conv_weight, rates, residues, skip, out_weight):
    channels, length = streams.shape[1:]
    groups, poles = rates.shape
    blocks, layers = lax.axis_size("ctx"), lax.axis_size("tp")
    rows, features = out_weight.shape
    share = channels // CORES
    square = blocks == 8 and rows == share

    rates, residues, skip = rates.T, residues.T, skip[None, :]
    (tails,) = call(tails_kernel, [((3, ROWS, channels), BF16)], "tails", streams)
    before = from_behind(tails, "ctx", 1)
    if square:
        near = swap(after(out_weight, tails), 2, 4)
    tiles = channels // TILE
    heads, query, gated, decay, step = call(
        prepare_kernel,
        [
            ((3, ROWS, channels), F32),
            ((length, channels), BF16),
            ((length, channels), F32),
            ((2, groups * poles, length), BF16),
            ((poles, channels), F32),
        ],
        "prepare",
        streams, conv_weight, rates,
        scratch=[pltpu.VMEM((3 * tiles, ROWS + length, TILE), F32)],
        flops=10**9,
    )
    ends, gated, first = call(
        states_kernel,
        [((blocks, poles, channels), BF16), ((length, channels), BF16), ((ROWS, channels), F32)],
        "states",
        before, heads, conv_weight, gated, decay,
        scratch=[pltpu.VMEM((3 * tiles, 2 * ROWS, TILE), F32)],
    )
    all_ends = lax.all_to_all(ends, "ctx", split_axis=0, concat_axis=0, tiled=True)
    lift, base = call(
        inside_kernel,
        [((length, groups * poles), BF16), ((length, channels), F32)],
        "inside",
        gated, skip, rates, residues,
        flops=10**9,
    )
    if square:
        base, near = lax.optimization_barrier((base, near))
        other_near = swap(after(out_weight, base), 4, 2)
    me = lax.axis_index("ctx").astype(jnp.int32)
    core = me % CORES
    smem = [pl.BlockSpec(memory_space=pltpu.SMEM)]
    outs = [((length, share), BF16), ((length, share), BF16), ((length, channels), BF16)]
    mine, other, mixed = call(
        finish_kernel,
        outs,
        "finish",
        jnp.stack([me, core]), all_ends, step, lift, query, first, base,
        specs=smem + whole(6),
        scratch=[pltpu.VMEM((poles, channels), F32)],
    )
    if rows != share:
        by_core = mixed.reshape(length, share // rows, CORES, rows).transpose(2, 0, 1, 3)
        by_core = by_core.reshape(CORES, length, share)
        mine = lax.dynamic_index_in_dim(by_core, core, 0, keepdims=False)
        other = lax.dynamic_index_in_dim(by_core, 1 - core, 0, keepdims=False)
    block = jnp.concatenate([mine, swap(other, 1)], axis=0)
    layer = lax.axis_index("tp").astype(jnp.int32)
    up, down = around(block, 1), around(block, -1)
    second = around(after(up, down), 1)
    if square:
        diagonal = swap(after(near, (down, other_near)), 4, 2)
        weight = (out_weight, near, other_near, diagonal)
    else:
        core_groups = [list(range(core, blocks, CORES)) for core in range(CORES)]
        weight = lax.all_gather(out_weight, "ctx", axis=0, axis_index_groups=core_groups)
        weight = tuple(weight.reshape(layers, share, features))
    first_row = jnp.where(core == 0, 1, 2)
    chip = me // CORES
    place = [chip, chip ^ first_row, chip ^ (3 - first_row), chip ^ 3] if square else [jnp.full_like(me, at) for at in range(4)]
    at = jnp.stack([layer] + place)
    (total,) = call(
        early_kernel,
        [((CORES * length, features), F32)],
        "early",
        at, block, up, down, *weight,
        specs=smem + whole(3 + len(weight)),
        scratch=[pltpu.VMEM((layers,) + block.shape, BF16)],
        flops=1,
    )
    sides = []
    for side, kind in ((1, BF16), (0, F32)):
        sides += call(
            functools.partial(late_kernel, side * length),
            [((length, features), kind)],
            "late",
            at, second, total, *weight,
            specs=smem + whole(2 + len(weight)),
        )
    other, mine = sides
    other = swap(other, 1)
    return (mine + other.astype(F32)).astype(BF16)


def solution(mesh):
    return jax.shard_map(
        local,
        mesh=mesh,
        in_specs=(
            P(None, "tp", "ctx"),
            P(None, None, "tp"),
            P("tp", None),
            P("tp", None),
            P("tp"),
            P("ctx", "tp"),
        ),
        out_specs=P("ctx", "tp"),
        check_vma=False,
    )
```

```python
import functools
import math

import jax
import jax.numpy as jnp
from jax import lax
from jax.experimental import pallas as pl
from jax.experimental.pallas import tpu as pltpu
from jax.sharding import PartitionSpec as P

F32 = jnp.float32
BF16 = jnp.bfloat16
ROWS = 8
TILE = 128
CORES = 2
COLUMNS = 256
VMEM_LIMIT = 24 * 1024 * 1024
PLAIN = (((1,), (0,)), ((), ()))
CONTRACT_LANES = (((1,), (1,)), ((), ()))


def from_behind(value, axis, steps):
    count = lax.axis_size(axis)
    leading, last = (max(0, -steps), min(count, count - steps))
    return lax.ppermute(value, axis, [(source, source + steps) for source in range(leading, last)])


def dot(left, right, dims=PLAIN):
    return lax.dot_general(left, right, dims, preferred_element_type=F32)


def halves(value):
    high = value.astype(BF16)
    return high, (value - high.astype(F32)).astype(BF16)


def iota(shape, axis):
    return lax.broadcasted_iota(jnp.int32, shape, axis)


def identity(size):
    return (iota((size, size), 0) == iota((size, size), 1)).astype(BF16)


def turned(value, unit):
    return dot(unit, value, CONTRACT_LANES)


def whole(count):
    return [pl.BlockSpec(memory_space=pltpu.VMEM)] * count


def call(kernel, outs, name, *operands, specs=None, scratch=(), flops=10**8):
    return pl.pallas_call(
        kernel,
        out_shape=tuple(jax.ShapeDtypeStruct(*out) for out in outs),
        in_specs=whole(len(operands)) if specs is None else specs,
        out_specs=tuple(whole(len(outs))),
        scratch_shapes=scratch,
        compiler_params=pltpu.CompilerParams(vmem_limit_bytes=VMEM_LIMIT),
        cost_estimate=pl.CostEstimate(flops=flops, bytes_accessed=flops // 100, transcendentals=0),
        name=name,
    )(*operands)


def tile_of(index, size=TILE):
    return pl.ds(pl.multiple_of(index * size, size), size)


def unrolled(count, body):
    def step(index, carry):
        body(index)
        return carry

    lax.fori_loop(0, count, step, 0, unroll=math.gcd(count, 4))


def tails_kernel(streams_ref, tails_ref):
    length = streams_ref.shape[2]
    pick = (iota((2 * ROWS, length), 1) == iota((2 * ROWS, length), 0) + (length - ROWS)).astype(BF16)
    for stream in range(streams_ref.shape[0]):
        rows = dot(pick, streams_ref[stream], CONTRACT_LANES)
        tails_ref[stream] = rows[:ROWS].astype(BF16)


def short_conv(stream, chans, rows, padded, taps_ref):
    total = None
    for shift in range(taps_ref.shape[1]):
        term = taps_ref[stream, shift : shift + 1, chans] * padded[pl.ds(ROWS - shift, rows), :]
        total = term if total is None else total + term
    return total


def prepare_kernel(streams_ref, taps_ref, rates_ref, heads_ref, query_ref, gated_ref, decay_ref, step_ref, padded_ref):
    channels, length = streams_ref.shape[1:]
    poles, groups = rates_ref.shape
    width = channels // groups
    in_tile = TILE // width
    unit = identity(length)
    lag = (length - 1) - iota((poles, length), 1).astype(F32)
    owner = iota((poles, TILE), 1) // width

    def turn(index):
        chans = tile_of(index)
        for stream in range(3):
            tokens = turned(streams_ref[stream, chans, :], unit)
            padded_ref[index * 3 + stream, :ROWS, :] = jnp.zeros((ROWS, TILE), F32)
            padded_ref[index * 3 + stream, ROWS:, :] = tokens
            heads_ref[stream, :, chans] = tokens[:ROWS]

    def decays(index):
        rates = pltpu.roll(rates_ref[...], groups - index * in_tile, 1)
        decay = []
        wide = jnp.zeros((poles, TILE), F32)
        for g in range(in_tile):
            rate = jnp.broadcast_to(rates[:, g : g + 1], (poles, length))
            decay.append(jnp.exp(-rate * lag))
            wide = jnp.where(owner == g, rate[:, :TILE], wide)
        step_ref[:, tile_of(index)] = jnp.exp(-wide * length)
        for part, value in enumerate(halves(jnp.concatenate(decay, axis=0))):
            decay_ref[part, tile_of(index, in_tile * poles), :] = value

    def filters(index):
        chans = tile_of(index)
        query, left, right = (
            short_conv(stream, chans, length, padded_ref.at[index * 3 + stream], taps_ref) for stream in range(3)
        )
        query_ref[:, chans] = query.astype(BF16)
        gated_ref[:, chans] = left * right

    unrolled(channels // TILE, turn)
    unrolled(channels // TILE, decays)
    unrolled(channels // TILE, filters)


def states_kernel(before_ref, heads_ref, taps_ref, gated_ref, decay_ref, ends_ref, final_ref, first_ref, padded_ref):
    length, channels = gated_ref.shape
    poles = ends_ref.shape[1]
    in_tile = decay_ref.shape[1] // poles * TILE // channels
    owner = iota((poles, TILE), 1) // (TILE // in_tile)

    def begin(index):
        chans = tile_of(index)
        for stream in range(3):
            padded_ref[index * 3 + stream, :ROWS, :] = before_ref[stream, :, chans].astype(F32)
            padded_ref[index * 3 + stream, ROWS:, :] = heads_ref[stream, :, chans]
        query, left, right = (
            short_conv(stream, chans, ROWS, padded_ref.at[index * 3 + stream], taps_ref) for stream in range(3)
        )
        first_ref[:, chans] = query
        final_ref[:, chans] = jnp.concatenate([left * right, gated_ref[ROWS:, chans]], axis=0).astype(BF16)

    def leave(index):
        chans = tile_of(index)
        gated = final_ref[:, chans]
        states = tile_of(index, in_tile * poles)
        every = dot(decay_ref[0, states, :], gated) + dot(decay_ref[1, states, :], gated)
        ends = jnp.zeros((poles, TILE), F32)
        for g in range(in_tile):
            ends = jnp.where(owner == g, every[g * poles : (g + 1) * poles], ends)
        ends = ends.astype(BF16)
        for block in range(ends_ref.shape[0]):
            ends_ref[block, :, chans] = ends

    unrolled(channels // TILE, begin)
    unrolled(channels // TILE, leave)


def inside_kernel(gated_ref, skip_ref, rates_ref, residues_ref, lift_ref, base_ref):
    length, channels = gated_ref.shape
    poles, groups = rates_ref.shape
    width = channels // groups
    in_tile = TILE // width
    unit = identity(length)
    time = iota((poles, length), 1).astype(F32)
    member = (iota((in_tile, in_tile * poles), 1) // poles == iota((in_tile, in_tile * poles), 0)).astype(BF16)
    causal = iota((length, length), 1) >= iota((length, length), 0)

    def tile(index):
        chans = tile_of(index)
        shift = groups - index * in_tile
        rates = pltpu.roll(rates_ref[...], shift, 1)
        coef = pltpu.roll(residues_ref[...], shift, 1) * jnp.sqrt(2.0 * rates) / math.sqrt(poles)
        impulse, lift = [], []
        for g in range(in_tile):
            rate = jnp.broadcast_to(rates[:, g : g + 1], (poles, length))
            scale = jnp.broadcast_to(coef[:, g : g + 1], (poles, length))
            impulse.append(scale * jnp.exp(-rate * time))
            lift.append(scale * jnp.exp(-rate * (time + 1.0)))
        states = tile_of(index, in_tile * poles)
        lift_ref[:, states] = turned(jnp.concatenate(lift, axis=0).astype(BF16), unit).astype(BF16)
        high, low = halves(jnp.concatenate(impulse, axis=0))
        response = dot(member, high) + dot(member, low)
        gated = gated_ref[:, chans]
        signal = turned(gated, unit).astype(BF16)
        parts = []
        for pair in range(in_tile // 2):
            blocks = []
            for g in (2 * pair, 2 * pair + 1):
                spread = jnp.broadcast_to(response[g : g + 1], (length, length))
                shifted = pltpu.roll(spread, 0, 1, stride=1, stride_axis=0)
                blocks.append(jnp.where(causal, shifted, 0.0).astype(BF16))
            both = dot(signal[pair * 2 * width : (pair + 1) * 2 * width], jnp.concatenate(blocks, axis=1))
            parts += [both[:width, :length], both[width:, length:]]
        high, low = halves(jnp.concatenate(parts, axis=0))
        base_ref[:, chans] = turned(high, unit) + turned(low, unit) + skip_ref[:, chans] * gated.astype(F32)

    unrolled(channels // TILE, tile)


def finish_kernel(at_ref, ends_ref, step_ref, lift_ref, query_ref, first_ref, base_ref, mine_ref, other_ref, mixed_ref, state_ref):
    length, channels = mixed_ref.shape
    poles = step_ref.shape[0]
    in_tile = lift_ref.shape[1] // poles * TILE // channels
    me, core = at_ref[0], at_ref[1]

    def earlier(block, state):
        return jnp.where(block < me, step_ref[...] * state + ends_ref[block].astype(F32), state)

    state_ref[...] = lax.fori_loop(0, ends_ref.shape[0] - 1, earlier, jnp.zeros((poles, channels), F32))
    owner = iota((poles, TILE), 1) // (TILE // in_tile)

    def tile(index):
        chans = tile_of(index)
        entering = state_ref[:, chans]
        apart = jnp.concatenate([jnp.where(owner == g, entering, 0.0) for g in range(in_tile)], axis=0)
        high, low = halves(apart)
        states = tile_of(index, in_tile * poles)
        lift = lift_ref[:, states]
        carried = dot(lift, high) + dot(lift, low)
        query = jnp.concatenate([first_ref[:, chans], query_ref[:, chans].astype(F32)[ROWS:]], axis=0)
        mixed_ref[:, chans] = (query * (base_ref[:, chans] + carried)).astype(BF16)

    unrolled(channels // TILE, tile)
    share = channels // CORES
    mine_ref[...] = mixed_ref[:, tile_of(core, share)]
    other_ref[...] = mixed_ref[:, tile_of(1 - core, share)]


def project_kernel(at_ref, own_ref, below_ref, above_ref, second_ref, far_ref, *rest):
    *weight_refs, mine_ref, other_ref, layers_ref = rest
    layer = at_ref[0]
    edge = (layer == 0) | (layer == 3)
    layers_ref[layer] = own_ref[...]
    layers_ref[jnp.where(layer == 0, 1, layer - 1)] = jnp.where(layer == 0, above_ref[...], below_ref[...])
    layers_ref[lax.rem(layer + 2, 4)] = second_ref[...]
    layers_ref[jnp.where(edge, 3 - layer, layer + 1)] = jnp.where(edge, far_ref[...], above_ref[...])
    length, features = mine_ref.shape
    for column in range(0, features, COLUMNS):
        columns = slice(column, column + COLUMNS)
        total = None
        for at, ref in enumerate(weight_refs):
            term = dot(layers_ref[at_ref[1 + at]], ref[:, columns])
            total = term if total is None else total + term
        mine_ref[:, columns] = total[:length]
        other_ref[:, columns] = total[length:].astype(BF16)


def swap(value, *bits):
    count = lax.axis_size("ctx")
    pairs = [(source, source ^ bits[source % len(bits)]) for source in range(count)]
    return lax.ppermute(value, "ctx", pairs)


def after(value, earlier):
    return lax.optimization_barrier((value, earlier))[0]


def over_layers(block):
    layer = lax.axis_index("tp")
    below = lax.ppermute(block, "tp", [(0, 1), (1, 2), (2, 3)])
    above = lax.ppermute(block, "tp", [(1, 0), (2, 1), (3, 2)])
    onward = jnp.where(layer == 1, above, jnp.where(layer == 2, below, block))
    second = lax.ppermute(onward, "tp", [(0, 2), (3, 1), (2, 3), (1, 0)])
    far = lax.ppermute(block, "tp", [(0, 3), (3, 0)])
    return below, above, second, far


def local(streams, conv_weight, rates, residues, skip, out_weight):
    channels, length = streams.shape[1:]
    groups, poles = rates.shape
    blocks, layers = lax.axis_size("ctx"), lax.axis_size("tp")
    rows, features = out_weight.shape
    share = channels // CORES
    square = blocks == 8 and rows == share

    rates, residues, skip = rates.T, residues.T, skip[None, :]
    (tails,) = call(tails_kernel, [((3, ROWS, channels), BF16)], "tails", streams)
    before = from_behind(tails, "ctx", 1)
    if square:
        near = swap(out_weight, 2, 4)
    tiles = channels // TILE
    heads, query, gated, decay, step = call(
        prepare_kernel,
        [
            ((3, ROWS, channels), F32),
            ((length, channels), BF16),
            ((length, channels), F32),
            ((2, groups * poles, length), BF16),
            ((poles, channels), F32),
        ],
        "prepare",
        streams, conv_weight, rates,
        scratch=[pltpu.VMEM((3 * tiles, ROWS + length, TILE), F32)],
        flops=10**9,
    )
    ends, gated, first = call(
        states_kernel,
        [((blocks, poles, channels), BF16), ((length, channels), BF16), ((ROWS, channels), F32)],
        "states",
        before, heads, conv_weight, gated, decay,
        scratch=[pltpu.VMEM((3 * tiles, 2 * ROWS, TILE), F32)],
    )
    all_ends = lax.all_to_all(ends, "ctx", split_axis=0, concat_axis=0, tiled=True)
    lift, base = call(
        inside_kernel,
        [((length, groups * poles), BF16), ((length, channels), F32)],
        "inside",
        gated, skip, rates, residues,
        flops=10**9,
    )
    if square:
        base, near = lax.optimization_barrier((base, near))
        other_near = swap(after(out_weight, base), 4, 2)
    me = lax.axis_index("ctx").astype(jnp.int32)
    core = me % CORES
    smem = [pl.BlockSpec(memory_space=pltpu.SMEM)]
    outs = [((length, share), BF16), ((length, share), BF16), ((length, channels), BF16)]
    mine, other, mixed = call(
        finish_kernel,
        outs,
        "finish",
        jnp.stack([me, core]), all_ends, step, lift, query, first, base,
        specs=smem + whole(6),
        scratch=[pltpu.VMEM((poles, channels), F32)],
    )
    if rows != share:
        by_core = mixed.reshape(length, share // rows, CORES, rows).transpose(2, 0, 1, 3)
        by_core = by_core.reshape(CORES, length, share)
        mine = lax.dynamic_index_in_dim(by_core, core, 0, keepdims=False)
        other = lax.dynamic_index_in_dim(by_core, 1 - core, 0, keepdims=False)
    block = jnp.concatenate([mine, swap(other, 1)], axis=0)
    layer = lax.axis_index("tp").astype(jnp.int32)
    blocks_of_layers = over_layers(block)
    if square:
        diagonal = swap(after(near, block), 4, 2)
        weight = (out_weight, near, other_near, diagonal)
    else:
        core_groups = [list(range(core, blocks, CORES)) for core in range(CORES)]
        weight = lax.all_gather(out_weight, "ctx", axis=0, axis_index_groups=core_groups)
        weight = tuple(weight.reshape(layers, share, features))
    first_row = jnp.where(core == 0, 1, 2)
    chip = me // CORES
    place = [chip, chip ^ first_row, chip ^ (3 - first_row), chip ^ 3] if square else [jnp.full_like(me, at) for at in range(4)]
    mine, other = call(
        project_kernel,
        [((length, features), F32), ((length, features), BF16)],
        "project",
        jnp.stack([layer] + place), block, *blocks_of_layers, *weight,
        specs=smem + whole(5 + len(weight)),
        scratch=[pltpu.VMEM((layers,) + block.shape, BF16)],
        flops=10**9,
    )
    other = swap(other, 1)
    return (mine + other.astype(F32)).astype(BF16)


def solution(mesh):
    return jax.shard_map(
        local,
        mesh=mesh,
        in_specs=(
            P(None, "tp", "ctx"),
            P(None, None, "tp"),
            P("tp", None),
            P("tp", None),
            P("tp"),
            P("ctx", "tp"),
        ),
        out_specs=P("ctx", "tp"),
        check_vma=False,
    )
```

```python
import functools
import math

import jax
import jax.numpy as jnp
from jax import lax
from jax.experimental import pallas as pl
from jax.experimental.pallas import tpu as pltpu
from jax.sharding import PartitionSpec as P

F32 = jnp.float32
BF16 = jnp.bfloat16
ROWS = 8
TILE = 128
CORES = 2
COLUMNS = 256
VMEM_LIMIT = 24 * 1024 * 1024
PLAIN = (((1,), (0,)), ((), ()))
CONTRACT_LANES = (((1,), (1,)), ((), ()))


def from_behind(value, axis, steps):
    count = lax.axis_size(axis)
    leading, last = (max(0, -steps), min(count, count - steps))
    return lax.ppermute(value, axis, [(source, source + steps) for source in range(leading, last)])


def dot(left, right, dims=PLAIN):
    return lax.dot_general(left, right, dims, preferred_element_type=F32)


def halves(value):
    high = value.astype(BF16)
    return high, (value - high.astype(F32)).astype(BF16)


def iota(shape, axis):
    return lax.broadcasted_iota(jnp.int32, shape, axis)


def identity(size):
    return (iota((size, size), 0) == iota((size, size), 1)).astype(BF16)


def turned(value, unit):
    return dot(unit, value, CONTRACT_LANES)


def whole(count):
    return [pl.BlockSpec(memory_space=pltpu.VMEM)] * count


def call(kernel, outs, name, *operands, specs=None, scratch=(), flops=10**8):
    return pl.pallas_call(
        kernel,
        out_shape=tuple(jax.ShapeDtypeStruct(*out) for out in outs),
        in_specs=whole(len(operands)) if specs is None else specs,
        out_specs=tuple(whole(len(outs))),
        scratch_shapes=scratch,
        compiler_params=pltpu.CompilerParams(vmem_limit_bytes=VMEM_LIMIT),
        cost_estimate=pl.CostEstimate(flops=flops, bytes_accessed=flops // 100, transcendentals=0),
        name=name,
    )(*operands)


def tile_of(index, size=TILE):
    return pl.ds(pl.multiple_of(index * size, size), size)


def unrolled(count, body):
    def step(index, carry):
        body(index)
        return carry

    lax.fori_loop(0, count, step, 0, unroll=math.gcd(count, 4))


def tails_kernel(streams_ref, tails_ref):
    length = streams_ref.shape[2]
    pick = (iota((2 * ROWS, length), 1) == iota((2 * ROWS, length), 0) + (length - ROWS)).astype(BF16)
    for stream in range(streams_ref.shape[0]):
        rows = dot(pick, streams_ref[stream], CONTRACT_LANES)
        tails_ref[stream] = rows[:ROWS].astype(BF16)


def short_conv(stream, chans, rows, padded, taps_ref):
    total = None
    for shift in range(taps_ref.shape[1]):
        term = taps_ref[stream, shift : shift + 1, chans] * padded[pl.ds(ROWS - shift, rows), :]
        total = term if total is None else total + term
    return total


def prepare_kernel(
    streams_ref, taps_ref, rates_ref, residues_ref,
    heads_ref, query_ref, gated_ref, decay_ref, step_ref, coef_ref, padded_ref,
):
    channels, length = streams_ref.shape[1:]
    poles, groups = rates_ref.shape
    width = channels // groups
    in_tile = TILE // width
    unit = identity(length)
    lag = (length - 1) - iota((poles, length), 1).astype(F32)
    owner = iota((poles, TILE), 1) // width
    coef_ref[...] = residues_ref[...] * jnp.sqrt(2.0 * rates_ref[...]) / math.sqrt(poles)

    def turn(index):
        chans = tile_of(index)
        for stream in range(3):
            tokens = turned(streams_ref[stream, chans, :], unit)
            padded_ref[index * 3 + stream, :ROWS, :] = jnp.zeros((ROWS, TILE), F32)
            padded_ref[index * 3 + stream, ROWS:, :] = tokens
            heads_ref[stream, :, chans] = tokens[:ROWS]

    def decays(index):
        rates = pltpu.roll(rates_ref[...], groups - index * in_tile, 1)
        decay = []
        wide = jnp.zeros((poles, TILE), F32)
        for g in range(in_tile):
            rate = jnp.broadcast_to(rates[:, g : g + 1], (poles, length))
            decay.append(jnp.exp(-rate * lag))
            wide = jnp.where(owner == g, rate[:, :TILE], wide)
        step_ref[:, tile_of(index)] = jnp.exp(-wide * length)
        for part, value in enumerate(halves(jnp.concatenate(decay, axis=0))):
            decay_ref[part, tile_of(index, in_tile * poles), :] = value

    def filters(index):
        chans = tile_of(index)
        query, left, right = (
            short_conv(stream, chans, length, padded_ref.at[index * 3 + stream], taps_ref) for stream in range(3)
        )
        query_ref[:, chans] = query.astype(BF16)
        gated_ref[:, chans] = left * right

    unrolled(channels // TILE, turn)
    unrolled(channels // TILE, decays)
    unrolled(channels // TILE, filters)


def states_kernel(before_ref, heads_ref, taps_ref, gated_ref, decay_ref, ends_ref, final_ref, first_ref, padded_ref):
    length, channels = gated_ref.shape
    poles = ends_ref.shape[1]
    in_tile = decay_ref.shape[1] // poles * TILE // channels
    owner = iota((poles, TILE), 1) // (TILE // in_tile)

    def begin(index):
        chans = tile_of(index)
        for stream in range(3):
            padded_ref[index * 3 + stream, :ROWS, :] = before_ref[stream, :, chans].astype(F32)
            padded_ref[index * 3 + stream, ROWS:, :] = heads_ref[stream, :, chans]
        query, left, right = (
            short_conv(stream, chans, ROWS, padded_ref.at[index * 3 + stream], taps_ref) for stream in range(3)
        )
        first_ref[:, chans] = query
        final_ref[:, chans] = jnp.concatenate([left * right, gated_ref[ROWS:, chans]], axis=0).astype(BF16)

    def leave(index):
        chans = tile_of(index)
        gated = final_ref[:, chans]
        states = tile_of(index, in_tile * poles)
        every = dot(decay_ref[0, states, :], gated) + dot(decay_ref[1, states, :], gated)
        ends = jnp.zeros((poles, TILE), F32)
        for g in range(in_tile):
            ends = jnp.where(owner == g, every[g * poles : (g + 1) * poles], ends)
        ends = ends.astype(BF16)
        for block in range(ends_ref.shape[0]):
            ends_ref[block, :, chans] = ends

    unrolled(channels // TILE, begin)
    unrolled(channels // TILE, leave)


def inside_kernel(gated_ref, skip_ref, rates_ref, coef_ref, lift_ref, base_ref):
    length, channels = gated_ref.shape
    poles, groups = rates_ref.shape
    width = channels // groups
    in_tile = TILE // width
    unit = identity(length)
    time = iota((poles, length), 1).astype(F32)
    member = (iota((in_tile, in_tile * poles), 1) // poles == iota((in_tile, in_tile * poles), 0)).astype(BF16)
    causal = iota((length, length), 1) >= iota((length, length), 0)

    def tile(index):
        chans = tile_of(index)
        shift = groups - index * in_tile
        rates = pltpu.roll(rates_ref[...], shift, 1)
        coef = pltpu.roll(coef_ref[...], shift, 1)
        impulse, lift = [], []
        for g in range(in_tile):
            rate = jnp.broadcast_to(rates[:, g : g + 1], (poles, length))
            scale = jnp.broadcast_to(coef[:, g : g + 1], (poles, length))
            impulse.append(scale * jnp.exp(-rate * time))
            lift.append(scale * jnp.exp(-rate * (time + 1.0)))
        states = tile_of(index, in_tile * poles)
        lift_ref[:, states] = turned(jnp.concatenate(lift, axis=0).astype(BF16), unit).astype(BF16)
        high, low = halves(jnp.concatenate(impulse, axis=0))
        response = dot(member, high) + dot(member, low)
        gated = gated_ref[:, chans]
        signal = turned(gated, unit).astype(BF16)
        parts = []
        for pair in range(in_tile // 2):
            blocks = []
            for g in (2 * pair, 2 * pair + 1):
                spread = jnp.broadcast_to(response[g : g + 1], (length, length))
                shifted = pltpu.roll(spread, 0, 1, stride=1, stride_axis=0)
                blocks.append(jnp.where(causal, shifted, 0.0).astype(BF16))
            both = dot(signal[pair * 2 * width : (pair + 1) * 2 * width], jnp.concatenate(blocks, axis=1))
            parts += [both[:width, :length], both[width:, length:]]
        high, low = halves(jnp.concatenate(parts, axis=0))
        base_ref[:, chans] = turned(high, unit) + turned(low, unit) + skip_ref[:, chans] * gated.astype(F32)

    unrolled(channels // TILE, tile)


def finish_kernel(at_ref, ends_ref, step_ref, lift_ref, query_ref, first_ref, base_ref, mine_ref, other_ref, mixed_ref, state_ref):
    length, channels = mixed_ref.shape
    poles = step_ref.shape[0]
    in_tile = lift_ref.shape[1] // poles * TILE // channels
    me, core = at_ref[0], at_ref[1]

    def earlier(block, state):
        return jnp.where(block < me, step_ref[...] * state + ends_ref[block].astype(F32), state)

    state_ref[...] = lax.fori_loop(0, ends_ref.shape[0] - 1, earlier, jnp.zeros((poles, channels), F32))
    owner = iota((poles, TILE), 1) // (TILE // in_tile)

    def tile(index):
        chans = tile_of(index)
        entering = state_ref[:, chans]
        apart = jnp.concatenate([jnp.where(owner == g, entering, 0.0) for g in range(in_tile)], axis=0)
        high, low = halves(apart)
        states = tile_of(index, in_tile * poles)
        lift = lift_ref[:, states]
        carried = dot(lift, high) + dot(lift, low)
        query = jnp.concatenate([first_ref[:, chans], query_ref[:, chans].astype(F32)[ROWS:]], axis=0)
        mixed_ref[:, chans] = (query * (base_ref[:, chans] + carried)).astype(BF16)

    unrolled(channels // TILE, tile)
    share = channels // CORES
    mine_ref[...] = mixed_ref[:, tile_of(core, share)]
    other_ref[...] = mixed_ref[:, tile_of(1 - core, share)]


def project_kernel(at_ref, own_ref, beside_ref, beyond_ref, across_ref, *rest):
    *weight_refs, mine_ref, other_ref, layers_ref = rest
    layer = at_ref[0]
    for bits, ref in enumerate((own_ref, beside_ref, beyond_ref, across_ref)):
        layers_ref[layer ^ bits] = ref[...]
    length, features = mine_ref.shape
    for column in range(0, features, COLUMNS):
        columns = slice(column, column + COLUMNS)
        total = None
        for at, ref in enumerate(weight_refs):
            term = dot(layers_ref[at_ref[1 + at]], ref[:, columns])
            total = term if total is None else total + term
        mine_ref[:, columns] = total[:length]
        other_ref[:, columns] = total[length:].astype(BF16)


def swap(value, *bits):
    count = lax.axis_size("ctx")
    pairs = [(source, source ^ bits[source % len(bits)]) for source in range(count)]
    return lax.ppermute(value, "ctx", pairs)


def after(value, earlier):
    return lax.optimization_barrier((value, earlier))[0]


def trade(value, bits):
    count = lax.axis_size("tp")
    return lax.ppermute(value, "tp", [(source, source ^ bits) for source in range(count)])


def local(streams, conv_weight, rates, residues, skip, out_weight):
    channels, length = streams.shape[1:]
    groups, poles = rates.shape
    blocks, layers = lax.axis_size("ctx"), lax.axis_size("tp")
    rows, features = out_weight.shape
    share = channels // CORES
    square = blocks == 8 and rows == share

    rates, residues, skip = rates.T, residues.T, skip[None, :]
    (tails,) = call(tails_kernel, [((3, ROWS, channels), BF16)], "tails", streams)
    before = from_behind(tails, "ctx", 1)
    if square:
        near = swap(out_weight, 2, 4)
    tiles = channels // TILE
    heads, query, gated, decay, step, coef = call(
        prepare_kernel,
        [
            ((3, ROWS, channels), F32),
            ((length, channels), BF16),
            ((length, channels), F32),
            ((2, groups * poles, length), BF16),
            ((poles, channels), F32),
            ((poles, groups), F32),
        ],
        "prepare",
        streams, conv_weight, rates, residues,
        scratch=[pltpu.VMEM((3 * tiles, ROWS + length, TILE), F32)],
        flops=10**9,
    )
    ends, gated, first = call(
        states_kernel,
        [((blocks, poles, channels), BF16), ((length, channels), BF16), ((ROWS, channels), F32)],
        "states",
        before, heads, conv_weight, gated, decay,
        scratch=[pltpu.VMEM((3 * tiles, 2 * ROWS, TILE), F32)],
    )
    all_ends = lax.all_to_all(ends, "ctx", split_axis=0, concat_axis=0, tiled=True)
    lift, base = call(
        inside_kernel,
        [((length, groups * poles), BF16), ((length, channels), F32)],
        "inside",
        gated, skip, rates, coef,
        flops=10**9,
    )
    if square:
        base, near = lax.optimization_barrier((base, near))
        other_near = swap(after(out_weight, base), 4, 2)
    me = lax.axis_index("ctx").astype(jnp.int32)
    core = me % CORES
    smem = [pl.BlockSpec(memory_space=pltpu.SMEM)]
    outs = [((length, share), BF16), ((length, share), BF16), ((length, channels), BF16)]
    mine, other, mixed = call(
        finish_kernel,
        outs,
        "finish",
        jnp.stack([me, core]), all_ends, step, lift, query, first, base,
        specs=smem + whole(6),
        scratch=[pltpu.VMEM((poles, channels), F32)],
    )
    if rows != share:
        by_core = mixed.reshape(length, share // rows, CORES, rows).transpose(2, 0, 1, 3)
        by_core = by_core.reshape(CORES, length, share)
        mine = lax.dynamic_index_in_dim(by_core, core, 0, keepdims=False)
        other = lax.dynamic_index_in_dim(by_core, 1 - core, 0, keepdims=False)
    block = jnp.concatenate([mine, swap(other, 1)], axis=0)
    layer = lax.axis_index("tp").astype(jnp.int32)
    beside, across = trade(block, 1), trade(block, 3)
    beyond = trade(across, 1)
    if square:
        diagonal = swap(after(near, block), 4, 2)
        weight = (out_weight, near, other_near, diagonal)
    else:
        core_groups = [list(range(core, blocks, CORES)) for core in range(CORES)]
        weight = lax.all_gather(out_weight, "ctx", axis=0, axis_index_groups=core_groups)
        weight = tuple(weight.reshape(layers, share, features))
    first_row = jnp.where(core == 0, 1, 2)
    chip = me // CORES
    place = [chip, chip ^ first_row, chip ^ (3 - first_row), chip ^ 3] if square else [jnp.full_like(me, at) for at in range(4)]
    mine, other = call(
        project_kernel,
        [((length, features), F32), ((length, features), BF16)],
        "project",
        jnp.stack([layer] + place), block, beside, beyond, across, *weight,
        specs=smem + whole(4 + len(weight)),
        scratch=[pltpu.VMEM((layers,) + block.shape, BF16)],
        flops=10**9,
    )
    other = swap(other, 1)
    return (mine + other.astype(F32)).astype(BF16)


def solution(mesh):
    return jax.shard_map(
        local,
        mesh=mesh,
        in_specs=(
            P(None, "tp", "ctx"),
            P(None, None, "tp"),
            P("tp", None),
            P("tp", None),
            P("tp"),
            P("ctx", "tp"),
        ),
        out_specs=P("ctx", "tp"),
        check_vma=False,
    )
```

```python
import functools
import math

import jax
import jax.numpy as jnp
from jax import lax
from jax.experimental import pallas as pl
from jax.experimental.pallas import tpu as pltpu
from jax.sharding import PartitionSpec as P

F32 = jnp.float32
BF16 = jnp.bfloat16
ROWS = 8
TILE = 128
CORES = 2
COLUMNS = 256
VMEM_LIMIT = 24 * 1024 * 1024
PLAIN = (((1,), (0,)), ((), ()))
CONTRACT_LANES = (((1,), (1,)), ((), ()))


def from_behind(value, axis, steps):
    count = lax.axis_size(axis)
    leading, last = (max(0, -steps), min(count, count - steps))
    return lax.ppermute(value, axis, [(source, source + steps) for source in range(leading, last)])


def dot(left, right, dims=PLAIN):
    return lax.dot_general(left, right, dims, preferred_element_type=F32)


def halves(value):
    high = value.astype(BF16)
    return high, (value - high.astype(F32)).astype(BF16)


def iota(shape, axis):
    return lax.broadcasted_iota(jnp.int32, shape, axis)


def identity(size):
    return (iota((size, size), 0) == iota((size, size), 1)).astype(BF16)


def turned(value, unit):
    return dot(unit, value, CONTRACT_LANES)


def whole(count):
    return [pl.BlockSpec(memory_space=pltpu.VMEM)] * count


def call(kernel, outs, name, *operands, specs=None, scratch=(), flops=10**8):
    return pl.pallas_call(
        kernel,
        out_shape=tuple(jax.ShapeDtypeStruct(*out) for out in outs),
        in_specs=whole(len(operands)) if specs is None else specs,
        out_specs=tuple(whole(len(outs))),
        scratch_shapes=scratch,
        compiler_params=pltpu.CompilerParams(vmem_limit_bytes=VMEM_LIMIT),
        cost_estimate=pl.CostEstimate(flops=flops, bytes_accessed=flops // 100, transcendentals=0),
        name=name,
    )(*operands)


def tile_of(index, size=TILE):
    return pl.ds(pl.multiple_of(index * size, size), size)


def unrolled(count, body):
    def step(index, carry):
        body(index)
        return carry

    lax.fori_loop(0, count, step, 0, unroll=math.gcd(count, 4))


def tails_kernel(streams_ref, tails_ref):
    length = streams_ref.shape[2]
    pick = (iota((2 * ROWS, length), 1) == iota((2 * ROWS, length), 0) + (length - ROWS)).astype(BF16)
    for stream in range(streams_ref.shape[0]):
        rows = dot(pick, streams_ref[stream], CONTRACT_LANES)
        tails_ref[stream] = rows[:ROWS].astype(BF16)


def short_conv(stream, chans, rows, padded, taps_ref):
    total = None
    for shift in range(taps_ref.shape[1]):
        term = taps_ref[stream, shift : shift + 1, chans] * padded[pl.ds(ROWS - shift, rows), :]
        total = term if total is None else total + term
    return total


def prepare_kernel(
    streams_ref, taps_ref, rates_ref, residues_ref, skip_ref,
    heads_ref, query_ref, gated_ref, decay_ref, step_ref, coef_ref, direct_ref, padded_ref,
):
    channels, length = streams_ref.shape[1:]
    poles, groups = rates_ref.shape
    width = channels // groups
    in_tile = TILE // width
    unit = identity(length)
    lag = (length - 1) - iota((poles, length), 1).astype(F32)
    owner = iota((poles, TILE), 1) // width
    coef_ref[...] = residues_ref[...] * jnp.sqrt(2.0 * rates_ref[...]) / math.sqrt(poles)
    direct_ref[...] = skip_ref[...]

    def turn(index):
        chans = tile_of(index)
        for stream in range(3):
            tokens = turned(streams_ref[stream, chans, :], unit)
            padded_ref[index * 3 + stream, :ROWS, :] = jnp.zeros((ROWS, TILE), F32)
            padded_ref[index * 3 + stream, ROWS:, :] = tokens
            heads_ref[stream, :, chans] = tokens[:ROWS]

    def decays(index):
        rates = pltpu.roll(rates_ref[...], groups - index * in_tile, 1)
        decay = []
        wide = jnp.zeros((poles, TILE), F32)
        for g in range(in_tile):
            rate = jnp.broadcast_to(rates[:, g : g + 1], (poles, length))
            decay.append(jnp.exp(-rate * lag))
            wide = jnp.where(owner == g, rate[:, :TILE], wide)
        step_ref[:, tile_of(index)] = jnp.exp(-wide * length)
        for part, value in enumerate(halves(jnp.concatenate(decay, axis=0))):
            decay_ref[part, tile_of(index, in_tile * poles), :] = value

    def filters(index):
        chans = tile_of(index)
        query, left, right = (
            short_conv(stream, chans, length, padded_ref.at[index * 3 + stream], taps_ref) for stream in range(3)
        )
        query_ref[:, chans] = query.astype(BF16)
        gated_ref[:, chans] = left * right

    unrolled(channels // TILE, turn)
    unrolled(channels // TILE, decays)
    unrolled(channels // TILE, filters)


def states_kernel(before_ref, heads_ref, taps_ref, gated_ref, decay_ref, ends_ref, final_ref, first_ref, padded_ref):
    length, channels = gated_ref.shape
    poles = ends_ref.shape[1]
    in_tile = decay_ref.shape[1] // poles * TILE // channels
    owner = iota((poles, TILE), 1) // (TILE // in_tile)

    def begin(index):
        chans = tile_of(index)
        for stream in range(3):
            padded_ref[index * 3 + stream, :ROWS, :] = before_ref[stream, :, chans].astype(F32)
            padded_ref[index * 3 + stream, ROWS:, :] = heads_ref[stream, :, chans]
        query, left, right = (
            short_conv(stream, chans, ROWS, padded_ref.at[index * 3 + stream], taps_ref) for stream in range(3)
        )
        first_ref[:, chans] = query
        final_ref[:, chans] = jnp.concatenate([left * right, gated_ref[ROWS:, chans]], axis=0).astype(BF16)

    def leave(index):
        chans = tile_of(index)
        gated = final_ref[:, chans]
        states = tile_of(index, in_tile * poles)
        every = dot(decay_ref[0, states, :], gated) + dot(decay_ref[1, states, :], gated)
        ends = jnp.zeros((poles, TILE), F32)
        for g in range(in_tile):
            ends = jnp.where(owner == g, every[g * poles : (g + 1) * poles], ends)
        ends = ends.astype(BF16)
        for block in range(ends_ref.shape[0]):
            ends_ref[block, :, chans] = ends

    unrolled(channels // TILE, begin)
    unrolled(channels // TILE, leave)


def inside_kernel(gated_ref, skip_ref, rates_ref, coef_ref, lift_ref, base_ref):
    length, channels = gated_ref.shape
    poles, groups = rates_ref.shape
    width = channels // groups
    in_tile = TILE // width
    unit = identity(length)
    time = iota((poles, length), 1).astype(F32)
    member = (iota((in_tile, in_tile * poles), 1) // poles == iota((in_tile, in_tile * poles), 0)).astype(BF16)
    causal = iota((length, length), 1) >= iota((length, length), 0)

    def tile(index):
        chans = tile_of(index)
        shift = groups - index * in_tile
        rates = pltpu.roll(rates_ref[...], shift, 1)
        coef = pltpu.roll(coef_ref[...], shift, 1)
        impulse, lift = [], []
        for g in range(in_tile):
            rate = jnp.broadcast_to(rates[:, g : g + 1], (poles, length))
            scale = jnp.broadcast_to(coef[:, g : g + 1], (poles, length))
            impulse.append(scale * jnp.exp(-rate * time))
            lift.append(scale * jnp.exp(-rate * (time + 1.0)))
        states = tile_of(index, in_tile * poles)
        lift_ref[:, states] = turned(jnp.concatenate(lift, axis=0).astype(BF16), unit).astype(BF16)
        high, low = halves(jnp.concatenate(impulse, axis=0))
        response = dot(member, high) + dot(member, low)
        gated = gated_ref[:, chans]
        signal = turned(gated, unit).astype(BF16)
        parts = []
        for pair in range(in_tile // 2):
            blocks = []
            for g in (2 * pair, 2 * pair + 1):
                spread = jnp.broadcast_to(response[g : g + 1], (length, length))
                shifted = pltpu.roll(spread, 0, 1, stride=1, stride_axis=0)
                blocks.append(jnp.where(causal, shifted, 0.0).astype(BF16))
            both = dot(signal[pair * 2 * width : (pair + 1) * 2 * width], jnp.concatenate(blocks, axis=1))
            parts += [both[:width, :length], both[width:, length:]]
        high, low = halves(jnp.concatenate(parts, axis=0))
        base_ref[:, chans] = turned(high, unit) + turned(low, unit) + skip_ref[:, chans] * gated.astype(F32)

    unrolled(channels // TILE, tile)


def finish_kernel(at_ref, ends_ref, step_ref, lift_ref, query_ref, first_ref, base_ref, mine_ref, other_ref, mixed_ref, state_ref):
    length, channels = mixed_ref.shape
    poles = step_ref.shape[0]
    in_tile = lift_ref.shape[1] // poles * TILE // channels
    me, core = at_ref[0], at_ref[1]

    def earlier(block, state):
        return jnp.where(block < me, step_ref[...] * state + ends_ref[block].astype(F32), state)

    state_ref[...] = lax.fori_loop(0, ends_ref.shape[0] - 1, earlier, jnp.zeros((poles, channels), F32))
    owner = iota((poles, TILE), 1) // (TILE // in_tile)

    def tile(index):
        chans = tile_of(index)
        entering = state_ref[:, chans]
        apart = jnp.concatenate([jnp.where(owner == g, entering, 0.0) for g in range(in_tile)], axis=0)
        high, low = halves(apart)
        states = tile_of(index, in_tile * poles)
        lift = lift_ref[:, states]
        carried = dot(lift, high) + dot(lift, low)
        query = jnp.concatenate([first_ref[:, chans], query_ref[:, chans].astype(F32)[ROWS:]], axis=0)
        mixed_ref[:, chans] = (query * (base_ref[:, chans] + carried)).astype(BF16)

    unrolled(channels // TILE, tile)
    share = channels // CORES
    mine_ref[...] = mixed_ref[:, tile_of(core, share)]
    other_ref[...] = mixed_ref[:, tile_of(1 - core, share)]


def project_kernel(at_ref, own_ref, beside_ref, beyond_ref, across_ref, *rest):
    *weight_hbms, mine_ref, other_ref, layers_ref, weight_ref, sems = rest
    copies = [
        pltpu.make_async_copy(hbm, weight_ref.at[at], sems.at[at]) for at, hbm in enumerate(weight_hbms)
    ]
    for copy in copies:
        copy.start()
    layer = at_ref[0]
    for bits, ref in enumerate((own_ref, beside_ref, beyond_ref, across_ref)):
        layers_ref[layer ^ bits] = ref[...]
    for copy in copies:
        copy.wait()
    length, features = mine_ref.shape
    for column in range(0, features, COLUMNS):
        columns = slice(column, column + COLUMNS)
        total = None
        for at in range(len(copies)):
            term = dot(layers_ref[at_ref[1 + at]], weight_ref[at, :, columns])
            total = term if total is None else total + term
        mine_ref[:, columns] = total[:length]
        other_ref[:, columns] = total[length:].astype(BF16)


def swap(value, *bits):
    count = lax.axis_size("ctx")
    pairs = [(source, source ^ bits[source % len(bits)]) for source in range(count)]
    return lax.ppermute(value, "ctx", pairs)


def after(value, earlier):
    return lax.optimization_barrier((value, earlier))[0]


def trade(value, bits):
    count = lax.axis_size("tp")
    return lax.ppermute(value, "tp", [(source, source ^ bits) for source in range(count)])


def local(streams, conv_weight, rates, residues, skip, out_weight):
    channels, length = streams.shape[1:]
    groups, poles = rates.shape
    blocks, layers = lax.axis_size("ctx"), lax.axis_size("tp")
    rows, features = out_weight.shape
    share = channels // CORES
    square = blocks == 8 and rows == share

    rates, residues, skip = rates.T, residues.T, skip[None, :]
    (tails,) = call(tails_kernel, [((3, ROWS, channels), BF16)], "tails", streams)
    before = from_behind(tails, "ctx", 1)
    if square:
        near = swap(out_weight, 2, 4)
    tiles = channels // TILE
    heads, query, gated, decay, step, coef, skip = call(
        prepare_kernel,
        [
            ((3, ROWS, channels), F32),
            ((length, channels), BF16),
            ((length, channels), F32),
            ((2, groups * poles, length), BF16),
            ((poles, channels), F32),
            ((poles, groups), F32),
            ((1, channels), F32),
        ],
        "prepare",
        streams, conv_weight, rates, residues, skip,
        scratch=[pltpu.VMEM((3 * tiles, ROWS + length, TILE), F32)],
        flops=10**9,
    )
    ends, gated, first = call(
        states_kernel,
        [((blocks, poles, channels), BF16), ((length, channels), BF16), ((ROWS, channels), F32)],
        "states",
        before, heads, conv_weight, gated, decay,
        scratch=[pltpu.VMEM((3 * tiles, 2 * ROWS, TILE), F32)],
    )
    all_ends = lax.all_to_all(ends, "ctx", split_axis=0, concat_axis=0, tiled=True)
    lift, base = call(
        inside_kernel,
        [((length, groups * poles), BF16), ((length, channels), F32)],
        "inside",
        gated, skip, rates, coef,
        flops=10**9,
    )
    if square:
        other_near = swap(after(out_weight, gated), 4, 2)
    me = lax.axis_index("ctx").astype(jnp.int32)
    core = me % CORES
    smem = [pl.BlockSpec(memory_space=pltpu.SMEM)]
    outs = [((length, share), BF16), ((length, share), BF16), ((length, channels), BF16)]
    mine, other, mixed = call(
        finish_kernel,
        outs,
        "finish",
        jnp.stack([me, core]), all_ends, step, lift, query, first, base,
        specs=smem + whole(6),
        scratch=[pltpu.VMEM((poles, channels), F32)],
    )
    if rows != share:
        by_core = mixed.reshape(length, share // rows, CORES, rows).transpose(2, 0, 1, 3)
        by_core = by_core.reshape(CORES, length, share)
        mine = lax.dynamic_index_in_dim(by_core, core, 0, keepdims=False)
        other = lax.dynamic_index_in_dim(by_core, 1 - core, 0, keepdims=False)
    block = jnp.concatenate([mine, swap(other, 1)], axis=0)
    layer = lax.axis_index("tp").astype(jnp.int32)
    beside, across = trade(block, 1), trade(block, 3)
    beyond = trade(after(across, other_near) if square else across, 1)
    if square:
        diagonal = swap(after(near, block), 4, 2)
        weight = (out_weight, near, other_near, diagonal)
    else:
        core_groups = [list(range(core, blocks, CORES)) for core in range(CORES)]
        weight = lax.all_gather(out_weight, "ctx", axis=0, axis_index_groups=core_groups)
        weight = tuple(weight.reshape(layers, share, features))
    first_row = jnp.where(core == 0, 1, 2)
    chip = me // CORES
    place = [chip, chip ^ first_row, chip ^ (3 - first_row), chip ^ 3] if square else [jnp.full_like(me, at) for at in range(4)]
    mine, other = call(
        project_kernel,
        [((length, features), F32), ((length, features), BF16)],
        "project",
        jnp.stack([layer] + place), block, beside, beyond, across, *(pltpu.with_memory_space_constraint(part, pltpu.HBM) for part in weight),
        specs=smem + whole(4) + [pl.BlockSpec(memory_space=pltpu.HBM)] * len(weight),
        scratch=[
            pltpu.VMEM((layers,) + block.shape, BF16),
            pltpu.VMEM((layers, share, features), BF16),
            pltpu.SemaphoreType.DMA((layers,)),
        ],
        flops=10**9,
    )
    other = swap(other, 1)
    return (mine + other.astype(F32)).astype(BF16)


def solution(mesh):
    return jax.shard_map(
        local,
        mesh=mesh,
        in_specs=(
            P(None, "tp", "ctx"),
            P(None, None, "tp"),
            P("tp", None),
            P("tp", None),
            P("tp"),
            P("ctx", "tp"),
        ),
        out_specs=P("ctx", "tp"),
        check_vma=False,
    )
```

```python
import functools
import math

import jax
import jax.numpy as jnp
from jax import lax
from jax.experimental import pallas as pl
from jax.experimental.pallas import tpu as pltpu
from jax.sharding import PartitionSpec as P

F32 = jnp.float32
BF16 = jnp.bfloat16
ROWS = 8
TILE = 128
CORES = 2
COLUMNS = 256
STRIP = 32
VMEM_LIMIT = 24 * 1024 * 1024
PLAIN = (((1,), (0,)), ((), ()))
CONTRACT_LANES = (((1,), (1,)), ((), ()))


def from_behind(value, axis, steps):
    count = lax.axis_size(axis)
    leading, last = (max(0, -steps), min(count, count - steps))
    return lax.ppermute(value, axis, [(source, source + steps) for source in range(leading, last)])


def dot(left, right, dims=PLAIN):
    return lax.dot_general(left, right, dims, preferred_element_type=F32)


def halves(value):
    high = value.astype(BF16)
    return high, (value - high.astype(F32)).astype(BF16)


def iota(shape, axis):
    return lax.broadcasted_iota(jnp.int32, shape, axis)


def identity(size):
    return (iota((size, size), 0) == iota((size, size), 1)).astype(BF16)


def turned(value, unit):
    return dot(unit, value, CONTRACT_LANES)


def whole(count):
    return [pl.BlockSpec(memory_space=pltpu.VMEM)] * count


def call(kernel, outs, name, *operands, specs=None, scratch=(), flops=10**8):
    return pl.pallas_call(
        kernel,
        out_shape=tuple(jax.ShapeDtypeStruct(*out) for out in outs),
        in_specs=whole(len(operands)) if specs is None else specs,
        out_specs=tuple(whole(len(outs))),
        scratch_shapes=scratch,
        compiler_params=pltpu.CompilerParams(vmem_limit_bytes=VMEM_LIMIT),
        cost_estimate=pl.CostEstimate(flops=flops, bytes_accessed=flops // 100, transcendentals=0),
        name=name,
    )(*operands)


def tile_of(index, size=TILE):
    return pl.ds(pl.multiple_of(index * size, size), size)


def unrolled(count, body):
    def step(index, carry):
        body(index)
        return carry

    lax.fori_loop(0, count, step, 0, unroll=math.gcd(count, 4))


def tails_kernel(streams_ref, tails_ref):
    length = streams_ref.shape[2]
    pick = (iota((2 * ROWS, length), 1) == iota((2 * ROWS, length), 0) + (length - ROWS)).astype(BF16)
    for stream in range(streams_ref.shape[0]):
        rows = dot(pick, streams_ref[stream], CONTRACT_LANES)
        tails_ref[stream] = rows[:ROWS].astype(BF16)


def short_conv(stream, chans, rows, padded, taps_ref):
    total = None
    for shift in range(taps_ref.shape[1]):
        term = taps_ref[stream, shift : shift + 1, chans] * padded[pl.ds(ROWS - shift, rows), :]
        total = term if total is None else total + term
    return total


def prepare_kernel(
    streams_ref, taps_ref, rates_ref, residues_ref, skip_ref,
    heads_ref, query_ref, gated_ref, decay_ref, step_ref, coef_ref, direct_ref, padded_ref,
):
    channels, length = streams_ref.shape[1:]
    poles, groups = rates_ref.shape
    width = channels // groups
    in_tile = TILE // width
    unit = identity(length)
    lag = (length - 1) - iota((poles, length), 1).astype(F32)
    owner = iota((poles, TILE), 1) // width
    coef_ref[...] = residues_ref[...] * jnp.sqrt(2.0 * rates_ref[...]) / math.sqrt(poles)
    direct_ref[...] = skip_ref[...]

    def turn(index):
        chans = tile_of(index)
        for stream in range(3):
            tokens = turned(streams_ref[stream, chans, :], unit)
            padded_ref[index * 3 + stream, :ROWS, :] = jnp.zeros((ROWS, TILE), F32)
            padded_ref[index * 3 + stream, ROWS:, :] = tokens
            heads_ref[stream, :, chans] = tokens[:ROWS]

    def decays(index):
        rates = pltpu.roll(rates_ref[...], groups - index * in_tile, 1)
        decay = []
        wide = jnp.zeros((poles, TILE), F32)
        for g in range(in_tile):
            rate = jnp.broadcast_to(rates[:, g : g + 1], (poles, length))
            decay.append(jnp.exp(-rate * lag))
            wide = jnp.where(owner == g, rate[:, :TILE], wide)
        step_ref[:, tile_of(index)] = jnp.exp(-wide * length)
        for part, value in enumerate(halves(jnp.concatenate(decay, axis=0))):
            decay_ref[part, tile_of(index, in_tile * poles), :] = value

    def filters(index):
        chans = tile_of(index)
        query, left, right = (
            short_conv(stream, chans, length, padded_ref.at[index * 3 + stream], taps_ref) for stream in range(3)
        )
        query_ref[:, chans] = query.astype(BF16)
        gated_ref[:, chans] = left * right

    unrolled(channels // TILE, turn)
    unrolled(channels // TILE, decays)
    unrolled(channels // TILE, filters)


def states_kernel(before_ref, heads_ref, taps_ref, gated_ref, decay_ref, ends_ref, final_ref, first_ref, padded_ref):
    length, channels = gated_ref.shape
    poles = ends_ref.shape[1]
    in_tile = decay_ref.shape[1] // poles * TILE // channels
    owner = iota((poles, TILE), 1) // (TILE // in_tile)

    def begin(index):
        chans = tile_of(index)
        for stream in range(3):
            padded_ref[index * 3 + stream, :ROWS, :] = before_ref[stream, :, chans].astype(F32)
            padded_ref[index * 3 + stream, ROWS:, :] = heads_ref[stream, :, chans]
        query, left, right = (
            short_conv(stream, chans, ROWS, padded_ref.at[index * 3 + stream], taps_ref) for stream in range(3)
        )
        first_ref[:, chans] = query
        final_ref[:, chans] = jnp.concatenate([left * right, gated_ref[ROWS:, chans]], axis=0).astype(BF16)

    def leave(index):
        chans = tile_of(index)
        gated = final_ref[:, chans]
        states = tile_of(index, in_tile * poles)
        every = dot(decay_ref[0, states, :], gated) + dot(decay_ref[1, states, :], gated)
        ends = jnp.zeros((poles, TILE), F32)
        for g in range(in_tile):
            ends = jnp.where(owner == g, every[g * poles : (g + 1) * poles], ends)
        ends = ends.astype(BF16)
        for block in range(ends_ref.shape[0]):
            ends_ref[block, :, chans] = ends

    unrolled(channels // TILE, begin)
    unrolled(channels // TILE, leave)


def inside_kernel(gated_ref, skip_ref, rates_ref, coef_ref, lift_ref, base_ref):
    length, channels = gated_ref.shape
    poles, groups = rates_ref.shape
    width = channels // groups
    in_tile = TILE // width
    unit = identity(length)
    time = iota((poles, length), 1).astype(F32)
    member = (iota((in_tile, in_tile * poles), 1) // poles == iota((in_tile, in_tile * poles), 0)).astype(BF16)
    strip = STRIP
    lane = iota((width, length), 1)
    causal = iota((strip, length), 1) >= iota((strip, length), 0)

    def tile(index):
        chans = tile_of(index)
        shift = groups - index * in_tile
        rates = pltpu.roll(rates_ref[...], shift, 1)
        coef = pltpu.roll(coef_ref[...], shift, 1)
        impulse, lift = [], []
        for g in range(in_tile):
            rate = jnp.broadcast_to(rates[:, g : g + 1], (poles, length))
            scale = jnp.broadcast_to(coef[:, g : g + 1], (poles, length))
            impulse.append(scale * jnp.exp(-rate * time))
            lift.append(scale * jnp.exp(-rate * (time + 1.0)))
        states = tile_of(index, in_tile * poles)
        lift_ref[:, states] = turned(jnp.concatenate(lift, axis=0).astype(BF16), unit).astype(BF16)
        high, low = halves(jnp.concatenate(impulse, axis=0))
        response = dot(member, high) + dot(member, low)
        gated = gated_ref[:, chans]
        pieces = [turned(gated[at : at + strip], unit).astype(BF16) for at in range(0, length, strip)]
        parts = []
        for pair in range(in_tile // 2):
            blocks = []
            for g in (2 * pair, 2 * pair + 1):
                spread = jnp.broadcast_to(response[g : g + 1], (strip, length))
                shifted = pltpu.roll(spread, 0, 1, stride=1, stride_axis=0)
                blocks.append(jnp.where(causal, shifted, 0.0).astype(BF16))
            rows = slice(pair * 2 * width, (pair + 1) * 2 * width)
            signal = jnp.concatenate([piece[rows] for piece in pieces], axis=0)
            both = dot(signal, jnp.concatenate(blocks, axis=1))
            for g in range(2):
                total = None
                for at in range(length // strip):
                    first = at * 2 * width + g * width
                    term = both[first : first + width, g * length : (g + 1) * length]
                    if at:
                        term = jnp.where(lane >= at * strip, pltpu.roll(term, at * strip, 1), 0.0)
                    total = term if total is None else total + term
                parts.append(total)
        high, low = halves(jnp.concatenate(parts, axis=0))
        base_ref[:, chans] = turned(high, unit) + turned(low, unit) + skip_ref[:, chans] * gated.astype(F32)

    unrolled(channels // TILE, tile)


def finish_kernel(at_ref, ends_ref, step_ref, lift_ref, query_ref, first_ref, base_ref, mixed_ref, state_ref):
    length, share = mixed_ref.shape
    poles, channels = step_ref.shape
    in_tile = lift_ref.shape[1] // poles * TILE // channels
    me, half = at_ref[0], at_ref[1]
    here = tile_of(half, share)
    step = step_ref[:, here]

    def earlier(block, state):
        return jnp.where(block < me, step * state + ends_ref[block, :, here].astype(F32), state)

    state_ref[...] = lax.fori_loop(0, ends_ref.shape[0] - 1, earlier, jnp.zeros((poles, share), F32))
    owner = iota((poles, TILE), 1) // (TILE // in_tile)

    def tile(index):
        at = half * (share // TILE) + index
        chans = tile_of(at)
        entering = state_ref[:, tile_of(index)]
        apart = jnp.concatenate([jnp.where(owner == g, entering, 0.0) for g in range(in_tile)], axis=0)
        high, low = halves(apart)
        lift = lift_ref[:, tile_of(at, in_tile * poles)]
        carried = dot(lift, high) + dot(lift, low)
        query = jnp.concatenate([first_ref[:, chans], query_ref[:, chans].astype(F32)[ROWS:]], axis=0)
        mixed_ref[:, tile_of(index)] = (query * (base_ref[:, chans] + carried)).astype(BF16)

    unrolled(share // TILE, tile)


def early_kernel(at_ref, own_ref, beside_ref, across_ref, *rest):
    *weight_hbms, total_ref, rows_ref, layers_ref, weight_ref, sems = rest
    copies = [
        pltpu.make_async_copy(hbm, weight_ref.at[at], sems.at[at]) for at, hbm in enumerate(weight_hbms)
    ]
    for copy in copies:
        copy.start()
    layer = at_ref[0]
    for bits, ref in ((0, own_ref), (1, beside_ref), (3, across_ref)):
        layers_ref[layer ^ bits] = ref[...]
    layers_ref[layer ^ 2] = jnp.zeros_like(own_ref)
    for copy in copies:
        copy.wait()
    for column in range(0, total_ref.shape[1], COLUMNS):
        columns = slice(column, column + COLUMNS)
        total = None
        for at in range(len(copies)):
            term = dot(layers_ref[at_ref[1 + at]], weight_ref[at, :, columns])
            total = term if total is None else total + term
        total_ref[:, columns] = total
    for at in range(len(copies)):

        @pl.when(at_ref[1 + at] == layer ^ 2)
        def _():
            rows_ref[...] = weight_ref[at]


def late_kernel(first, beyond_ref, total_ref, rows_ref, out_ref):
    tokens = pl.ds(first, out_ref.shape[0])
    out_ref[...] = (total_ref[tokens, :] + dot(beyond_ref[tokens, :], rows_ref[...])).astype(out_ref.dtype)


def swap(value, *bits):
    count = lax.axis_size("ctx")
    pairs = [(source, source ^ bits[source % len(bits)]) for source in range(count)]
    return lax.ppermute(value, "ctx", pairs)


def after(value, earlier):
    return lax.optimization_barrier((value, earlier))[0]


def trade(value, bits):
    count = lax.axis_size("tp")
    return lax.ppermute(value, "tp", [(source, source ^ bits) for source in range(count)])


def local(streams, conv_weight, rates, residues, skip, out_weight):
    channels, length = streams.shape[1:]
    groups, poles = rates.shape
    blocks, layers = lax.axis_size("ctx"), lax.axis_size("tp")
    rows, features = out_weight.shape
    share = channels // CORES
    square = blocks == 8 and rows == share

    rates, residues, skip = rates.T, residues.T, skip[None, :]
    (tails,) = call(tails_kernel, [((3, ROWS, channels), BF16)], "tails", streams)
    before = from_behind(tails, "ctx", 1)
    if square:
        near = swap(out_weight, 2, 4)
    tiles = channels // TILE
    heads, query, gated, decay, step, coef, skip = call(
        prepare_kernel,
        [
            ((3, ROWS, channels), F32),
            ((length, channels), BF16),
            ((length, channels), F32),
            ((2, groups * poles, length), BF16),
            ((poles, channels), F32),
            ((poles, groups), F32),
            ((1, channels), F32),
        ],
        "prepare",
        streams, conv_weight, rates, residues, skip,
        scratch=[pltpu.VMEM((3 * tiles, ROWS + length, TILE), F32)],
        flops=10**9,
    )
    ends, gated, first = call(
        states_kernel,
        [((blocks, poles, channels), BF16), ((length, channels), BF16), ((ROWS, channels), F32)],
        "states",
        before, heads, conv_weight, gated, decay,
        scratch=[pltpu.VMEM((3 * tiles, 2 * ROWS, TILE), F32)],
    )
    all_ends = lax.all_to_all(ends, "ctx", split_axis=0, concat_axis=0, tiled=True)
    lift, base = call(
        inside_kernel,
        [((length, groups * poles), BF16), ((length, channels), F32)],
        "inside",
        gated, skip, rates, coef,
        flops=10**9,
    )
    if square:
        other_near = swap(after(out_weight, gated), 4, 2)
    me = lax.axis_index("ctx").astype(jnp.int32)
    core = me % CORES
    smem = [pl.BlockSpec(memory_space=pltpu.SMEM)]

    def finished(half):
        return call(
            finish_kernel,
            [((length, share), BF16)],
            "finish",
            jnp.stack([me, half]), all_ends, step, lift, query, first, base,
            specs=smem + whole(6),
            scratch=[pltpu.VMEM((poles, share), F32)],
        )[0]

    if rows == share:
        other, mine = finished(1 - core), finished(core)
    else:
        mixed = jnp.concatenate([finished(jnp.full_like(me, half)) for half in range(CORES)], axis=1)
        by_core = mixed.reshape(length, share // rows, CORES, rows).transpose(2, 0, 1, 3)
        by_core = by_core.reshape(CORES, length, share)
        mine = lax.dynamic_index_in_dim(by_core, core, 0, keepdims=False)
        other = lax.dynamic_index_in_dim(by_core, 1 - core, 0, keepdims=False)
    block = jnp.concatenate([mine, swap(other, 1)], axis=0)
    layer = lax.axis_index("tp").astype(jnp.int32)
    beside, across = trade(block, 1), trade(block, 3)
    beyond = trade(after(across, other_near) if square else across, 1)
    if square:
        diagonal = swap(after(near, block), 4, 2)
        weight = (out_weight, near, other_near, diagonal)
    else:
        core_groups = [list(range(core, blocks, CORES)) for core in range(CORES)]
        weight = lax.all_gather(out_weight, "ctx", axis=0, axis_index_groups=core_groups)
        weight = tuple(weight.reshape(layers, share, features))
    first_row = jnp.where(core == 0, 1, 2)
    chip = me // CORES
    place = [chip, chip ^ first_row, chip ^ (3 - first_row), chip ^ 3] if square else [jnp.full_like(me, at) for at in range(4)]
    total, last_rows = call(
        early_kernel,
        [((CORES * length, features), F32), ((share, features), BF16)],
        "early",
        jnp.stack([layer] + place), block, beside, across,
        *(pltpu.with_memory_space_constraint(part, pltpu.HBM) for part in weight),
        specs=smem + whole(3) + [pl.BlockSpec(memory_space=pltpu.HBM)] * len(weight),
        scratch=[
            pltpu.VMEM((layers,) + block.shape, BF16),
            pltpu.VMEM((layers, share, features), BF16),
            pltpu.SemaphoreType.DMA((layers,)),
        ],
        flops=0,
    )
    sides = []
    for side, kind in ((1, BF16), (0, F32)):
        sides += call(
            functools.partial(late_kernel, side * length), [((length, features), kind)], "late", beyond, total, last_rows, flops=0
        )
    other, mine = sides
    other = swap(other, 1)
    return (mine + other.astype(F32)).astype(BF16)


def solution(mesh):
    return jax.shard_map(
        local,
        mesh=mesh,
        in_specs=(
            P(None, "tp", "ctx"),
            P(None, None, "tp"),
            P("tp", None),
            P("tp", None),
            P("tp"),
            P("ctx", "tp"),
        ),
        out_specs=P("ctx", "tp"),
        check_vma=False,
    )
```

```python
import functools
import math

import jax
import jax.numpy as jnp
from jax import lax
from jax.experimental import pallas as pl
from jax.experimental.pallas import tpu as pltpu
from jax.sharding import PartitionSpec as P

F32 = jnp.float32
BF16 = jnp.bfloat16
ROWS = 8
TILE = 128
CORES = 2
COLUMNS = 256
STRIP = 32
VMEM_LIMIT = 24 * 1024 * 1024
PLAIN = (((1,), (0,)), ((), ()))
CONTRACT_LANES = (((1,), (1,)), ((), ()))


def from_behind(value, axis, steps):
    count = lax.axis_size(axis)
    leading, last = (max(0, -steps), min(count, count - steps))
    return lax.ppermute(value, axis, [(source, source + steps) for source in range(leading, last)])


def dot(left, right, dims=PLAIN):
    return lax.dot_general(left, right, dims, preferred_element_type=F32)


def halves(value):
    high = value.astype(BF16)
    return high, (value - high.astype(F32)).astype(BF16)


def iota(shape, axis):
    return lax.broadcasted_iota(jnp.int32, shape, axis)


def identity(size):
    return (iota((size, size), 0) == iota((size, size), 1)).astype(BF16)


def turned(value, unit):
    return dot(unit, value, CONTRACT_LANES)


def whole(count):
    return [pl.BlockSpec(memory_space=pltpu.VMEM)] * count


def call(kernel, outs, name, *operands, specs=None, scratch=(), flops=10**8):
    return pl.pallas_call(
        kernel,
        out_shape=tuple(jax.ShapeDtypeStruct(*out) for out in outs),
        in_specs=whole(len(operands)) if specs is None else specs,
        out_specs=tuple(whole(len(outs))),
        scratch_shapes=scratch,
        compiler_params=pltpu.CompilerParams(vmem_limit_bytes=VMEM_LIMIT),
        cost_estimate=pl.CostEstimate(flops=flops, bytes_accessed=flops // 100, transcendentals=0),
        name=name,
    )(*operands)


def tile_of(index, size=TILE):
    return pl.ds(pl.multiple_of(index * size, size), size)


def unrolled(count, body):
    def step(index, carry):
        body(index)
        return carry

    lax.fori_loop(0, count, step, 0, unroll=math.gcd(count, 4))


def tails_kernel(streams_ref, tails_ref):
    length = streams_ref.shape[2]
    pick = (iota((2 * ROWS, length), 1) == iota((2 * ROWS, length), 0) + (length - ROWS)).astype(BF16)
    for stream in range(streams_ref.shape[0]):
        rows = dot(pick, streams_ref[stream], CONTRACT_LANES)
        tails_ref[stream] = rows[:ROWS].astype(BF16)


def short_conv(stream, chans, rows, padded, taps_ref):
    total = None
    for shift in range(taps_ref.shape[1]):
        term = taps_ref[stream, shift : shift + 1, chans] * padded[pl.ds(ROWS - shift, rows), :]
        total = term if total is None else total + term
    return total


def prepare_kernel(
    streams_ref, taps_ref, rates_ref, residues_ref, skip_ref,
    heads_ref, query_ref, gated_ref, decay_ref, step_ref, coef_ref, direct_ref, padded_ref,
):
    channels, length = streams_ref.shape[1:]
    poles, groups = rates_ref.shape
    width = channels // groups
    in_tile = TILE // width
    unit = identity(length)
    lag = (length - 1) - iota((poles, length), 1).astype(F32)
    owner = iota((poles, TILE), 1) // width
    coef_ref[...] = residues_ref[...] * jnp.sqrt(2.0 * rates_ref[...]) / math.sqrt(poles)
    direct_ref[...] = skip_ref[...]

    def turn(index):
        chans = tile_of(index)
        for stream in range(3):
            tokens = turned(streams_ref[stream, chans, :], unit)
            padded_ref[index * 3 + stream, :ROWS, :] = jnp.zeros((ROWS, TILE), F32)
            padded_ref[index * 3 + stream, ROWS:, :] = tokens
            heads_ref[stream, :, chans] = tokens[:ROWS]

    def decays(index):
        rates = pltpu.roll(rates_ref[...], groups - index * in_tile, 1)
        decay = []
        wide = jnp.zeros((poles, TILE), F32)
        for g in range(in_tile):
            rate = jnp.broadcast_to(rates[:, g : g + 1], (poles, length))
            decay.append(jnp.exp(-rate * lag))
            wide = jnp.where(owner == g, rate[:, :TILE], wide)
        step_ref[:, tile_of(index)] = jnp.exp(-wide * length)
        for part, value in enumerate(halves(jnp.concatenate(decay, axis=0))):
            decay_ref[part, tile_of(index, in_tile * poles), :] = value

    def filters(index):
        chans = tile_of(index)
        query, left, right = (
            short_conv(stream, chans, length, padded_ref.at[index * 3 + stream], taps_ref) for stream in range(3)
        )
        query_ref[:, chans] = query.astype(BF16)
        gated_ref[:, chans] = left * right

    unrolled(channels // TILE, turn)
    unrolled(channels // TILE, decays)
    unrolled(channels // TILE, filters)


def states_kernel(before_ref, heads_ref, taps_ref, gated_ref, decay_ref, ends_ref, final_ref, first_ref, padded_ref):
    length, channels = gated_ref.shape
    poles = ends_ref.shape[1]
    in_tile = decay_ref.shape[1] // poles * TILE // channels
    owner = iota((poles, TILE), 1) // (TILE // in_tile)

    def begin(index):
        chans = tile_of(index)
        for stream in range(3):
            padded_ref[index * 3 + stream, :ROWS, :] = before_ref[stream, :, chans].astype(F32)
            padded_ref[index * 3 + stream, ROWS:, :] = heads_ref[stream, :, chans]
        query, left, right = (
            short_conv(stream, chans, ROWS, padded_ref.at[index * 3 + stream], taps_ref) for stream in range(3)
        )
        first_ref[:, chans] = query
        final_ref[:, chans] = jnp.concatenate([left * right, gated_ref[ROWS:, chans]], axis=0).astype(BF16)

    def leave(index):
        chans = tile_of(index)
        gated = final_ref[:, chans]
        states = tile_of(index, in_tile * poles)
        every = dot(decay_ref[0, states, :], gated) + dot(decay_ref[1, states, :], gated)
        ends = jnp.zeros((poles, TILE), F32)
        for g in range(in_tile):
            ends = jnp.where(owner == g, every[g * poles : (g + 1) * poles], ends)
        ends = ends.astype(BF16)
        for block in range(ends_ref.shape[0]):
            ends_ref[block, :, chans] = ends

    unrolled(channels // TILE, begin)
    unrolled(channels // TILE, leave)


def inside_kernel(
    gated_ref, skip_ref, rates_ref, coef_ref, lift_ref, base_ref, response_ref, signal_ref, sum_ref
):
    length, channels = gated_ref.shape
    poles, groups = rates_ref.shape
    width = channels // groups
    in_tile = TILE // width
    tiles = channels // TILE
    strip = STRIP
    unit = identity(length)
    time = iota((poles, length), 1).astype(F32)
    member = (iota((in_tile, in_tile * poles), 1) // poles == iota((in_tile, in_tile * poles), 0)).astype(BF16)
    lane = iota((width, length), 1)
    causal = iota((strip, length), 1) >= iota((strip, length), 0)

    def factors(index):
        shift = groups - index * in_tile
        rates = pltpu.roll(rates_ref[...], shift, 1)
        coef = pltpu.roll(coef_ref[...], shift, 1)
        once = jnp.exp(-rates)
        impulse, lift = [], []
        for g in range(in_tile):
            term = jnp.broadcast_to(coef[:, g : g + 1], (poles, length)) * jnp.exp(-rates[:, g : g + 1] * time)
            impulse.append(term)
            lift.append(term * once[:, g : g + 1])
        high, low = halves(jnp.concatenate(impulse, axis=0))
        response_ref[pl.ds(pl.multiple_of(index * in_tile, in_tile), in_tile), :] = dot(member, high) + dot(member, low)
        lift = jnp.concatenate(lift, axis=0).astype(BF16)
        lift_ref[:, tile_of(index, in_tile * poles)] = turned(lift, unit).astype(BF16)

    def signals(index):
        gated = gated_ref[:, tile_of(index)]
        for at in range(length // strip):
            piece = turned(gated[at * strip : (at + 1) * strip], unit).astype(BF16)
            signal_ref[at, tile_of(index), :] = piece

    def products(index):
        for pair in range(in_tile // 2):
            group = index * in_tile + 2 * pair
            responses = response_ref[pl.ds(group, 2), :]
            blocks = []
            for g in range(2):
                spread = jnp.broadcast_to(responses[g : g + 1], (strip, length))
                shifted = pltpu.roll(spread, 0, 1, stride=1, stride_axis=0)
                blocks.append(jnp.where(causal, shifted, 0.0).astype(BF16))
            rows = pl.ds(pl.multiple_of(group * width, 2 * width), 2 * width)
            signal = jnp.concatenate([signal_ref[at, rows, :] for at in range(length // strip)], axis=0)
            both = dot(signal, jnp.concatenate(blocks, axis=1))
            for g in range(2):
                total = None
                for at in range(length // strip):
                    first = at * 2 * width + g * width
                    term = both[first : first + width, g * length : (g + 1) * length]
                    if at:
                        term = jnp.where(lane >= at * strip, pltpu.roll(term, at * strip, 1), 0.0)
                    total = term if total is None else total + term
                sum_ref[pl.ds(pl.multiple_of((group + g) * width, width), width), :] = total

    def back(index):
        chans = tile_of(index)
        high, low = halves(sum_ref[chans, :])
        direct = skip_ref[:, chans] * gated_ref[:, chans].astype(F32)
        base_ref[:, chans] = turned(high, unit) + turned(low, unit) + direct

    unrolled(tiles, signals)
    unrolled(tiles, factors)
    unrolled(tiles, products)
    unrolled(tiles, back)


def finish_kernel(at_ref, ends_ref, step_ref, lift_ref, query_ref, first_ref, base_ref, mixed_ref, state_ref):
    length, share = mixed_ref.shape
    poles, channels = step_ref.shape
    in_tile = lift_ref.shape[1] // poles * TILE // channels
    me, half = at_ref[0], at_ref[1]
    here = tile_of(half, share)
    step = step_ref[:, here]

    def earlier(block, state):
        return jnp.where(block < me, step * state + ends_ref[block, :, here].astype(F32), state)

    state_ref[...] = lax.fori_loop(0, ends_ref.shape[0] - 1, earlier, jnp.zeros((poles, share), F32))
    owner = iota((poles, TILE), 1) // (TILE // in_tile)

    def tile(index):
        at = half * (share // TILE) + index
        chans = tile_of(at)
        entering = state_ref[:, tile_of(index)]
        apart = jnp.concatenate([jnp.where(owner == g, entering, 0.0) for g in range(in_tile)], axis=0)
        high, low = halves(apart)
        lift = lift_ref[:, tile_of(at, in_tile * poles)]
        carried = dot(lift, high) + dot(lift, low)
        query = jnp.concatenate([first_ref[:, chans], query_ref[:, chans].astype(F32)[ROWS:]], axis=0)
        mixed_ref[:, tile_of(index)] = (query * (base_ref[:, chans] + carried)).astype(BF16)

    unrolled(share // TILE, tile)


def early_kernel(at_ref, own_ref, beside_ref, across_ref, *rest):
    *weight_hbms, total_ref, rows_ref, block_ref, layers_ref, weight_ref, sems = rest
    copies = [
        pltpu.make_async_copy(hbm, weight_ref.at[at], sems.at[at]) for at, hbm in enumerate(weight_hbms)
    ]
    for copy in copies:
        copy.start()
    layer = at_ref[0]
    last = layer ^ 2
    for bits, ref in ((0, own_ref), (1, beside_ref), (3, across_ref)):
        layers_ref[layer ^ bits] = ref[...]
    layers_ref[last] = jnp.zeros_like(own_ref)
    block_ref[...] = layers_ref[at_ref[1 + len(copies)]]
    for copy in copies:
        copy.wait()
    for column in range(0, total_ref.shape[1], COLUMNS):
        columns = slice(column, column + COLUMNS)
        total = None
        for at in range(len(copies)):
            term = dot(layers_ref[at_ref[1 + at]], weight_ref[at, :, columns])
            total = term if total is None else total + term
        total_ref[:, columns] = total
    rows_ref[...] = jnp.zeros_like(rows_ref)
    for at in range(len(copies)):

        @pl.when(at_ref[1 + at] == last)
        def _():
            rows_ref[...] = weight_ref[at]


def late_kernel(first, at_ref, beyond_ref, total_ref, rows_ref, block_ref, weight_ref, out_ref):
    tokens = pl.ds(first, out_ref.shape[0])
    beyond = beyond_ref[tokens, :]
    block = jnp.where(at_ref[4] == at_ref[0] ^ 2, beyond, block_ref[tokens, :])
    total = total_ref[tokens, :] + dot(block, weight_ref[...]) + dot(beyond, rows_ref[...])
    out_ref[...] = total.astype(out_ref.dtype)


def swap(value, *bits):
    count = lax.axis_size("ctx")
    pairs = [(source, source ^ bits[source % len(bits)]) for source in range(count)]
    return lax.ppermute(value, "ctx", pairs)


def after(value, earlier):
    return lax.optimization_barrier((value, earlier))[0]


def trade(value, bits):
    count = lax.axis_size("tp")
    return lax.ppermute(value, "tp", [(source, source ^ bits) for source in range(count)])


def local(streams, conv_weight, rates, residues, skip, out_weight):
    channels, length = streams.shape[1:]
    groups, poles = rates.shape
    blocks, layers = lax.axis_size("ctx"), lax.axis_size("tp")
    rows, features = out_weight.shape
    share = channels // CORES
    square = blocks == 8 and rows == share

    rates, residues, skip = rates.T, residues.T, skip[None, :]
    (tails,) = call(tails_kernel, [((3, ROWS, channels), BF16)], "tails", streams)
    before = from_behind(tails, "ctx", 1)
    if square:
        near = swap(out_weight, 2, 4)
    tiles = channels // TILE
    heads, query, gated, decay, step, coef, skip = call(
        prepare_kernel,
        [
            ((3, ROWS, channels), F32),
            ((length, channels), BF16),
            ((length, channels), F32),
            ((2, groups * poles, length), BF16),
            ((poles, channels), F32),
            ((poles, groups), F32),
            ((1, channels), F32),
        ],
        "prepare",
        streams, conv_weight, rates, residues, skip,
        scratch=[pltpu.VMEM((3 * tiles, ROWS + length, TILE), F32)],
        flops=10**9,
    )
    ends, gated, first = call(
        states_kernel,
        [((blocks, poles, channels), BF16), ((length, channels), BF16), ((ROWS, channels), F32)],
        "states",
        before, heads, conv_weight, gated, decay,
        scratch=[pltpu.VMEM((3 * tiles, 2 * ROWS, TILE), F32)],
    )
    all_ends = lax.all_to_all(ends, "ctx", split_axis=0, concat_axis=0, tiled=True)
    lift, base = call(
        inside_kernel,
        [((length, groups * poles), BF16), ((length, channels), F32)],
        "inside",
        gated, skip, rates, coef,
        scratch=[
            pltpu.VMEM((groups, length), F32),
            pltpu.VMEM((length // STRIP, channels, STRIP), BF16),
            pltpu.VMEM((channels, length), F32),
        ],
        flops=10**9,
    )
    if square:
        other_near = swap(after(out_weight, gated), 4, 2)
    me = lax.axis_index("ctx").astype(jnp.int32)
    core = me % CORES
    smem = [pl.BlockSpec(memory_space=pltpu.SMEM)]

    def finished(half):
        return call(
            finish_kernel,
            [((length, share), BF16)],
            "finish",
            jnp.stack([me, half]), all_ends, step, lift, query, first, base,
            specs=smem + whole(6),
            flops=3 * 10**9,
            scratch=[pltpu.VMEM((poles, share), F32)],
        )[0]

    if rows == share:
        other, mine = finished(1 - core), finished(core)
    else:
        mixed = jnp.concatenate([finished(jnp.full_like(me, half)) for half in range(CORES)], axis=1)
        by_core = mixed.reshape(length, share // rows, CORES, rows).transpose(2, 0, 1, 3)
        by_core = by_core.reshape(CORES, length, share)
        mine = lax.dynamic_index_in_dim(by_core, core, 0, keepdims=False)
        other = lax.dynamic_index_in_dim(by_core, 1 - core, 0, keepdims=False)
    block = jnp.concatenate([mine, swap(other, 1)], axis=0)
    layer = lax.axis_index("tp").astype(jnp.int32)
    beside, across = trade(block, 1), trade(block, 3)
    beyond = trade(after(across, other_near) if square else across, 1)
    if square:
        diagonal = swap(after(near, block), 4, 2)
        weight = (out_weight, near, other_near, diagonal)
    else:
        core_groups = [list(range(core, blocks, CORES)) for core in range(CORES)]
        weight = lax.all_gather(out_weight, "ctx", axis=0, axis_index_groups=core_groups)
        weight = tuple(weight.reshape(layers, share, features))
    first_row = jnp.where(core == 0, 1, 2)
    chip = me // CORES
    place = [chip, chip ^ first_row, chip ^ (3 - first_row), chip ^ 3] if square else [jnp.full_like(me, at) for at in range(4)]
    at = jnp.stack([layer] + place)
    *sooner, latest = weight
    total, last_rows, last_block = call(
        early_kernel,
        [((CORES * length, features), F32), ((share, features), BF16), (block.shape, BF16)],
        "early",
        at, block, beside, across,
        *(pltpu.with_memory_space_constraint(part, pltpu.HBM) for part in sooner),
        specs=smem + whole(3) + [pl.BlockSpec(memory_space=pltpu.HBM)] * len(sooner),
        scratch=[
            pltpu.VMEM((layers,) + block.shape, BF16),
            pltpu.VMEM((len(sooner), share, features), BF16),
            pltpu.SemaphoreType.DMA((len(sooner),)),
        ],
        flops=10**10,
    )
    sides = []
    for side, kind in ((1, BF16), (0, F32)):
        sides += call(
            functools.partial(late_kernel, side * length),
            [((length, features), kind)],
            "late",
            at, beyond, total, last_rows, last_block, latest,
            specs=smem + whole(5),
            flops=0,
        )
    other, mine = sides
    other = swap(other, 1)
    return (mine + other.astype(F32)).astype(BF16)


def solution(mesh):
    return jax.shard_map(
        local,
        mesh=mesh,
        in_specs=(
            P(None, "tp", "ctx"),
            P(None, None, "tp"),
            P("tp", None),
            P("tp", None),
            P("tp"),
            P("ctx", "tp"),
        ),
        out_specs=P("ctx", "tp"),
        check_vma=False,
    )
```

```python
import functools
import math

import jax
import jax.numpy as jnp
from jax import lax
from jax.experimental import pallas as pl
from jax.experimental.pallas import tpu as pltpu
from jax.sharding import PartitionSpec as P

F32 = jnp.float32
BF16 = jnp.bfloat16
ROWS = 8
TILE = 128
CORES = 2
COLUMNS = 256
STRIP = 32
VMEM_LIMIT = 24 * 1024 * 1024
PLAIN = (((1,), (0,)), ((), ()))
CONTRACT_LANES = (((1,), (1,)), ((), ()))


def from_behind(value, axis, steps):
    count = lax.axis_size(axis)
    leading, last = (max(0, -steps), min(count, count - steps))
    return lax.ppermute(value, axis, [(source, source + steps) for source in range(leading, last)])


def dot(left, right, dims=PLAIN):
    return lax.dot_general(left, right, dims, preferred_element_type=F32)


def halves(value):
    high = value.astype(BF16)
    return high, (value - high.astype(F32)).astype(BF16)


def iota(shape, axis):
    return lax.broadcasted_iota(jnp.int32, shape, axis)


def identity(size):
    return (iota((size, size), 0) == iota((size, size), 1)).astype(BF16)


def turned(value, unit):
    return dot(unit, value, CONTRACT_LANES)


def whole(count):
    return [pl.BlockSpec(memory_space=pltpu.VMEM)] * count


def call(kernel, outs, name, *operands, specs=None, scratch=(), flops=10**8):
    return pl.pallas_call(
        kernel,
        out_shape=tuple(jax.ShapeDtypeStruct(*out) for out in outs),
        in_specs=whole(len(operands)) if specs is None else specs,
        out_specs=tuple(whole(len(outs))),
        scratch_shapes=scratch,
        compiler_params=pltpu.CompilerParams(vmem_limit_bytes=VMEM_LIMIT),
        cost_estimate=pl.CostEstimate(flops=flops, bytes_accessed=flops // 100, transcendentals=0),
        name=name,
    )(*operands)


def tile_of(index, size=TILE):
    return pl.ds(pl.multiple_of(index * size, size), size)


def unrolled(count, body):
    def step(index, carry):
        body(index)
        return carry

    lax.fori_loop(0, count, step, 0, unroll=math.gcd(count, 4))


def tails_kernel(streams_ref, tails_ref):
    length = streams_ref.shape[2]
    pick = (iota((2 * ROWS, length), 1) == iota((2 * ROWS, length), 0) + (length - ROWS)).astype(BF16)
    for stream in range(streams_ref.shape[0]):
        rows = dot(pick, streams_ref[stream], CONTRACT_LANES)
        tails_ref[stream] = rows[:ROWS].astype(BF16)


def short_conv(stream, chans, rows, padded, taps_ref):
    total = None
    for shift in range(taps_ref.shape[1]):
        term = taps_ref[stream, shift : shift + 1, chans] * padded[pl.ds(ROWS - shift, rows), :]
        total = term if total is None else total + term
    return total


def prepare_kernel(
    streams_ref, taps_ref, rates_ref, residues_ref, skip_ref,
    heads_ref, query_ref, gated_ref, decay_ref, step_ref, response_ref, lift_ref, direct_ref, padded_ref,
):
    channels, length = streams_ref.shape[1:]
    poles, groups = rates_ref.shape
    width = channels // groups
    in_tile = TILE // width
    unit = identity(length)
    lag = (length - 1) - iota((poles, length), 1).astype(F32)
    owner = iota((poles, TILE), 1) // width
    time = iota((poles, length), 1).astype(F32)
    member = (iota((in_tile, in_tile * poles), 1) // poles == iota((in_tile, in_tile * poles), 0)).astype(BF16)
    scale = residues_ref[...] * jnp.sqrt(2.0 * rates_ref[...]) / math.sqrt(poles)
    direct_ref[...] = skip_ref[...]

    def turn(index):
        chans = tile_of(index)
        for stream in range(3):
            tokens = turned(streams_ref[stream, chans, :], unit)
            padded_ref[index * 3 + stream, :ROWS, :] = jnp.zeros((ROWS, TILE), F32)
            padded_ref[index * 3 + stream, ROWS:, :] = tokens
            heads_ref[stream, :, chans] = tokens[:ROWS]

    def factors(index):
        shift = groups - index * in_tile
        rates = pltpu.roll(rates_ref[...], shift, 1)
        coef = pltpu.roll(scale, shift, 1)
        once = jnp.exp(-rates)
        decay, impulse, lift = [], [], []
        wide = jnp.zeros((poles, TILE), F32)
        for g in range(in_tile):
            rate = jnp.broadcast_to(rates[:, g : g + 1], (poles, length))
            decay.append(jnp.exp(-rate * lag))
            impulse.append(jnp.broadcast_to(coef[:, g : g + 1], (poles, length)) * jnp.exp(-rate * time))
            lift.append(impulse[-1] * once[:, g : g + 1])
            wide = jnp.where(owner == g, rate[:, :TILE], wide)
        step_ref[:, tile_of(index)] = jnp.exp(-wide * length)
        states = tile_of(index, in_tile * poles)
        for part, value in enumerate(halves(jnp.concatenate(decay, axis=0))):
            decay_ref[part, states, :] = value
        high, low = halves(jnp.concatenate(impulse, axis=0))
        response_ref[pl.ds(pl.multiple_of(index * in_tile, in_tile), in_tile), :] = dot(member, high) + dot(member, low)
        lift_ref[:, states] = turned(jnp.concatenate(lift, axis=0).astype(BF16), unit).astype(BF16)

    def filters(index):
        chans = tile_of(index)
        query, left, right = (
            short_conv(stream, chans, length, padded_ref.at[index * 3 + stream], taps_ref) for stream in range(3)
        )
        query_ref[:, chans] = query.astype(BF16)
        gated_ref[:, chans] = left * right

    unrolled(channels // TILE, turn)
    unrolled(channels // TILE, factors)
    unrolled(channels // TILE, filters)


def states_kernel(before_ref, heads_ref, taps_ref, gated_ref, decay_ref, ends_ref, final_ref, first_ref, padded_ref):
    length, channels = gated_ref.shape
    poles = ends_ref.shape[1]
    in_tile = decay_ref.shape[1] // poles * TILE // channels
    owner = iota((poles, TILE), 1) // (TILE // in_tile)

    def begin(index):
        chans = tile_of(index)
        for stream in range(3):
            padded_ref[index * 3 + stream, :ROWS, :] = before_ref[stream, :, chans].astype(F32)
            padded_ref[index * 3 + stream, ROWS:, :] = heads_ref[stream, :, chans]
        query, left, right = (
            short_conv(stream, chans, ROWS, padded_ref.at[index * 3 + stream], taps_ref) for stream in range(3)
        )
        first_ref[:, chans] = query
        final_ref[:, chans] = jnp.concatenate([left * right, gated_ref[ROWS:, chans]], axis=0).astype(BF16)

    def leave(index):
        chans = tile_of(index)
        gated = final_ref[:, chans]
        states = tile_of(index, in_tile * poles)
        every = dot(decay_ref[0, states, :], gated) + dot(decay_ref[1, states, :], gated)
        ends = jnp.zeros((poles, TILE), F32)
        for g in range(in_tile):
            ends = jnp.where(owner == g, every[g * poles : (g + 1) * poles], ends)
        ends = ends.astype(BF16)
        for block in range(ends_ref.shape[0]):
            ends_ref[block, :, chans] = ends

    unrolled(channels // TILE, begin)
    unrolled(channels // TILE, leave)


def inside_kernel(gated_ref, skip_ref, response_ref, base_ref, signal_ref, sum_ref):
    length, channels = gated_ref.shape
    groups = response_ref.shape[0]
    width = channels // groups
    in_tile = TILE // width
    tiles = channels // TILE
    strip = STRIP
    unit = identity(length)
    lane = iota((width, length), 1)
    causal = iota((strip, length), 1) >= iota((strip, length), 0)

    def signals(index):
        gated = gated_ref[:, tile_of(index)]
        for at in range(length // strip):
            piece = turned(gated[at * strip : (at + 1) * strip], unit).astype(BF16)
            signal_ref[at, tile_of(index), :] = piece

    def products(index):
        for pair in range(in_tile // 2):
            group = index * in_tile + 2 * pair
            responses = response_ref[pl.ds(group, 2), :]
            blocks = []
            for g in range(2):
                spread = jnp.broadcast_to(responses[g : g + 1], (strip, length))
                shifted = pltpu.roll(spread, 0, 1, stride=1, stride_axis=0)
                blocks.append(jnp.where(causal, shifted, 0.0).astype(BF16))
            rows = pl.ds(pl.multiple_of(group * width, 2 * width), 2 * width)
            signal = jnp.concatenate([signal_ref[at, rows, :] for at in range(length // strip)], axis=0)
            both = dot(signal, jnp.concatenate(blocks, axis=1))
            for g in range(2):
                total = None
                for at in range(length // strip):
                    first = at * 2 * width + g * width
                    term = both[first : first + width, g * length : (g + 1) * length]
                    if at:
                        term = jnp.where(lane >= at * strip, pltpu.roll(term, at * strip, 1), 0.0)
                    total = term if total is None else total + term
                sum_ref[pl.ds(pl.multiple_of((group + g) * width, width), width), :] = total

    def back(index):
        chans = tile_of(index)
        high, low = halves(sum_ref[chans, :])
        direct = skip_ref[:, chans] * gated_ref[:, chans].astype(F32)
        base_ref[:, chans] = turned(high, unit) + turned(low, unit) + direct

    unrolled(tiles, signals)
    unrolled(tiles, products)
    unrolled(tiles, back)


def finish_kernel(at_ref, ends_ref, step_ref, lift_ref, query_ref, first_ref, base_ref, mixed_ref, state_ref):
    length, share = mixed_ref.shape
    poles, channels = step_ref.shape
    in_tile = lift_ref.shape[1] // poles * TILE // channels
    me, half = at_ref[0], at_ref[1]
    here = tile_of(half, share)
    step = step_ref[:, here]

    def earlier(block, state):
        return jnp.where(block < me, step * state + ends_ref[block, :, here].astype(F32), state)

    state_ref[...] = lax.fori_loop(0, ends_ref.shape[0] - 1, earlier, jnp.zeros((poles, share), F32))
    owner = iota((poles, TILE), 1) // (TILE // in_tile)

    def tile(index):
        at = half * (share // TILE) + index
        chans = tile_of(at)
        entering = state_ref[:, tile_of(index)]
        apart = jnp.concatenate([jnp.where(owner == g, entering, 0.0) for g in range(in_tile)], axis=0)
        high, low = halves(apart)
        lift = lift_ref[:, tile_of(at, in_tile * poles)]
        carried = dot(lift, high) + dot(lift, low)
        query = jnp.concatenate([first_ref[:, chans], query_ref[:, chans].astype(F32)[ROWS:]], axis=0)
        mixed_ref[:, tile_of(index)] = (query * (base_ref[:, chans] + carried)).astype(BF16)

    unrolled(share // TILE, tile)


def early_kernel(at_ref, own_ref, beside_ref, across_ref, *rest):
    *weight_hbms, total_ref, rows_ref, block_ref, layers_ref, weight_ref, sems = rest
    copies = [
        pltpu.make_async_copy(hbm, weight_ref.at[at], sems.at[at]) for at, hbm in enumerate(weight_hbms)
    ]
    for copy in copies:
        copy.start()
    layer = at_ref[0]
    last = layer ^ 2
    for bits, ref in ((0, own_ref), (1, beside_ref), (3, across_ref)):
        layers_ref[layer ^ bits] = ref[...]
    layers_ref[last] = jnp.zeros_like(own_ref)
    block_ref[...] = layers_ref[at_ref[1 + len(copies)]]
    for copy in copies:
        copy.wait()
    for column in range(0, total_ref.shape[1], COLUMNS):
        columns = slice(column, column + COLUMNS)
        total = None
        for at in range(len(copies)):
            term = dot(layers_ref[at_ref[1 + at]], weight_ref[at, :, columns])
            total = term if total is None else total + term
        total_ref[:, columns] = total
    rows_ref[...] = jnp.zeros_like(rows_ref)
    for at in range(len(copies)):

        @pl.when(at_ref[1 + at] == last)
        def _():
            rows_ref[...] = weight_ref[at]


def joined_kernel(at_ref, total_ref, rows_ref, block_ref, weight_ref, out_ref, last_ref):
    out_ref[...] = total_ref[...] + dot(block_ref[...], weight_ref[...])
    last_ref[...] = rows_ref[...]

    @pl.when(at_ref[4] == at_ref[0] ^ 2)
    def _():
        last_ref[...] = weight_ref[...]


def late_kernel(first, beyond_ref, total_ref, rows_ref, out_ref):
    tokens = pl.ds(first, out_ref.shape[0])
    out_ref[...] = (total_ref[tokens, :] + dot(beyond_ref[tokens, :], rows_ref[...])).astype(out_ref.dtype)


def swap(value, *bits):
    count = lax.axis_size("ctx")
    pairs = [(source, source ^ bits[source % len(bits)]) for source in range(count)]
    return lax.ppermute(value, "ctx", pairs)


def after(value, earlier):
    return lax.optimization_barrier((value, earlier))[0]


def trade(value, bits):
    count = lax.axis_size("tp")
    return lax.ppermute(value, "tp", [(source, source ^ bits) for source in range(count)])


def local(streams, conv_weight, rates, residues, skip, out_weight):
    channels, length = streams.shape[1:]
    groups, poles = rates.shape
    blocks, layers = lax.axis_size("ctx"), lax.axis_size("tp")
    rows, features = out_weight.shape
    share = channels // CORES
    square = blocks == 8 and rows == share

    rates, residues, skip = rates.T, residues.T, skip[None, :]
    (tails,) = call(tails_kernel, [((3, ROWS, channels), BF16)], "tails", streams)
    before = from_behind(tails, "ctx", 1)
    if square:
        near = swap(out_weight, 2, 4)
    tiles = channels // TILE
    heads, query, gated, decay, step, response, lift, skip = call(
        prepare_kernel,
        [
            ((3, ROWS, channels), F32),
            ((length, channels), BF16),
            ((length, channels), F32),
            ((2, groups * poles, length), BF16),
            ((poles, channels), F32),
            ((groups, length), F32),
            ((length, groups * poles), BF16),
            ((1, channels), F32),
        ],
        "prepare",
        streams, conv_weight, rates, residues, skip,
        scratch=[pltpu.VMEM((3 * tiles, ROWS + length, TILE), F32)],
        flops=10**9,
    )
    ends, gated, first = call(
        states_kernel,
        [((blocks, poles, channels), BF16), ((length, channels), BF16), ((ROWS, channels), F32)],
        "states",
        before, heads, conv_weight, gated, decay,
        scratch=[pltpu.VMEM((3 * tiles, 2 * ROWS, TILE), F32)],
    )
    all_ends = lax.all_to_all(ends, "ctx", split_axis=0, concat_axis=0, tiled=True)
    (base,) = call(
        inside_kernel,
        [((length, channels), F32)],
        "inside",
        gated, skip, response,
        scratch=[
            pltpu.VMEM((length // STRIP, channels, STRIP), BF16),
            pltpu.VMEM((channels, length), F32),
        ],
        flops=10**9,
    )
    if square:
        other_near = swap(after(out_weight, (gated, near)), 4, 2)
    me = lax.axis_index("ctx").astype(jnp.int32)
    core = me % CORES
    smem = [pl.BlockSpec(memory_space=pltpu.SMEM)]

    def finished(half):
        return call(
            finish_kernel,
            [((length, share), BF16)],
            "finish",
            jnp.stack([me, half]), all_ends, step, lift, query, first, base,
            specs=smem + whole(6),
            flops=3 * 10**9,
            scratch=[pltpu.VMEM((poles, share), F32)],
        )[0]

    if rows == share:
        other, mine = finished(1 - core), finished(core)
    else:
        mixed = jnp.concatenate([finished(jnp.full_like(me, half)) for half in range(CORES)], axis=1)
        by_core = mixed.reshape(length, share // rows, CORES, rows).transpose(2, 0, 1, 3)
        by_core = by_core.reshape(CORES, length, share)
        mine = lax.dynamic_index_in_dim(by_core, core, 0, keepdims=False)
        other = lax.dynamic_index_in_dim(by_core, 1 - core, 0, keepdims=False)
    block = jnp.concatenate([mine, swap(other, 1)], axis=0)
    layer = lax.axis_index("tp").astype(jnp.int32)
    beside, across = trade(block, 1), trade(block, 3)
    beyond = trade(after(across, (beside, other_near)) if square else across, 1)
    if square:
        diagonal = swap(after(near, block), 4, 2)
        weight = (out_weight, near, other_near, diagonal)
    else:
        core_groups = [list(range(core, blocks, CORES)) for core in range(CORES)]
        weight = lax.all_gather(out_weight, "ctx", axis=0, axis_index_groups=core_groups)
        weight = tuple(weight.reshape(layers, share, features))
    first_row = jnp.where(core == 0, 1, 2)
    chip = me // CORES
    place = [chip, chip ^ first_row, chip ^ (3 - first_row), chip ^ 3] if square else [jnp.full_like(me, at) for at in range(4)]
    at = jnp.stack([layer] + place)
    *sooner, latest = weight
    total, last_rows, last_block = call(
        early_kernel,
        [((CORES * length, features), F32), ((share, features), BF16), (block.shape, BF16)],
        "early",
        at, block, beside, across,
        *(pltpu.with_memory_space_constraint(part, pltpu.HBM) for part in sooner),
        specs=smem + whole(3) + [pl.BlockSpec(memory_space=pltpu.HBM)] * len(sooner),
        scratch=[
            pltpu.VMEM((layers,) + block.shape, BF16),
            pltpu.VMEM((len(sooner), share, features), BF16),
            pltpu.SemaphoreType.DMA((len(sooner),)),
        ],
        flops=10**10,
    )
    total, last_rows = call(
        joined_kernel,
        [((CORES * length, features), F32), ((share, features), BF16)],
        "joined",
        at, total, last_rows, last_block, latest,
        specs=smem + whole(4),
        flops=0,
    )
    sides = []
    for side, kind in ((1, BF16), (0, F32)):
        sides += call(
            functools.partial(late_kernel, side * length),
            [((length, features), kind)],
            "late",
            beyond, total, last_rows,
            flops=0,
        )
    other, mine = sides
    other = swap(other, 1)
    return (mine + other.astype(F32)).astype(BF16)


def solution(mesh):
    return jax.shard_map(
        local,
        mesh=mesh,
        in_specs=(
            P(None, "tp", "ctx"),
            P(None, None, "tp"),
            P("tp", None),
            P("tp", None),
            P("tp"),
            P("ctx", "tp"),
        ),
        out_specs=P("ctx", "tp"),
        check_vma=False,
    )
```

```python
import functools
import math

import jax
import jax.numpy as jnp
from jax import lax
from jax.experimental import pallas as pl
from jax.experimental.pallas import tpu as pltpu
from jax.sharding import PartitionSpec as P

F32 = jnp.float32
BF16 = jnp.bfloat16
ROWS = 8
TILE = 128
CORES = 2
COLUMNS = 256
STRIP = 32
VMEM_LIMIT = 24 * 1024 * 1024
PLAIN = (((1,), (0,)), ((), ()))
CONTRACT_LANES = (((1,), (1,)), ((), ()))


def from_behind(value, axis, steps):
    count = lax.axis_size(axis)
    leading, last = (max(0, -steps), min(count, count - steps))
    return lax.ppermute(value, axis, [(source, source + steps) for source in range(leading, last)])


def dot(left, right, dims=PLAIN):
    return lax.dot_general(left, right, dims, preferred_element_type=F32)


def halves(value):
    high = value.astype(BF16)
    return high, (value - high.astype(F32)).astype(BF16)


def iota(shape, axis):
    return lax.broadcasted_iota(jnp.int32, shape, axis)


def identity(size):
    return (iota((size, size), 0) == iota((size, size), 1)).astype(BF16)


def turned(value, unit):
    return dot(unit, value, CONTRACT_LANES)


def whole(count):
    return [pl.BlockSpec(memory_space=pltpu.VMEM)] * count


def call(kernel, outs, name, *operands, specs=None, scratch=(), flops=10**8):
    return pl.pallas_call(
        kernel,
        out_shape=tuple(jax.ShapeDtypeStruct(*out) for out in outs),
        in_specs=whole(len(operands)) if specs is None else specs,
        out_specs=tuple(whole(len(outs))),
        scratch_shapes=scratch,
        compiler_params=pltpu.CompilerParams(vmem_limit_bytes=VMEM_LIMIT),
        cost_estimate=pl.CostEstimate(flops=flops, bytes_accessed=flops // 100, transcendentals=0),
        name=name,
    )(*operands)


def tile_of(index, size=TILE):
    return pl.ds(pl.multiple_of(index * size, size), size)


def unrolled(count, body):
    def step(index, carry):
        body(index)
        return carry

    lax.fori_loop(0, count, step, 0, unroll=math.gcd(count, 4))


def tails_kernel(*refs):
    count = len(refs) // 2 - 1
    sources, tails_ref, fetched, sems = refs[:count], refs[count], refs[count + 1 : -1], refs[-1]
    copies = [
        pltpu.make_async_copy(source, target, sems.at[at]) for at, (source, target) in enumerate(zip(sources, fetched))
    ]
    for copy in copies:
        copy.start()
    streams_ref = fetched[0]
    length = streams_ref.shape[2]
    pick = (iota((2 * ROWS, length), 1) == iota((2 * ROWS, length), 0) + (length - ROWS)).astype(BF16)
    copies[0].wait()
    for stream in range(streams_ref.shape[0]):
        rows = dot(pick, streams_ref[stream], CONTRACT_LANES)
        tails_ref[stream] = rows[:ROWS].astype(BF16)
    for copy in copies[1:]:
        copy.wait()


def short_conv(stream, chans, rows, padded, taps_ref):
    total = None
    for shift in range(taps_ref.shape[1]):
        term = taps_ref[stream, shift : shift + 1, chans] * padded[pl.ds(ROWS - shift, rows), :]
        total = term if total is None else total + term
    return total


def prepare_kernel(
    streams_ref, taps_ref, rates_ref, residues_ref,
    heads_ref, query_ref, gated_ref, decay_ref, step_ref, response_ref, lift_ref, padded_ref,
):
    channels, length = streams_ref.shape[1:]
    poles, groups = rates_ref.shape
    width = channels // groups
    in_tile = TILE // width
    unit = identity(length)
    lag = (length - 1) - iota((poles, length), 1).astype(F32)
    owner = iota((poles, TILE), 1) // width
    time = iota((poles, length), 1).astype(F32)
    member = (iota((in_tile, in_tile * poles), 1) // poles == iota((in_tile, in_tile * poles), 0)).astype(BF16)
    scale = residues_ref[...] * jnp.sqrt(2.0 * rates_ref[...]) / math.sqrt(poles)

    def turn(index):
        chans = tile_of(index)
        for stream in range(3):
            tokens = turned(streams_ref[stream, chans, :], unit)
            padded_ref[index * 3 + stream, :ROWS, :] = jnp.zeros((ROWS, TILE), F32)
            padded_ref[index * 3 + stream, ROWS:, :] = tokens
            heads_ref[stream, :, chans] = tokens[:ROWS]

    def factors(index):
        shift = groups - index * in_tile
        rates = pltpu.roll(rates_ref[...], shift, 1)
        coef = pltpu.roll(scale, shift, 1)
        once = jnp.exp(-rates)
        decay, impulse, lift = [], [], []
        wide = jnp.zeros((poles, TILE), F32)
        for g in range(in_tile):
            rate = jnp.broadcast_to(rates[:, g : g + 1], (poles, length))
            decay.append(jnp.exp(-rate * lag))
            impulse.append(jnp.broadcast_to(coef[:, g : g + 1], (poles, length)) * jnp.exp(-rate * time))
            lift.append(impulse[-1] * once[:, g : g + 1])
            wide = jnp.where(owner == g, rate[:, :TILE], wide)
        step_ref[:, tile_of(index)] = jnp.exp(-wide * length)
        states = tile_of(index, in_tile * poles)
        for part, value in enumerate(halves(jnp.concatenate(decay, axis=0))):
            decay_ref[part, states, :] = value
        high, low = halves(jnp.concatenate(impulse, axis=0))
        response_ref[pl.ds(pl.multiple_of(index * in_tile, in_tile), in_tile), :] = dot(member, high) + dot(member, low)
        lift_ref[:, states] = turned(jnp.concatenate(lift, axis=0).astype(BF16), unit).astype(BF16)

    def filters(index):
        chans = tile_of(index)
        query, left, right = (
            short_conv(stream, chans, length, padded_ref.at[index * 3 + stream], taps_ref) for stream in range(3)
        )
        query_ref[:, chans] = query.astype(BF16)
        gated_ref[:, chans] = left * right

    unrolled(channels // TILE, turn)
    unrolled(channels // TILE, factors)
    unrolled(channels // TILE, filters)


def states_kernel(before_ref, heads_ref, taps_ref, gated_ref, decay_ref, ends_ref, final_ref, first_ref, padded_ref):
    length, channels = gated_ref.shape
    poles = ends_ref.shape[1]
    in_tile = decay_ref.shape[1] // poles * TILE // channels
    owner = iota((poles, TILE), 1) // (TILE // in_tile)

    def begin(index):
        chans = tile_of(index)
        for stream in range(3):
            padded_ref[index * 3 + stream, :ROWS, :] = before_ref[stream, :, chans].astype(F32)
            padded_ref[index * 3 + stream, ROWS:, :] = heads_ref[stream, :, chans]
        query, left, right = (
            short_conv(stream, chans, ROWS, padded_ref.at[index * 3 + stream], taps_ref) for stream in range(3)
        )
        first_ref[:, chans] = query
        final_ref[:, chans] = jnp.concatenate([left * right, gated_ref[ROWS:, chans]], axis=0).astype(BF16)

    def leave(index):
        chans = tile_of(index)
        gated = final_ref[:, chans]
        states = tile_of(index, in_tile * poles)
        every = dot(decay_ref[0, states, :], gated) + dot(decay_ref[1, states, :], gated)
        ends = jnp.zeros((poles, TILE), F32)
        for g in range(in_tile):
            ends = jnp.where(owner == g, every[g * poles : (g + 1) * poles], ends)
        ends = ends.astype(BF16)
        for block in range(ends_ref.shape[0]):
            ends_ref[block, :, chans] = ends

    unrolled(channels // TILE, begin)
    unrolled(channels // TILE, leave)


def inside_kernel(gated_ref, skip_ref, response_ref, base_ref, signal_ref, sum_ref):
    length, channels = gated_ref.shape
    groups = response_ref.shape[0]
    width = channels // groups
    in_tile = TILE // width
    tiles = channels // TILE
    strip = STRIP
    unit = identity(length)
    lane = iota((width, length), 1)
    causal = iota((strip, length), 1) >= iota((strip, length), 0)

    def signals(index):
        gated = gated_ref[:, tile_of(index)]
        for at in range(length // strip):
            piece = turned(gated[at * strip : (at + 1) * strip], unit).astype(BF16)
            signal_ref[at, tile_of(index), :] = piece

    def products(index):
        for pair in range(in_tile // 2):
            group = index * in_tile + 2 * pair
            responses = response_ref[pl.ds(group, 2), :]
            blocks = []
            for g in range(2):
                spread = jnp.broadcast_to(responses[g : g + 1], (strip, length))
                shifted = pltpu.roll(spread, 0, 1, stride=1, stride_axis=0)
                blocks.append(jnp.where(causal, shifted, 0.0).astype(BF16))
            rows = pl.ds(pl.multiple_of(group * width, 2 * width), 2 * width)
            signal = jnp.concatenate([signal_ref[at, rows, :] for at in range(length // strip)], axis=0)
            both = dot(signal, jnp.concatenate(blocks, axis=1))
            for g in range(2):
                total = None
                for at in range(length // strip):
                    first = at * 2 * width + g * width
                    term = both[first : first + width, g * length : (g + 1) * length]
                    if at:
                        term = jnp.where(lane >= at * strip, pltpu.roll(term, at * strip, 1), 0.0)
                    total = term if total is None else total + term
                sum_ref[pl.ds(pl.multiple_of((group + g) * width, width), width), :] = total

    def back(index):
        chans = tile_of(index)
        high, low = halves(sum_ref[chans, :])
        direct = skip_ref[:, chans] * gated_ref[:, chans].astype(F32)
        base_ref[:, chans] = turned(high, unit) + turned(low, unit) + direct

    unrolled(tiles, signals)
    unrolled(tiles, products)
    unrolled(tiles, back)


def finish_kernel(at_ref, ends_ref, step_ref, lift_ref, query_ref, first_ref, base_ref, mixed_ref, state_ref):
    length, share = mixed_ref.shape
    poles, channels = step_ref.shape
    in_tile = lift_ref.shape[1] // poles * TILE // channels
    me, half = at_ref[0], at_ref[1]
    here = tile_of(half, share)
    step = step_ref[:, here]

    def earlier(block, state):
        return jnp.where(block < me, step * state + ends_ref[block, :, here].astype(F32), state)

    state_ref[...] = lax.fori_loop(0, ends_ref.shape[0] - 1, earlier, jnp.zeros((poles, share), F32))
    owner = iota((poles, TILE), 1) // (TILE // in_tile)

    def tile(index):
        at = half * (share // TILE) + index
        chans = tile_of(at)
        entering = state_ref[:, tile_of(index)]
        apart = jnp.concatenate([jnp.where(owner == g, entering, 0.0) for g in range(in_tile)], axis=0)
        high, low = halves(apart)
        lift = lift_ref[:, tile_of(at, in_tile * poles)]
        carried = dot(lift, high) + dot(lift, low)
        query = jnp.concatenate([first_ref[:, chans], query_ref[:, chans].astype(F32)[ROWS:]], axis=0)
        mixed_ref[:, tile_of(index)] = (query * (base_ref[:, chans] + carried)).astype(BF16)

    unrolled(share // TILE, tile)


def early_kernel(at_ref, own_ref, beside_ref, across_ref, *rest):
    *weight_hbms, total_ref, rows_ref, block_ref, layers_ref, weight_ref, sems = rest
    copies = [
        pltpu.make_async_copy(hbm, weight_ref.at[at], sems.at[at]) for at, hbm in enumerate(weight_hbms)
    ]
    for copy in copies:
        copy.start()
    layer = at_ref[0]
    last = layer ^ 2
    for bits, ref in ((0, own_ref), (1, beside_ref), (3, across_ref)):
        layers_ref[layer ^ bits] = ref[...]
    layers_ref[last] = jnp.zeros_like(own_ref)
    block_ref[...] = layers_ref[at_ref[1 + len(copies)]]
    for copy in copies:
        copy.wait()
    for column in range(0, total_ref.shape[1], COLUMNS):
        columns = slice(column, column + COLUMNS)
        total = None
        for at in range(len(copies)):
            term = dot(layers_ref[at_ref[1 + at]], weight_ref[at, :, columns])
            total = term if total is None else total + term
        total_ref[:, columns] = total
    rows_ref[...] = jnp.zeros_like(rows_ref)
    for at in range(len(copies)):

        @pl.when(at_ref[1 + at] == last)
        def _():
            rows_ref[...] = weight_ref[at]


def joined_kernel(at_ref, total_ref, rows_ref, block_ref, weight_ref, out_ref, last_ref):
    out_ref[...] = total_ref[...] + dot(block_ref[...], weight_ref[...])
    last_ref[...] = rows_ref[...]

    @pl.when(at_ref[4] == at_ref[0] ^ 2)
    def _():
        last_ref[...] = weight_ref[...]


def late_kernel(first, beyond_ref, total_ref, rows_ref, out_ref):
    tokens = pl.ds(first, out_ref.shape[0])
    out_ref[...] = (total_ref[tokens, :] + dot(beyond_ref[tokens, :], rows_ref[...])).astype(out_ref.dtype)


def swap(value, *bits):
    count = lax.axis_size("ctx")
    pairs = [(source, source ^ bits[source % len(bits)]) for source in range(count)]
    return lax.ppermute(value, "ctx", pairs)


def after(value, earlier):
    return lax.optimization_barrier((value, earlier))[0]


def trade(value, bits):
    count = lax.axis_size("tp")
    return lax.ppermute(value, "tp", [(source, source ^ bits) for source in range(count)])


def local(streams, conv_weight, rates, residues, skip, out_weight):
    channels, length = streams.shape[1:]
    groups, poles = rates.shape
    blocks, layers = lax.axis_size("ctx"), lax.axis_size("tp")
    rows, features = out_weight.shape
    share = channels // CORES
    square = blocks == 8 and rows == share

    inputs = (streams, conv_weight, rates.T, residues.T, skip[None, :])
    tails, streams, conv_weight, rates, residues, skip = call(
        tails_kernel,
        [((3, ROWS, channels), BF16)] + [(part.shape, part.dtype) for part in inputs],
        "tails",
        *(pltpu.with_memory_space_constraint(part, pltpu.HBM) for part in inputs),
        specs=[pl.BlockSpec(memory_space=pltpu.HBM)] * len(inputs),
        scratch=[pltpu.SemaphoreType.DMA((len(inputs),))],
    )
    before = from_behind(tails, "ctx", 1)
    if square:
        near = swap(out_weight, 2, 4)
    tiles = channels // TILE
    heads, query, gated, decay, step, response, lift = call(
        prepare_kernel,
        [
            ((3, ROWS, channels), F32),
            ((length, channels), BF16),
            ((length, channels), F32),
            ((2, groups * poles, length), BF16),
            ((poles, channels), F32),
            ((groups, length), F32),
            ((length, groups * poles), BF16),
        ],
        "prepare",
        streams, conv_weight, rates, residues,
        scratch=[pltpu.VMEM((3 * tiles, ROWS + length, TILE), F32)],
        flops=10**9,
    )
    ends, gated, first = call(
        states_kernel,
        [((blocks, poles, channels), BF16), ((length, channels), BF16), ((ROWS, channels), F32)],
        "states",
        before, heads, conv_weight, gated, decay,
        scratch=[pltpu.VMEM((3 * tiles, 2 * ROWS, TILE), F32)],
    )
    all_ends = lax.all_to_all(ends, "ctx", split_axis=0, concat_axis=0, tiled=True)
    (base,) = call(
        inside_kernel,
        [((length, channels), F32)],
        "inside",
        gated, skip, response,
        scratch=[
            pltpu.VMEM((length // STRIP, channels, STRIP), BF16),
            pltpu.VMEM((channels, length), F32),
        ],
        flops=10**9,
    )
    if square:
        other_near = swap(after(out_weight, (base, near)), 4, 2)
    me = lax.axis_index("ctx").astype(jnp.int32)
    core = me % CORES
    smem = [pl.BlockSpec(memory_space=pltpu.SMEM)]

    def finished(half):
        return call(
            finish_kernel,
            [((length, share), BF16)],
            "finish",
            jnp.stack([me, half]), all_ends, step, lift, query, first, base,
            specs=smem + whole(6),
            flops=3 * 10**9,
            scratch=[pltpu.VMEM((poles, share), F32)],
        )[0]

    if rows == share:
        other, mine = finished(1 - core), finished(core)
    else:
        mixed = jnp.concatenate([finished(jnp.full_like(me, half)) for half in range(CORES)], axis=1)
        by_core = mixed.reshape(length, share // rows, CORES, rows).transpose(2, 0, 1, 3)
        by_core = by_core.reshape(CORES, length, share)
        mine = lax.dynamic_index_in_dim(by_core, core, 0, keepdims=False)
        other = lax.dynamic_index_in_dim(by_core, 1 - core, 0, keepdims=False)
    block = jnp.concatenate([mine, swap(other, 1)], axis=0)
    layer = lax.axis_index("tp").astype(jnp.int32)
    beside, across = trade(block, 1), trade(block, 3)
    beyond = trade(after(across, other_near) if square else across, 1)
    if square:
        diagonal = swap(after(near, block), 4, 2)
        weight = (out_weight, near, other_near, diagonal)
    else:
        core_groups = [list(range(core, blocks, CORES)) for core in range(CORES)]
        weight = lax.all_gather(out_weight, "ctx", axis=0, axis_index_groups=core_groups)
        weight = tuple(weight.reshape(layers, share, features))
    first_row = jnp.where(core == 0, 1, 2)
    chip = me // CORES
    place = [chip, chip ^ first_row, chip ^ (3 - first_row), chip ^ 3] if square else [jnp.full_like(me, at) for at in range(4)]
    at = jnp.stack([layer] + place)
    *sooner, latest = weight
    total, last_rows, last_block = call(
        early_kernel,
        [((CORES * length, features), F32), ((share, features), BF16), (block.shape, BF16)],
        "early",
        at, block, beside, across,
        *(pltpu.with_memory_space_constraint(part, pltpu.HBM) for part in sooner),
        specs=smem + whole(3) + [pl.BlockSpec(memory_space=pltpu.HBM)] * len(sooner),
        scratch=[
            pltpu.VMEM((layers,) + block.shape, BF16),
            pltpu.VMEM((len(sooner), share, features), BF16),
            pltpu.SemaphoreType.DMA((len(sooner),)),
        ],
        flops=10**10,
    )
    total, last_rows = call(
        joined_kernel,
        [((CORES * length, features), F32), ((share, features), BF16)],
        "joined",
        at, total, last_rows, last_block, latest,
        specs=smem + whole(4),
        flops=0,
    )
    sides = []
    for side, kind in ((1, BF16), (0, F32)):
        sides += call(
            functools.partial(late_kernel, side * length),
            [((length, features), kind)],
            "late",
            beyond, total, last_rows,
            flops=0,
        )
    other, mine = sides
    other = swap(other, 1)
    return (mine + other.astype(F32)).astype(BF16)


def solution(mesh):
    return jax.shard_map(
        local,
        mesh=mesh,
        in_specs=(
            P(None, "tp", "ctx"),
            P(None, None, "tp"),
            P("tp", None),
            P("tp", None),
            P("tp"),
            P("ctx", "tp"),
        ),
        out_specs=P("ctx", "tp"),
        check_vma=False,
    )
```

```python
import functools
import math

import jax
import jax.numpy as jnp
from jax import lax
from jax.experimental import pallas as pl
from jax.experimental.pallas import tpu as pltpu
from jax.sharding import PartitionSpec as P

F32 = jnp.float32
BF16 = jnp.bfloat16
ROWS = 8
TILE = 128
CORES = 2
COLUMNS = 256
STRIP = 32
VMEM_LIMIT = 24 * 1024 * 1024
PLAIN = (((1,), (0,)), ((), ()))
CONTRACT_LANES = (((1,), (1,)), ((), ()))


def from_behind(value, axis, steps):
    count = lax.axis_size(axis)
    leading, last = (max(0, -steps), min(count, count - steps))
    return lax.ppermute(value, axis, [(source, source + steps) for source in range(leading, last)])


def dot(left, right, dims=PLAIN):
    return lax.dot_general(left, right, dims, preferred_element_type=F32)


def halves(value):
    high = value.astype(BF16)
    return high, (value - high.astype(F32)).astype(BF16)


def iota(shape, axis):
    return lax.broadcasted_iota(jnp.int32, shape, axis)


def identity(size):
    return (iota((size, size), 0) == iota((size, size), 1)).astype(BF16)


def turned(value, unit):
    return dot(unit, value, CONTRACT_LANES)


def whole(count):
    return [pl.BlockSpec(memory_space=pltpu.VMEM)] * count


def call(kernel, outs, name, *operands, specs=None, scratch=(), flops=10**8):
    return pl.pallas_call(
        kernel,
        out_shape=tuple(jax.ShapeDtypeStruct(*out) for out in outs),
        in_specs=whole(len(operands)) if specs is None else specs,
        out_specs=tuple(whole(len(outs))),
        scratch_shapes=scratch,
        compiler_params=pltpu.CompilerParams(vmem_limit_bytes=VMEM_LIMIT),
        cost_estimate=pl.CostEstimate(flops=flops, bytes_accessed=flops // 100, transcendentals=0),
        name=name,
    )(*operands)


def tile_of(index, size=TILE):
    return pl.ds(pl.multiple_of(index * size, size), size)


def unrolled(count, body):
    def step(index, carry):
        body(index)
        return carry

    lax.fori_loop(0, count, step, 0, unroll=math.gcd(count, 4))


def tails_kernel(*refs):
    count = len(refs) // 2 - 1
    sources, tails_ref, fetched, sems = refs[:count], refs[count], refs[count + 1 : -1], refs[-1]
    copies = [
        pltpu.make_async_copy(source, target, sems.at[at]) for at, (source, target) in enumerate(zip(sources, fetched))
    ]
    for copy in copies:
        copy.start()
    streams_ref = fetched[0]
    length = streams_ref.shape[2]
    pick = (iota((2 * ROWS, length), 1) == iota((2 * ROWS, length), 0) + (length - ROWS)).astype(BF16)
    copies[0].wait()
    for stream in range(streams_ref.shape[0]):
        rows = dot(pick, streams_ref[stream], CONTRACT_LANES)
        tails_ref[stream] = rows[:ROWS].astype(BF16)
    for copy in copies[1:]:
        copy.wait()


def short_conv(stream, chans, rows, padded, taps_ref):
    total = None
    for shift in range(taps_ref.shape[1]):
        term = taps_ref[stream, shift : shift + 1, chans] * padded[pl.ds(ROWS - shift, rows), :]
        total = term if total is None else total + term
    return total


def prepare_kernel(
    streams_ref, taps_ref, rates_ref, residues_ref,
    heads_ref, query_ref, gated_ref, decay_ref, step_ref, response_ref, lift_ref, padded_ref,
):
    channels, length = streams_ref.shape[1:]
    poles, groups = rates_ref.shape
    width = channels // groups
    in_tile = TILE // width
    unit = identity(length)
    lag = (length - 1) - iota((poles, length), 1).astype(F32)
    owner = iota((poles, TILE), 1) // width
    time = iota((poles, length), 1).astype(F32)
    member = (iota((in_tile, in_tile * poles), 1) // poles == iota((in_tile, in_tile * poles), 0)).astype(BF16)
    scale = residues_ref[...] * jnp.sqrt(2.0 * rates_ref[...]) / math.sqrt(poles)

    def turn(index):
        chans = tile_of(index)
        for stream in range(3):
            tokens = turned(streams_ref[stream, chans, :], unit)
            padded_ref[index * 3 + stream, :ROWS, :] = jnp.zeros((ROWS, TILE), F32)
            padded_ref[index * 3 + stream, ROWS:, :] = tokens
            heads_ref[stream, :, chans] = tokens[:ROWS]

    def factors(index):
        shift = groups - index * in_tile
        rates = pltpu.roll(rates_ref[...], shift, 1)
        coef = pltpu.roll(scale, shift, 1)
        once = jnp.exp(-rates)
        decay, impulse, lift = [], [], []
        wide = jnp.zeros((poles, TILE), F32)
        for g in range(in_tile):
            rate = jnp.broadcast_to(rates[:, g : g + 1], (poles, length))
            decay.append(jnp.exp(-rate * lag))
            impulse.append(jnp.broadcast_to(coef[:, g : g + 1], (poles, length)) * jnp.exp(-rate * time))
            lift.append(impulse[-1] * once[:, g : g + 1])
            wide = jnp.where(owner == g, rate[:, :TILE], wide)
        step_ref[:, tile_of(index)] = jnp.exp(-wide * length)
        states = tile_of(index, in_tile * poles)
        for part, value in enumerate(halves(jnp.concatenate(decay, axis=0))):
            decay_ref[part, states, :] = value
        high, low = halves(jnp.concatenate(impulse, axis=0))
        response_ref[pl.ds(pl.multiple_of(index * in_tile, in_tile), in_tile), :] = dot(member, high) + dot(member, low)
        lift_ref[:, states] = turned(jnp.concatenate(lift, axis=0).astype(BF16), unit).astype(BF16)

    def filters(index):
        chans = tile_of(index)
        query, left, right = (
            short_conv(stream, chans, length, padded_ref.at[index * 3 + stream], taps_ref) for stream in range(3)
        )
        query_ref[:, chans] = query.astype(BF16)
        gated_ref[:, chans] = left * right

    unrolled(channels // TILE, turn)
    unrolled(channels // TILE, factors)
    unrolled(channels // TILE, filters)


def states_kernel(before_ref, heads_ref, taps_ref, gated_ref, decay_ref, ends_ref, final_ref, first_ref, padded_ref):
    length, channels = gated_ref.shape
    poles = ends_ref.shape[1]
    in_tile = decay_ref.shape[1] // poles * TILE // channels
    owner = iota((poles, TILE), 1) // (TILE // in_tile)

    def begin(index):
        chans = tile_of(index)
        for stream in range(3):
            padded_ref[index * 3 + stream, :ROWS, :] = before_ref[stream, :, chans].astype(F32)
            padded_ref[index * 3 + stream, ROWS:, :] = heads_ref[stream, :, chans]
        query, left, right = (
            short_conv(stream, chans, ROWS, padded_ref.at[index * 3 + stream], taps_ref) for stream in range(3)
        )
        first_ref[:, chans] = query
        final_ref[:, chans] = jnp.concatenate([left * right, gated_ref[ROWS:, chans]], axis=0).astype(BF16)

    def leave(index):
        chans = tile_of(index)
        gated = final_ref[:, chans]
        states = tile_of(index, in_tile * poles)
        every = dot(decay_ref[0, states, :], gated) + dot(decay_ref[1, states, :], gated)
        ends = jnp.zeros((poles, TILE), F32)
        for g in range(in_tile):
            ends = jnp.where(owner == g, every[g * poles : (g + 1) * poles], ends)
        ends = ends.astype(BF16)
        for block in range(ends_ref.shape[0]):
            ends_ref[block, :, chans] = ends

    unrolled(channels // TILE, begin)
    unrolled(channels // TILE, leave)


def inside_kernel(gated_ref, skip_ref, response_ref, base_ref, signal_ref, sum_ref):
    length, channels = gated_ref.shape
    groups = response_ref.shape[0]
    width = channels // groups
    in_tile = TILE // width
    tiles = channels // TILE
    strip = STRIP
    unit = identity(length)
    lane = iota((width, length), 1)
    causal = iota((strip, length), 1) >= iota((strip, length), 0)

    def signals(index):
        gated = gated_ref[:, tile_of(index)]
        for at in range(length // strip):
            piece = turned(gated[at * strip : (at + 1) * strip], unit).astype(BF16)
            signal_ref[at, tile_of(index), :] = piece

    def products(index):
        for pair in range(in_tile // 2):
            group = index * in_tile + 2 * pair
            responses = response_ref[pl.ds(group, 2), :]
            blocks = []
            for g in range(2):
                spread = jnp.broadcast_to(responses[g : g + 1], (strip, length))
                shifted = pltpu.roll(spread, 0, 1, stride=1, stride_axis=0)
                blocks.append(jnp.where(causal, shifted, 0.0).astype(BF16))
            rows = pl.ds(pl.multiple_of(group * width, 2 * width), 2 * width)
            signal = jnp.concatenate([signal_ref[at, rows, :] for at in range(length // strip)], axis=0)
            both = dot(signal, jnp.concatenate(blocks, axis=1))
            for g in range(2):
                total = None
                for at in range(length // strip):
                    first = at * 2 * width + g * width
                    term = both[first : first + width, g * length : (g + 1) * length]
                    if at:
                        term = jnp.where(lane >= at * strip, pltpu.roll(term, at * strip, 1), 0.0)
                    total = term if total is None else total + term
                sum_ref[pl.ds(pl.multiple_of((group + g) * width, width), width), :] = total

    def back(index):
        chans = tile_of(index)
        high, low = halves(sum_ref[chans, :])
        direct = skip_ref[:, chans] * gated_ref[:, chans].astype(F32)
        base_ref[:, chans] = turned(high, unit) + turned(low, unit) + direct

    unrolled(tiles, signals)
    unrolled(tiles, products)
    unrolled(tiles, back)


def finish_kernel(at_ref, ends_ref, step_ref, lift_ref, query_ref, first_ref, base_ref, mixed_ref, state_ref):
    length, share = mixed_ref.shape
    poles, channels = step_ref.shape
    in_tile = lift_ref.shape[1] // poles * TILE // channels
    me, half = at_ref[0], at_ref[1]
    here = tile_of(half, share)
    step = step_ref[:, here]

    def earlier(block, state):
        return jnp.where(block < me, step * state + ends_ref[block, :, here].astype(F32), state)

    state_ref[...] = lax.fori_loop(0, ends_ref.shape[0] - 1, earlier, jnp.zeros((poles, share), F32))
    owner = iota((poles, TILE), 1) // (TILE // in_tile)

    def tile(index):
        at = half * (share // TILE) + index
        chans = tile_of(at)
        entering = state_ref[:, tile_of(index)]
        apart = jnp.concatenate([jnp.where(owner == g, entering, 0.0) for g in range(in_tile)], axis=0)
        high, low = halves(apart)
        lift = lift_ref[:, tile_of(at, in_tile * poles)]
        carried = dot(lift, high) + dot(lift, low)
        query = jnp.concatenate([first_ref[:, chans], query_ref[:, chans].astype(F32)[ROWS:]], axis=0)
        mixed_ref[:, tile_of(index)] = (query * (base_ref[:, chans] + carried)).astype(BF16)

    unrolled(share // TILE, tile)


def corner_kernel(block_ref, corner_ref):
    corner_ref[...] = block_ref[: corner_ref.shape[0], : corner_ref.shape[1]]


def early_kernel(at_ref, own_ref, beside_ref, across_ref, corner_ref, *rest):
    *weight_hbms, total_ref, rows_ref, block_ref, layers_ref, weight_ref, sems = rest
    copies = [
        pltpu.make_async_copy(hbm, weight_ref.at[at], sems.at[at]) for at, hbm in enumerate(weight_hbms)
    ]
    for copy in copies:
        copy.start()
    layer = at_ref[0]
    last = layer ^ 2
    for bits, ref in ((0, own_ref), (1, beside_ref), (3, across_ref)):
        layers_ref[layer ^ bits] = ref[...]
    layers_ref[layer ^ 1, : corner_ref.shape[0], : corner_ref.shape[1]] = corner_ref[...]
    layers_ref[last] = jnp.zeros_like(own_ref)
    block_ref[...] = layers_ref[at_ref[1 + len(copies)]]
    for copy in copies:
        copy.wait()
    for column in range(0, total_ref.shape[1], COLUMNS):
        columns = slice(column, column + COLUMNS)
        total = None
        for at in range(len(copies)):
            term = dot(layers_ref[at_ref[1 + at]], weight_ref[at, :, columns])
            total = term if total is None else total + term
        total_ref[:, columns] = total
    rows_ref[...] = jnp.zeros_like(rows_ref)
    for at in range(len(copies)):

        @pl.when(at_ref[1 + at] == last)
        def _():
            rows_ref[...] = weight_ref[at]


def joined_kernel(at_ref, total_ref, rows_ref, block_ref, weight_ref, out_ref, last_ref):
    out_ref[...] = total_ref[...] + dot(block_ref[...], weight_ref[...])
    last_ref[...] = rows_ref[...]

    @pl.when(at_ref[4] == at_ref[0] ^ 2)
    def _():
        last_ref[...] = weight_ref[...]


def late_kernel(first, beyond_ref, total_ref, rows_ref, out_ref):
    tokens = pl.ds(first, out_ref.shape[0])
    out_ref[...] = (total_ref[tokens, :] + dot(beyond_ref[tokens, :], rows_ref[...])).astype(out_ref.dtype)


def swap(value, *bits):
    count = lax.axis_size("ctx")
    pairs = [(source, source ^ bits[source % len(bits)]) for source in range(count)]
    return lax.ppermute(value, "ctx", pairs)


def after(value, earlier):
    return lax.optimization_barrier((value, earlier))[0]


def trade(value, bits):
    count = lax.axis_size("tp")
    return lax.ppermute(value, "tp", [(source, source ^ bits) for source in range(count)])


def local(streams, conv_weight, rates, residues, skip, out_weight):
    channels, length = streams.shape[1:]
    groups, poles = rates.shape
    blocks, layers = lax.axis_size("ctx"), lax.axis_size("tp")
    rows, features = out_weight.shape
    share = channels // CORES
    square = blocks == 8 and rows == share

    inputs = (streams, conv_weight, rates.T, residues.T, skip[None, :])
    tails, streams, conv_weight, rates, residues, skip = call(
        tails_kernel,
        [((3, ROWS, channels), BF16)] + [(part.shape, part.dtype) for part in inputs],
        "tails",
        *(pltpu.with_memory_space_constraint(part, pltpu.HBM) for part in inputs),
        specs=[pl.BlockSpec(memory_space=pltpu.HBM)] * len(inputs),
        scratch=[pltpu.SemaphoreType.DMA((len(inputs),))],
    )
    before = from_behind(tails, "ctx", 1)
    if square:
        near = swap(out_weight, 2, 4)
    tiles = channels // TILE
    heads, query, gated, decay, step, response, lift = call(
        prepare_kernel,
        [
            ((3, ROWS, channels), F32),
            ((length, channels), BF16),
            ((length, channels), F32),
            ((2, groups * poles, length), BF16),
            ((poles, channels), F32),
            ((groups, length), F32),
            ((length, groups * poles), BF16),
        ],
        "prepare",
        streams, conv_weight, rates, residues,
        scratch=[pltpu.VMEM((3 * tiles, ROWS + length, TILE), F32)],
        flops=10**9,
    )
    ends, gated, first = call(
        states_kernel,
        [((blocks, poles, channels), BF16), ((length, channels), BF16), ((ROWS, channels), F32)],
        "states",
        before, heads, conv_weight, gated, decay,
        scratch=[pltpu.VMEM((3 * tiles, 2 * ROWS, TILE), F32)],
    )
    all_ends = lax.all_to_all(ends, "ctx", split_axis=0, concat_axis=0, tiled=True)
    (base,) = call(
        inside_kernel,
        [((length, channels), F32)],
        "inside",
        gated, skip, response,
        scratch=[
            pltpu.VMEM((length // STRIP, channels, STRIP), BF16),
            pltpu.VMEM((channels, length), F32),
        ],
        flops=10**9,
    )
    if square:
        other_near = swap(after(out_weight, (base, near)), 4, 2)
    me = lax.axis_index("ctx").astype(jnp.int32)
    core = me % CORES
    smem = [pl.BlockSpec(memory_space=pltpu.SMEM)]

    def finished(half):
        return call(
            finish_kernel,
            [((length, share), BF16)],
            "finish",
            jnp.stack([me, half]), all_ends, step, lift, query, first, base,
            specs=smem + whole(6),
            flops=3 * 10**9,
            scratch=[pltpu.VMEM((poles, share), F32)],
        )[0]

    if rows == share:
        other, mine = finished(1 - core), finished(core)
    else:
        mixed = jnp.concatenate([finished(jnp.full_like(me, half)) for half in range(CORES)], axis=1)
        by_core = mixed.reshape(length, share // rows, CORES, rows).transpose(2, 0, 1, 3)
        by_core = by_core.reshape(CORES, length, share)
        mine = lax.dynamic_index_in_dim(by_core, core, 0, keepdims=False)
        other = lax.dynamic_index_in_dim(by_core, 1 - core, 0, keepdims=False)
    block = jnp.concatenate([mine, swap(other, 1)], axis=0)
    layer = lax.axis_index("tp").astype(jnp.int32)
    beside, across = trade(block, 1), trade(block, 3)
    (corner,) = call(corner_kernel, [((2 * ROWS, TILE), BF16)], "corner", beside, flops=0)
    beyond = trade(after(across, (corner, other_near)) if square else across, 1)
    if square:
        diagonal = swap(after(near, block), 4, 2)
        weight = (out_weight, near, other_near, diagonal)
    else:
        core_groups = [list(range(core, blocks, CORES)) for core in range(CORES)]
        weight = lax.all_gather(out_weight, "ctx", axis=0, axis_index_groups=core_groups)
        weight = tuple(weight.reshape(layers, share, features))
    first_row = jnp.where(core == 0, 1, 2)
    chip = me // CORES
    place = [chip, chip ^ first_row, chip ^ (3 - first_row), chip ^ 3] if square else [jnp.full_like(me, at) for at in range(4)]
    at = jnp.stack([layer] + place)
    *sooner, latest = weight
    total, last_rows, last_block = call(
        early_kernel,
        [((CORES * length, features), F32), ((share, features), BF16), (block.shape, BF16)],
        "early",
        at, block, beside, across, corner,
        *(pltpu.with_memory_space_constraint(part, pltpu.HBM) for part in sooner),
        specs=smem + whole(4) + [pl.BlockSpec(memory_space=pltpu.HBM)] * len(sooner),
        scratch=[
            pltpu.VMEM((layers,) + block.shape, BF16),
            pltpu.VMEM((len(sooner), share, features), BF16),
            pltpu.SemaphoreType.DMA((len(sooner),)),
        ],
        flops=10**10,
    )
    total, last_rows = call(
        joined_kernel,
        [((CORES * length, features), F32), ((share, features), BF16)],
        "joined",
        at, total, last_rows, last_block, latest,
        specs=smem + whole(4),
        flops=0,
    )
    sides = []
    for side, kind in ((1, BF16), (0, F32)):
        sides += call(
            functools.partial(late_kernel, side * length),
            [((length, features), kind)],
            "late",
            beyond, total, last_rows,
            flops=0,
        )
    other, mine = sides
    other = swap(other, 1)
    return (mine + other.astype(F32)).astype(BF16)


def solution(mesh):
    return jax.shard_map(
        local,
        mesh=mesh,
        in_specs=(
            P(None, "tp", "ctx"),
            P(None, None, "tp"),
            P("tp", None),
            P("tp", None),
            P("tp"),
            P("ctx", "tp"),
        ),
        out_specs=P("ctx", "tp"),
        check_vma=False,
    )
```

```python
import functools
import math

import jax
import jax.numpy as jnp
from jax import lax
from jax.experimental import pallas as pl
from jax.experimental.pallas import tpu as pltpu
from jax.sharding import PartitionSpec as P

F32 = jnp.float32
BF16 = jnp.bfloat16
ROWS = 8
TILE = 128
CORES = 2
COLUMNS = 256
STRIP = 32
VMEM_LIMIT = 24 * 1024 * 1024
PLAIN = (((1,), (0,)), ((), ()))
CONTRACT_LANES = (((1,), (1,)), ((), ()))


def from_behind(value, axis, steps):
    count = lax.axis_size(axis)
    leading, last = (max(0, -steps), min(count, count - steps))
    return lax.ppermute(value, axis, [(source, source + steps) for source in range(leading, last)])


def dot(left, right, dims=PLAIN):
    return lax.dot_general(left, right, dims, preferred_element_type=F32)


def halves(value):
    high = value.astype(BF16)
    return high, (value - high.astype(F32)).astype(BF16)


def iota(shape, axis):
    return lax.broadcasted_iota(jnp.int32, shape, axis)


def identity(size):
    return (iota((size, size), 0) == iota((size, size), 1)).astype(BF16)


def turned(value, unit):
    return dot(unit, value, CONTRACT_LANES)


def whole(count):
    return [pl.BlockSpec(memory_space=pltpu.VMEM)] * count


def call(kernel, outs, name, *operands, specs=None, scratch=(), flops=10**8):
    return pl.pallas_call(
        kernel,
        out_shape=tuple(jax.ShapeDtypeStruct(*out) for out in outs),
        in_specs=whole(len(operands)) if specs is None else specs,
        out_specs=tuple(whole(len(outs))),
        scratch_shapes=scratch,
        compiler_params=pltpu.CompilerParams(vmem_limit_bytes=VMEM_LIMIT),
        cost_estimate=pl.CostEstimate(flops=flops, bytes_accessed=flops // 100, transcendentals=0),
        name=name,
    )(*operands)


def tile_of(index, size=TILE):
    return pl.ds(pl.multiple_of(index * size, size), size)


def unrolled(count, body):
    def step(index, carry):
        body(index)
        return carry

    lax.fori_loop(0, count, step, 0, unroll=math.gcd(count, 4))


def tails_kernel(*refs):
    count = len(refs) // 2 - 1
    sources, tails_ref, fetched, sems = refs[:count], refs[count], refs[count + 1 : -1], refs[-1]
    copies = [
        pltpu.make_async_copy(source, target, sems.at[at]) for at, (source, target) in enumerate(zip(sources, fetched))
    ]
    for copy in copies:
        copy.start()
    streams_ref = fetched[0]
    length = streams_ref.shape[2]
    pick = (iota((2 * ROWS, length), 1) == iota((2 * ROWS, length), 0) + (length - ROWS)).astype(BF16)
    copies[0].wait()
    for stream in range(streams_ref.shape[0]):
        rows = dot(pick, streams_ref[stream], CONTRACT_LANES)
        tails_ref[stream] = rows[:ROWS].astype(BF16)
    for copy in copies[1:]:
        copy.wait()


def short_conv(stream, chans, rows, padded, taps_ref):
    total = None
    for shift in range(taps_ref.shape[1]):
        term = taps_ref[stream, shift : shift + 1, chans] * padded[pl.ds(ROWS - shift, rows), :]
        total = term if total is None else total + term
    return total


def prepare_kernel(
    streams_ref, taps_ref, rates_ref, residues_ref,
    heads_ref, query_ref, gated_ref, decay_ref, step_ref, response_ref, lift_ref, padded_ref,
):
    channels, length = streams_ref.shape[1:]
    poles, groups = rates_ref.shape
    width = channels // groups
    in_tile = TILE // width
    unit = identity(length)
    lag = (length - 1) - iota((poles, length), 1).astype(F32)
    owner = iota((poles, TILE), 1) // width
    time = iota((poles, length), 1).astype(F32)
    member = (iota((in_tile, in_tile * poles), 1) // poles == iota((in_tile, in_tile * poles), 0)).astype(BF16)
    scale = residues_ref[...] * jnp.sqrt(2.0 * rates_ref[...]) / math.sqrt(poles)

    def turn(index):
        chans = tile_of(index)
        for stream in range(3):
            tokens = turned(streams_ref[stream, chans, :], unit)
            padded_ref[index * 3 + stream, :ROWS, :] = jnp.zeros((ROWS, TILE), F32)
            padded_ref[index * 3 + stream, ROWS:, :] = tokens
            heads_ref[stream, :, chans] = tokens[:ROWS]

    def factors(index):
        shift = groups - index * in_tile
        rates = pltpu.roll(rates_ref[...], shift, 1)
        coef = pltpu.roll(scale, shift, 1)
        once = jnp.exp(-rates)
        decay, impulse, lift = [], [], []
        wide = jnp.zeros((poles, TILE), F32)
        for g in range(in_tile):
            rate = jnp.broadcast_to(rates[:, g : g + 1], (poles, length))
            decay.append(jnp.exp(-rate * lag))
            impulse.append(jnp.broadcast_to(coef[:, g : g + 1], (poles, length)) * jnp.exp(-rate * time))
            lift.append(impulse[-1] * once[:, g : g + 1])
            wide = jnp.where(owner == g, rate[:, :TILE], wide)
        step_ref[:, tile_of(index)] = jnp.exp(-wide * length)
        states = tile_of(index, in_tile * poles)
        for part, value in enumerate(halves(jnp.concatenate(decay, axis=0))):
            decay_ref[part, states, :] = value
        high, low = halves(jnp.concatenate(impulse, axis=0))
        response_ref[pl.ds(pl.multiple_of(index * in_tile, in_tile), in_tile), :] = dot(member, high) + dot(member, low)
        lift_ref[:, states] = turned(jnp.concatenate(lift, axis=0).astype(BF16), unit).astype(BF16)

    def filters(index):
        chans = tile_of(index)
        query, left, right = (
            short_conv(stream, chans, length, padded_ref.at[index * 3 + stream], taps_ref) for stream in range(3)
        )
        query_ref[:, chans] = query.astype(BF16)
        gated_ref[:, chans] = left * right

    unrolled(channels // TILE, turn)
    unrolled(channels // TILE, factors)
    unrolled(channels // TILE, filters)


def states_kernel(before_ref, heads_ref, taps_ref, gated_ref, decay_ref, ends_ref, final_ref, first_ref, padded_ref):
    length, channels = gated_ref.shape
    poles = ends_ref.shape[1]
    in_tile = decay_ref.shape[1] // poles * TILE // channels
    owner = iota((poles, TILE), 1) // (TILE // in_tile)

    def begin(index):
        chans = tile_of(index)
        for stream in range(3):
            padded_ref[index * 3 + stream, :ROWS, :] = before_ref[stream, :, chans].astype(F32)
            padded_ref[index * 3 + stream, ROWS:, :] = heads_ref[stream, :, chans]
        query, left, right = (
            short_conv(stream, chans, ROWS, padded_ref.at[index * 3 + stream], taps_ref) for stream in range(3)
        )
        first_ref[:, chans] = query
        final_ref[:, chans] = jnp.concatenate([left * right, gated_ref[ROWS:, chans]], axis=0).astype(BF16)

    def leave(index):
        chans = tile_of(index)
        gated = final_ref[:, chans]
        states = tile_of(index, in_tile * poles)
        every = dot(decay_ref[0, states, :], gated) + dot(decay_ref[1, states, :], gated)
        ends = jnp.zeros((poles, TILE), F32)
        for g in range(in_tile):
            ends = jnp.where(owner == g, every[g * poles : (g + 1) * poles], ends)
        ends = ends.astype(BF16)
        for block in range(ends_ref.shape[0]):
            ends_ref[block, :, chans] = ends

    unrolled(channels // TILE, begin)
    unrolled(channels // TILE, leave)


def inside_kernel(gated_ref, skip_ref, response_ref, base_ref, signal_ref, sum_ref):
    length, channels = gated_ref.shape
    groups = response_ref.shape[0]
    width = channels // groups
    in_tile = TILE // width
    tiles = channels // TILE
    strip = STRIP
    unit = identity(length)
    lane = iota((width, length), 1)
    causal = iota((strip, length), 1) >= iota((strip, length), 0)

    def signals(index):
        gated = gated_ref[:, tile_of(index)]
        for at in range(length // strip):
            piece = turned(gated[at * strip : (at + 1) * strip], unit).astype(BF16)
            signal_ref[at, tile_of(index), :] = piece

    def products(index):
        for pair in range(in_tile // 2):
            group = index * in_tile + 2 * pair
            responses = response_ref[pl.ds(group, 2), :]
            blocks = []
            for g in range(2):
                spread = jnp.broadcast_to(responses[g : g + 1], (strip, length))
                shifted = pltpu.roll(spread, 0, 1, stride=1, stride_axis=0)
                blocks.append(jnp.where(causal, shifted, 0.0).astype(BF16))
            rows = pl.ds(pl.multiple_of(group * width, 2 * width), 2 * width)
            signal = jnp.concatenate([signal_ref[at, rows, :] for at in range(length // strip)], axis=0)
            both = dot(signal, jnp.concatenate(blocks, axis=1))
            for g in range(2):
                total = None
                for at in range(length // strip):
                    first = at * 2 * width + g * width
                    term = both[first : first + width, g * length : (g + 1) * length]
                    if at:
                        term = jnp.where(lane >= at * strip, pltpu.roll(term, at * strip, 1), 0.0)
                    total = term if total is None else total + term
                sum_ref[pl.ds(pl.multiple_of((group + g) * width, width), width), :] = total

    def back(index):
        chans = tile_of(index)
        high, low = halves(sum_ref[chans, :])
        direct = skip_ref[:, chans] * gated_ref[:, chans].astype(F32)
        base_ref[:, chans] = turned(high, unit) + turned(low, unit) + direct

    unrolled(tiles, signals)
    unrolled(tiles, products)
    unrolled(tiles, back)


def finish_kernel(at_ref, ends_ref, step_ref, lift_ref, query_ref, first_ref, base_ref, mixed_ref, state_ref):
    length, share = mixed_ref.shape
    poles, channels = step_ref.shape
    in_tile = lift_ref.shape[1] // poles * TILE // channels
    me, half = at_ref[0], at_ref[1]
    here = tile_of(half, share)
    step = step_ref[:, here]

    def earlier(block, state):
        return jnp.where(block < me, step * state + ends_ref[block, :, here].astype(F32), state)

    state_ref[...] = lax.fori_loop(0, ends_ref.shape[0] - 1, earlier, jnp.zeros((poles, share), F32))
    owner = iota((poles, TILE), 1) // (TILE // in_tile)

    def tile(index):
        at = half * (share // TILE) + index
        chans = tile_of(at)
        entering = state_ref[:, tile_of(index)]
        apart = jnp.concatenate([jnp.where(owner == g, entering, 0.0) for g in range(in_tile)], axis=0)
        high, low = halves(apart)
        lift = lift_ref[:, tile_of(at, in_tile * poles)]
        carried = dot(lift, high) + dot(lift, low)
        query = jnp.concatenate([first_ref[:, chans], query_ref[:, chans].astype(F32)[ROWS:]], axis=0)
        mixed_ref[:, tile_of(index)] = (query * (base_ref[:, chans] + carried)).astype(BF16)

    unrolled(share // TILE, tile)


def early_kernel(at_ref, own_ref, beside_ref, middle_ref, ends_ref, *rest):
    *weight_hbms, total_ref, rows_ref, block_ref, layers_ref, weight_ref, sems = rest
    count = len(weight_hbms)
    layer = at_ref[0]
    last = layer ^ 2
    copies = [pltpu.make_async_copy(hbm, weight_ref.at[at], sems.at[at]) for at, hbm in enumerate(weight_hbms)]
    fetches = [pltpu.make_async_copy(hbm, rows_ref, sems.at[count]) for hbm in weight_hbms]
    for copy in copies:
        copy.start()
    for at, fetch in enumerate(fetches):
        pl.when(at_ref[1 + at] == last)(fetch.start)
    layers_ref[layer] = own_ref[...]
    layers_ref[layer ^ 1] = beside_ref[...]
    layers_ref[layer ^ 3] = jnp.where((layer == 0) | (layer == 3), ends_ref[...], middle_ref[...])
    layers_ref[last] = jnp.zeros_like(own_ref)
    block_ref[...] = layers_ref[at_ref[1 + count]]
    for at, copy in enumerate(copies):
        copy.wait()
        block = layers_ref[at_ref[1 + at]]
        for column in range(0, total_ref.shape[1], COLUMNS):
            columns = slice(column, column + COLUMNS)
            term = dot(block, weight_ref[at, :, columns])
            total_ref[:, columns] = total_ref[:, columns] + term if at else term
    for at, fetch in enumerate(fetches):
        pl.when(at_ref[1 + at] == last)(fetch.wait)


def joined_kernel(total_ref, block_ref, weight_ref, out_ref):
    out_ref[...] = total_ref[...] + dot(block_ref[...], weight_ref[...])


def late_kernel(first, at_ref, inwards_ref, outwards_ref, total_ref, rows_ref, weight_ref, out_ref):
    tokens = pl.ds(first, out_ref.shape[0])
    edge = (at_ref[0] == 0) | (at_ref[0] == 3)
    beyond = jnp.where(edge, outwards_ref[tokens, :], inwards_ref[tokens, :])

    def add(rows):
        out_ref[...] = (total_ref[tokens, :] + dot(beyond, rows[...])).astype(out_ref.dtype)

    latest = at_ref[4] == at_ref[0] ^ 2
    pl.when(latest)(lambda: add(weight_ref))
    pl.when(jnp.logical_not(latest))(lambda: add(rows_ref))


def swap(value, *bits):
    count = lax.axis_size("ctx")
    pairs = [(source, source ^ bits[source % len(bits)]) for source in range(count)]
    return lax.ppermute(value, "ctx", pairs)


def after(value, earlier):
    return lax.optimization_barrier((value, earlier))[0]


def along(value, *pairs):
    return lax.ppermute(value, "tp", pairs)


def local(streams, conv_weight, rates, residues, skip, out_weight):
    channels, length = streams.shape[1:]
    groups, poles = rates.shape
    blocks, layers = lax.axis_size("ctx"), lax.axis_size("tp")
    rows, features = out_weight.shape
    share = channels // CORES
    square = blocks == 8 and rows == share

    inputs = (streams, conv_weight, rates.T, residues.T, skip[None, :])
    tails, streams, conv_weight, rates, residues, skip = call(
        tails_kernel,
        [((3, ROWS, channels), BF16)] + [(part.shape, part.dtype) for part in inputs],
        "tails",
        *(pltpu.with_memory_space_constraint(part, pltpu.HBM) for part in inputs),
        specs=[pl.BlockSpec(memory_space=pltpu.HBM)] * len(inputs),
        scratch=[pltpu.SemaphoreType.DMA((len(inputs),))],
    )
    before = from_behind(tails, "ctx", 1)
    if square:
        near = swap(out_weight, 2, 4)
    tiles = channels // TILE
    heads, query, gated, decay, step, response, lift = call(
        prepare_kernel,
        [
            ((3, ROWS, channels), F32),
            ((length, channels), BF16),
            ((length, channels), F32),
            ((2, groups * poles, length), BF16),
            ((poles, channels), F32),
            ((groups, length), F32),
            ((length, groups * poles), BF16),
        ],
        "prepare",
        streams, conv_weight, rates, residues,
        scratch=[pltpu.VMEM((3 * tiles, ROWS + length, TILE), F32)],
        flops=10**9,
    )
    ends, gated, first = call(
        states_kernel,
        [((blocks, poles, channels), BF16), ((length, channels), BF16), ((ROWS, channels), F32)],
        "states",
        before, heads, conv_weight, gated, decay,
        scratch=[pltpu.VMEM((3 * tiles, 2 * ROWS, TILE), F32)],
    )
    all_ends = lax.all_to_all(ends, "ctx", split_axis=0, concat_axis=0, tiled=True)
    (base,) = call(
        inside_kernel,
        [((length, channels), F32)],
        "inside",
        gated, skip, response,
        scratch=[
            pltpu.VMEM((length // STRIP, channels, STRIP), BF16),
            pltpu.VMEM((channels, length), F32),
        ],
        flops=10**9,
    )
    if square:
        other_near = swap(after(out_weight, (gated, near)), 4, 2)
    me = lax.axis_index("ctx").astype(jnp.int32)
    core = me % CORES
    smem = [pl.BlockSpec(memory_space=pltpu.SMEM)]

    def finished(half):
        return call(
            finish_kernel,
            [((length, share), BF16)],
            "finish",
            jnp.stack([me, half]), all_ends, step, lift, query, first, base,
            specs=smem + whole(6),
            flops=3 * 10**9,
            scratch=[pltpu.VMEM((poles, share), F32)],
        )[0]

    if rows == share:
        other, mine = finished(1 - core), finished(core)
    else:
        mixed = jnp.concatenate([finished(jnp.full_like(me, half)) for half in range(CORES)], axis=1)
        by_core = mixed.reshape(length, share // rows, CORES, rows).transpose(2, 0, 1, 3)
        by_core = by_core.reshape(CORES, length, share)
        mine = lax.dynamic_index_in_dim(by_core, core, 0, keepdims=False)
        other = lax.dynamic_index_in_dim(by_core, 1 - core, 0, keepdims=False)
    block = jnp.concatenate([mine, swap(other, 1)], axis=0)
    layer = lax.axis_index("tp").astype(jnp.int32)
    beside = along(block, (0, 1), (1, 0), (2, 3), (3, 2))
    middle = along(block, (1, 2), (2, 1))
    ends = along(block, (0, 3), (3, 0))
    inwards = along(beside, (1, 2), (2, 1))
    outwards = along(after(middle, other_near) if square else middle, (1, 0), (2, 3))
    if square:
        diagonal = swap(after(near, block), 4, 2)
        weight = (out_weight, near, other_near, diagonal)
    else:
        core_groups = [list(range(core, blocks, CORES)) for core in range(CORES)]
        weight = lax.all_gather(out_weight, "ctx", axis=0, axis_index_groups=core_groups)
        weight = tuple(weight.reshape(layers, share, features))
    first_row = jnp.where(core == 0, 1, 2)
    chip = me // CORES
    place = [chip, chip ^ first_row, chip ^ (3 - first_row), chip ^ 3] if square else [jnp.full_like(me, at) for at in range(4)]
    at = jnp.stack([layer] + place)
    *sooner, latest = weight
    total, last_rows, last_block = call(
        early_kernel,
        [((CORES * length, features), F32), ((share, features), BF16), (block.shape, BF16)],
        "early",
        at, block, beside, middle, ends,
        *(pltpu.with_memory_space_constraint(part, pltpu.HBM) for part in sooner),
        specs=smem + whole(4) + [pl.BlockSpec(memory_space=pltpu.HBM)] * len(sooner),
        scratch=[
            pltpu.VMEM((layers,) + block.shape, BF16),
            pltpu.VMEM((len(sooner), share, features), BF16),
            pltpu.SemaphoreType.DMA((len(sooner) + 1,)),
        ],
        flops=10**10,
    )
    (total,) = call(
        joined_kernel, [((CORES * length, features), F32)], "joined", total, last_block, latest, flops=0
    )
    sides = []
    for side, kind in ((1, BF16), (0, F32)):
        sides += call(
            functools.partial(late_kernel, side * length),
            [((length, features), kind)],
            "late",
            at, inwards, outwards, total, last_rows, latest,
            specs=smem + whole(5),
            flops=0,
        )
    other, mine = sides
    other = swap(other, 1)
    return (mine + other.astype(F32)).astype(BF16)


def solution(mesh):
    return jax.shard_map(
        local,
        mesh=mesh,
        in_specs=(
            P(None, "tp", "ctx"),
            P(None, None, "tp"),
            P("tp", None),
            P("tp", None),
            P("tp"),
            P("ctx", "tp"),
        ),
        out_specs=P("ctx", "tp"),
        check_vma=False,
    )
```

```python
import functools
import math

import jax
import jax.numpy as jnp
from jax import lax
from jax.experimental import pallas as pl
from jax.experimental.pallas import tpu as pltpu
from jax.sharding import PartitionSpec as P

F32 = jnp.float32
BF16 = jnp.bfloat16
ROWS = 8
TILE = 128
CORES = 2
COLUMNS = 256
STRIP = 32
VMEM_LIMIT = 24 * 1024 * 1024
PLAIN = (((1,), (0,)), ((), ()))
CONTRACT_LANES = (((1,), (1,)), ((), ()))


def from_behind(value, axis, steps):
    count = lax.axis_size(axis)
    leading, last = (max(0, -steps), min(count, count - steps))
    return lax.ppermute(value, axis, [(source, source + steps) for source in range(leading, last)])


def dot(left, right, dims=PLAIN):
    return lax.dot_general(left, right, dims, preferred_element_type=F32)


def halves(value):
    high = value.astype(BF16)
    return high, (value - high.astype(F32)).astype(BF16)


def iota(shape, axis):
    return lax.broadcasted_iota(jnp.int32, shape, axis)


def identity(size):
    return (iota((size, size), 0) == iota((size, size), 1)).astype(BF16)


def turned(value, unit):
    return dot(unit, value, CONTRACT_LANES)


def whole(count):
    return [pl.BlockSpec(memory_space=pltpu.VMEM)] * count


def call(kernel, outs, name, *operands, specs=None, scratch=(), flops=10**8):
    return pl.pallas_call(
        kernel,
        out_shape=tuple(jax.ShapeDtypeStruct(*out) for out in outs),
        in_specs=whole(len(operands)) if specs is None else specs,
        out_specs=tuple(whole(len(outs))),
        scratch_shapes=scratch,
        compiler_params=pltpu.CompilerParams(vmem_limit_bytes=VMEM_LIMIT),
        cost_estimate=pl.CostEstimate(flops=flops, bytes_accessed=flops // 100, transcendentals=0),
        name=name,
    )(*operands)


def tile_of(index, size=TILE):
    return pl.ds(pl.multiple_of(index * size, size), size)


def unrolled(count, body):
    def step(index, carry):
        body(index)
        return carry

    lax.fori_loop(0, count, step, 0, unroll=math.gcd(count, 4))


def tails_kernel(*refs):
    count = len(refs) // 2 - 1
    sources, tails_ref, fetched, sems = refs[:count], refs[count], refs[count + 1 : -1], refs[-1]
    copies = [
        pltpu.make_async_copy(source, target, sems.at[at]) for at, (source, target) in enumerate(zip(sources, fetched))
    ]
    for copy in copies:
        copy.start()
    streams_ref = fetched[0]
    length = streams_ref.shape[2]
    pick = (iota((2 * ROWS, length), 1) == iota((2 * ROWS, length), 0) + (length - ROWS)).astype(BF16)
    copies[0].wait()
    for stream in range(streams_ref.shape[0]):
        rows = dot(pick, streams_ref[stream], CONTRACT_LANES)
        tails_ref[stream] = rows[:ROWS].astype(BF16)
    for copy in copies[1:]:
        copy.wait()


def short_conv(stream, chans, rows, padded, taps_ref):
    total = None
    for shift in range(taps_ref.shape[1]):
        term = taps_ref[stream, shift : shift + 1, chans] * padded[pl.ds(ROWS - shift, rows), :]
        total = term if total is None else total + term
    return total


def prepare_kernel(
    streams_ref, taps_ref, rates_ref, residues_ref,
    heads_ref, query_ref, gated_ref, decay_ref, step_ref, response_ref, lift_ref, padded_ref,
):
    channels, length = streams_ref.shape[1:]
    poles, groups = rates_ref.shape
    width = channels // groups
    in_tile = TILE // width
    unit = identity(length)
    lag = (length - 1) - iota((poles, length), 1).astype(F32)
    owner = iota((poles, TILE), 1) // width
    time = iota((poles, length), 1).astype(F32)
    member = (iota((in_tile, in_tile * poles), 1) // poles == iota((in_tile, in_tile * poles), 0)).astype(BF16)
    scale = residues_ref[...] * jnp.sqrt(2.0 * rates_ref[...]) / math.sqrt(poles)

    def turn(index):
        chans = tile_of(index)
        for stream in range(3):
            tokens = turned(streams_ref[stream, chans, :], unit)
            padded_ref[index * 3 + stream, :ROWS, :] = jnp.zeros((ROWS, TILE), F32)
            padded_ref[index * 3 + stream, ROWS:, :] = tokens
            heads_ref[stream, :, chans] = tokens[:ROWS]

    def factors(index):
        shift = groups - index * in_tile
        rates = pltpu.roll(rates_ref[...], shift, 1)
        coef = pltpu.roll(scale, shift, 1)
        decay, impulse, lift = [], [], []
        wide = jnp.zeros((poles, TILE), F32)
        for g in range(in_tile):
            rate = jnp.broadcast_to(rates[:, g : g + 1], (poles, length))
            decay.append(jnp.exp(-rate * lag))
            amplitude = jnp.broadcast_to(coef[:, g : g + 1], (poles, length))
            impulse.append(amplitude * jnp.exp(-rate * time))
            lift.append(amplitude * jnp.exp(-rate * (time + 1.0)))
            wide = jnp.where(owner == g, rate[:, :TILE], wide)
        step_ref[:, tile_of(index)] = jnp.exp(-wide * length)
        states = tile_of(index, in_tile * poles)
        decay_ref[states, :] = jnp.concatenate(decay, axis=0).astype(BF16)
        high, low = halves(jnp.concatenate(impulse, axis=0))
        response_ref[pl.ds(pl.multiple_of(index * in_tile, in_tile), in_tile), :] = dot(member, high) + dot(member, low)
        lift_ref[:, states] = turned(jnp.concatenate(lift, axis=0).astype(BF16), unit).astype(BF16)

    def filters(index):
        chans = tile_of(index)
        query, left, right = (
            short_conv(stream, chans, length, padded_ref.at[index * 3 + stream], taps_ref) for stream in range(3)
        )
        query_ref[:, chans] = query.astype(BF16)
        gated_ref[:, chans] = left * right

    unrolled(channels // TILE, turn)
    unrolled(channels // TILE, factors)
    unrolled(channels // TILE, filters)


def states_kernel(before_ref, heads_ref, taps_ref, gated_ref, decay_ref, ends_ref, final_ref, first_ref, padded_ref):
    length, channels = gated_ref.shape
    poles = ends_ref.shape[1]
    in_tile = decay_ref.shape[0] // poles * TILE // channels
    owner = iota((poles, TILE), 1) // (TILE // in_tile)

    def begin(index):
        chans = tile_of(index)
        for stream in range(3):
            padded_ref[index * 3 + stream, :ROWS, :] = before_ref[stream, :, chans].astype(F32)
            padded_ref[index * 3 + stream, ROWS:, :] = heads_ref[stream, :, chans]
        query, left, right = (
            short_conv(stream, chans, ROWS, padded_ref.at[index * 3 + stream], taps_ref) for stream in range(3)
        )
        first_ref[:, chans] = query
        final_ref[:, chans] = jnp.concatenate([left * right, gated_ref[ROWS:, chans]], axis=0).astype(BF16)

    def leave(index):
        chans = tile_of(index)
        gated = final_ref[:, chans]
        states = tile_of(index, in_tile * poles)
        every = dot(decay_ref[states, :], gated)
        ends = jnp.zeros((poles, TILE), F32)
        for g in range(in_tile):
            ends = jnp.where(owner == g, every[g * poles : (g + 1) * poles], ends)
        ends = ends.astype(BF16)
        for block in range(ends_ref.shape[0]):
            ends_ref[block, :, chans] = ends

    unrolled(channels // TILE, begin)
    unrolled(channels // TILE, leave)


def inside_kernel(gated_ref, skip_ref, response_ref, base_ref, signal_ref, sum_ref):
    length, channels = gated_ref.shape
    groups = response_ref.shape[0]
    width = channels // groups
    in_tile = TILE // width
    tiles = channels // TILE
    strip = STRIP
    unit = identity(length)
    lane = iota((width, length), 1)
    causal = iota((strip, length), 1) >= iota((strip, length), 0)

    def signals(index):
        gated = gated_ref[:, tile_of(index)]
        for at in range(length // strip):
            piece = turned(gated[at * strip : (at + 1) * strip], unit).astype(BF16)
            signal_ref[at, tile_of(index), :] = piece

    def products(index):
        for pair in range(in_tile // 2):
            group = index * in_tile + 2 * pair
            responses = response_ref[pl.ds(group, 2), :]
            blocks = []
            for g in range(2):
                spread = jnp.broadcast_to(responses[g : g + 1], (strip, length))
                shifted = pltpu.roll(spread, 0, 1, stride=1, stride_axis=0)
                blocks.append(jnp.where(causal, shifted, 0.0).astype(BF16))
            rows = pl.ds(pl.multiple_of(group * width, 2 * width), 2 * width)
            signal = jnp.concatenate([signal_ref[at, rows, :] for at in range(length // strip)], axis=0)
            both = dot(signal, jnp.concatenate(blocks, axis=1))
            for g in range(2):
                total = None
                for at in range(length // strip):
                    first = at * 2 * width + g * width
                    term = both[first : first + width, g * length : (g + 1) * length]
                    if at:
                        term = jnp.where(lane >= at * strip, pltpu.roll(term, at * strip, 1), 0.0)
                    total = term if total is None else total + term
                sum_ref[pl.ds(pl.multiple_of((group + g) * width, width), width), :] = total

    def back(index):
        chans = tile_of(index)
        high, low = halves(sum_ref[chans, :])
        direct = skip_ref[:, chans] * gated_ref[:, chans].astype(F32)
        base_ref[:, chans] = turned(high, unit) + turned(low, unit) + direct

    unrolled(tiles, signals)
    unrolled(tiles, products)
    unrolled(tiles, back)


def finish_kernel(at_ref, ends_ref, step_ref, lift_ref, query_ref, first_ref, base_ref, mixed_ref, state_ref):
    length, share = mixed_ref.shape
    poles, channels = step_ref.shape
    in_tile = lift_ref.shape[1] // poles * TILE // channels
    me, half = at_ref[0], at_ref[1]
    here = tile_of(half, share)
    step = step_ref[:, here]

    def earlier(block, state):
        return jnp.where(block < me, step * state + ends_ref[block, :, here].astype(F32), state)

    state_ref[...] = lax.fori_loop(0, ends_ref.shape[0] - 1, earlier, jnp.zeros((poles, share), F32))
    owner = iota((poles, TILE), 1) // (TILE // in_tile)

    def tile(index):
        at = half * (share // TILE) + index
        chans = tile_of(at)
        entering = state_ref[:, tile_of(index)]
        apart = jnp.concatenate([jnp.where(owner == g, entering, 0.0) for g in range(in_tile)], axis=0)
        carried = dot(lift_ref[:, tile_of(at, in_tile * poles)], apart.astype(BF16))
        query = jnp.concatenate([first_ref[:, chans], query_ref[:, chans].astype(F32)[ROWS:]], axis=0)
        mixed_ref[:, tile_of(index)] = (query * (base_ref[:, chans] + carried)).astype(BF16)

    unrolled(share // TILE, tile)


def early_kernel(at_ref, own_ref, beside_ref, across_ref, *rest):
    *weight_hbms, total_ref, rows_ref, block_ref, layers_ref, weight_ref, sems = rest
    count = len(weight_hbms)
    layer = at_ref[0]
    last = layer ^ 2
    copies = [pltpu.make_async_copy(hbm, weight_ref.at[at], sems.at[at]) for at, hbm in enumerate(weight_hbms)]
    fetches = [pltpu.make_async_copy(hbm, rows_ref, sems.at[count]) for hbm in weight_hbms]
    for copy in copies:
        copy.start()
    for at, fetch in enumerate(fetches):
        pl.when(at_ref[1 + at] == last)(fetch.start)
    for bits, ref in ((0, own_ref), (1, beside_ref), (3, across_ref)):
        layers_ref[layer ^ bits] = ref[...]
    layers_ref[last] = jnp.zeros_like(own_ref)
    block_ref[...] = layers_ref[at_ref[1 + count]]
    for at, copy in enumerate(copies):
        copy.wait()
        block = layers_ref[at_ref[1 + at]]
        for column in range(0, total_ref.shape[1], COLUMNS):
            columns = slice(column, column + COLUMNS)
            term = dot(block, weight_ref[at, :, columns])
            total_ref[:, columns] = total_ref[:, columns] + term if at else term
    for at, fetch in enumerate(fetches):
        pl.when(at_ref[1 + at] == last)(fetch.wait)


def joined_kernel(at_ref, total_ref, rows_ref, block_ref, weight_ref, out_ref, last_ref):
    out_ref[...] = total_ref[...] + dot(block_ref[...], weight_ref[...])

    def keep(rows):
        last_ref[...] = rows[...]

    latest = at_ref[4] == at_ref[0] ^ 2
    pl.when(latest)(lambda: keep(weight_ref))
    pl.when(jnp.logical_not(latest))(lambda: keep(rows_ref))


def late_kernel(first, beyond_ref, total_ref, rows_ref, out_ref):
    tokens = pl.ds(first, out_ref.shape[0])
    out_ref[...] = (total_ref[tokens, :] + dot(beyond_ref[tokens, :], rows_ref[...])).astype(out_ref.dtype)


def swap(value, *bits):
    count = lax.axis_size("ctx")
    pairs = [(source, source ^ bits[source % len(bits)]) for source in range(count)]
    return lax.ppermute(value, "ctx", pairs)


def after(value, earlier):
    return lax.optimization_barrier((value, earlier))[0]


def trade(value, bits):
    count = lax.axis_size("tp")
    return lax.ppermute(value, "tp", [(source, source ^ bits) for source in range(count)])


def local(streams, conv_weight, rates, residues, skip, out_weight):
    channels, length = streams.shape[1:]
    groups, poles = rates.shape
    blocks, layers = lax.axis_size("ctx"), lax.axis_size("tp")
    rows, features = out_weight.shape
    share = channels // CORES
    square = blocks == 8 and rows == share

    inputs = (streams, conv_weight, rates.T, residues.T, skip[None, :])
    tails, streams, conv_weight, rates, residues, skip = call(
        tails_kernel,
        [((3, ROWS, channels), BF16)] + [(part.shape, part.dtype) for part in inputs],
        "tails",
        *(pltpu.with_memory_space_constraint(part, pltpu.HBM) for part in inputs),
        specs=[pl.BlockSpec(memory_space=pltpu.HBM)] * len(inputs),
        scratch=[pltpu.SemaphoreType.DMA((len(inputs),))],
    )
    before = from_behind(tails, "ctx", 1)
    if square:
        near = swap(out_weight, 2, 4)
    tiles = channels // TILE
    heads, query, gated, decay, step, response, lift = call(
        prepare_kernel,
        [
            ((3, ROWS, channels), F32),
            ((length, channels), BF16),
            ((length, channels), F32),
            ((groups * poles, length), BF16),
            ((poles, channels), F32),
            ((groups, length), F32),
            ((length, groups * poles), BF16),
        ],
        "prepare",
        streams, conv_weight, rates, residues,
        scratch=[pltpu.VMEM((3 * tiles, ROWS + length, TILE), F32)],
        flops=10**9,
    )
    ends, gated, first = call(
        states_kernel,
        [((blocks, poles, channels), BF16), ((length, channels), BF16), ((ROWS, channels), F32)],
        "states",
        before, heads, conv_weight, gated, decay,
        scratch=[pltpu.VMEM((3 * tiles, 2 * ROWS, TILE), F32)],
    )
    all_ends = lax.all_to_all(ends, "ctx", split_axis=0, concat_axis=0, tiled=True)
    (base,) = call(
        inside_kernel,
        [((length, channels), F32)],
        "inside",
        gated, skip, response,
        scratch=[
            pltpu.VMEM((length // STRIP, channels, STRIP), BF16),
            pltpu.VMEM((channels, length), F32),
        ],
        flops=10**9,
    )
    if square:
        other_near = swap(after(out_weight, (base, near)), 4, 2)
    me = lax.axis_index("ctx").astype(jnp.int32)
    core = me % CORES
    smem = [pl.BlockSpec(memory_space=pltpu.SMEM)]

    def finished(half):
        return call(
            finish_kernel,
            [((length, share), BF16)],
            "finish",
            jnp.stack([me, half]), all_ends, step, lift, query, first, base,
            specs=smem + whole(6),
            flops=3 * 10**9,
            scratch=[pltpu.VMEM((poles, share), F32)],
        )[0]

    if rows == share:
        other, mine = finished(1 - core), finished(core)
    else:
        mixed = jnp.concatenate([finished(jnp.full_like(me, half)) for half in range(CORES)], axis=1)
        by_core = mixed.reshape(length, share // rows, CORES, rows).transpose(2, 0, 1, 3)
        by_core = by_core.reshape(CORES, length, share)
        mine = lax.dynamic_index_in_dim(by_core, core, 0, keepdims=False)
        other = lax.dynamic_index_in_dim(by_core, 1 - core, 0, keepdims=False)
    block = jnp.concatenate([mine, swap(other, 1)], axis=0)
    layer = lax.axis_index("tp").astype(jnp.int32)
    beside, across = trade(block, 1), trade(block, 3)
    beyond = trade(after(across, other_near) if square else across, 1)
    if square:
        diagonal = swap(after(near, block), 4, 2)
        weight = (out_weight, near, other_near, diagonal)
    else:
        core_groups = [list(range(core, blocks, CORES)) for core in range(CORES)]
        weight = lax.all_gather(out_weight, "ctx", axis=0, axis_index_groups=core_groups)
        weight = tuple(weight.reshape(layers, share, features))
    first_row = jnp.where(core == 0, 1, 2)
    chip = me // CORES
    place = [chip, chip ^ first_row, chip ^ (3 - first_row), chip ^ 3] if square else [jnp.full_like(me, at) for at in range(4)]
    at = jnp.stack([layer] + place)
    *sooner, latest = weight
    total, last_rows, last_block = call(
        early_kernel,
        [((CORES * length, features), F32), ((share, features), BF16), (block.shape, BF16)],
        "early",
        at, block, beside, across,
        *(pltpu.with_memory_space_constraint(part, pltpu.HBM) for part in sooner),
        specs=smem + whole(3) + [pl.BlockSpec(memory_space=pltpu.HBM)] * len(sooner),
        scratch=[
            pltpu.VMEM((layers,) + block.shape, BF16),
            pltpu.VMEM((len(sooner), share, features), BF16),
            pltpu.SemaphoreType.DMA((len(sooner) + 1,)),
        ],
        flops=10**10,
    )
    total, last_rows = call(
        joined_kernel,
        [((CORES * length, features), F32), ((share, features), BF16)],
        "joined",
        at, total, last_rows, last_block, latest,
        specs=smem + whole(4),
        flops=0,
    )
    sides = []
    for side, kind in ((1, BF16), (0, F32)):
        sides += call(
            functools.partial(late_kernel, side * length),
            [((length, features), kind)],
            "late",
            beyond, total, last_rows,
            flops=0,
        )
    other, mine = sides
    other = swap(other, 1)
    return (mine + other.astype(F32)).astype(BF16)


def solution(mesh):
    return jax.shard_map(
        local,
        mesh=mesh,
        in_specs=(
            P(None, "tp", "ctx"),
            P(None, None, "tp"),
            P("tp", None),
            P("tp", None),
            P("tp"),
            P("ctx", "tp"),
        ),
        out_specs=P("ctx", "tp"),
        check_vma=False,
    )
```

```python
import functools
import math

import jax
import jax.numpy as jnp
from jax import lax
from jax.experimental import pallas as pl
from jax.experimental.pallas import tpu as pltpu
from jax.sharding import PartitionSpec as P

F32 = jnp.float32
BF16 = jnp.bfloat16
ROWS = 8
TILE = 128
CORES = 2
COLUMNS = 256
STRIP = 32
VMEM_LIMIT = 24 * 1024 * 1024
PLAIN = (((1,), (0,)), ((), ()))
CONTRACT_LANES = (((1,), (1,)), ((), ()))


def from_behind(value, axis, steps):
    count = lax.axis_size(axis)
    leading, last = (max(0, -steps), min(count, count - steps))
    return lax.ppermute(value, axis, [(source, source + steps) for source in range(leading, last)])


def dot(left, right, dims=PLAIN):
    return lax.dot_general(left, right, dims, preferred_element_type=F32)


def halves(value):
    high = value.astype(BF16)
    return high, (value - high.astype(F32)).astype(BF16)


def iota(shape, axis):
    return lax.broadcasted_iota(jnp.int32, shape, axis)


def identity(size):
    return (iota((size, size), 0) == iota((size, size), 1)).astype(BF16)


def turned(value, unit):
    return dot(unit, value, CONTRACT_LANES)


def whole(count):
    return [pl.BlockSpec(memory_space=pltpu.VMEM)] * count


def call(kernel, outs, name, *operands, specs=None, scratch=(), flops=10**8):
    return pl.pallas_call(
        kernel,
        out_shape=tuple(jax.ShapeDtypeStruct(*out) for out in outs),
        in_specs=whole(len(operands)) if specs is None else specs,
        out_specs=tuple(whole(len(outs))),
        scratch_shapes=scratch,
        compiler_params=pltpu.CompilerParams(vmem_limit_bytes=VMEM_LIMIT),
        cost_estimate=pl.CostEstimate(flops=flops, bytes_accessed=flops // 100, transcendentals=0),
        name=name,
    )(*operands)


def tile_of(index, size=TILE):
    return pl.ds(pl.multiple_of(index * size, size), size)


def unrolled(count, body):
    def step(index, carry):
        body(index)
        return carry

    lax.fori_loop(0, count, step, 0, unroll=math.gcd(count, 4))


def tails_kernel(*refs):
    count = len(refs) // 2 - 1
    sources, tails_ref, fetched, sems = refs[:count], refs[count], refs[count + 1 : -1], refs[-1]
    copies = [
        pltpu.make_async_copy(source, target, sems.at[at]) for at, (source, target) in enumerate(zip(sources, fetched))
    ]
    for copy in copies:
        copy.start()
    streams_ref = fetched[0]
    length = streams_ref.shape[2]
    pick = (iota((2 * ROWS, length), 1) == iota((2 * ROWS, length), 0) + (length - ROWS)).astype(BF16)
    copies[0].wait()
    for stream in range(streams_ref.shape[0]):
        rows = dot(pick, streams_ref[stream], CONTRACT_LANES)
        tails_ref[stream] = rows[:ROWS].astype(BF16)
    for copy in copies[1:]:
        copy.wait()


def short_conv(stream, chans, rows, padded, taps_ref):
    total = None
    for shift in range(taps_ref.shape[1]):
        term = taps_ref[stream, shift : shift + 1, chans] * padded[pl.ds(ROWS - shift, rows), :]
        total = term if total is None else total + term
    return total


def prepare_kernel(
    streams_ref, taps_ref, rates_ref, residues_ref,
    heads_ref, query_ref, gated_ref, decay_ref, step_ref, response_ref, lift_ref, padded_ref,
):
    channels, length = streams_ref.shape[1:]
    poles, groups = rates_ref.shape
    width = channels // groups
    in_tile = TILE // width
    unit = identity(length)
    lag = (length - 1) - iota((poles, length), 1).astype(F32)
    owner = iota((poles, TILE), 1) // width
    time = iota((poles, length), 1).astype(F32)
    member = (iota((in_tile, in_tile * poles), 1) // poles == iota((in_tile, in_tile * poles), 0)).astype(BF16)
    scale = residues_ref[...] * jnp.sqrt(2.0 * rates_ref[...]) / math.sqrt(poles)

    def turn(index):
        chans = tile_of(index)
        for stream in range(3):
            tokens = turned(streams_ref[stream, chans, :], unit)
            padded_ref[index * 3 + stream, :ROWS, :] = jnp.zeros((ROWS, TILE), F32)
            padded_ref[index * 3 + stream, ROWS:, :] = tokens
            heads_ref[stream, :, chans] = tokens[:ROWS]

    def factors(index):
        shift = groups - index * in_tile
        rates = pltpu.roll(rates_ref[...], shift, 1)
        coef = pltpu.roll(scale, shift, 1)
        decay, impulse, lift = [], [], []
        wide = jnp.zeros((poles, TILE), F32)
        for g in range(in_tile):
            rate = jnp.broadcast_to(rates[:, g : g + 1], (poles, length))
            decay.append(jnp.exp(-rate * lag))
            amplitude = jnp.broadcast_to(coef[:, g : g + 1], (poles, length))
            impulse.append(amplitude * jnp.exp(-rate * time))
            lift.append(amplitude * jnp.exp(-rate * (time + 1.0)))
            wide = jnp.where(owner == g, rate[:, :TILE], wide)
        step_ref[:, tile_of(index)] = jnp.exp(-wide * length)
        states = tile_of(index, in_tile * poles)
        decay_ref[states, :] = jnp.concatenate(decay, axis=0).astype(BF16)
        high, low = halves(jnp.concatenate(impulse, axis=0))
        response_ref[pl.ds(pl.multiple_of(index * in_tile, in_tile), in_tile), :] = dot(member, high) + dot(member, low)
        lift_ref[:, states] = turned(jnp.concatenate(lift, axis=0).astype(BF16), unit).astype(BF16)

    def filters(index):
        chans = tile_of(index)
        query, left, right = (
            short_conv(stream, chans, length, padded_ref.at[index * 3 + stream], taps_ref) for stream in range(3)
        )
        query_ref[:, chans] = query.astype(BF16)
        gated_ref[:, chans] = left * right

    unrolled(channels // TILE, turn)
    unrolled(channels // TILE, factors)
    unrolled(channels // TILE, filters)


def states_kernel(before_ref, heads_ref, taps_ref, gated_ref, decay_ref, ends_ref, final_ref, first_ref, padded_ref):
    length, channels = gated_ref.shape
    poles = ends_ref.shape[1]
    in_tile = decay_ref.shape[0] // poles * TILE // channels
    owner = iota((poles, TILE), 1) // (TILE // in_tile)

    def begin(index):
        chans = tile_of(index)
        for stream in range(3):
            padded_ref[index * 3 + stream, :ROWS, :] = before_ref[stream, :, chans].astype(F32)
            padded_ref[index * 3 + stream, ROWS:, :] = heads_ref[stream, :, chans]
        query, left, right = (
            short_conv(stream, chans, ROWS, padded_ref.at[index * 3 + stream], taps_ref) for stream in range(3)
        )
        first_ref[:, chans] = query
        final_ref[:, chans] = jnp.concatenate([left * right, gated_ref[ROWS:, chans]], axis=0).astype(BF16)

    def leave(index):
        chans = tile_of(index)
        gated = final_ref[:, chans]
        states = tile_of(index, in_tile * poles)
        every = dot(decay_ref[states, :], gated)
        ends = jnp.zeros((poles, TILE), F32)
        for g in range(in_tile):
            ends = jnp.where(owner == g, every[g * poles : (g + 1) * poles], ends)
        ends = ends.astype(BF16)
        for block in range(ends_ref.shape[0]):
            ends_ref[block, :, chans] = ends

    unrolled(channels // TILE, begin)
    unrolled(channels // TILE, leave)


def inside_kernel(gated_ref, skip_ref, response_ref, base_ref, signal_ref, sum_ref):
    length, channels = gated_ref.shape
    groups = response_ref.shape[0]
    width = channels // groups
    in_tile = TILE // width
    tiles = channels // TILE
    strip = STRIP
    unit = identity(length)
    lane = iota((width, length), 1)
    causal = iota((strip, length), 1) >= iota((strip, length), 0)

    def signals(index):
        gated = gated_ref[:, tile_of(index)]
        for at in range(length // strip):
            piece = turned(gated[at * strip : (at + 1) * strip], unit).astype(BF16)
            signal_ref[at, tile_of(index), :] = piece

    def products(index):
        for pair in range(in_tile // 2):
            group = index * in_tile + 2 * pair
            responses = response_ref[pl.ds(group, 2), :]
            blocks = []
            for g in range(2):
                spread = jnp.broadcast_to(responses[g : g + 1], (strip, length))
                shifted = pltpu.roll(spread, 0, 1, stride=1, stride_axis=0)
                blocks.append(jnp.where(causal, shifted, 0.0).astype(BF16))
            rows = pl.ds(pl.multiple_of(group * width, 2 * width), 2 * width)
            signal = jnp.concatenate([signal_ref[at, rows, :] for at in range(length // strip)], axis=0)
            both = dot(signal, jnp.concatenate(blocks, axis=1))
            for g in range(2):
                total = None
                for at in range(length // strip):
                    first = at * 2 * width + g * width
                    term = both[first : first + width, g * length : (g + 1) * length]
                    if at:
                        term = jnp.where(lane >= at * strip, pltpu.roll(term, at * strip, 1), 0.0)
                    total = term if total is None else total + term
                sum_ref[pl.ds(pl.multiple_of((group + g) * width, width), width), :] = total

    def back(index):
        chans = tile_of(index)
        high, low = halves(sum_ref[chans, :])
        direct = skip_ref[:, chans] * gated_ref[:, chans].astype(F32)
        base_ref[:, chans] = turned(high, unit) + turned(low, unit) + direct

    unrolled(tiles, signals)
    unrolled(tiles, products)
    unrolled(tiles, back)


def finish_kernel(at_ref, ends_ref, step_ref, lift_ref, query_ref, first_ref, base_ref, mixed_ref, state_ref):
    length, share = mixed_ref.shape
    poles, channels = step_ref.shape
    in_tile = lift_ref.shape[1] // poles * TILE // channels
    me, half = at_ref[0], at_ref[1]
    here = tile_of(half, share)
    step = step_ref[:, here]

    def earlier(block, state):
        return jnp.where(block < me, step * state + ends_ref[block, :, here].astype(F32), state)

    state_ref[...] = lax.fori_loop(0, ends_ref.shape[0] - 1, earlier, jnp.zeros((poles, share), F32))
    owner = iota((poles, TILE), 1) // (TILE // in_tile)

    def tile(index):
        at = half * (share // TILE) + index
        chans = tile_of(at)
        entering = state_ref[:, tile_of(index)]
        apart = jnp.concatenate([jnp.where(owner == g, entering, 0.0) for g in range(in_tile)], axis=0)
        carried = dot(lift_ref[:, tile_of(at, in_tile * poles)], apart.astype(BF16))
        query = jnp.concatenate([first_ref[:, chans], query_ref[:, chans].astype(F32)[ROWS:]], axis=0)
        mixed_ref[:, tile_of(index)] = (query * (base_ref[:, chans] + carried)).astype(BF16)

    unrolled(share // TILE, tile)


def corner_kernel(block_ref, corner_ref):
    corner_ref[...] = block_ref[: corner_ref.shape[0], : corner_ref.shape[1]]


def early_kernel(at_ref, own_ref, beside_ref, theirs_ref, across_ref, corner_ref, *rest):
    *weight_hbms, total_ref, rows_ref, block_ref, layers_ref, weight_ref, sems = rest
    count = len(weight_hbms)
    layer = at_ref[0]
    last = layer ^ 2
    copies = [pltpu.make_async_copy(hbm, weight_ref.at[at], sems.at[at]) for at, hbm in enumerate(weight_hbms)]
    fetches = [pltpu.make_async_copy(hbm, rows_ref, sems.at[count]) for hbm in weight_hbms]
    for copy in copies:
        copy.start()
    for at, fetch in enumerate(fetches):
        pl.when(at_ref[1 + at] == last)(fetch.start)
    length = beside_ref.shape[0]
    layers_ref[layer] = own_ref[...]
    layers_ref[layer ^ 1, :length] = beside_ref[...]
    layers_ref[layer ^ 1, length:] = theirs_ref[...]
    layers_ref[layer ^ 1, : corner_ref.shape[0], : corner_ref.shape[1]] = corner_ref[...]
    layers_ref[layer ^ 3] = across_ref[...]
    layers_ref[last] = jnp.zeros_like(own_ref)
    block_ref[...] = layers_ref[at_ref[1 + count]]
    for at, copy in enumerate(copies):
        copy.wait()
        block = layers_ref[at_ref[1 + at]]
        for column in range(0, total_ref.shape[1], COLUMNS):
            columns = slice(column, column + COLUMNS)
            term = dot(block, weight_ref[at, :, columns])
            total_ref[:, columns] = total_ref[:, columns] + term if at else term
    for at, fetch in enumerate(fetches):
        pl.when(at_ref[1 + at] == last)(fetch.wait)


def joined_kernel(at_ref, total_ref, rows_ref, block_ref, weight_ref, out_ref, last_ref):
    out_ref[...] = total_ref[...] + dot(block_ref[...], weight_ref[...])

    def keep(rows):
        last_ref[...] = rows[...]

    latest = at_ref[4] == at_ref[0] ^ 2
    pl.when(latest)(lambda: keep(weight_ref))
    pl.when(jnp.logical_not(latest))(lambda: keep(rows_ref))


def late_kernel(first, beyond_ref, total_ref, rows_ref, out_ref):
    tokens = pl.ds(first, out_ref.shape[0])
    out_ref[...] = (total_ref[tokens, :] + dot(beyond_ref[tokens, :], rows_ref[...])).astype(out_ref.dtype)


def swap(value, *bits):
    count = lax.axis_size("ctx")
    pairs = [(source, source ^ bits[source % len(bits)]) for source in range(count)]
    return lax.ppermute(value, "ctx", pairs)


def after(value, earlier):
    return lax.optimization_barrier((value, earlier))[0]


def trade(value, bits):
    count = lax.axis_size("tp")
    return lax.ppermute(value, "tp", [(source, source ^ bits) for source in range(count)])


def local(streams, conv_weight, rates, residues, skip, out_weight):
    channels, length = streams.shape[1:]
    groups, poles = rates.shape
    blocks, layers = lax.axis_size("ctx"), lax.axis_size("tp")
    rows, features = out_weight.shape
    share = channels // CORES
    square = blocks == 8 and rows == share

    inputs = (streams, conv_weight, rates.T, residues.T, skip[None, :])
    tails, streams, conv_weight, rates, residues, skip = call(
        tails_kernel,
        [((3, ROWS, channels), BF16)] + [(part.shape, part.dtype) for part in inputs],
        "tails",
        *(pltpu.with_memory_space_constraint(part, pltpu.HBM) for part in inputs),
        specs=[pl.BlockSpec(memory_space=pltpu.HBM)] * len(inputs),
        scratch=[pltpu.SemaphoreType.DMA((len(inputs),))],
    )
    before = from_behind(tails, "ctx", 1)
    if square:
        near = swap(out_weight, 2, 4)
    tiles = channels // TILE
    heads, query, gated, decay, step, response, lift = call(
        prepare_kernel,
        [
            ((3, ROWS, channels), F32),
            ((length, channels), BF16),
            ((length, channels), F32),
            ((groups * poles, length), BF16),
            ((poles, channels), F32),
            ((groups, length), F32),
            ((length, groups * poles), BF16),
        ],
        "prepare",
        streams, conv_weight, rates, residues,
        scratch=[pltpu.VMEM((3 * tiles, ROWS + length, TILE), F32)],
        flops=10**9,
    )
    ends, gated, first = call(
        states_kernel,
        [((blocks, poles, channels), BF16), ((length, channels), BF16), ((ROWS, channels), F32)],
        "states",
        before, heads, conv_weight, gated, decay,
        scratch=[pltpu.VMEM((3 * tiles, 2 * ROWS, TILE), F32)],
    )
    all_ends = lax.all_to_all(ends, "ctx", split_axis=0, concat_axis=0, tiled=True)
    (base,) = call(
        inside_kernel,
        [((length, channels), F32)],
        "inside",
        gated, skip, response,
        scratch=[
            pltpu.VMEM((length // STRIP, channels, STRIP), BF16),
            pltpu.VMEM((channels, length), F32),
        ],
        flops=10**9,
    )
    if square:
        other_near = swap(after(out_weight, (base, near)), 4, 2)
    me = lax.axis_index("ctx").astype(jnp.int32)
    core = me % CORES
    smem = [pl.BlockSpec(memory_space=pltpu.SMEM)]

    def finished(half):
        return call(
            finish_kernel,
            [((length, share), BF16)],
            "finish",
            jnp.stack([me, half]), all_ends, step, lift, query, first, base,
            specs=smem + whole(6),
            flops=3 * 10**9,
            scratch=[pltpu.VMEM((poles, share), F32)],
        )[0]

    if rows == share:
        other, mine = finished(1 - core), finished(core)
    else:
        mixed = jnp.concatenate([finished(jnp.full_like(me, half)) for half in range(CORES)], axis=1)
        by_core = mixed.reshape(length, share // rows, CORES, rows).transpose(2, 0, 1, 3)
        by_core = by_core.reshape(CORES, length, share)
        mine = lax.dynamic_index_in_dim(by_core, core, 0, keepdims=False)
        other = lax.dynamic_index_in_dim(by_core, 1 - core, 0, keepdims=False)
    theirs = swap(other, 1)
    block = jnp.concatenate([mine, theirs], axis=0)
    layer = lax.axis_index("tp").astype(jnp.int32)
    beside, beside_theirs, across = trade(mine, 1), trade(theirs, 1), trade(block, 3)
    (corner,) = call(corner_kernel, [((2 * ROWS, TILE), BF16)], "corner", beside, flops=3 * 10**9)
    beyond = trade(after(across, (corner, other_near)) if square else across, 1)
    if square:
        diagonal = swap(after(near, block), 4, 2)
        weight = (out_weight, near, other_near, diagonal)
    else:
        core_groups = [list(range(core, blocks, CORES)) for core in range(CORES)]
        weight = lax.all_gather(out_weight, "ctx", axis=0, axis_index_groups=core_groups)
        weight = tuple(weight.reshape(layers, share, features))
    first_row = jnp.where(core == 0, 1, 2)
    chip = me // CORES
    place = [chip, chip ^ first_row, chip ^ (3 - first_row), chip ^ 3] if square else [jnp.full_like(me, at) for at in range(4)]
    at = jnp.stack([layer] + place)
    *sooner, latest = weight
    total, last_rows, last_block = call(
        early_kernel,
        [((CORES * length, features), F32), ((share, features), BF16), (block.shape, BF16)],
        "early",
        at, block, beside, beside_theirs, across, corner,
        *(pltpu.with_memory_space_constraint(part, pltpu.HBM) for part in sooner),
        specs=smem + whole(5) + [pl.BlockSpec(memory_space=pltpu.HBM)] * len(sooner),
        scratch=[
            pltpu.VMEM((layers,) + block.shape, BF16),
            pltpu.VMEM((len(sooner), share, features), BF16),
            pltpu.SemaphoreType.DMA((len(sooner) + 1,)),
        ],
        flops=10**10,
    )
    total, last_rows = call(
        joined_kernel,
        [((CORES * length, features), F32), ((share, features), BF16)],
        "joined",
        at, total, last_rows, last_block, latest,
        specs=smem + whole(4),
        flops=0,
    )
    sides = []
    for side, kind in ((1, BF16), (0, F32)):
        sides += call(
            functools.partial(late_kernel, side * length),
            [((length, features), kind)],
            "late",
            beyond, total, last_rows,
            flops=0,
        )
    other, mine = sides
    other = swap(other, 1)
    return (mine + other.astype(F32)).astype(BF16)


def solution(mesh):
    return jax.shard_map(
        local,
        mesh=mesh,
        in_specs=(
            P(None, "tp", "ctx"),
            P(None, None, "tp"),
            P("tp", None),
            P("tp", None),
            P("tp"),
            P("ctx", "tp"),
        ),
        out_specs=P("ctx", "tp"),
        check_vma=False,
    )
```

```python
import functools
import math

import jax
import jax.numpy as jnp
from jax import lax
from jax.experimental import pallas as pl
from jax.experimental.pallas import tpu as pltpu
from jax.sharding import PartitionSpec as P

F32 = jnp.float32
BF16 = jnp.bfloat16
ROWS = 8
TILE = 128
CORES = 2
COLUMNS = 256
STRIP = 32
VMEM_LIMIT = 24 * 1024 * 1024
PLAIN = (((1,), (0,)), ((), ()))
CONTRACT_LANES = (((1,), (1,)), ((), ()))


def from_behind(value, axis, steps):
    count = lax.axis_size(axis)
    leading, last = (max(0, -steps), min(count, count - steps))
    return lax.ppermute(value, axis, [(source, source + steps) for source in range(leading, last)])


def dot(left, right, dims=PLAIN):
    return lax.dot_general(left, right, dims, preferred_element_type=F32)


def halves(value):
    high = value.astype(BF16)
    return high, (value - high.astype(F32)).astype(BF16)


def iota(shape, axis):
    return lax.broadcasted_iota(jnp.int32, shape, axis)


def identity(size):
    return (iota((size, size), 0) == iota((size, size), 1)).astype(BF16)


def turned(value, unit):
    return dot(unit, value, CONTRACT_LANES)


def whole(count):
    return [pl.BlockSpec(memory_space=pltpu.VMEM)] * count


def call(kernel, outs, name, *operands, specs=None, scratch=(), flops=10**8):
    return pl.pallas_call(
        kernel,
        out_shape=tuple(jax.ShapeDtypeStruct(*out) for out in outs),
        in_specs=whole(len(operands)) if specs is None else specs,
        out_specs=tuple(whole(len(outs))),
        scratch_shapes=scratch,
        compiler_params=pltpu.CompilerParams(vmem_limit_bytes=VMEM_LIMIT),
        cost_estimate=pl.CostEstimate(flops=flops, bytes_accessed=flops // 100, transcendentals=0),
        name=name,
    )(*operands)


def tile_of(index, size=TILE):
    return pl.ds(pl.multiple_of(index * size, size), size)


def unrolled(count, body):
    def step(index, carry):
        body(index)
        return carry

    lax.fori_loop(0, count, step, 0, unroll=math.gcd(count, 4))


def tails_kernel(*refs):
    count = len(refs) // 2 - 1
    sources, tails_ref, fetched, sems = refs[:count], refs[count], refs[count + 1 : -1], refs[-1]
    copies = [
        pltpu.make_async_copy(source, target, sems.at[at]) for at, (source, target) in enumerate(zip(sources, fetched))
    ]
    for copy in copies:
        copy.start()
    streams_ref = fetched[0]
    length = streams_ref.shape[2]
    pick = (iota((2 * ROWS, length), 1) == iota((2 * ROWS, length), 0) + (length - ROWS)).astype(BF16)
    copies[0].wait()
    for stream in range(streams_ref.shape[0]):
        rows = dot(pick, streams_ref[stream], CONTRACT_LANES)
        tails_ref[stream] = rows[:ROWS].astype(BF16)
    for copy in copies[1:]:
        copy.wait()


def short_conv(stream, chans, rows, padded, taps_ref):
    total = None
    for shift in range(taps_ref.shape[1]):
        term = taps_ref[stream, shift : shift + 1, chans] * padded[pl.ds(ROWS - shift, rows), :]
        total = term if total is None else total + term
    return total


def prepare_kernel(
    streams_ref, taps_ref, rates_ref, residues_ref,
    heads_ref, query_ref, gated_ref, decay_ref, step_ref, response_ref, lift_ref, padded_ref,
):
    channels, length = streams_ref.shape[1:]
    poles, groups = rates_ref.shape
    width = channels // groups
    in_tile = TILE // width
    unit = identity(length)
    lag = (length - 1) - iota((poles, length), 1).astype(F32)
    owner = iota((poles, TILE), 1) // width
    time = iota((poles, length), 1).astype(F32)
    member = (iota((in_tile, in_tile * poles), 1) // poles == iota((in_tile, in_tile * poles), 0)).astype(BF16)
    scale = residues_ref[...] * jnp.sqrt(2.0 * rates_ref[...]) / math.sqrt(poles)

    def turn(index):
        chans = tile_of(index)
        for stream in range(3):
            tokens = turned(streams_ref[stream, chans, :], unit)
            padded_ref[index * 3 + stream, :ROWS, :] = jnp.zeros((ROWS, TILE), F32)
            padded_ref[index * 3 + stream, ROWS:, :] = tokens
            heads_ref[stream, :, chans] = tokens[:ROWS]

    def factors(index):
        shift = groups - index * in_tile
        rates = pltpu.roll(rates_ref[...], shift, 1)
        coef = pltpu.roll(scale, shift, 1)
        decay, impulse, lift = [], [], []
        wide = jnp.zeros((poles, TILE), F32)
        for g in range(in_tile):
            rate = jnp.broadcast_to(rates[:, g : g + 1], (poles, length))
            decay.append(jnp.exp(-rate * lag))
            amplitude = jnp.broadcast_to(coef[:, g : g + 1], (poles, length))
            impulse.append(amplitude * jnp.exp(-rate * time))
            lift.append(amplitude * jnp.exp(-rate * (time + 1.0)))
            wide = jnp.where(owner == g, rate[:, :TILE], wide)
        step_ref[:, tile_of(index)] = jnp.exp(-wide * length)
        states = tile_of(index, in_tile * poles)
        decay_ref[states, :] = jnp.concatenate(decay, axis=0).astype(BF16)
        high, low = halves(jnp.concatenate(impulse, axis=0))
        response_ref[pl.ds(pl.multiple_of(index * in_tile, in_tile), in_tile), :] = dot(member, high) + dot(member, low)
        lift_ref[:, states] = turned(jnp.concatenate(lift, axis=0).astype(BF16), unit).astype(BF16)

    def filters(index):
        chans = tile_of(index)
        query, left, right = (
            short_conv(stream, chans, length, padded_ref.at[index * 3 + stream], taps_ref) for stream in range(3)
        )
        query_ref[:, chans] = query.astype(BF16)
        gated_ref[:, chans] = left * right

    unrolled(channels // TILE, turn)
    unrolled(channels // TILE, factors)
    unrolled(channels // TILE, filters)


def states_kernel(before_ref, heads_ref, taps_ref, gated_ref, decay_ref, ends_ref, final_ref, first_ref, padded_ref):
    length, channels = gated_ref.shape
    poles = ends_ref.shape[1]
    in_tile = decay_ref.shape[0] // poles * TILE // channels
    owner = iota((poles, TILE), 1) // (TILE // in_tile)

    def begin(index):
        chans = tile_of(index)
        for stream in range(3):
            padded_ref[index * 3 + stream, :ROWS, :] = before_ref[stream, :, chans].astype(F32)
            padded_ref[index * 3 + stream, ROWS:, :] = heads_ref[stream, :, chans]
        query, left, right = (
            short_conv(stream, chans, ROWS, padded_ref.at[index * 3 + stream], taps_ref) for stream in range(3)
        )
        first_ref[:, chans] = query
        final_ref[:, chans] = jnp.concatenate([left * right, gated_ref[ROWS:, chans]], axis=0).astype(BF16)

    def leave(index):
        chans = tile_of(index)
        gated = final_ref[:, chans]
        states = tile_of(index, in_tile * poles)
        every = dot(decay_ref[states, :], gated)
        ends = jnp.zeros((poles, TILE), F32)
        for g in range(in_tile):
            ends = jnp.where(owner == g, every[g * poles : (g + 1) * poles], ends)
        ends = ends.astype(BF16)
        for block in range(ends_ref.shape[0]):
            ends_ref[block, :, chans] = ends

    unrolled(channels // TILE, begin)
    unrolled(channels // TILE, leave)


def inside_kernel(gated_ref, skip_ref, response_ref, base_ref, signal_ref, sum_ref):
    length, channels = gated_ref.shape
    groups = response_ref.shape[0]
    width = channels // groups
    in_tile = TILE // width
    tiles = channels // TILE
    strip = STRIP
    unit = identity(length)
    lane = iota((width, length), 1)
    causal = iota((strip, length), 1) >= iota((strip, length), 0)

    def signals(index):
        gated = gated_ref[:, tile_of(index)]
        for at in range(length // strip):
            piece = turned(gated[at * strip : (at + 1) * strip], unit).astype(BF16)
            signal_ref[at, tile_of(index), :] = piece

    def products(index):
        for pair in range(in_tile // 2):
            group = index * in_tile + 2 * pair
            responses = response_ref[pl.ds(group, 2), :]
            blocks = []
            for g in range(2):
                spread = jnp.broadcast_to(responses[g : g + 1], (strip, length))
                shifted = pltpu.roll(spread, 0, 1, stride=1, stride_axis=0)
                blocks.append(jnp.where(causal, shifted, 0.0).astype(BF16))
            rows = pl.ds(pl.multiple_of(group * width, 2 * width), 2 * width)
            signal = jnp.concatenate([signal_ref[at, rows, :] for at in range(length // strip)], axis=0)
            both = dot(signal, jnp.concatenate(blocks, axis=1))
            for g in range(2):
                total = None
                for at in range(length // strip):
                    first = at * 2 * width + g * width
                    term = both[first : first + width, g * length : (g + 1) * length]
                    if at:
                        term = jnp.where(lane >= at * strip, pltpu.roll(term, at * strip, 1), 0.0)
                    total = term if total is None else total + term
                sum_ref[pl.ds(pl.multiple_of((group + g) * width, width), width), :] = total

    def back(index):
        chans = tile_of(index)
        high, low = halves(sum_ref[chans, :])
        direct = skip_ref[:, chans] * gated_ref[:, chans].astype(F32)
        base_ref[:, chans] = turned(high, unit) + turned(low, unit) + direct

    unrolled(tiles, signals)
    unrolled(tiles, products)
    unrolled(tiles, back)


def finish_kernel(at_ref, ends_ref, step_ref, lift_ref, query_ref, first_ref, base_ref, mixed_ref, state_ref):
    length, share = mixed_ref.shape
    poles, channels = step_ref.shape
    in_tile = lift_ref.shape[1] // poles * TILE // channels
    me, half = at_ref[0], at_ref[1]
    here = tile_of(half, share)
    step = step_ref[:, here]

    def earlier(block, state):
        return jnp.where(block < me, step * state + ends_ref[block, :, here].astype(F32), state)

    state_ref[...] = lax.fori_loop(0, ends_ref.shape[0] - 1, earlier, jnp.zeros((poles, share), F32))
    owner = iota((poles, TILE), 1) // (TILE // in_tile)

    def tile(index):
        at = half * (share // TILE) + index
        chans = tile_of(at)
        entering = state_ref[:, tile_of(index)]
        apart = jnp.concatenate([jnp.where(owner == g, entering, 0.0) for g in range(in_tile)], axis=0)
        carried = dot(lift_ref[:, tile_of(at, in_tile * poles)], apart.astype(BF16))
        query = jnp.concatenate([first_ref[:, chans], query_ref[:, chans].astype(F32)[ROWS:]], axis=0)
        mixed_ref[:, tile_of(index)] = (query * (base_ref[:, chans] + carried)).astype(BF16)

    unrolled(share // TILE, tile)


def corner_kernel(block_ref, corner_ref):
    corner_ref[...] = block_ref[: corner_ref.shape[0], : corner_ref.shape[1]]


def early_kernel(at_ref, own_ref, beside_ref, middle_ref, across_ref, corner_ref, *rest):
    *weight_hbms, total_ref, rows_ref, block_ref, layers_ref, weight_ref, sems = rest
    count = len(weight_hbms)
    layer = at_ref[0]
    last = layer ^ 2
    copies = [pltpu.make_async_copy(hbm, weight_ref.at[at], sems.at[at]) for at, hbm in enumerate(weight_hbms)]
    fetches = [pltpu.make_async_copy(hbm, rows_ref, sems.at[count]) for hbm in weight_hbms]
    for copy in copies:
        copy.start()
    for at, fetch in enumerate(fetches):
        pl.when(at_ref[1 + at] == last)(fetch.start)
    edge = (layer == 0) | (layer == 3)
    corner = tuple(slice(0, size) for size in corner_ref.shape)
    layers_ref[layer] = own_ref[...]
    layers_ref[layer ^ 1] = beside_ref[...]
    layers_ref[layer ^ 3] = jnp.where(edge, across_ref[...], middle_ref[...])
    layers_ref[(layer ^ 3, *corner)] = jnp.where(edge, across_ref[corner], corner_ref[...])
    layers_ref[last] = jnp.zeros_like(own_ref)
    block_ref[...] = layers_ref[at_ref[1 + count]]
    for at, copy in enumerate(copies):
        copy.wait()
        block = layers_ref[at_ref[1 + at]]
        for column in range(0, total_ref.shape[1], COLUMNS):
            columns = slice(column, column + COLUMNS)
            term = dot(block, weight_ref[at, :, columns])
            total_ref[:, columns] = total_ref[:, columns] + term if at else term
    for at, fetch in enumerate(fetches):
        pl.when(at_ref[1 + at] == last)(fetch.wait)


def joined_kernel(at_ref, total_ref, rows_ref, block_ref, weight_ref, out_ref, last_ref):
    out_ref[...] = total_ref[...] + dot(block_ref[...], weight_ref[...])

    def keep(rows):
        last_ref[...] = rows[...]

    latest = at_ref[4] == at_ref[0] ^ 2
    pl.when(latest)(lambda: keep(weight_ref))
    pl.when(jnp.logical_not(latest))(lambda: keep(rows_ref))


def late_kernel(first, at_ref, inwards_ref, outwards_ref, total_ref, rows_ref, out_ref):
    tokens = pl.ds(first, out_ref.shape[0])
    edge = (at_ref[0] == 0) | (at_ref[0] == 3)
    beyond = jnp.where(edge, outwards_ref[tokens, :], inwards_ref[tokens, :])
    out_ref[...] = (total_ref[tokens, :] + dot(beyond, rows_ref[...])).astype(out_ref.dtype)


def swap(value, *bits):
    count = lax.axis_size("ctx")
    pairs = [(source, source ^ bits[source % len(bits)]) for source in range(count)]
    return lax.ppermute(value, "ctx", pairs)


def after(value, earlier):
    return lax.optimization_barrier((value, earlier))[0]


def along(value, *pairs):
    return lax.ppermute(value, "tp", pairs)


def local(streams, conv_weight, rates, residues, skip, out_weight):
    channels, length = streams.shape[1:]
    groups, poles = rates.shape
    blocks, layers = lax.axis_size("ctx"), lax.axis_size("tp")
    rows, features = out_weight.shape
    share = channels // CORES
    square = blocks == 8 and rows == share

    inputs = (streams, conv_weight, rates.T, residues.T, skip[None, :])
    tails, streams, conv_weight, rates, residues, skip = call(
        tails_kernel,
        [((3, ROWS, channels), BF16)] + [(part.shape, part.dtype) for part in inputs],
        "tails",
        *(pltpu.with_memory_space_constraint(part, pltpu.HBM) for part in inputs),
        specs=[pl.BlockSpec(memory_space=pltpu.HBM)] * len(inputs),
        scratch=[pltpu.SemaphoreType.DMA((len(inputs),))],
    )
    before = from_behind(tails, "ctx", 1)
    if square:
        near = swap(out_weight, 2, 4)
    tiles = channels // TILE
    heads, query, gated, decay, step, response, lift = call(
        prepare_kernel,
        [
            ((3, ROWS, channels), F32),
            ((length, channels), BF16),
            ((length, channels), F32),
            ((groups * poles, length), BF16),
            ((poles, channels), F32),
            ((groups, length), F32),
            ((length, groups * poles), BF16),
        ],
        "prepare",
        streams, conv_weight, rates, residues,
        scratch=[pltpu.VMEM((3 * tiles, ROWS + length, TILE), F32)],
        flops=10**9,
    )
    ends, gated, first = call(
        states_kernel,
        [((blocks, poles, channels), BF16), ((length, channels), BF16), ((ROWS, channels), F32)],
        "states",
        before, heads, conv_weight, gated, decay,
        scratch=[pltpu.VMEM((3 * tiles, 2 * ROWS, TILE), F32)],
    )
    all_ends = lax.all_to_all(ends, "ctx", split_axis=0, concat_axis=0, tiled=True)
    (base,) = call(
        inside_kernel,
        [((length, channels), F32)],
        "inside",
        gated, skip, response,
        scratch=[
            pltpu.VMEM((length // STRIP, channels, STRIP), BF16),
            pltpu.VMEM((channels, length), F32),
        ],
        flops=10**9,
    )
    if square:
        other_near = swap(after(out_weight, (gated, near)), 4, 2)
    me = lax.axis_index("ctx").astype(jnp.int32)
    core = me % CORES
    smem = [pl.BlockSpec(memory_space=pltpu.SMEM)]

    def finished(half):
        return call(
            finish_kernel,
            [((length, share), BF16)],
            "finish",
            jnp.stack([me, half]), all_ends, step, lift, query, first, base,
            specs=smem + whole(6),
            flops=3 * 10**9,
            scratch=[pltpu.VMEM((poles, share), F32)],
        )[0]

    if rows == share:
        other, mine = finished(1 - core), finished(core)
    else:
        mixed = jnp.concatenate([finished(jnp.full_like(me, half)) for half in range(CORES)], axis=1)
        by_core = mixed.reshape(length, share // rows, CORES, rows).transpose(2, 0, 1, 3)
        by_core = by_core.reshape(CORES, length, share)
        mine = lax.dynamic_index_in_dim(by_core, core, 0, keepdims=False)
        other = lax.dynamic_index_in_dim(by_core, 1 - core, 0, keepdims=False)
    block = jnp.concatenate([mine, swap(other, 1)], axis=0)
    layer = lax.axis_index("tp").astype(jnp.int32)
    middle = along(block, (1, 2), (2, 1))
    beside = along(block, (0, 1), (1, 0), (2, 3), (3, 2))
    across = along(block, (0, 3), (3, 0))
    (corner,) = call(corner_kernel, [((2 * ROWS, TILE), BF16)], "corner", middle, flops=3 * 10**9)
    outwards = along(after(middle, corner), (1, 0), (2, 3))
    inwards = along(after(beside, (corner, other_near)) if square else beside, (1, 2), (2, 1))
    if square:
        diagonal = swap(after(near, block), 4, 2)
        weight = (out_weight, near, other_near, diagonal)
    else:
        core_groups = [list(range(core, blocks, CORES)) for core in range(CORES)]
        weight = lax.all_gather(out_weight, "ctx", axis=0, axis_index_groups=core_groups)
        weight = tuple(weight.reshape(layers, share, features))
    first_row = jnp.where(core == 0, 1, 2)
    chip = me // CORES
    place = [chip, chip ^ first_row, chip ^ (3 - first_row), chip ^ 3] if square else [jnp.full_like(me, at) for at in range(4)]
    at = jnp.stack([layer] + place)
    *sooner, latest = weight
    total, last_rows, last_block = call(
        early_kernel,
        [((CORES * length, features), F32), ((share, features), BF16), (block.shape, BF16)],
        "early",
        at, block, beside, middle, across, corner,
        *(pltpu.with_memory_space_constraint(part, pltpu.HBM) for part in sooner),
        specs=smem + whole(5) + [pl.BlockSpec(memory_space=pltpu.HBM)] * len(sooner),
        scratch=[
            pltpu.VMEM((layers,) + block.shape, BF16),
            pltpu.VMEM((len(sooner), share, features), BF16),
            pltpu.SemaphoreType.DMA((len(sooner) + 1,)),
        ],
        flops=10**10,
    )
    total, last_rows = call(
        joined_kernel,
        [((CORES * length, features), F32), ((share, features), BF16)],
        "joined",
        at, total, last_rows, last_block, latest,
        specs=smem + whole(4),
        flops=0,
    )
    sides = []
    for side, kind in ((1, BF16), (0, F32)):
        sides += call(
            functools.partial(late_kernel, side * length),
            [((length, features), kind)],
            "late",
            at, inwards, outwards, total, last_rows,
            specs=smem + whole(4),
            flops=0,
        )
    other, mine = sides
    other = swap(other, 1)
    return (mine + other.astype(F32)).astype(BF16)


def solution(mesh):
    return jax.shard_map(
        local,
        mesh=mesh,
        in_specs=(
            P(None, "tp", "ctx"),
            P(None, None, "tp"),
            P("tp", None),
            P("tp", None),
            P("tp"),
            P("ctx", "tp"),
        ),
        out_specs=P("ctx", "tp"),
        check_vma=False,
    )
```

```python
import functools
import math

import jax
import jax.numpy as jnp
from jax import lax
from jax.experimental import pallas as pl
from jax.experimental.pallas import tpu as pltpu
from jax.sharding import PartitionSpec as P

F32 = jnp.float32
BF16 = jnp.bfloat16
ROWS = 8
TILE = 128
CORES = 2
COLUMNS = 256
STRIP = 32
VMEM_LIMIT = 24 * 1024 * 1024
PLAIN = (((1,), (0,)), ((), ()))
CONTRACT_LANES = (((1,), (1,)), ((), ()))


def from_behind(value, axis, steps):
    count = lax.axis_size(axis)
    leading, last = (max(0, -steps), min(count, count - steps))
    return lax.ppermute(value, axis, [(source, source + steps) for source in range(leading, last)])


def dot(left, right, dims=PLAIN):
    return lax.dot_general(left, right, dims, preferred_element_type=F32)


def halves(value):
    high = value.astype(BF16)
    return high, (value - high.astype(F32)).astype(BF16)


def iota(shape, axis):
    return lax.broadcasted_iota(jnp.int32, shape, axis)


def identity(size):
    return (iota((size, size), 0) == iota((size, size), 1)).astype(BF16)


def turned(value, unit):
    return dot(unit, value, CONTRACT_LANES)


def whole(count):
    return [pl.BlockSpec(memory_space=pltpu.VMEM)] * count


def call(kernel, outs, name, *operands, specs=None, scratch=(), flops=10**8):
    return pl.pallas_call(
        kernel,
        out_shape=tuple(jax.ShapeDtypeStruct(*out) for out in outs),
        in_specs=whole(len(operands)) if specs is None else specs,
        out_specs=tuple(whole(len(outs))),
        scratch_shapes=scratch,
        compiler_params=pltpu.CompilerParams(vmem_limit_bytes=VMEM_LIMIT),
        cost_estimate=pl.CostEstimate(flops=flops, bytes_accessed=flops // 100, transcendentals=0),
        name=name,
    )(*operands)


def tile_of(index, size=TILE):
    return pl.ds(pl.multiple_of(index * size, size), size)


def unrolled(count, body):
    def step(index, carry):
        body(index)
        return carry

    lax.fori_loop(0, count, step, 0, unroll=math.gcd(count, 4))


def tails_kernel(*refs):
    count = len(refs) // 2 - 1
    sources, tails_ref, fetched, sems = refs[:count], refs[count], refs[count + 1 : -1], refs[-1]
    copies = [
        pltpu.make_async_copy(source, target, sems.at[at]) for at, (source, target) in enumerate(zip(sources, fetched))
    ]
    for copy in copies:
        copy.start()
    streams_ref = fetched[0]
    length = streams_ref.shape[2]
    pick = (iota((2 * ROWS, length), 1) == iota((2 * ROWS, length), 0) + (length - ROWS)).astype(BF16)
    copies[0].wait()
    for stream in range(streams_ref.shape[0]):
        rows = dot(pick, streams_ref[stream], CONTRACT_LANES)
        tails_ref[stream] = rows[:ROWS].astype(BF16)
    for copy in copies[1:]:
        copy.wait()


def short_conv(stream, chans, rows, padded, taps_ref):
    total = None
    for shift in range(taps_ref.shape[1]):
        term = taps_ref[stream, shift : shift + 1, chans] * padded[pl.ds(ROWS - shift, rows), :]
        total = term if total is None else total + term
    return total


def prepare_kernel(
    streams_ref, taps_ref, rates_ref, residues_ref,
    heads_ref, query_ref, gated_ref, decay_ref, step_ref, response_ref, lift_ref, padded_ref,
):
    channels, length = streams_ref.shape[1:]
    poles, groups = rates_ref.shape
    width = channels // groups
    in_tile = TILE // width
    unit = identity(length)
    lag = (length - 1) - iota((poles, length), 1).astype(F32)
    owner = iota((poles, TILE), 1) // width
    time = iota((poles, length), 1).astype(F32)
    member = (iota((in_tile, in_tile * poles), 1) // poles == iota((in_tile, in_tile * poles), 0)).astype(BF16)
    scale = residues_ref[...] * jnp.sqrt(2.0 * rates_ref[...]) / math.sqrt(poles)

    def turn(index):
        chans = tile_of(index)
        for stream in range(3):
            tokens = turned(streams_ref[stream, chans, :], unit)
            padded_ref[index * 3 + stream, :ROWS, :] = jnp.zeros((ROWS, TILE), F32)
            padded_ref[index * 3 + stream, ROWS:, :] = tokens
            heads_ref[stream, :, chans] = tokens[:ROWS]

    def factors(index):
        shift = groups - index * in_tile
        rates = pltpu.roll(rates_ref[...], shift, 1)
        coef = pltpu.roll(scale, shift, 1)
        decay, impulse, lift = [], [], []
        wide = jnp.zeros((poles, TILE), F32)
        for g in range(in_tile):
            rate = jnp.broadcast_to(rates[:, g : g + 1], (poles, length))
            decay.append(jnp.exp(-rate * lag))
            amplitude = jnp.broadcast_to(coef[:, g : g + 1], (poles, length))
            impulse.append(amplitude * jnp.exp(-rate * time))
            lift.append(amplitude * jnp.exp(-rate * (time + 1.0)))
            wide = jnp.where(owner == g, rate[:, :TILE], wide)
        step_ref[:, tile_of(index)] = -wide * length
        states = tile_of(index, in_tile * poles)
        decay_ref[states, :] = jnp.concatenate(decay, axis=0).astype(BF16)
        high, low = halves(jnp.concatenate(impulse, axis=0))
        response_ref[pl.ds(pl.multiple_of(index * in_tile, in_tile), in_tile), :] = dot(member, high) + dot(member, low)
        lift_ref[:, states] = turned(jnp.concatenate(lift, axis=0).astype(BF16), unit).astype(BF16)

    def filters(index):
        chans = tile_of(index)
        query, left, right = (
            short_conv(stream, chans, length, padded_ref.at[index * 3 + stream], taps_ref) for stream in range(3)
        )
        query_ref[:, chans] = query.astype(BF16)
        gated_ref[:, chans] = left * right

    unrolled(channels // TILE, turn)
    unrolled(channels // TILE, factors)
    unrolled(channels // TILE, filters)


def states_kernel(
    before_ref, heads_ref, taps_ref, gated_ref, decay_ref, ends_ref, sent_ref, final_ref, first_ref, padded_ref
):
    length, channels = gated_ref.shape
    poles = ends_ref.shape[0]
    in_tile = decay_ref.shape[0] // poles * TILE // channels
    owner = iota((poles, TILE), 1) // (TILE // in_tile)

    def begin(index):
        chans = tile_of(index)
        for stream in range(3):
            padded_ref[index * 3 + stream, :ROWS, :] = before_ref[stream, :, chans].astype(F32)
            padded_ref[index * 3 + stream, ROWS:, :] = heads_ref[stream, :, chans]
        query, left, right = (
            short_conv(stream, chans, ROWS, padded_ref.at[index * 3 + stream], taps_ref) for stream in range(3)
        )
        first_ref[:, chans] = query
        final_ref[:, chans] = jnp.concatenate([left * right, gated_ref[ROWS:, chans]], axis=0).astype(BF16)

    def leave(index):
        chans = tile_of(index)
        gated = final_ref[:, chans]
        states = tile_of(index, in_tile * poles)
        every = dot(decay_ref[states, :], gated)
        ends = jnp.zeros((poles, TILE), F32)
        for g in range(in_tile):
            ends = jnp.where(owner == g, every[g * poles : (g + 1) * poles], ends)
        ends_ref[:, chans] = ends
        sent_ref[:, chans] = ends.astype(BF16)

    unrolled(channels // TILE, begin)
    unrolled(channels // TILE, leave)


def inside_kernel(begin, gated_ref, skip_ref, response_ref, base_ref, signal_ref, sum_ref):
    length = gated_ref.shape[0]
    width = gated_ref.shape[1] // response_ref.shape[0]
    in_tile = TILE // width
    tiles = base_ref.shape[1] // TILE
    strip = STRIP
    unit = identity(length)
    lane = iota((width, length), 1)
    causal = iota((strip, length), 1) >= iota((strip, length), 0)

    def signals(index):
        gated = gated_ref[:, tile_of(begin + index)]
        for at in range(length // strip):
            piece = turned(gated[at * strip : (at + 1) * strip], unit).astype(BF16)
            signal_ref[at, tile_of(index), :] = piece

    def products(index):
        for pair in range(in_tile // 2):
            group = index * in_tile + 2 * pair
            responses = response_ref[pl.ds(begin * in_tile + group, 2), :]
            blocks = []
            for g in range(2):
                spread = jnp.broadcast_to(responses[g : g + 1], (strip, length))
                shifted = pltpu.roll(spread, 0, 1, stride=1, stride_axis=0)
                blocks.append(jnp.where(causal, shifted, 0.0).astype(BF16))
            rows = pl.ds(pl.multiple_of(group * width, 2 * width), 2 * width)
            signal = jnp.concatenate([signal_ref[at, rows, :] for at in range(length // strip)], axis=0)
            both = dot(signal, jnp.concatenate(blocks, axis=1))
            for g in range(2):
                total = None
                for at in range(length // strip):
                    first = at * 2 * width + g * width
                    term = both[first : first + width, g * length : (g + 1) * length]
                    if at:
                        term = jnp.where(lane >= at * strip, pltpu.roll(term, at * strip, 1), 0.0)
                    total = term if total is None else total + term
                sum_ref[pl.ds(pl.multiple_of((group + g) * width, width), width), :] = total

    def back(index):
        chans = tile_of(index)
        here = tile_of(begin + index)
        high, low = halves(sum_ref[chans, :])
        direct = skip_ref[:, here] * gated_ref[:, here].astype(F32)
        base_ref[:, chans] = turned(high, unit) + turned(low, unit) + direct

    unrolled(tiles, signals)
    unrolled(tiles, products)
    unrolled(tiles, back)


def join_kernel(bit, me_ref, arrived_ref, ends_ref, entering_ref, wide_ref, joined_ref, sent_ref, later_ref):
    me = me_ref[0]
    high = (me >> bit) % 2 == 1
    arrived = arrived_ref[...].astype(F32)
    wide = wide_ref[...]
    over = jnp.exp(wide * (1 << bit))
    joined = jnp.where(high, over * arrived + ends_ref[...], over * ends_ref[...] + arrived)
    joined_ref[...] = joined
    sent_ref[...] = joined.astype(BF16)
    before = (me % (1 << bit)).astype(F32)
    later_ref[...] = entering_ref[...] + jnp.where(high, jnp.exp(wide * before) * arrived, 0.0)


def finish_kernel(
    bit, at_ref, arrived_ref, entering_ref, wide_ref, lift_ref, query_ref, first_ref, left_ref, right_ref, mixed_ref, state_ref
):
    length, share = mixed_ref.shape
    poles, channels = wide_ref.shape
    in_tile = lift_ref.shape[1] // poles * TILE // channels
    me, half = at_ref[0], at_ref[1]
    here = tile_of(half, share)
    high = (me >> bit) % 2 == 1
    before = (me % (1 << bit)).astype(F32)
    reached = jnp.exp(wide_ref[:, here] * before) * arrived_ref[:, here].astype(F32)
    state_ref[...] = entering_ref[:, here] + jnp.where(high, reached, 0.0)
    owner = iota((poles, TILE), 1) // (TILE // in_tile)

    def tile(index):
        at = half * (share // TILE) + index
        chans = tile_of(at)
        entering = state_ref[:, tile_of(index)]
        apart = jnp.concatenate([jnp.where(owner == g, entering, 0.0) for g in range(in_tile)], axis=0)
        carried = dot(lift_ref[:, tile_of(at, in_tile * poles)], apart.astype(BF16))
        query = jnp.concatenate([first_ref[:, chans], query_ref[:, chans].astype(F32)[ROWS:]], axis=0)
        base = jnp.where(half == 0, left_ref[:, tile_of(index)], right_ref[:, tile_of(index)])
        mixed_ref[:, tile_of(index)] = (query * (base + carried)).astype(BF16)

    unrolled(share // TILE, tile)


def early_kernel(at_ref, own_ref, beside_ref, across_ref, *rest):
    *weight_hbms, total_ref, rows_ref, block_ref, layers_ref, weight_ref, sems = rest
    count = len(weight_hbms)
    layer = at_ref[0]
    last = layer ^ 2
    copies = [pltpu.make_async_copy(hbm, weight_ref.at[at], sems.at[at]) for at, hbm in enumerate(weight_hbms)]
    fetches = [pltpu.make_async_copy(hbm, rows_ref, sems.at[count]) for hbm in weight_hbms]
    for copy in copies:
        copy.start()
    for at, fetch in enumerate(fetches):
        pl.when(at_ref[1 + at] == last)(fetch.start)
    for bits, ref in ((0, own_ref), (1, beside_ref), (3, across_ref)):
        layers_ref[layer ^ bits] = ref[...]
    layers_ref[last] = jnp.zeros_like(own_ref)
    block_ref[...] = layers_ref[at_ref[1 + count]]
    for at, copy in enumerate(copies):
        copy.wait()
        block = layers_ref[at_ref[1 + at]]
        for column in range(0, total_ref.shape[1], COLUMNS):
            columns = slice(column, column + COLUMNS)
            term = dot(block, weight_ref[at, :, columns])
            total_ref[:, columns] = total_ref[:, columns] + term if at else term
    for at, fetch in enumerate(fetches):
        pl.when(at_ref[1 + at] == last)(fetch.wait)


def joined_kernel(at_ref, total_ref, rows_ref, block_ref, weight_ref, out_ref, last_ref):
    out_ref[...] = total_ref[...] + dot(block_ref[...], weight_ref[...])

    def keep(rows):
        last_ref[...] = rows[...]

    latest = at_ref[4] == at_ref[0] ^ 2
    pl.when(latest)(lambda: keep(weight_ref))
    pl.when(jnp.logical_not(latest))(lambda: keep(rows_ref))


def late_kernel(first, beyond_ref, total_ref, rows_ref, out_ref):
    tokens = pl.ds(first, out_ref.shape[0])
    out_ref[...] = (total_ref[tokens, :] + dot(beyond_ref[tokens, :], rows_ref[...])).astype(out_ref.dtype)


def swap(value, *bits):
    count = lax.axis_size("ctx")
    pairs = [(source, source ^ bits[source % len(bits)]) for source in range(count)]
    return lax.ppermute(value, "ctx", pairs)


def after(value, earlier):
    return lax.optimization_barrier((value, earlier))[0]


def trade(value, bits):
    count = lax.axis_size("tp")
    return lax.ppermute(value, "tp", [(source, source ^ bits) for source in range(count)])


def local(streams, conv_weight, rates, residues, skip, out_weight):
    channels, length = streams.shape[1:]
    groups, poles = rates.shape
    blocks, layers = lax.axis_size("ctx"), lax.axis_size("tp")
    rows, features = out_weight.shape
    share = channels // CORES
    square = blocks == 8 and rows == share

    inputs = (streams, conv_weight, rates.T, residues.T, skip[None, :])
    tails, streams, conv_weight, rates, residues, skip = call(
        tails_kernel,
        [((3, ROWS, channels), BF16)] + [(part.shape, part.dtype) for part in inputs],
        "tails",
        *(pltpu.with_memory_space_constraint(part, pltpu.HBM) for part in inputs),
        specs=[pl.BlockSpec(memory_space=pltpu.HBM)] * len(inputs),
        scratch=[pltpu.SemaphoreType.DMA((len(inputs),))],
    )
    before = from_behind(tails, "ctx", 1)
    if square:
        near = swap(out_weight, 2, 4)
    tiles = channels // TILE
    heads, query, gated, decay, wide, response, lift = call(
        prepare_kernel,
        [
            ((3, ROWS, channels), F32),
            ((length, channels), BF16),
            ((length, channels), F32),
            ((groups * poles, length), BF16),
            ((poles, channels), F32),
            ((groups, length), F32),
            ((length, groups * poles), BF16),
        ],
        "prepare",
        streams, conv_weight, rates, residues,
        scratch=[pltpu.VMEM((3 * tiles, ROWS + length, TILE), F32)],
        flops=10**9,
    )
    ends, sent, gated, first = call(
        states_kernel,
        [((poles, channels), F32), ((poles, channels), BF16), ((length, channels), BF16), ((ROWS, channels), F32)],
        "states",
        before, heads, conv_weight, gated, decay,
        scratch=[pltpu.VMEM((3 * tiles, 2 * ROWS, TILE), F32)],
    )
    me = lax.axis_index("ctx").astype(jnp.int32)

    def within(half):
        return call(
            functools.partial(inside_kernel, half * tiles // 2),
            [((length, channels // 2), F32)],
            "inside",
            gated, skip, response,
            scratch=[
                pltpu.VMEM((length // STRIP, channels // 2, STRIP), BF16),
                pltpu.VMEM((channels // 2, length), F32),
            ],
            flops=10**9,
        )[0]

    bases, entering = [], jnp.zeros((poles, channels), F32)
    steps = (blocks - 1).bit_length()
    for bit in range(steps):
        arrived = swap(sent, 1 << bit)
        if bit < steps - 1:
            ends, sent, entering = call(
                functools.partial(join_kernel, bit),
                [((poles, channels), F32), ((poles, channels), BF16), ((poles, channels), F32)],
                "join",
                me[None], arrived, ends, entering, wide,
                specs=[pl.BlockSpec(memory_space=pltpu.SMEM)] + whole(4),
            )
        if bit == steps - 2:
            bases.append(within(0))
            sent = after(sent, bases[0])
    bases.append(within(1))
    if square:
        other_near = swap(after(out_weight, (bases[-1], near)), 4, 2)
    core = me % CORES
    smem = [pl.BlockSpec(memory_space=pltpu.SMEM)]

    def finished(half):
        return call(
            functools.partial(finish_kernel, steps - 1),
            [((length, share), BF16)],
            "finish",
            jnp.stack([me, half]), arrived, entering, wide, lift, query, first, *bases,
            specs=smem + whole(8),
            flops=3 * 10**9,
            scratch=[pltpu.VMEM((poles, share), F32)],
        )[0]

    if rows == share:
        other, mine = finished(1 - core), finished(core)
    else:
        mixed = jnp.concatenate([finished(jnp.full_like(me, half)) for half in range(CORES)], axis=1)
        by_core = mixed.reshape(length, share // rows, CORES, rows).transpose(2, 0, 1, 3)
        by_core = by_core.reshape(CORES, length, share)
        mine = lax.dynamic_index_in_dim(by_core, core, 0, keepdims=False)
        other = lax.dynamic_index_in_dim(by_core, 1 - core, 0, keepdims=False)
    block = jnp.concatenate([mine, swap(other, 1)], axis=0)
    layer = lax.axis_index("tp").astype(jnp.int32)
    beside, across = trade(block, 1), trade(block, 3)
    beyond = trade(after(across, other_near) if square else across, 1)
    if square:
        diagonal = swap(after(near, block), 4, 2)
        weight = (out_weight, near, other_near, diagonal)
    else:
        core_groups = [list(range(core, blocks, CORES)) for core in range(CORES)]
        weight = lax.all_gather(out_weight, "ctx", axis=0, axis_index_groups=core_groups)
        weight = tuple(weight.reshape(layers, share, features))
    first_row = jnp.where(core == 0, 1, 2)
    chip = me // CORES
    place = [chip, chip ^ first_row, chip ^ (3 - first_row), chip ^ 3] if square else [jnp.full_like(me, at) for at in range(4)]
    at = jnp.stack([layer] + place)
    *sooner, latest = weight
    total, last_rows, last_block = call(
        early_kernel,
        [((CORES * length, features), F32), ((share, features), BF16), (block.shape, BF16)],
        "early",
        at, block, beside, across,
        *(pltpu.with_memory_space_constraint(part, pltpu.HBM) for part in sooner),
        specs=smem + whole(3) + [pl.BlockSpec(memory_space=pltpu.HBM)] * len(sooner),
        scratch=[
            pltpu.VMEM((layers,) + block.shape, BF16),
            pltpu.VMEM((len(sooner), share, features), BF16),
            pltpu.SemaphoreType.DMA((len(sooner) + 1,)),
        ],
        flops=10**10,
    )
    total, last_rows = call(
        joined_kernel,
        [((CORES * length, features), F32), ((share, features), BF16)],
        "joined",
        at, total, last_rows, last_block, latest,
        specs=smem + whole(4),
        flops=0,
    )
    sides = []
    for side, kind in ((1, BF16), (0, F32)):
        sides += call(
            functools.partial(late_kernel, side * length),
            [((length, features), kind)],
            "late",
            beyond, total, last_rows,
            flops=0,
        )
    other, mine = sides
    other = swap(other, 1)
    return (mine + other.astype(F32)).astype(BF16)


def solution(mesh):
    return jax.shard_map(
        local,
        mesh=mesh,
        in_specs=(
            P(None, "tp", "ctx"),
            P(None, None, "tp"),
            P("tp", None),
            P("tp", None),
            P("tp"),
            P("ctx", "tp"),
        ),
        out_specs=P("ctx", "tp"),
        check_vma=False,
    )
```

```python
import functools
import math

import jax
import jax.numpy as jnp
from jax import lax
from jax.experimental import pallas as pl
from jax.experimental.pallas import tpu as pltpu
from jax.sharding import PartitionSpec as P

F32 = jnp.float32
BF16 = jnp.bfloat16
ROWS = 8
TILE = 128
CORES = 2
COLUMNS = 256
STRIP = 32
VMEM_LIMIT = 24 * 1024 * 1024
PLAIN = (((1,), (0,)), ((), ()))
CONTRACT_LANES = (((1,), (1,)), ((), ()))


def from_behind(value, axis, steps):
    count = lax.axis_size(axis)
    leading, last = (max(0, -steps), min(count, count - steps))
    return lax.ppermute(value, axis, [(source, source + steps) for source in range(leading, last)])


def dot(left, right, dims=PLAIN):
    return lax.dot_general(left, right, dims, preferred_element_type=F32)


def halves(value):
    high = value.astype(BF16)
    return high, (value - high.astype(F32)).astype(BF16)


def iota(shape, axis):
    return lax.broadcasted_iota(jnp.int32, shape, axis)


def identity(size):
    return (iota((size, size), 0) == iota((size, size), 1)).astype(BF16)


def turned(value, unit):
    return dot(unit, value, CONTRACT_LANES)


def whole(count):
    return [pl.BlockSpec(memory_space=pltpu.VMEM)] * count


def call(kernel, outs, name, *operands, specs=None, scratch=(), flops=10**8, aliases=None, out_specs=None):
    return pl.pallas_call(
        kernel,
        out_shape=tuple(jax.ShapeDtypeStruct(*out) for out in outs),
        in_specs=whole(len(operands)) if specs is None else specs,
        out_specs=tuple(out_specs or whole(len(outs))),
        scratch_shapes=scratch,
        input_output_aliases=aliases or {},
        compiler_params=pltpu.CompilerParams(vmem_limit_bytes=VMEM_LIMIT),
        cost_estimate=pl.CostEstimate(flops=flops, bytes_accessed=flops // 100, transcendentals=0),
        name=name,
    )(*operands)


def tile_of(index, size=TILE):
    return pl.ds(pl.multiple_of(index * size, size), size)


def unrolled(count, body):
    def step(index, carry):
        body(index)
        return carry

    lax.fori_loop(0, count, step, 0, unroll=math.gcd(count, 4))


def tails_kernel(*refs):
    count = len(refs) // 2 - 1
    sources, tails_ref, fetched, sems = refs[:count], refs[count], refs[count + 1 : -1], refs[-1]
    copies = [
        pltpu.make_async_copy(source, target, sems.at[at]) for at, (source, target) in enumerate(zip(sources, fetched))
    ]
    for copy in copies:
        copy.start()
    streams_ref = fetched[0]
    length = streams_ref.shape[2]
    pick = (iota((2 * ROWS, length), 1) == iota((2 * ROWS, length), 0) + (length - ROWS)).astype(BF16)
    copies[0].wait()
    for stream in range(streams_ref.shape[0]):
        rows = dot(pick, streams_ref[stream], CONTRACT_LANES)
        tails_ref[stream] = rows[:ROWS].astype(BF16)
    for copy in copies[1:]:
        copy.wait()


def short_conv(stream, chans, rows, padded, taps_ref):
    total = None
    for shift in range(taps_ref.shape[1]):
        term = taps_ref[stream, shift : shift + 1, chans] * padded[pl.ds(ROWS - shift, rows), :]
        total = term if total is None else total + term
    return total


def prepare_kernel(
    streams_ref, taps_ref, rates_ref, residues_ref,
    heads_ref, query_ref, gated_ref, decay_ref, step_ref, response_ref, lift_ref, padded_ref,
):
    channels, length = streams_ref.shape[1:]
    poles, groups = rates_ref.shape
    width = channels // groups
    in_tile = TILE // width
    unit = identity(length)
    lag = (length - 1) - iota((poles, length), 1).astype(F32)
    owner = iota((poles, TILE), 1) // width
    time = iota((poles, length), 1).astype(F32)
    member = (iota((in_tile, in_tile * poles), 1) // poles == iota((in_tile, in_tile * poles), 0)).astype(BF16)
    scale = residues_ref[...] * jnp.sqrt(2.0 * rates_ref[...]) / math.sqrt(poles)

    def turn(index):
        chans = tile_of(index)
        for stream in range(3):
            tokens = turned(streams_ref[stream, chans, :], unit)
            padded_ref[index * 3 + stream, :ROWS, :] = jnp.zeros((ROWS, TILE), F32)
            padded_ref[index * 3 + stream, ROWS:, :] = tokens
            heads_ref[stream, :, chans] = tokens[:ROWS]

    def factors(index):
        shift = groups - index * in_tile
        rates = pltpu.roll(rates_ref[...], shift, 1)
        coef = pltpu.roll(scale, shift, 1)
        decay, impulse, lift = [], [], []
        wide = jnp.zeros((poles, TILE), F32)
        for g in range(in_tile):
            rate = jnp.broadcast_to(rates[:, g : g + 1], (poles, length))
            decay.append(jnp.exp(-rate * lag))
            amplitude = jnp.broadcast_to(coef[:, g : g + 1], (poles, length))
            impulse.append(amplitude * jnp.exp(-rate * time))
            lift.append(amplitude * jnp.exp(-rate * (time + 1.0)))
            wide = jnp.where(owner == g, rate[:, :TILE], wide)
        step_ref[:, tile_of(index)] = -wide * length
        states = tile_of(index, in_tile * poles)
        decay_ref[states, :] = jnp.concatenate(decay, axis=0).astype(BF16)
        high, low = halves(jnp.concatenate(impulse, axis=0))
        response_ref[pl.ds(pl.multiple_of(index * in_tile, in_tile), in_tile), :] = dot(member, high) + dot(member, low)
        lift_ref[:, states] = turned(jnp.concatenate(lift, axis=0).astype(BF16), unit).astype(BF16)

    def filters(index):
        chans = tile_of(index)
        query, left, right = (
            short_conv(stream, chans, length, padded_ref.at[index * 3 + stream], taps_ref) for stream in range(3)
        )
        query_ref[:, chans] = query.astype(BF16)
        gated_ref[:, chans] = left * right

    unrolled(channels // TILE, turn)
    unrolled(channels // TILE, factors)
    unrolled(channels // TILE, filters)


def states_kernel(
    before_ref, heads_ref, taps_ref, gated_ref, decay_ref, ends_ref, sent_ref, final_ref, first_ref, padded_ref
):
    length, channels = gated_ref.shape
    poles = ends_ref.shape[0]
    in_tile = decay_ref.shape[0] // poles * TILE // channels
    owner = iota((poles, TILE), 1) // (TILE // in_tile)

    def begin(index):
        chans = tile_of(index)
        for stream in range(3):
            padded_ref[index * 3 + stream, :ROWS, :] = before_ref[stream, :, chans].astype(F32)
            padded_ref[index * 3 + stream, ROWS:, :] = heads_ref[stream, :, chans]
        query, left, right = (
            short_conv(stream, chans, ROWS, padded_ref.at[index * 3 + stream], taps_ref) for stream in range(3)
        )
        first_ref[:, chans] = query
        final_ref[:, chans] = jnp.concatenate([left * right, gated_ref[ROWS:, chans]], axis=0).astype(BF16)

    def leave(index):
        chans = tile_of(index)
        gated = final_ref[:, chans]
        states = tile_of(index, in_tile * poles)
        every = dot(decay_ref[states, :], gated)
        ends = jnp.zeros((poles, TILE), F32)
        for g in range(in_tile):
            ends = jnp.where(owner == g, every[g * poles : (g + 1) * poles], ends)
        ends_ref[:, chans] = ends
        sent_ref[:, chans] = ends.astype(BF16)

    unrolled(channels // TILE, begin)
    unrolled(channels // TILE, leave)


def inside_kernel(begin, gated_ref, skip_ref, response_ref, base_ref, signal_ref, sum_ref):
    length = gated_ref.shape[0]
    width = gated_ref.shape[1] // response_ref.shape[0]
    in_tile = TILE // width
    tiles = base_ref.shape[1] // TILE
    strip = STRIP
    unit = identity(length)
    lane = iota((width, length), 1)
    causal = iota((strip, length), 1) >= iota((strip, length), 0)

    def signals(index):
        gated = gated_ref[:, tile_of(begin + index)]
        for at in range(length // strip):
            piece = turned(gated[at * strip : (at + 1) * strip], unit).astype(BF16)
            signal_ref[at, tile_of(index), :] = piece

    def products(index):
        for pair in range(in_tile // 2):
            group = index * in_tile + 2 * pair
            responses = response_ref[pl.ds(begin * in_tile + group, 2), :]
            blocks = []
            for g in range(2):
                spread = jnp.broadcast_to(responses[g : g + 1], (strip, length))
                shifted = pltpu.roll(spread, 0, 1, stride=1, stride_axis=0)
                blocks.append(jnp.where(causal, shifted, 0.0).astype(BF16))
            rows = pl.ds(pl.multiple_of(group * width, 2 * width), 2 * width)
            signal = jnp.concatenate([signal_ref[at, rows, :] for at in range(length // strip)], axis=0)
            both = dot(signal, jnp.concatenate(blocks, axis=1))
            for g in range(2):
                total = None
                for at in range(length // strip):
                    first = at * 2 * width + g * width
                    term = both[first : first + width, g * length : (g + 1) * length]
                    if at:
                        term = jnp.where(lane >= at * strip, pltpu.roll(term, at * strip, 1), 0.0)
                    total = term if total is None else total + term
                sum_ref[pl.ds(pl.multiple_of((group + g) * width, width), width), :] = total

    def back(index):
        chans = tile_of(index)
        here = tile_of(begin + index)
        high, low = halves(sum_ref[chans, :])
        direct = skip_ref[:, here] * gated_ref[:, here].astype(F32)
        base_ref[:, chans] = turned(high, unit) + turned(low, unit) + direct

    unrolled(tiles, signals)
    unrolled(tiles, products)
    unrolled(tiles, back)


def join_kernel(bit, me_ref, arrived_ref, ends_ref, entering_ref, wide_ref, sent_ref, later_ref, *joined_ref):
    me = me_ref[0]
    high = (me >> bit) % 2 == 1
    arrived = arrived_ref[...].astype(F32)
    wide = wide_ref[...]
    over = jnp.exp(wide * (1 << bit))
    joined = jnp.where(high, over * arrived + ends_ref[...], over * ends_ref[...] + arrived)
    sent_ref[...] = joined.astype(BF16)
    for ref in joined_ref:
        ref[...] = joined
    before = (me % (1 << bit)).astype(F32)
    later_ref[...] = entering_ref[...] + jnp.where(high, jnp.exp(wide * before) * arrived, 0.0)


def finish_kernel(
    bit, at_ref, arrived_ref, entering_ref, wide_ref, lift_ref, query_ref, first_ref, left_ref, right_ref, mixed_ref, state_ref
):
    length, share = mixed_ref.shape
    poles, channels = wide_ref.shape
    in_tile = lift_ref.shape[1] // poles * TILE // channels
    me, half = at_ref[0], at_ref[1]
    here = tile_of(half, share)
    high = (me >> bit) % 2 == 1
    before = (me % (1 << bit)).astype(F32)
    reached = jnp.exp(wide_ref[:, here] * before) * arrived_ref[:, here].astype(F32)
    state_ref[...] = entering_ref[:, here] + jnp.where(high, reached, 0.0)
    owner = iota((poles, TILE), 1) // (TILE // in_tile)

    def tile(index):
        at = half * (share // TILE) + index
        chans = tile_of(at)
        entering = state_ref[:, tile_of(index)]
        apart = jnp.concatenate([jnp.where(owner == g, entering, 0.0) for g in range(in_tile)], axis=0)
        carried = dot(lift_ref[:, tile_of(at, in_tile * poles)], apart.astype(BF16))
        query = jnp.concatenate([first_ref[:, chans], query_ref[:, chans].astype(F32)[ROWS:]], axis=0)
        base = jnp.where(half == 0, left_ref[:, tile_of(index)], right_ref[:, tile_of(index)])
        mixed_ref[:, tile_of(index)] = (query * (base + carried)).astype(BF16)

    unrolled(share // TILE, tile)


def early_kernel(at_ref, own_ref, beside_ref, across_ref, *rest):
    *weight_hbms, total_ref, rows_ref, block_ref, layers_ref, weight_ref, sems = rest
    count = len(weight_hbms)
    layer = at_ref[0]
    last = layer ^ 2
    copies = [pltpu.make_async_copy(hbm, weight_ref.at[at], sems.at[at]) for at, hbm in enumerate(weight_hbms)]
    fetches = [pltpu.make_async_copy(hbm, rows_ref, sems.at[count]) for hbm in weight_hbms]
    for copy in copies:
        copy.start()
    for at, fetch in enumerate(fetches):
        pl.when(at_ref[1 + at] == last)(fetch.start)
    for bits, ref in ((0, own_ref), (1, beside_ref), (3, across_ref)):
        layers_ref[layer ^ bits] = ref[...]
    layers_ref[last] = jnp.zeros_like(own_ref)
    block_ref[...] = layers_ref[at_ref[1 + count]]
    for at, copy in enumerate(copies):
        copy.wait()
        block = layers_ref[at_ref[1 + at]]
        for column in range(0, total_ref.shape[1], COLUMNS):
            columns = slice(column, column + COLUMNS)
            term = dot(block, weight_ref[at, :, columns])
            total_ref[:, columns] = total_ref[:, columns] + term if at else term
    for at, fetch in enumerate(fetches):
        pl.when(at_ref[1 + at] == last)(fetch.wait)


def joined_kernel(at_ref, total_ref, rows_ref, block_ref, weight_ref, out_ref, last_ref, sem):
    del rows_ref
    latest = at_ref[4] == at_ref[0] ^ 2
    keep = pltpu.make_async_copy(weight_ref, last_ref, sem)
    pl.when(latest)(keep.start)
    out_ref[...] = total_ref[...] + dot(block_ref[...], weight_ref[...])
    pl.when(latest)(keep.wait)


def late_kernel(first, beyond_ref, total_ref, rows_ref, out_ref):
    tokens = pl.ds(first, out_ref.shape[0])
    out_ref[...] = (total_ref[tokens, :] + dot(beyond_ref[tokens, :], rows_ref[...])).astype(out_ref.dtype)


def swap(value, *bits):
    count = lax.axis_size("ctx")
    pairs = [(source, source ^ bits[source % len(bits)]) for source in range(count)]
    return lax.ppermute(value, "ctx", pairs)


def after(value, earlier):
    return lax.optimization_barrier((value, earlier))[0]


def trade(value, bits):
    count = lax.axis_size("tp")
    return lax.ppermute(value, "tp", [(source, source ^ bits) for source in range(count)])


def local(streams, conv_weight, rates, residues, skip, out_weight):
    channels, length = streams.shape[1:]
    groups, poles = rates.shape
    blocks, layers = lax.axis_size("ctx"), lax.axis_size("tp")
    rows, features = out_weight.shape
    share = channels // CORES
    square = blocks == 8 and rows == share

    inputs = (streams, conv_weight, rates.T, residues.T, skip[None, :])
    tails, streams, conv_weight, rates, residues, skip = call(
        tails_kernel,
        [((3, ROWS, channels), BF16)] + [(part.shape, part.dtype) for part in inputs],
        "tails",
        *(pltpu.with_memory_space_constraint(part, pltpu.HBM) for part in inputs),
        specs=[pl.BlockSpec(memory_space=pltpu.HBM)] * len(inputs),
        scratch=[pltpu.SemaphoreType.DMA((len(inputs),))],
    )
    before = from_behind(tails, "ctx", 1)
    if square:
        near = swap(out_weight, 2, 4)
    tiles = channels // TILE
    heads, query, gated, decay, wide, response, lift = call(
        prepare_kernel,
        [
            ((3, ROWS, channels), F32),
            ((length, channels), BF16),
            ((length, channels), F32),
            ((groups * poles, length), BF16),
            ((poles, channels), F32),
            ((groups, length), F32),
            ((length, groups * poles), BF16),
        ],
        "prepare",
        streams, conv_weight, rates, residues,
        scratch=[pltpu.VMEM((3 * tiles, ROWS + length, TILE), F32)],
        flops=10**9,
    )
    ends, sent, gated, first = call(
        states_kernel,
        [((poles, channels), F32), ((poles, channels), BF16), ((length, channels), BF16), ((ROWS, channels), F32)],
        "states",
        before, heads, conv_weight, gated, decay,
        scratch=[pltpu.VMEM((3 * tiles, 2 * ROWS, TILE), F32)],
    )
    me = lax.axis_index("ctx").astype(jnp.int32)

    def within(half):
        return call(
            functools.partial(inside_kernel, half * tiles // 2),
            [((length, channels // 2), F32)],
            "inside",
            gated, skip, response,
            scratch=[
                pltpu.VMEM((length // STRIP, channels // 2, STRIP), BF16),
                pltpu.VMEM((channels // 2, length), F32),
            ],
            flops=10**9,
        )[0]

    bases, ends, entering = [], [ends], jnp.zeros((poles, channels), F32)
    steps = (blocks - 1).bit_length()
    for bit in range(steps):
        arrived = swap(sent, 1 << bit)
        if bit < steps - 1:
            outs = [((poles, channels), BF16), ((poles, channels), F32), ((poles, channels), F32)]
            sent, entering, *ends = call(
                functools.partial(join_kernel, bit),
                outs[: 2 if bit == steps - 2 else 3],
                "join",
                me[None], arrived, ends[0], entering, wide,
                specs=[pl.BlockSpec(memory_space=pltpu.SMEM)] + whole(4),
            )
        if bit == steps - 2:
            bases.append(within(0))
            sent = after(sent, bases[0])
    bases.append(within(1))
    if square:
        other_near = swap(after(out_weight, (bases[-1], near)), 4, 2)
    core = me % CORES
    smem = [pl.BlockSpec(memory_space=pltpu.SMEM)]

    def finished(half):
        return call(
            functools.partial(finish_kernel, steps - 1),
            [((length, share), BF16)],
            "finish",
            jnp.stack([me, half]), arrived, entering, wide, lift, query, first, *bases,
            specs=smem + whole(8),
            flops=3 * 10**9,
            scratch=[pltpu.VMEM((poles, share), F32)],
        )[0]

    if rows == share:
        other, mine = finished(1 - core), finished(core)
    else:
        mixed = jnp.concatenate([finished(jnp.full_like(me, half)) for half in range(CORES)], axis=1)
        by_core = mixed.reshape(length, share // rows, CORES, rows).transpose(2, 0, 1, 3)
        by_core = by_core.reshape(CORES, length, share)
        mine = lax.dynamic_index_in_dim(by_core, core, 0, keepdims=False)
        other = lax.dynamic_index_in_dim(by_core, 1 - core, 0, keepdims=False)
    block = jnp.concatenate([mine, swap(other, 1)], axis=0)
    layer = lax.axis_index("tp").astype(jnp.int32)
    beside, across = trade(block, 1), trade(block, 3)
    beyond = trade(after(across, other_near) if square else across, 1)
    if square:
        diagonal = swap(after(near, block), 4, 2)
        weight = (out_weight, near, other_near, diagonal)
    else:
        core_groups = [list(range(core, blocks, CORES)) for core in range(CORES)]
        weight = lax.all_gather(out_weight, "ctx", axis=0, axis_index_groups=core_groups)
        weight = tuple(weight.reshape(layers, share, features))
    first_row = jnp.where(core == 0, 1, 2)
    chip = me // CORES
    place = [chip, chip ^ first_row, chip ^ (3 - first_row), chip ^ 3] if square else [jnp.full_like(me, at) for at in range(4)]
    at = jnp.stack([layer] + place)
    *sooner, latest = weight
    total, last_rows, last_block = call(
        early_kernel,
        [((CORES * length, features), F32), ((share, features), BF16), (block.shape, BF16)],
        "early",
        at, block, beside, across,
        *(pltpu.with_memory_space_constraint(part, pltpu.HBM) for part in sooner),
        specs=smem + whole(3) + [pl.BlockSpec(memory_space=pltpu.HBM)] * len(sooner),
        scratch=[
            pltpu.VMEM((layers,) + block.shape, BF16),
            pltpu.VMEM((len(sooner), share, features), BF16),
            pltpu.SemaphoreType.DMA((len(sooner) + 1,)),
        ],
        flops=10**10,
    )
    anywhere = [pl.BlockSpec(memory_space=pl.ANY)]
    total, last_rows = call(
        joined_kernel,
        [((CORES * length, features), F32), ((share, features), BF16)],
        "joined",
        at, total, last_rows, last_block, latest,
        specs=smem + whole(1) + anywhere + whole(2),
        out_specs=whole(1) + anywhere,
        scratch=[pltpu.SemaphoreType.DMA],
        flops=0,
        aliases={2: 1},
    )
    sides = []
    for side, kind in ((1, BF16), (0, F32)):
        sides += call(
            functools.partial(late_kernel, side * length),
            [((length, features), kind)],
            "late",
            beyond, total, last_rows,
            flops=0,
        )
    other, mine = sides
    other = swap(other, 1)
    return (mine + other.astype(F32)).astype(BF16)


def solution(mesh):
    return jax.shard_map(
        local,
        mesh=mesh,
        in_specs=(
            P(None, "tp", "ctx"),
            P(None, None, "tp"),
            P("tp", None),
            P("tp", None),
            P("tp"),
            P("ctx", "tp"),
        ),
        out_specs=P("ctx", "tp"),
        check_vma=False,
    )
```

```python
import functools
import math

import jax
import jax.numpy as jnp
from jax import lax
from jax.experimental import pallas as pl
from jax.experimental.pallas import tpu as pltpu
from jax.sharding import PartitionSpec as P

F32 = jnp.float32
BF16 = jnp.bfloat16
ROWS = 8
TILE = 128
CORES = 2
COLUMNS = 256
STRIP = 32
VMEM_LIMIT = 24 * 1024 * 1024
PLAIN = (((1,), (0,)), ((), ()))
CONTRACT_LANES = (((1,), (1,)), ((), ()))


def from_behind(value, axis, steps):
    count = lax.axis_size(axis)
    leading, last = (max(0, -steps), min(count, count - steps))
    return lax.ppermute(value, axis, [(source, source + steps) for source in range(leading, last)])


def dot(left, right, dims=PLAIN):
    return lax.dot_general(left, right, dims, preferred_element_type=F32)


def halves(value):
    high = value.astype(BF16)
    return high, (value - high.astype(F32)).astype(BF16)


def iota(shape, axis):
    return lax.broadcasted_iota(jnp.int32, shape, axis)


def identity(size):
    return (iota((size, size), 0) == iota((size, size), 1)).astype(BF16)


def turned(value, unit):
    return dot(unit, value, CONTRACT_LANES)


def whole(count):
    return [pl.BlockSpec(memory_space=pltpu.VMEM)] * count


def call(kernel, outs, name, *operands, specs=None, scratch=(), flops=10**8, aliases=None, out_specs=None):
    return pl.pallas_call(
        kernel,
        out_shape=tuple(jax.ShapeDtypeStruct(*out) for out in outs),
        in_specs=whole(len(operands)) if specs is None else specs,
        out_specs=tuple(out_specs or whole(len(outs))),
        scratch_shapes=scratch,
        input_output_aliases=aliases or {},
        compiler_params=pltpu.CompilerParams(vmem_limit_bytes=VMEM_LIMIT),
        cost_estimate=pl.CostEstimate(flops=flops, bytes_accessed=flops // 100, transcendentals=0),
        name=name,
    )(*operands)


def tile_of(index, size=TILE):
    return pl.ds(pl.multiple_of(index * size, size), size)


def unrolled(count, body):
    def step(index, carry):
        body(index)
        return carry

    lax.fori_loop(0, count, step, 0, unroll=math.gcd(count, 4))


def tails_kernel(*refs):
    count = len(refs) // 2 - 1
    sources, tails_ref, fetched, sems = refs[:count], refs[count], refs[count + 1 : -1], refs[-1]
    copies = [
        pltpu.make_async_copy(source, target, sems.at[at]) for at, (source, target) in enumerate(zip(sources, fetched))
    ]
    for copy in copies:
        copy.start()
    streams_ref = fetched[0]
    length = streams_ref.shape[2]
    pick = (iota((2 * ROWS, length), 1) == iota((2 * ROWS, length), 0) + (length - ROWS)).astype(BF16)
    copies[0].wait()
    for stream in range(streams_ref.shape[0]):
        rows = dot(pick, streams_ref[stream], CONTRACT_LANES)
        tails_ref[stream] = rows[:ROWS].astype(BF16)
    for copy in copies[1:]:
        copy.wait()


def short_conv(stream, chans, rows, padded, taps_ref):
    total = None
    for shift in range(taps_ref.shape[1]):
        term = taps_ref[stream, shift : shift + 1, chans] * padded[pl.ds(ROWS - shift, rows), :]
        total = term if total is None else total + term
    return total


def prepare_kernel(
    streams_ref, taps_ref, rates_ref, residues_ref,
    heads_ref, query_ref, gated_ref, decay_ref, step_ref, response_ref, lift_ref, padded_ref,
):
    channels, length = streams_ref.shape[1:]
    poles, groups = rates_ref.shape
    width = channels // groups
    in_tile = TILE // width
    unit = identity(length)
    lag = (length - 1) - iota((poles, length), 1).astype(F32)
    owner = iota((poles, TILE), 1) // width
    time = iota((poles, length), 1).astype(F32)
    member = (iota((in_tile, in_tile * poles), 1) // poles == iota((in_tile, in_tile * poles), 0)).astype(BF16)
    scale = residues_ref[...] * jnp.sqrt(2.0 * rates_ref[...]) / math.sqrt(poles)

    def turn(index):
        chans = tile_of(index)
        for stream in range(3):
            tokens = turned(streams_ref[stream, chans, :], unit)
            padded_ref[index * 3 + stream, :ROWS, :] = jnp.zeros((ROWS, TILE), F32)
            padded_ref[index * 3 + stream, ROWS:, :] = tokens
            heads_ref[stream, :, chans] = tokens[:ROWS]

    def factors(index):
        shift = groups - index * in_tile
        rates = pltpu.roll(rates_ref[...], shift, 1)
        coef = pltpu.roll(scale, shift, 1)
        decay, impulse, lift = [], [], []
        wide = jnp.zeros((poles, TILE), F32)
        for g in range(in_tile):
            rate = jnp.broadcast_to(rates[:, g : g + 1], (poles, length))
            decay.append(jnp.exp(-rate * lag))
            amplitude = jnp.broadcast_to(coef[:, g : g + 1], (poles, length))
            impulse.append(amplitude * jnp.exp(-rate * time))
            lift.append(amplitude * jnp.exp(-rate * (time + 1.0)))
            wide = jnp.where(owner == g, rate[:, :TILE], wide)
        step_ref[:, tile_of(index)] = -wide * length
        states = tile_of(index, in_tile * poles)
        decay_ref[states, :] = jnp.concatenate(decay, axis=0).astype(BF16)
        high, low = halves(jnp.concatenate(impulse, axis=0))
        response_ref[pl.ds(pl.multiple_of(index * in_tile, in_tile), in_tile), :] = dot(member, high) + dot(member, low)
        lift_ref[:, states] = turned(jnp.concatenate(lift, axis=0).astype(BF16), unit).astype(BF16)

    def filters(index):
        chans = tile_of(index)
        query, left, right = (
            short_conv(stream, chans, length, padded_ref.at[index * 3 + stream], taps_ref) for stream in range(3)
        )
        query_ref[:, chans] = query.astype(BF16)
        gated_ref[:, chans] = left * right

    unrolled(channels // TILE, turn)
    unrolled(channels // TILE, factors)
    unrolled(channels // TILE, filters)


def states_kernel(
    before_ref, heads_ref, taps_ref, gated_ref, decay_ref, ends_ref, sent_ref, final_ref, first_ref, padded_ref
):
    length, channels = gated_ref.shape
    poles = ends_ref.shape[0]
    in_tile = decay_ref.shape[0] // poles * TILE // channels
    owner = iota((poles, TILE), 1) // (TILE // in_tile)

    def begin(index):
        chans = tile_of(index)
        for stream in range(3):
            padded_ref[index * 3 + stream, :ROWS, :] = before_ref[stream, :, chans].astype(F32)
            padded_ref[index * 3 + stream, ROWS:, :] = heads_ref[stream, :, chans]
        query, left, right = (
            short_conv(stream, chans, ROWS, padded_ref.at[index * 3 + stream], taps_ref) for stream in range(3)
        )
        first_ref[:, chans] = query
        final_ref[:, chans] = jnp.concatenate([left * right, gated_ref[ROWS:, chans]], axis=0).astype(BF16)

    def leave(index):
        chans = tile_of(index)
        gated = final_ref[:, chans]
        states = tile_of(index, in_tile * poles)
        every = dot(decay_ref[states, :], gated)
        ends = jnp.zeros((poles, TILE), F32)
        for g in range(in_tile):
            ends = jnp.where(owner == g, every[g * poles : (g + 1) * poles], ends)
        ends_ref[:, chans] = ends
        sent_ref[:, chans] = ends.astype(BF16)

    unrolled(channels // TILE, begin)
    unrolled(channels // TILE, leave)


def inside_kernel(begin, gated_ref, skip_ref, response_ref, base_ref, signal_ref, sum_ref):
    length = gated_ref.shape[0]
    width = gated_ref.shape[1] // response_ref.shape[0]
    in_tile = TILE // width
    tiles = base_ref.shape[1] // TILE
    strip = STRIP
    unit = identity(length)
    lane = iota((width, length), 1)
    causal = iota((strip, length), 1) >= iota((strip, length), 0)

    def signals(index):
        gated = gated_ref[:, tile_of(begin + index)]
        for at in range(length // strip):
            piece = turned(gated[at * strip : (at + 1) * strip], unit).astype(BF16)
            signal_ref[at, tile_of(index), :] = piece

    def products(index):
        for pair in range(in_tile // 2):
            group = index * in_tile + 2 * pair
            responses = response_ref[pl.ds(begin * in_tile + group, 2), :]
            blocks = []
            for g in range(2):
                spread = jnp.broadcast_to(responses[g : g + 1], (strip, length))
                shifted = pltpu.roll(spread, 0, 1, stride=1, stride_axis=0)
                blocks.append(jnp.where(causal, shifted, 0.0).astype(BF16))
            rows = pl.ds(pl.multiple_of(group * width, 2 * width), 2 * width)
            signal = jnp.concatenate([signal_ref[at, rows, :] for at in range(length // strip)], axis=0)
            both = dot(signal, jnp.concatenate(blocks, axis=1))
            for g in range(2):
                total = None
                for at in range(length // strip):
                    first = at * 2 * width + g * width
                    term = both[first : first + width, g * length : (g + 1) * length]
                    if at:
                        term = jnp.where(lane >= at * strip, pltpu.roll(term, at * strip, 1), 0.0)
                    total = term if total is None else total + term
                sum_ref[pl.ds(pl.multiple_of((group + g) * width, width), width), :] = total

    def back(index):
        chans = tile_of(index)
        here = tile_of(begin + index)
        high, low = halves(sum_ref[chans, :])
        direct = skip_ref[:, here] * gated_ref[:, here].astype(F32)
        base_ref[:, chans] = turned(high, unit) + turned(low, unit) + direct

    unrolled(tiles, signals)
    unrolled(tiles, products)
    unrolled(tiles, back)


def join_kernel(bit, me_ref, arrived_ref, ends_ref, entering_ref, wide_ref, sent_ref, later_ref, *joined_ref):
    me = me_ref[0]
    high = (me >> bit) % 2 == 1
    arrived = arrived_ref[...].astype(F32)
    wide = wide_ref[...]
    over = jnp.exp(wide * (1 << bit))
    joined = jnp.where(high, over * arrived + ends_ref[...], over * ends_ref[...] + arrived)
    sent_ref[...] = joined.astype(BF16)
    for ref in joined_ref:
        ref[...] = joined
    before = (me % (1 << bit)).astype(F32)
    later_ref[...] = entering_ref[...] + jnp.where(high, jnp.exp(wide * before) * arrived, 0.0)


def finish_kernel(
    bit, at_ref, arrived_ref, entering_ref, wide_ref, lift_ref, query_ref, first_ref, left_ref, right_ref, mixed_ref, state_ref
):
    length, share = mixed_ref.shape
    poles, channels = wide_ref.shape
    in_tile = lift_ref.shape[1] // poles * TILE // channels
    me, half = at_ref[0], at_ref[1]
    here = tile_of(half, share)
    high = (me >> bit) % 2 == 1
    before = (me % (1 << bit)).astype(F32)
    reached = jnp.exp(wide_ref[:, here] * before) * arrived_ref[:, here].astype(F32)
    state_ref[...] = entering_ref[:, here] + jnp.where(high, reached, 0.0)
    owner = iota((poles, TILE), 1) // (TILE // in_tile)

    def tile(index):
        at = half * (share // TILE) + index
        chans = tile_of(at)
        entering = state_ref[:, tile_of(index)]
        apart = jnp.concatenate([jnp.where(owner == g, entering, 0.0) for g in range(in_tile)], axis=0)
        carried = dot(lift_ref[:, tile_of(at, in_tile * poles)], apart.astype(BF16))
        query = jnp.concatenate([first_ref[:, chans], query_ref[:, chans].astype(F32)[ROWS:]], axis=0)
        base = jnp.where(half == 0, left_ref[:, tile_of(index)], right_ref[:, tile_of(index)])
        mixed_ref[:, tile_of(index)] = (query * (base + carried)).astype(BF16)

    unrolled(share // TILE, tile)


def early_kernel(at_ref, own_ref, beside_ref, across_ref, *rest):
    *weight_hbms, total_ref, rows_ref, block_ref, layers_ref, weight_ref, sems = rest
    count = len(weight_hbms)
    layer = at_ref[0]
    last = layer ^ 2
    copies = [pltpu.make_async_copy(hbm, weight_ref.at[at], sems.at[at]) for at, hbm in enumerate(weight_hbms)]
    fetches = [pltpu.make_async_copy(hbm, rows_ref, sems.at[count]) for hbm in weight_hbms]
    for copy in copies:
        copy.start()
    for at, fetch in enumerate(fetches):
        pl.when(at_ref[1 + at] == last)(fetch.start)
    for bits, ref in ((0, own_ref), (1, beside_ref), (3, across_ref)):
        layers_ref[layer ^ bits] = ref[...]
    layers_ref[last] = jnp.zeros_like(own_ref)
    block_ref[...] = layers_ref[at_ref[1 + count]]
    for at, copy in enumerate(copies):
        copy.wait()
        block = layers_ref[at_ref[1 + at]]
        for column in range(0, total_ref.shape[1], COLUMNS):
            columns = slice(column, column + COLUMNS)
            term = dot(block, weight_ref[at, :, columns])
            total_ref[:, columns] = total_ref[:, columns] + term if at else term
    for at, fetch in enumerate(fetches):
        pl.when(at_ref[1 + at] == last)(fetch.wait)


def joined_kernel(total_ref, block_ref, weight_ref, out_ref):
    out_ref[...] = total_ref[...] + dot(block_ref[...], weight_ref[...])


def keep_kernel(at_ref, rows_ref, weight_ref, last_ref, sem):
    del rows_ref
    latest = at_ref[4] == at_ref[0] ^ 2
    copy = pltpu.make_async_copy(weight_ref, last_ref, sem)
    pl.when(latest)(copy.start)
    pl.when(latest)(copy.wait)


def late_kernel(first, beyond_ref, total_ref, rows_ref, out_ref):
    tokens = pl.ds(first, out_ref.shape[0])
    out_ref[...] = (total_ref[tokens, :] + dot(beyond_ref[tokens, :], rows_ref[...])).astype(out_ref.dtype)


def swap(value, *bits):
    count = lax.axis_size("ctx")
    pairs = [(source, source ^ bits[source % len(bits)]) for source in range(count)]
    return lax.ppermute(value, "ctx", pairs)


def after(value, earlier):
    return lax.optimization_barrier((value, earlier))[0]


def trade(value, bits):
    count = lax.axis_size("tp")
    return lax.ppermute(value, "tp", [(source, source ^ bits) for source in range(count)])


def local(streams, conv_weight, rates, residues, skip, out_weight):
    channels, length = streams.shape[1:]
    groups, poles = rates.shape
    blocks, layers = lax.axis_size("ctx"), lax.axis_size("tp")
    rows, features = out_weight.shape
    share = channels // CORES
    square = blocks == 8 and rows == share

    inputs = (streams, conv_weight, rates.T, residues.T, skip[None, :])
    tails, streams, conv_weight, rates, residues, skip = call(
        tails_kernel,
        [((3, ROWS, channels), BF16)] + [(part.shape, part.dtype) for part in inputs],
        "tails",
        *(pltpu.with_memory_space_constraint(part, pltpu.HBM) for part in inputs),
        specs=[pl.BlockSpec(memory_space=pltpu.HBM)] * len(inputs),
        scratch=[pltpu.SemaphoreType.DMA((len(inputs),))],
    )
    before = from_behind(tails, "ctx", 1)
    if square:
        near = swap(out_weight, 2, 4)
    tiles = channels // TILE
    heads, query, gated, decay, wide, response, lift = call(
        prepare_kernel,
        [
            ((3, ROWS, channels), F32),
            ((length, channels), BF16),
            ((length, channels), F32),
            ((groups * poles, length), BF16),
            ((poles, channels), F32),
            ((groups, length), F32),
            ((length, groups * poles), BF16),
        ],
        "prepare",
        streams, conv_weight, rates, residues,
        scratch=[pltpu.VMEM((3 * tiles, ROWS + length, TILE), F32)],
        flops=10**9,
    )
    ends, sent, gated, first = call(
        states_kernel,
        [((poles, channels), F32), ((poles, channels), BF16), ((length, channels), BF16), ((ROWS, channels), F32)],
        "states",
        before, heads, conv_weight, gated, decay,
        scratch=[pltpu.VMEM((3 * tiles, 2 * ROWS, TILE), F32)],
    )
    me = lax.axis_index("ctx").astype(jnp.int32)

    def within(half):
        return call(
            functools.partial(inside_kernel, half * tiles // 2),
            [((length, channels // 2), F32)],
            "inside",
            gated, skip, response,
            scratch=[
                pltpu.VMEM((length // STRIP, channels // 2, STRIP), BF16),
                pltpu.VMEM((channels // 2, length), F32),
            ],
            flops=10**9,
        )[0]

    bases, ends, entering = [], [ends], jnp.zeros((poles, channels), F32)
    steps = (blocks - 1).bit_length()
    for bit in range(steps):
        arrived = swap(sent, 1 << bit)
        if bit < steps - 1:
            outs = [((poles, channels), BF16), ((poles, channels), F32), ((poles, channels), F32)]
            sent, entering, *ends = call(
                functools.partial(join_kernel, bit),
                outs[: 2 if bit == steps - 2 else 3],
                "join",
                me[None], arrived, ends[0], entering, wide,
                specs=[pl.BlockSpec(memory_space=pltpu.SMEM)] + whole(4),
            )
        if bit == steps - 2:
            bases.append(within(0))
            sent = after(sent, bases[0])
    bases.append(within(1))
    if square:
        other_near = swap(after(out_weight, (bases[-1], near)), 4, 2)
    core = me % CORES
    smem = [pl.BlockSpec(memory_space=pltpu.SMEM)]

    def finished(half):
        return call(
            functools.partial(finish_kernel, steps - 1),
            [((length, share), BF16)],
            "finish",
            jnp.stack([me, half]), arrived, entering, wide, lift, query, first, *bases,
            specs=smem + whole(8),
            flops=3 * 10**9,
            scratch=[pltpu.VMEM((poles, share), F32)],
        )[0]

    if rows == share:
        other, mine = finished(1 - core), finished(core)
    else:
        mixed = jnp.concatenate([finished(jnp.full_like(me, half)) for half in range(CORES)], axis=1)
        by_core = mixed.reshape(length, share // rows, CORES, rows).transpose(2, 0, 1, 3)
        by_core = by_core.reshape(CORES, length, share)
        mine = lax.dynamic_index_in_dim(by_core, core, 0, keepdims=False)
        other = lax.dynamic_index_in_dim(by_core, 1 - core, 0, keepdims=False)
    block = jnp.concatenate([mine, swap(other, 1)], axis=0)
    layer = lax.axis_index("tp").astype(jnp.int32)
    beside, across = trade(block, 1), trade(block, 3)
    beyond = trade(after(across, other_near) if square else across, 1)
    if square:
        diagonal = swap(after(near, block), 4, 2)
        weight = (out_weight, near, other_near, diagonal)
    else:
        core_groups = [list(range(core, blocks, CORES)) for core in range(CORES)]
        weight = lax.all_gather(out_weight, "ctx", axis=0, axis_index_groups=core_groups)
        weight = tuple(weight.reshape(layers, share, features))
    first_row = jnp.where(core == 0, 1, 2)
    chip = me // CORES
    place = [chip, chip ^ first_row, chip ^ (3 - first_row), chip ^ 3] if square else [jnp.full_like(me, at) for at in range(4)]
    at = jnp.stack([layer] + place)
    *sooner, latest = weight
    total, last_rows, last_block = call(
        early_kernel,
        [((CORES * length, features), F32), ((share, features), BF16), (block.shape, BF16)],
        "early",
        at, block, beside, across,
        *(pltpu.with_memory_space_constraint(part, pltpu.HBM) for part in sooner),
        specs=smem + whole(3) + [pl.BlockSpec(memory_space=pltpu.HBM)] * len(sooner),
        scratch=[
            pltpu.VMEM((layers,) + block.shape, BF16),
            pltpu.VMEM((len(sooner), share, features), BF16),
            pltpu.SemaphoreType.DMA((len(sooner) + 1,)),
        ],
        flops=10**10,
    )
    (total,) = call(
        joined_kernel, [((CORES * length, features), F32)], "joined", total, last_block, latest, flops=0
    )
    anywhere = [pl.BlockSpec(memory_space=pl.ANY)]
    (last_rows,) = call(
        keep_kernel,
        [((share, features), BF16)],
        "keep",
        at, last_rows, latest,
        specs=smem + anywhere * 2,
        out_specs=anywhere,
        scratch=[pltpu.SemaphoreType.DMA],
        flops=0,
        aliases={1: 0},
    )
    sides = []
    for side, kind in ((1, BF16), (0, F32)):
        sides += call(
            functools.partial(late_kernel, side * length),
            [((length, features), kind)],
            "late",
            beyond, total, last_rows,
            flops=0,
        )
    other, mine = sides
    other = swap(other, 1)
    return (mine + other.astype(F32)).astype(BF16)


def solution(mesh):
    return jax.shard_map(
        local,
        mesh=mesh,
        in_specs=(
            P(None, "tp", "ctx"),
            P(None, None, "tp"),
            P("tp", None),
            P("tp", None),
            P("tp"),
            P("ctx", "tp"),
        ),
        out_specs=P("ctx", "tp"),
        check_vma=False,
    )
```

```python
import functools
import math

import jax
import jax.numpy as jnp
from jax import lax
from jax.experimental import pallas as pl
from jax.experimental.pallas import tpu as pltpu
from jax.sharding import PartitionSpec as P

F32 = jnp.float32
BF16 = jnp.bfloat16
ROWS = 8
TILE = 128
CORES = 2
COLUMNS = 256
STRIP = 32
VMEM_LIMIT = 24 * 1024 * 1024
PLAIN = (((1,), (0,)), ((), ()))
CONTRACT_LANES = (((1,), (1,)), ((), ()))


def from_behind(value, axis, steps):
    count = lax.axis_size(axis)
    leading, last = (max(0, -steps), min(count, count - steps))
    return lax.ppermute(value, axis, [(source, source + steps) for source in range(leading, last)])


def dot(left, right, dims=PLAIN):
    return lax.dot_general(left, right, dims, preferred_element_type=F32)


def halves(value):
    high = value.astype(BF16)
    return high, (value - high.astype(F32)).astype(BF16)


def iota(shape, axis):
    return lax.broadcasted_iota(jnp.int32, shape, axis)


def identity(size):
    return (iota((size, size), 0) == iota((size, size), 1)).astype(BF16)


def turned(value, unit):
    return dot(unit, value, CONTRACT_LANES)


def whole(count):
    return [pl.BlockSpec(memory_space=pltpu.VMEM)] * count


def call(kernel, outs, name, *operands, specs=None, scratch=(), flops=10**8, aliases=None, out_specs=None):
    return pl.pallas_call(
        kernel,
        out_shape=tuple(jax.ShapeDtypeStruct(*out) for out in outs),
        in_specs=whole(len(operands)) if specs is None else specs,
        out_specs=tuple(out_specs or whole(len(outs))),
        scratch_shapes=scratch,
        input_output_aliases=aliases or {},
        compiler_params=pltpu.CompilerParams(vmem_limit_bytes=VMEM_LIMIT),
        cost_estimate=pl.CostEstimate(flops=flops, bytes_accessed=flops // 100, transcendentals=0),
        name=name,
    )(*operands)


def tile_of(index, size=TILE):
    return pl.ds(pl.multiple_of(index * size, size), size)


def unrolled(count, body):
    def step(index, carry):
        body(index)
        return carry

    lax.fori_loop(0, count, step, 0, unroll=math.gcd(count, 4))


def tails_kernel(*refs):
    count = len(refs) // 2 - 1
    sources, tails_ref, fetched, sems = refs[:count], refs[count], refs[count + 1 : -1], refs[-1]
    copies = [
        pltpu.make_async_copy(source, target, sems.at[at]) for at, (source, target) in enumerate(zip(sources, fetched))
    ]
    for copy in copies:
        copy.start()
    streams_ref = fetched[0]
    length = streams_ref.shape[2]
    pick = (iota((2 * ROWS, length), 1) == iota((2 * ROWS, length), 0) + (length - ROWS)).astype(BF16)
    copies[0].wait()
    for stream in range(streams_ref.shape[0]):
        rows = dot(pick, streams_ref[stream], CONTRACT_LANES)
        tails_ref[stream] = rows[:ROWS].astype(BF16)
    for copy in copies[1:]:
        copy.wait()


def short_conv(stream, chans, rows, padded, taps_ref):
    total = None
    for shift in range(taps_ref.shape[1]):
        term = taps_ref[stream, shift : shift + 1, chans] * padded[pl.ds(ROWS - shift, rows), :]
        total = term if total is None else total + term
    return total


def prepare_kernel(
    streams_ref, taps_ref, rates_ref, residues_ref,
    heads_ref, query_ref, gated_ref, decay_ref, step_ref, response_ref, lift_ref, padded_ref,
):
    channels, length = streams_ref.shape[1:]
    poles, groups = rates_ref.shape
    width = channels // groups
    in_tile = TILE // width
    unit = identity(length)
    lag = (length - 1) - iota((poles, length), 1).astype(F32)
    owner = iota((poles, TILE), 1) // width
    time = iota((poles, length), 1).astype(F32)
    member = (iota((in_tile, in_tile * poles), 1) // poles == iota((in_tile, in_tile * poles), 0)).astype(BF16)
    scale = residues_ref[...] * jnp.sqrt(2.0 * rates_ref[...]) / math.sqrt(poles)

    def turn(index):
        chans = tile_of(index)
        for stream in range(3):
            tokens = turned(streams_ref[stream, chans, :], unit)
            padded_ref[index * 3 + stream, :ROWS, :] = jnp.zeros((ROWS, TILE), F32)
            padded_ref[index * 3 + stream, ROWS:, :] = tokens
            heads_ref[stream, :, chans] = tokens[:ROWS]

    def factors(index):
        shift = groups - index * in_tile
        rates = pltpu.roll(rates_ref[...], shift, 1)
        coef = pltpu.roll(scale, shift, 1)
        decay, impulse, lift = [], [], []
        wide = jnp.zeros((poles, TILE), F32)
        for g in range(in_tile):
            rate = jnp.broadcast_to(rates[:, g : g + 1], (poles, length))
            decay.append(jnp.exp(-rate * lag))
            amplitude = jnp.broadcast_to(coef[:, g : g + 1], (poles, length))
            impulse.append(amplitude * jnp.exp(-rate * time))
            lift.append(amplitude * jnp.exp(-rate * (time + 1.0)))
            wide = jnp.where(owner == g, rate[:, :TILE], wide)
        step_ref[:, tile_of(index)] = -wide * length
        states = tile_of(index, in_tile * poles)
        decay_ref[states, :] = jnp.concatenate(decay, axis=0).astype(BF16)
        high, low = halves(jnp.concatenate(impulse, axis=0))
        response_ref[pl.ds(pl.multiple_of(index * in_tile, in_tile), in_tile), :] = dot(member, high) + dot(member, low)
        lift_ref[:, states] = turned(jnp.concatenate(lift, axis=0).astype(BF16), unit).astype(BF16)

    def filters(index):
        chans = tile_of(index)
        query, left, right = (
            short_conv(stream, chans, length, padded_ref.at[index * 3 + stream], taps_ref) for stream in range(3)
        )
        query_ref[:, chans] = query.astype(BF16)
        gated_ref[:, chans] = left * right

    unrolled(channels // TILE, turn)
    unrolled(channels // TILE, factors)
    unrolled(channels // TILE, filters)


def states_kernel(
    before_ref, heads_ref, taps_ref, gated_ref, decay_ref, ends_ref, sent_ref, final_ref, first_ref, padded_ref
):
    length, channels = gated_ref.shape
    poles = ends_ref.shape[0]
    in_tile = decay_ref.shape[0] // poles * TILE // channels
    owner = iota((poles, TILE), 1) // (TILE // in_tile)

    def begin(index):
        chans = tile_of(index)
        for stream in range(3):
            padded_ref[index * 3 + stream, :ROWS, :] = before_ref[stream, :, chans].astype(F32)
            padded_ref[index * 3 + stream, ROWS:, :] = heads_ref[stream, :, chans]
        query, left, right = (
            short_conv(stream, chans, ROWS, padded_ref.at[index * 3 + stream], taps_ref) for stream in range(3)
        )
        first_ref[:, chans] = query
        final_ref[:, chans] = jnp.concatenate([left * right, gated_ref[ROWS:, chans]], axis=0).astype(BF16)

    def leave(index):
        chans = tile_of(index)
        gated = final_ref[:, chans]
        states = tile_of(index, in_tile * poles)
        every = dot(decay_ref[states, :], gated)
        ends = jnp.zeros((poles, TILE), F32)
        for g in range(in_tile):
            ends = jnp.where(owner == g, every[g * poles : (g + 1) * poles], ends)
        ends_ref[:, chans] = ends
        sent_ref[:, chans] = ends.astype(BF16)

    unrolled(channels // TILE, begin)
    unrolled(channels // TILE, leave)


def inside_kernel(begin, gated_ref, skip_ref, response_ref, base_ref, signal_ref, sum_ref):
    length = gated_ref.shape[0]
    width = gated_ref.shape[1] // response_ref.shape[0]
    in_tile = TILE // width
    tiles = base_ref.shape[1] // TILE
    strip = STRIP
    unit = identity(length)
    lane = iota((width, length), 1)
    causal = iota((strip, length), 1) >= iota((strip, length), 0)

    def signals(index):
        gated = gated_ref[:, tile_of(begin + index)]
        for at in range(length // strip):
            piece = turned(gated[at * strip : (at + 1) * strip], unit).astype(BF16)
            signal_ref[at, tile_of(index), :] = piece

    def products(index):
        for pair in range(in_tile // 2):
            group = index * in_tile + 2 * pair
            responses = response_ref[pl.ds(begin * in_tile + group, 2), :]
            blocks = []
            for g in range(2):
                spread = jnp.broadcast_to(responses[g : g + 1], (strip, length))
                shifted = pltpu.roll(spread, 0, 1, stride=1, stride_axis=0)
                blocks.append(jnp.where(causal, shifted, 0.0).astype(BF16))
            rows = pl.ds(pl.multiple_of(group * width, 2 * width), 2 * width)
            signal = jnp.concatenate([signal_ref[at, rows, :] for at in range(length // strip)], axis=0)
            both = dot(signal, jnp.concatenate(blocks, axis=1))
            for g in range(2):
                total = None
                for at in range(length // strip):
                    first = at * 2 * width + g * width
                    term = both[first : first + width, g * length : (g + 1) * length]
                    if at:
                        term = jnp.where(lane >= at * strip, pltpu.roll(term, at * strip, 1), 0.0)
                    total = term if total is None else total + term
                sum_ref[pl.ds(pl.multiple_of((group + g) * width, width), width), :] = total

    def back(index):
        chans = tile_of(index)
        here = tile_of(begin + index)
        high, low = halves(sum_ref[chans, :])
        direct = skip_ref[:, here] * gated_ref[:, here].astype(F32)
        base_ref[:, chans] = turned(high, unit) + turned(low, unit) + direct

    unrolled(tiles, signals)
    unrolled(tiles, products)
    unrolled(tiles, back)


def join_kernel(bit, arrived_ref, ends_ref, entering_ref, wide_ref, sent_ref, later_ref, *joined_ref):
    me = lax.axis_index("ctx")
    high = (me >> bit) % 2 == 1
    arrived = arrived_ref[...].astype(F32)
    wide = wide_ref[...]
    over = jnp.exp(wide * (1 << bit))
    joined = jnp.where(high, over * arrived + ends_ref[...], over * ends_ref[...] + arrived)
    sent_ref[...] = joined.astype(BF16)
    for ref in joined_ref:
        ref[...] = joined
    before = (me % (1 << bit)).astype(F32)
    later_ref[...] = entering_ref[...] + jnp.where(high, jnp.exp(wide * before) * arrived, 0.0)


def finish_kernel(
    bit, half, arrived_ref, entering_ref, wide_ref, lift_ref, query_ref, first_ref, left_ref, right_ref, mixed_ref, state_ref
):
    length, share = mixed_ref.shape
    poles, channels = wide_ref.shape
    in_tile = lift_ref.shape[1] // poles * TILE // channels
    me = lax.axis_index("ctx")
    half = half(me % CORES)
    here = tile_of(half, share)
    high = (me >> bit) % 2 == 1
    before = (me % (1 << bit)).astype(F32)
    reached = jnp.exp(wide_ref[:, here] * before) * arrived_ref[:, here].astype(F32)
    state_ref[...] = entering_ref[:, here] + jnp.where(high, reached, 0.0)
    owner = iota((poles, TILE), 1) // (TILE // in_tile)

    def tile(index):
        at = half * (share // TILE) + index
        chans = tile_of(at)
        entering = state_ref[:, tile_of(index)]
        apart = jnp.concatenate([jnp.where(owner == g, entering, 0.0) for g in range(in_tile)], axis=0)
        carried = dot(lift_ref[:, tile_of(at, in_tile * poles)], apart.astype(BF16))
        query = jnp.concatenate([first_ref[:, chans], query_ref[:, chans].astype(F32)[ROWS:]], axis=0)
        base = jnp.where(half == 0, left_ref[:, tile_of(index)], right_ref[:, tile_of(index)])
        mixed_ref[:, tile_of(index)] = (query * (base + carried)).astype(BF16)

    unrolled(share // TILE, tile)


def early_kernel(at_ref, own_ref, beside_ref, across_ref, *rest):
    *weight_hbms, total_ref, rows_ref, block_ref, layers_ref, weight_ref, sems = rest
    count = len(weight_hbms)
    layer = at_ref[0]
    last = layer ^ 2
    copies = [pltpu.make_async_copy(hbm, weight_ref.at[at], sems.at[at]) for at, hbm in enumerate(weight_hbms)]
    fetches = [pltpu.make_async_copy(hbm, rows_ref, sems.at[count]) for hbm in weight_hbms]
    for copy in copies:
        copy.start()
    for at, fetch in enumerate(fetches):
        pl.when(at_ref[1 + at] == last)(fetch.start)
    for bits, ref in ((0, own_ref), (1, beside_ref), (3, across_ref)):
        layers_ref[layer ^ bits] = ref[...]
    layers_ref[last] = jnp.zeros_like(own_ref)
    block_ref[...] = layers_ref[at_ref[1 + count]]
    for at, copy in enumerate(copies):
        copy.wait()
        block = layers_ref[at_ref[1 + at]]
        for column in range(0, total_ref.shape[1], COLUMNS):
            columns = slice(column, column + COLUMNS)
            term = dot(block, weight_ref[at, :, columns])
            total_ref[:, columns] = total_ref[:, columns] + term if at else term
    for at, fetch in enumerate(fetches):
        pl.when(at_ref[1 + at] == last)(fetch.wait)


def joined_kernel(total_ref, block_ref, weight_ref, out_ref):
    out_ref[...] = total_ref[...] + dot(block_ref[...], weight_ref[...])


def keep_kernel(square, rows_ref, weight_ref, last_ref, sem):
    del rows_ref
    chip = lax.axis_index("ctx") // CORES if square else 0
    latest = chip ^ 3 == lax.axis_index("tp") ^ 2
    copy = pltpu.make_async_copy(weight_ref, last_ref, sem)
    pl.when(latest)(copy.start)
    pl.when(latest)(copy.wait)


def late_kernel(first, beyond_ref, total_ref, rows_ref, out_ref):
    tokens = pl.ds(first, out_ref.shape[0])
    out_ref[...] = (total_ref[tokens, :] + dot(beyond_ref[tokens, :], rows_ref[...])).astype(out_ref.dtype)


def swap(value, *bits):
    count = lax.axis_size("ctx")
    pairs = [(source, source ^ bits[source % len(bits)]) for source in range(count)]
    return lax.ppermute(value, "ctx", pairs)


def after(value, earlier):
    return lax.optimization_barrier((value, earlier))[0]


def trade(value, bits):
    count = lax.axis_size("tp")
    return lax.ppermute(value, "tp", [(source, source ^ bits) for source in range(count)])


def local(streams, conv_weight, rates, residues, skip, out_weight):
    channels, length = streams.shape[1:]
    groups, poles = rates.shape
    blocks, layers = lax.axis_size("ctx"), lax.axis_size("tp")
    rows, features = out_weight.shape
    share = channels // CORES
    square = blocks == 8 and rows == share

    inputs = (streams, conv_weight, rates.T, residues.T, skip[None, :])
    tails, streams, conv_weight, rates, residues, skip = call(
        tails_kernel,
        [((3, ROWS, channels), BF16)] + [(part.shape, part.dtype) for part in inputs],
        "tails",
        *(pltpu.with_memory_space_constraint(part, pltpu.HBM) for part in inputs),
        specs=[pl.BlockSpec(memory_space=pltpu.HBM)] * len(inputs),
        scratch=[pltpu.SemaphoreType.DMA((len(inputs),))],
    )
    before = from_behind(tails, "ctx", 1)
    if square:
        near = swap(out_weight, 2, 4)
    tiles = channels // TILE
    heads, query, gated, decay, wide, response, lift = call(
        prepare_kernel,
        [
            ((3, ROWS, channels), F32),
            ((length, channels), BF16),
            ((length, channels), F32),
            ((groups * poles, length), BF16),
            ((poles, channels), F32),
            ((groups, length), F32),
            ((length, groups * poles), BF16),
        ],
        "prepare",
        streams, conv_weight, rates, residues,
        scratch=[pltpu.VMEM((3 * tiles, ROWS + length, TILE), F32)],
        flops=10**9,
    )
    ends, sent, gated, first = call(
        states_kernel,
        [((poles, channels), F32), ((poles, channels), BF16), ((length, channels), BF16), ((ROWS, channels), F32)],
        "states",
        before, heads, conv_weight, gated, decay,
        scratch=[pltpu.VMEM((3 * tiles, 2 * ROWS, TILE), F32)],
    )
    me = lax.axis_index("ctx").astype(jnp.int32)

    def within(half):
        return call(
            functools.partial(inside_kernel, half * tiles // 2),
            [((length, channels // 2), F32)],
            "inside",
            gated, skip, response,
            scratch=[
                pltpu.VMEM((length // STRIP, channels // 2, STRIP), BF16),
                pltpu.VMEM((channels // 2, length), F32),
            ],
            flops=10**9,
        )[0]

    bases, ends, entering = [], [ends], jnp.zeros((poles, channels), F32)
    steps = (blocks - 1).bit_length()
    for bit in range(steps):
        arrived = swap(sent, 1 << bit)
        if bit < steps - 1:
            outs = [((poles, channels), BF16), ((poles, channels), F32), ((poles, channels), F32)]
            sent, entering, *ends = call(
                functools.partial(join_kernel, bit),
                outs[: 2 if bit == steps - 2 else 3],
                "join",
                arrived, ends[0], entering, wide,
            )
        if bit == steps - 2:
            bases.append(within(0))
            sent = after(sent, bases[0])
    bases.append(within(1))
    if square:
        other_near = swap(after(out_weight, (entering, sent, near)), 4, 2)
    core = me % CORES
    smem = [pl.BlockSpec(memory_space=pltpu.SMEM)]

    def finished(half):
        return call(
            functools.partial(finish_kernel, steps - 1, half),
            [((length, share), BF16)],
            "finish",
            arrived, entering, wide, lift, query, first, *bases,
            flops=5 * 10**9,
            scratch=[pltpu.VMEM((poles, share), F32)],
        )[0]

    if rows == share:
        other, mine = finished(lambda core: 1 - core), finished(lambda core: core)
    else:
        mixed = jnp.concatenate([finished(lambda core, half=half: half) for half in range(CORES)], axis=1)
        by_core = mixed.reshape(length, share // rows, CORES, rows).transpose(2, 0, 1, 3)
        by_core = by_core.reshape(CORES, length, share)
        mine = lax.dynamic_index_in_dim(by_core, core, 0, keepdims=False)
        other = lax.dynamic_index_in_dim(by_core, 1 - core, 0, keepdims=False)
    block = jnp.concatenate([mine, swap(other, 1)], axis=0)
    layer = lax.axis_index("tp").astype(jnp.int32)
    beside, across = trade(block, 1), trade(block, 3)
    beyond = trade(after(across, other_near) if square else across, 1)
    if square:
        diagonal = swap(after(near, block), 4, 2)
        weight = (out_weight, near, other_near, diagonal)
    else:
        core_groups = [list(range(core, blocks, CORES)) for core in range(CORES)]
        weight = lax.all_gather(out_weight, "ctx", axis=0, axis_index_groups=core_groups)
        weight = tuple(weight.reshape(layers, share, features))
    first_row = jnp.where(core == 0, 1, 2)
    chip = me // CORES
    place = [chip, chip ^ first_row, chip ^ (3 - first_row), chip ^ 3] if square else [jnp.full_like(me, at) for at in range(4)]
    at = jnp.stack([layer] + place)
    *sooner, latest = weight
    total, last_rows, last_block = call(
        early_kernel,
        [((CORES * length, features), F32), ((share, features), BF16), (block.shape, BF16)],
        "early",
        at, block, beside, across,
        *(pltpu.with_memory_space_constraint(part, pltpu.HBM) for part in sooner),
        specs=smem + whole(3) + [pl.BlockSpec(memory_space=pltpu.HBM)] * len(sooner),
        scratch=[
            pltpu.VMEM((layers,) + block.shape, BF16),
            pltpu.VMEM((len(sooner), share, features), BF16),
            pltpu.SemaphoreType.DMA((len(sooner) + 1,)),
        ],
        flops=10**10,
    )
    (total,) = call(
        joined_kernel, [((CORES * length, features), F32)], "joined", total, last_block, latest, flops=0
    )
    anywhere = [pl.BlockSpec(memory_space=pl.ANY)]
    (last_rows,) = call(
        functools.partial(keep_kernel, square),
        [((share, features), BF16)],
        "keep",
        last_rows, latest,
        specs=anywhere * 2,
        out_specs=anywhere,
        scratch=[pltpu.SemaphoreType.DMA],
        flops=0,
        aliases={0: 0},
    )
    sides = []
    for side, kind in ((1, BF16), (0, F32)):
        sides += call(
            functools.partial(late_kernel, side * length),
            [((length, features), kind)],
            "late",
            beyond, total, last_rows,
            flops=0,
        )
    other, mine = sides
    other = swap(other, 1)
    return (mine + other.astype(F32)).astype(BF16)


def solution(mesh):
    return jax.shard_map(
        local,
        mesh=mesh,
        in_specs=(
            P(None, "tp", "ctx"),
            P(None, None, "tp"),
            P("tp", None),
            P("tp", None),
            P("tp"),
            P("ctx", "tp"),
        ),
        out_specs=P("ctx", "tp"),
        check_vma=False,
    )
```

```python
import functools
import math

import jax
import jax.numpy as jnp
from jax import lax
from jax.experimental import pallas as pl
from jax.experimental.pallas import tpu as pltpu
from jax.sharding import PartitionSpec as P

F32 = jnp.float32
BF16 = jnp.bfloat16
ROWS = 8
TILE = 128
CORES = 2
COLUMNS = 256
STRIP = 32
VMEM_LIMIT = 24 * 1024 * 1024
PLAIN = (((1,), (0,)), ((), ()))
CONTRACT_LANES = (((1,), (1,)), ((), ()))


def from_behind(value, axis, steps):
    count = lax.axis_size(axis)
    leading, last = (max(0, -steps), min(count, count - steps))
    return lax.ppermute(value, axis, [(source, source + steps) for source in range(leading, last)])


def dot(left, right, dims=PLAIN):
    return lax.dot_general(left, right, dims, preferred_element_type=F32)


def halves(value):
    high = value.astype(BF16)
    return high, (value - high.astype(F32)).astype(BF16)


def iota(shape, axis):
    return lax.broadcasted_iota(jnp.int32, shape, axis)


def identity(size):
    return (iota((size, size), 0) == iota((size, size), 1)).astype(BF16)


def turned(value, unit):
    return dot(unit, value, CONTRACT_LANES)


def whole(count):
    return [pl.BlockSpec(memory_space=pltpu.VMEM)] * count


def call(kernel, outs, name, *operands, specs=None, scratch=(), flops=10**8, aliases=None, out_specs=None):
    return pl.pallas_call(
        kernel,
        out_shape=tuple(jax.ShapeDtypeStruct(*out) for out in outs),
        in_specs=whole(len(operands)) if specs is None else specs,
        out_specs=tuple(out_specs or whole(len(outs))),
        scratch_shapes=scratch,
        input_output_aliases=aliases or {},
        compiler_params=pltpu.CompilerParams(vmem_limit_bytes=VMEM_LIMIT),
        cost_estimate=pl.CostEstimate(flops=flops, bytes_accessed=flops // 100, transcendentals=0),
        name=name,
    )(*operands)


def tile_of(index, size=TILE):
    return pl.ds(pl.multiple_of(index * size, size), size)


def unrolled(count, body):
    def step(index, carry):
        body(index)
        return carry

    lax.fori_loop(0, count, step, 0, unroll=math.gcd(count, 4))


def tails_kernel(*refs):
    count = len(refs) // 2 - 1
    sources, tails_ref, fetched, sems = refs[:count], refs[count], refs[count + 1 : -1], refs[-1]
    copies = [
        pltpu.make_async_copy(source, target, sems.at[at]) for at, (source, target) in enumerate(zip(sources, fetched))
    ]
    for copy in copies:
        copy.start()
    streams_ref = fetched[0]
    length = streams_ref.shape[2]
    pick = (iota((2 * ROWS, length), 1) == iota((2 * ROWS, length), 0) + (length - ROWS)).astype(BF16)
    copies[0].wait()
    for stream in range(streams_ref.shape[0]):
        rows = dot(pick, streams_ref[stream], CONTRACT_LANES)
        tails_ref[stream] = rows[:ROWS].astype(BF16)
    for copy in copies[1:]:
        copy.wait()


def short_conv(stream, chans, rows, padded, taps_ref):
    total = None
    for shift in range(taps_ref.shape[1]):
        term = taps_ref[stream, shift : shift + 1, chans] * padded[pl.ds(ROWS - shift, rows), :]
        total = term if total is None else total + term
    return total


def prepare_kernel(
    streams_ref, taps_ref, rates_ref, residues_ref,
    heads_ref, query_ref, gated_ref, decay_ref, step_ref, response_ref, lift_ref, padded_ref,
):
    channels, length = streams_ref.shape[1:]
    poles, groups = rates_ref.shape
    width = channels // groups
    in_tile = TILE // width
    unit = identity(length)
    lag = (length - 1) - iota((poles, length), 1).astype(F32)
    owner = iota((poles, TILE), 1) // width
    time = iota((poles, length), 1).astype(F32)
    member = (iota((in_tile, in_tile * poles), 1) // poles == iota((in_tile, in_tile * poles), 0)).astype(BF16)
    scale = residues_ref[...] * jnp.sqrt(2.0 * rates_ref[...]) / math.sqrt(poles)

    def turn(index):
        chans = tile_of(index)
        for stream in range(3):
            tokens = turned(streams_ref[stream, chans, :], unit)
            padded_ref[index * 3 + stream, :ROWS, :] = jnp.zeros((ROWS, TILE), F32)
            padded_ref[index * 3 + stream, ROWS:, :] = tokens
            heads_ref[stream, :, chans] = tokens[:ROWS]

    def factors(index):
        shift = groups - index * in_tile
        rates = pltpu.roll(rates_ref[...], shift, 1)
        coef = pltpu.roll(scale, shift, 1)
        decay, impulse, lift = [], [], []
        wide = jnp.zeros((poles, TILE), F32)
        for g in range(in_tile):
            rate = jnp.broadcast_to(rates[:, g : g + 1], (poles, length))
            decay.append(jnp.exp(-rate * lag))
            amplitude = jnp.broadcast_to(coef[:, g : g + 1], (poles, length))
            impulse.append(amplitude * jnp.exp(-rate * time))
            lift.append(amplitude * jnp.exp(-rate * (time + 1.0)))
            wide = jnp.where(owner == g, rate[:, :TILE], wide)
        step_ref[:, tile_of(index)] = -wide * length
        states = tile_of(index, in_tile * poles)
        decay_ref[states, :] = jnp.concatenate(decay, axis=0).astype(BF16)
        high, low = halves(jnp.concatenate(impulse, axis=0))
        response_ref[pl.ds(pl.multiple_of(index * in_tile, in_tile), in_tile), :] = dot(member, high) + dot(member, low)
        lift_ref[:, states] = turned(jnp.concatenate(lift, axis=0).astype(BF16), unit).astype(BF16)

    def filters(index):
        chans = tile_of(index)
        query, left, right = (
            short_conv(stream, chans, length, padded_ref.at[index * 3 + stream], taps_ref) for stream in range(3)
        )
        query_ref[:, chans] = query.astype(BF16)
        gated_ref[:, chans] = left * right

    unrolled(channels // TILE, turn)
    unrolled(channels // TILE, factors)
    unrolled(channels // TILE, filters)


def states_kernel(
    before_ref, heads_ref, taps_ref, gated_ref, decay_ref, ends_ref, sent_ref, final_ref, first_ref, padded_ref
):
    length, channels = gated_ref.shape
    poles = ends_ref.shape[0]
    in_tile = decay_ref.shape[0] // poles * TILE // channels
    owner = iota((poles, TILE), 1) // (TILE // in_tile)

    def begin(index):
        chans = tile_of(index)
        for stream in range(3):
            padded_ref[index * 3 + stream, :ROWS, :] = before_ref[stream, :, chans].astype(F32)
            padded_ref[index * 3 + stream, ROWS:, :] = heads_ref[stream, :, chans]
        query, left, right = (
            short_conv(stream, chans, ROWS, padded_ref.at[index * 3 + stream], taps_ref) for stream in range(3)
        )
        first_ref[:, chans] = query
        final_ref[:, chans] = jnp.concatenate([left * right, gated_ref[ROWS:, chans]], axis=0).astype(BF16)

    def leave(index):
        chans = tile_of(index)
        gated = final_ref[:, chans]
        states = tile_of(index, in_tile * poles)
        every = dot(decay_ref[states, :], gated)
        ends = jnp.zeros((poles, TILE), F32)
        for g in range(in_tile):
            ends = jnp.where(owner == g, every[g * poles : (g + 1) * poles], ends)
        ends_ref[:, chans] = ends
        sent_ref[:, chans] = ends.astype(BF16)

    unrolled(channels // TILE, begin)
    unrolled(channels // TILE, leave)


def inside_kernel(begin, gated_ref, skip_ref, response_ref, base_ref, signal_ref, sum_ref):
    length = gated_ref.shape[0]
    width = gated_ref.shape[1] // response_ref.shape[0]
    in_tile = TILE // width
    tiles = base_ref.shape[1] // TILE
    strip = STRIP
    unit = identity(length)
    lane = iota((width, length), 1)
    causal = iota((strip, length), 1) >= iota((strip, length), 0)

    def signals(index):
        gated = gated_ref[:, tile_of(begin + index)]
        for at in range(length // strip):
            piece = turned(gated[at * strip : (at + 1) * strip], unit).astype(BF16)
            signal_ref[at, tile_of(index), :] = piece

    def products(index):
        for pair in range(in_tile // 2):
            group = index * in_tile + 2 * pair
            responses = response_ref[pl.ds(begin * in_tile + group, 2), :]
            blocks = []
            for g in range(2):
                spread = jnp.broadcast_to(responses[g : g + 1], (strip, length))
                shifted = pltpu.roll(spread, 0, 1, stride=1, stride_axis=0)
                blocks.append(jnp.where(causal, shifted, 0.0).astype(BF16))
            rows = pl.ds(pl.multiple_of(group * width, 2 * width), 2 * width)
            signal = jnp.concatenate([signal_ref[at, rows, :] for at in range(length // strip)], axis=0)
            both = dot(signal, jnp.concatenate(blocks, axis=1))
            for g in range(2):
                total = None
                for at in range(length // strip):
                    first = at * 2 * width + g * width
                    term = both[first : first + width, g * length : (g + 1) * length]
                    if at:
                        term = jnp.where(lane >= at * strip, pltpu.roll(term, at * strip, 1), 0.0)
                    total = term if total is None else total + term
                sum_ref[pl.ds(pl.multiple_of((group + g) * width, width), width), :] = total

    def back(index):
        chans = tile_of(index)
        here = tile_of(begin + index)
        high, low = halves(sum_ref[chans, :])
        direct = skip_ref[:, here] * gated_ref[:, here].astype(F32)
        base_ref[:, chans] = turned(high, unit) + turned(low, unit) + direct

    unrolled(tiles, signals)
    unrolled(tiles, products)
    unrolled(tiles, back)


def join_kernel(bit, arrived_ref, ends_ref, entering_ref, wide_ref, sent_ref, later_ref, *joined_ref):
    me = lax.axis_index("ctx")
    high = (me >> bit) % 2 == 1
    arrived = arrived_ref[...].astype(F32)
    wide = wide_ref[...]
    over = jnp.exp(wide * (1 << bit))
    joined = jnp.where(high, over * arrived + ends_ref[...], over * ends_ref[...] + arrived)
    sent_ref[...] = joined.astype(BF16)
    for ref in joined_ref:
        ref[...] = joined
    before = (me % (1 << bit)).astype(F32)
    later_ref[...] = entering_ref[...] + jnp.where(high, jnp.exp(wide * before) * arrived, 0.0)


def finish_kernel(
    bit, half, arrived_ref, entering_ref, wide_ref, lift_ref, query_ref, first_ref, left_ref, right_ref, mixed_ref, state_ref
):
    length, share = mixed_ref.shape
    poles, channels = wide_ref.shape
    in_tile = lift_ref.shape[1] // poles * TILE // channels
    me = lax.axis_index("ctx")
    half = half(me % CORES)
    here = tile_of(half, share)
    high = (me >> bit) % 2 == 1
    before = (me % (1 << bit)).astype(F32)
    reached = jnp.exp(wide_ref[:, here] * before) * arrived_ref[:, here].astype(F32)
    state_ref[...] = entering_ref[:, here] + jnp.where(high, reached, 0.0)
    owner = iota((poles, TILE), 1) // (TILE // in_tile)

    def tile(index):
        at = half * (share // TILE) + index
        chans = tile_of(at)
        entering = state_ref[:, tile_of(index)]
        apart = jnp.concatenate([jnp.where(owner == g, entering, 0.0) for g in range(in_tile)], axis=0)
        carried = dot(lift_ref[:, tile_of(at, in_tile * poles)], apart.astype(BF16))
        query = jnp.concatenate([first_ref[:, chans], query_ref[:, chans].astype(F32)[ROWS:]], axis=0)
        base = jnp.where(half == 0, left_ref[:, tile_of(index)], right_ref[:, tile_of(index)])
        mixed_ref[:, tile_of(index)] = (query * (base + carried)).astype(BF16)

    unrolled(share // TILE, tile)


def early_kernel(at_ref, own_ref, beside_ref, across_ref, *rest):
    *weight_hbms, total_ref, rows_ref, block_ref, layers_ref, weight_ref, sems = rest
    count = len(weight_hbms)
    layer = at_ref[0]
    last = layer ^ 2
    copies = [pltpu.make_async_copy(hbm, weight_ref.at[at], sems.at[at]) for at, hbm in enumerate(weight_hbms)]
    fetches = [pltpu.make_async_copy(hbm, rows_ref, sems.at[count]) for hbm in weight_hbms]
    for copy in copies:
        copy.start()
    for at, fetch in enumerate(fetches):
        pl.when(at_ref[1 + at] == last)(fetch.start)
    for bits, ref in ((0, own_ref), (1, beside_ref), (3, across_ref)):
        layers_ref[layer ^ bits] = ref[...]
    layers_ref[last] = jnp.zeros_like(own_ref)
    block_ref[...] = layers_ref[at_ref[1 + count]]
    for at, copy in enumerate(copies):
        copy.wait()
        block = layers_ref[at_ref[1 + at]]
        for column in range(0, total_ref.shape[1], COLUMNS):
            columns = slice(column, column + COLUMNS)
            term = dot(block, weight_ref[at, :, columns])
            total_ref[:, columns] = total_ref[:, columns] + term if at else term
    for at, fetch in enumerate(fetches):
        pl.when(at_ref[1 + at] == last)(fetch.wait)


def joined_kernel(total_ref, block_ref, weight_ref, out_ref):
    out_ref[...] = total_ref[...] + dot(block_ref[...], weight_ref[...])


def keep_kernel(square, rows_ref, weight_ref, last_ref, sem):
    del rows_ref
    chip = lax.axis_index("ctx") // CORES if square else 0
    latest = chip ^ 3 == lax.axis_index("tp") ^ 2
    copy = pltpu.make_async_copy(weight_ref, last_ref, sem)
    pl.when(latest)(copy.start)
    pl.when(latest)(copy.wait)


def late_kernel(first, beyond_ref, total_ref, rows_ref, out_ref):
    tokens = pl.ds(first, out_ref.shape[0])
    out_ref[...] = (total_ref[tokens, :] + dot(beyond_ref[tokens, :], rows_ref[...])).astype(out_ref.dtype)


def swap(value, *bits):
    count = lax.axis_size("ctx")
    pairs = [(source, source ^ bits[source % len(bits)]) for source in range(count)]
    return lax.ppermute(value, "ctx", pairs)


def after(value, earlier):
    return lax.optimization_barrier((value, earlier))[0]


def trade(value, bits):
    count = lax.axis_size("tp")
    return lax.ppermute(value, "tp", [(source, source ^ bits) for source in range(count)])


def local(streams, conv_weight, rates, residues, skip, out_weight):
    channels, length = streams.shape[1:]
    groups, poles = rates.shape
    blocks, layers = lax.axis_size("ctx"), lax.axis_size("tp")
    rows, features = out_weight.shape
    share = channels // CORES
    square = blocks == 8 and rows == share

    inputs = (streams, conv_weight, rates.T, residues.T, skip[None, :])
    tails, streams, conv_weight, rates, residues, skip = call(
        tails_kernel,
        [((3, ROWS, channels), BF16)] + [(part.shape, part.dtype) for part in inputs],
        "tails",
        *(pltpu.with_memory_space_constraint(part, pltpu.HBM) for part in inputs),
        specs=[pl.BlockSpec(memory_space=pltpu.HBM)] * len(inputs),
        scratch=[pltpu.SemaphoreType.DMA((len(inputs),))],
    )
    before = from_behind(tails, "ctx", 1)
    if square:
        near = swap(out_weight, 2, 4)
    tiles = channels // TILE
    heads, query, gated, decay, wide, response, lift = call(
        prepare_kernel,
        [
            ((3, ROWS, channels), F32),
            ((length, channels), BF16),
            ((length, channels), F32),
            ((groups * poles, length), BF16),
            ((poles, channels), F32),
            ((groups, length), F32),
            ((length, groups * poles), BF16),
        ],
        "prepare",
        streams, conv_weight, rates, residues,
        scratch=[pltpu.VMEM((3 * tiles, ROWS + length, TILE), F32)],
        flops=10**9,
    )
    ends, sent, gated, first = call(
        states_kernel,
        [((poles, channels), F32), ((poles, channels), BF16), ((length, channels), BF16), ((ROWS, channels), F32)],
        "states",
        before, heads, conv_weight, gated, decay,
        scratch=[pltpu.VMEM((3 * tiles, 2 * ROWS, TILE), F32)],
    )
    me = lax.axis_index("ctx").astype(jnp.int32)

    def within(half):
        return call(
            functools.partial(inside_kernel, half * tiles // 2),
            [((length, channels // 2), F32)],
            "inside",
            gated, skip, response,
            scratch=[
                pltpu.VMEM((length // STRIP, channels // 2, STRIP), BF16),
                pltpu.VMEM((channels // 2, length), F32),
            ],
            flops=10**9,
        )[0]

    bases, ends, entering = [], [ends], jnp.zeros((poles, channels), F32)
    steps = (blocks - 1).bit_length()
    for bit in range(steps):
        arrived = swap(sent, 1 << bit)
        if bit < steps - 1:
            outs = [((poles, channels), BF16), ((poles, channels), F32), ((poles, channels), F32)]
            sent, entering, *ends = call(
                functools.partial(join_kernel, bit),
                outs[: 2 if bit == steps - 2 else 3],
                "join",
                arrived, ends[0], entering, wide,
            )
        if bit == steps - 2:
            bases = [within(0), within(1)]
            sent = after(sent, tuple(bases))
    if square:
        other_near = swap(after(out_weight, (entering, sent, near)), 4, 2)
    core = me % CORES
    smem = [pl.BlockSpec(memory_space=pltpu.SMEM)]

    def finished(half):
        return call(
            functools.partial(finish_kernel, steps - 1, half),
            [((length, share), BF16)],
            "finish",
            arrived, entering, wide, lift, query, first, *bases,
            flops=5 * 10**9,
            scratch=[pltpu.VMEM((poles, share), F32)],
        )[0]

    if rows == share:
        other, mine = finished(lambda core: 1 - core), finished(lambda core: core)
    else:
        mixed = jnp.concatenate([finished(lambda core, half=half: half) for half in range(CORES)], axis=1)
        by_core = mixed.reshape(length, share // rows, CORES, rows).transpose(2, 0, 1, 3)
        by_core = by_core.reshape(CORES, length, share)
        mine = lax.dynamic_index_in_dim(by_core, core, 0, keepdims=False)
        other = lax.dynamic_index_in_dim(by_core, 1 - core, 0, keepdims=False)
    block = jnp.concatenate([mine, swap(other, 1)], axis=0)
    layer = lax.axis_index("tp").astype(jnp.int32)
    beside, across = trade(block, 1), trade(block, 3)
    beyond = trade(after(across, other_near) if square else across, 1)
    if square:
        diagonal = swap(after(near, block), 4, 2)
        weight = (out_weight, near, other_near, diagonal)
    else:
        core_groups = [list(range(core, blocks, CORES)) for core in range(CORES)]
        weight = lax.all_gather(out_weight, "ctx", axis=0, axis_index_groups=core_groups)
        weight = tuple(weight.reshape(layers, share, features))
    first_row = jnp.where(core == 0, 1, 2)
    chip = me // CORES
    place = [chip, chip ^ first_row, chip ^ (3 - first_row), chip ^ 3] if square else [jnp.full_like(me, at) for at in range(4)]
    at = jnp.stack([layer] + place)
    *sooner, latest = weight
    total, last_rows, last_block = call(
        early_kernel,
        [((CORES * length, features), F32), ((share, features), BF16), (block.shape, BF16)],
        "early",
        at, block, beside, across,
        *(pltpu.with_memory_space_constraint(part, pltpu.HBM) for part in sooner),
        specs=smem + whole(3) + [pl.BlockSpec(memory_space=pltpu.HBM)] * len(sooner),
        scratch=[
            pltpu.VMEM((layers,) + block.shape, BF16),
            pltpu.VMEM((len(sooner), share, features), BF16),
            pltpu.SemaphoreType.DMA((len(sooner) + 1,)),
        ],
        flops=10**10,
    )
    (total,) = call(
        joined_kernel, [((CORES * length, features), F32)], "joined", total, last_block, latest, flops=0
    )
    anywhere = [pl.BlockSpec(memory_space=pl.ANY)]
    (last_rows,) = call(
        functools.partial(keep_kernel, square),
        [((share, features), BF16)],
        "keep",
        last_rows, latest,
        specs=anywhere * 2,
        out_specs=anywhere,
        scratch=[pltpu.SemaphoreType.DMA],
        flops=0,
        aliases={0: 0},
    )
    sides = []
    for side, kind in ((1, BF16), (0, F32)):
        sides += call(
            functools.partial(late_kernel, side * length),
            [((length, features), kind)],
            "late",
            beyond, total, last_rows,
            flops=0,
        )
    other, mine = sides
    other = swap(other, 1)
    return (mine + other.astype(F32)).astype(BF16)


def solution(mesh):
    return jax.shard_map(
        local,
        mesh=mesh,
        in_specs=(
            P(None, "tp", "ctx"),
            P(None, None, "tp"),
            P("tp", None),
            P("tp", None),
            P("tp"),
            P("ctx", "tp"),
        ),
        out_specs=P("ctx", "tp"),
        check_vma=False,
    )
```

```python
import functools
import math

import jax
import jax.numpy as jnp
from jax import lax
from jax.experimental import pallas as pl
from jax.experimental.pallas import tpu as pltpu
from jax.sharding import PartitionSpec as P

F32 = jnp.float32
BF16 = jnp.bfloat16
ROWS = 8
TILE = 128
CORES = 2
COLUMNS = 256
STRIP = 32
VMEM_LIMIT = 24 * 1024 * 1024
PLAIN = (((1,), (0,)), ((), ()))
CONTRACT_LANES = (((1,), (1,)), ((), ()))


def from_behind(value, axis, steps):
    count = lax.axis_size(axis)
    leading, last = (max(0, -steps), min(count, count - steps))
    return lax.ppermute(value, axis, [(source, source + steps) for source in range(leading, last)])


def dot(left, right, dims=PLAIN):
    return lax.dot_general(left, right, dims, preferred_element_type=F32)


def halves(value):
    high = value.astype(BF16)
    return high, (value - high.astype(F32)).astype(BF16)


def iota(shape, axis):
    return lax.broadcasted_iota(jnp.int32, shape, axis)


def identity(size):
    return (iota((size, size), 0) == iota((size, size), 1)).astype(BF16)


def turned(value, unit):
    return dot(unit, value, CONTRACT_LANES)


def whole(count):
    return [pl.BlockSpec(memory_space=pltpu.VMEM)] * count


def call(kernel, outs, name, *operands, specs=None, scratch=(), flops=10**8, aliases=None, out_specs=None):
    return pl.pallas_call(
        kernel,
        out_shape=tuple(jax.ShapeDtypeStruct(*out) for out in outs),
        in_specs=whole(len(operands)) if specs is None else specs,
        out_specs=tuple(out_specs or whole(len(outs))),
        scratch_shapes=scratch,
        input_output_aliases=aliases or {},
        compiler_params=pltpu.CompilerParams(vmem_limit_bytes=VMEM_LIMIT),
        cost_estimate=pl.CostEstimate(flops=flops, bytes_accessed=flops // 100, transcendentals=0),
        name=name,
    )(*operands)


def tile_of(index, size=TILE):
    return pl.ds(pl.multiple_of(index * size, size), size)


def unrolled(count, body):
    def step(index, carry):
        body(index)
        return carry

    lax.fori_loop(0, count, step, 0, unroll=math.gcd(count, 4))


def tails_kernel(*refs):
    count = len(refs) // 2 - 1
    sources, tails_ref, fetched, sems = refs[:count], refs[count], refs[count + 1 : -1], refs[-1]
    copies = [
        pltpu.make_async_copy(source, target, sems.at[at]) for at, (source, target) in enumerate(zip(sources, fetched))
    ]
    for copy in copies:
        copy.start()
    streams_ref = fetched[0]
    length = streams_ref.shape[2]
    pick = (iota((2 * ROWS, length), 1) == iota((2 * ROWS, length), 0) + (length - ROWS)).astype(BF16)
    copies[0].wait()
    for stream in range(streams_ref.shape[0]):
        rows = dot(pick, streams_ref[stream], CONTRACT_LANES)
        tails_ref[stream] = rows[:ROWS].astype(BF16)
    for copy in copies[1:]:
        copy.wait()


def short_conv(stream, chans, rows, padded, taps_ref):
    total = None
    for shift in range(taps_ref.shape[1]):
        term = taps_ref[stream, shift : shift + 1, chans] * padded[pl.ds(ROWS - shift, rows), :]
        total = term if total is None else total + term
    return total


def prepare_kernel(
    streams_ref, taps_ref, rates_ref, residues_ref,
    heads_ref, query_ref, gated_ref, decay_ref, step_ref, response_ref, lift_ref, padded_ref,
):
    channels, length = streams_ref.shape[1:]
    poles, groups = rates_ref.shape
    width = channels // groups
    in_tile = TILE // width
    unit = identity(length)
    lag = (length - 1) - iota((poles, length), 1).astype(F32)
    owner = iota((poles, TILE), 1) // width
    time = iota((poles, length), 1).astype(F32)
    member = (iota((in_tile, in_tile * poles), 1) // poles == iota((in_tile, in_tile * poles), 0)).astype(BF16)
    scale = residues_ref[...] * jnp.sqrt(2.0 * rates_ref[...]) / math.sqrt(poles)

    def turn(index):
        chans = tile_of(index)
        for stream in range(3):
            tokens = turned(streams_ref[stream, chans, :], unit)
            padded_ref[index * 3 + stream, :ROWS, :] = jnp.zeros((ROWS, TILE), F32)
            padded_ref[index * 3 + stream, ROWS:, :] = tokens
            heads_ref[stream, :, chans] = tokens[:ROWS]

    def factors(index):
        shift = groups - index * in_tile
        rates = pltpu.roll(rates_ref[...], shift, 1)
        coef = pltpu.roll(scale, shift, 1)
        decay, impulse, lift = [], [], []
        wide = jnp.zeros((poles, TILE), F32)
        for g in range(in_tile):
            rate = jnp.broadcast_to(rates[:, g : g + 1], (poles, length))
            decay.append(jnp.exp(-rate * lag))
            amplitude = jnp.broadcast_to(coef[:, g : g + 1], (poles, length))
            impulse.append(amplitude * jnp.exp(-rate * time))
            lift.append(amplitude * jnp.exp(-rate * (time + 1.0)))
            wide = jnp.where(owner == g, rate[:, :TILE], wide)
        step_ref[:, tile_of(index)] = -wide * length
        states = tile_of(index, in_tile * poles)
        decay_ref[states, :] = jnp.concatenate(decay, axis=0).astype(BF16)
        high, low = halves(jnp.concatenate(impulse, axis=0))
        response_ref[pl.ds(pl.multiple_of(index * in_tile, in_tile), in_tile), :] = dot(member, high) + dot(member, low)
        lift_ref[:, states] = turned(jnp.concatenate(lift, axis=0).astype(BF16), unit).astype(BF16)

    def filters(index):
        chans = tile_of(index)
        query, left, right = (
            short_conv(stream, chans, length, padded_ref.at[index * 3 + stream], taps_ref) for stream in range(3)
        )
        query_ref[:, chans] = query.astype(BF16)
        gated_ref[:, chans] = left * right

    unrolled(channels // TILE, turn)
    unrolled(channels // TILE, factors)
    unrolled(channels // TILE, filters)


def states_kernel(
    before_ref, heads_ref, taps_ref, gated_ref, decay_ref, ends_ref, sent_ref, final_ref, first_ref, padded_ref
):
    length, channels = gated_ref.shape
    poles = ends_ref.shape[0]
    in_tile = decay_ref.shape[0] // poles * TILE // channels
    owner = iota((poles, TILE), 1) // (TILE // in_tile)

    def begin(index):
        chans = tile_of(index)
        for stream in range(3):
            padded_ref[index * 3 + stream, :ROWS, :] = before_ref[stream, :, chans].astype(F32)
            padded_ref[index * 3 + stream, ROWS:, :] = heads_ref[stream, :, chans]
        query, left, right = (
            short_conv(stream, chans, ROWS, padded_ref.at[index * 3 + stream], taps_ref) for stream in range(3)
        )
        first_ref[:, chans] = query
        final_ref[:, chans] = jnp.concatenate([left * right, gated_ref[ROWS:, chans]], axis=0).astype(BF16)

    def leave(index):
        chans = tile_of(index)
        gated = final_ref[:, chans]
        states = tile_of(index, in_tile * poles)
        every = dot(decay_ref[states, :], gated)
        ends = jnp.zeros((poles, TILE), F32)
        for g in range(in_tile):
            ends = jnp.where(owner == g, every[g * poles : (g + 1) * poles], ends)
        ends_ref[:, chans] = ends
        sent_ref[:, chans] = ends.astype(BF16)

    unrolled(channels // TILE, begin)
    unrolled(channels // TILE, leave)


def inside_kernel(begin, gated_ref, skip_ref, response_ref, base_ref, signal_ref, sum_ref):
    length = gated_ref.shape[0]
    width = gated_ref.shape[1] // response_ref.shape[0]
    in_tile = TILE // width
    tiles = base_ref.shape[1] // TILE
    strip = STRIP
    unit = identity(length)
    lane = iota((width, length), 1)
    causal = iota((strip, length), 1) >= iota((strip, length), 0)

    def signals(index):
        gated = gated_ref[:, tile_of(begin + index)]
        for at in range(length // strip):
            piece = turned(gated[at * strip : (at + 1) * strip], unit).astype(BF16)
            signal_ref[at, tile_of(index), :] = piece

    def products(index):
        for pair in range(in_tile // 2):
            group = index * in_tile + 2 * pair
            responses = response_ref[pl.ds(begin * in_tile + group, 2), :]
            blocks = []
            for g in range(2):
                spread = jnp.broadcast_to(responses[g : g + 1], (strip, length))
                shifted = pltpu.roll(spread, 0, 1, stride=1, stride_axis=0)
                blocks.append(jnp.where(causal, shifted, 0.0).astype(BF16))
            rows = pl.ds(pl.multiple_of(group * width, 2 * width), 2 * width)
            signal = jnp.concatenate([signal_ref[at, rows, :] for at in range(length // strip)], axis=0)
            both = dot(signal, jnp.concatenate(blocks, axis=1))
            for g in range(2):
                total = None
                for at in range(length // strip):
                    first = at * 2 * width + g * width
                    term = both[first : first + width, g * length : (g + 1) * length]
                    if at:
                        term = jnp.where(lane >= at * strip, pltpu.roll(term, at * strip, 1), 0.0)
                    total = term if total is None else total + term
                sum_ref[pl.ds(pl.multiple_of((group + g) * width, width), width), :] = total

    def back(index):
        chans = tile_of(index)
        here = tile_of(begin + index)
        high, low = halves(sum_ref[chans, :])
        direct = skip_ref[:, here] * gated_ref[:, here].astype(F32)
        base_ref[:, chans] = turned(high, unit) + turned(low, unit) + direct

    unrolled(tiles, signals)
    unrolled(tiles, products)
    unrolled(tiles, back)


def join_kernel(bit, arrived_ref, ends_ref, entering_ref, wide_ref, sent_ref, later_ref, *joined_ref):
    me = lax.axis_index("ctx")
    high = (me >> bit) % 2 == 1
    arrived = arrived_ref[...].astype(F32)
    wide = wide_ref[...]
    over = jnp.exp(wide * (1 << bit))
    joined = jnp.where(high, over * arrived + ends_ref[...], over * ends_ref[...] + arrived)
    sent_ref[...] = joined.astype(BF16)
    for ref in joined_ref:
        ref[...] = joined
    before = (me % (1 << bit)).astype(F32)
    later_ref[...] = entering_ref[...] + jnp.where(high, jnp.exp(wide * before) * arrived, 0.0)


def finish_kernel(
    bit, half, arrived_ref, entering_ref, wide_ref, lift_ref, query_ref, first_ref, left_ref, right_ref, mixed_ref, state_ref
):
    length, share = mixed_ref.shape
    poles, channels = wide_ref.shape
    in_tile = lift_ref.shape[1] // poles * TILE // channels
    me = lax.axis_index("ctx")
    half = half(me % CORES)
    here = tile_of(half, share)
    high = (me >> bit) % 2 == 1
    before = (me % (1 << bit)).astype(F32)
    reached = jnp.exp(wide_ref[:, here] * before) * arrived_ref[:, here].astype(F32)
    state_ref[...] = entering_ref[:, here] + jnp.where(high, reached, 0.0)
    owner = iota((poles, TILE), 1) // (TILE // in_tile)

    def tile(index):
        at = half * (share // TILE) + index
        chans = tile_of(at)
        entering = state_ref[:, tile_of(index)]
        apart = jnp.concatenate([jnp.where(owner == g, entering, 0.0) for g in range(in_tile)], axis=0)
        carried = dot(lift_ref[:, tile_of(at, in_tile * poles)], apart.astype(BF16))
        query = jnp.concatenate([first_ref[:, chans], query_ref[:, chans].astype(F32)[ROWS:]], axis=0)
        base = jnp.where(half == 0, left_ref[:, tile_of(index)], right_ref[:, tile_of(index)])
        mixed_ref[:, tile_of(index)] = (query * (base + carried)).astype(BF16)

    unrolled(share // TILE, tile)


def early_kernel(at_ref, own_ref, beside_ref, across_ref, *rest):
    *weight_hbms, total_ref, rows_ref, block_ref, layers_ref, weight_ref, sems = rest
    count = len(weight_hbms)
    layer = at_ref[0]
    last = layer ^ 2
    copies = [pltpu.make_async_copy(hbm, weight_ref.at[at], sems.at[at]) for at, hbm in enumerate(weight_hbms)]
    fetches = [pltpu.make_async_copy(hbm, rows_ref, sems.at[count]) for hbm in weight_hbms]
    for copy in copies:
        copy.start()
    for at, fetch in enumerate(fetches):
        pl.when(at_ref[1 + at] == last)(fetch.start)
    for bits, ref in ((0, own_ref), (1, beside_ref), (3, across_ref)):
        layers_ref[layer ^ bits] = ref[...]
    layers_ref[last] = jnp.zeros_like(own_ref)
    block_ref[...] = layers_ref[at_ref[1 + count]]
    for at, copy in enumerate(copies):
        copy.wait()
        block = layers_ref[at_ref[1 + at]]
        for column in range(0, total_ref.shape[1], COLUMNS):
            columns = slice(column, column + COLUMNS)
            term = dot(block, weight_ref[at, :, columns])
            total_ref[:, columns] = total_ref[:, columns] + term if at else term
    for at, fetch in enumerate(fetches):
        pl.when(at_ref[1 + at] == last)(fetch.wait)


def keep_kernel(square, rows_ref, weight_ref, last_ref, sem):
    del rows_ref
    chip = lax.axis_index("ctx") // CORES if square else 0
    latest = chip ^ 3 == lax.axis_index("tp") ^ 2
    copy = pltpu.make_async_copy(weight_ref, last_ref, sem)
    pl.when(latest)(copy.start)
    pl.when(latest)(copy.wait)


def late_kernel(first, beyond_ref, total_ref, rows_ref, block_ref, weight_ref, out_ref):
    tokens = pl.ds(first, out_ref.shape[0])
    total = total_ref[tokens, :] + dot(block_ref[tokens, :], weight_ref[...])
    out_ref[...] = (total + dot(beyond_ref[tokens, :], rows_ref[...])).astype(out_ref.dtype)


def swap(value, *bits):
    count = lax.axis_size("ctx")
    pairs = [(source, source ^ bits[source % len(bits)]) for source in range(count)]
    return lax.ppermute(value, "ctx", pairs)


def after(value, earlier):
    return lax.optimization_barrier((value, earlier))[0]


def trade(value, bits):
    count = lax.axis_size("tp")
    return lax.ppermute(value, "tp", [(source, source ^ bits) for source in range(count)])


def local(streams, conv_weight, rates, residues, skip, out_weight):
    channels, length = streams.shape[1:]
    groups, poles = rates.shape
    blocks, layers = lax.axis_size("ctx"), lax.axis_size("tp")
    rows, features = out_weight.shape
    share = channels // CORES
    square = blocks == 8 and rows == share

    inputs = (streams, conv_weight, rates.T, residues.T, skip[None, :])
    tails, streams, conv_weight, rates, residues, skip = call(
        tails_kernel,
        [((3, ROWS, channels), BF16)] + [(part.shape, part.dtype) for part in inputs],
        "tails",
        *(pltpu.with_memory_space_constraint(part, pltpu.HBM) for part in inputs),
        specs=[pl.BlockSpec(memory_space=pltpu.HBM)] * len(inputs),
        scratch=[pltpu.SemaphoreType.DMA((len(inputs),))],
    )
    before = from_behind(tails, "ctx", 1)
    if square:
        near = swap(out_weight, 2, 4)
    tiles = channels // TILE
    heads, query, gated, decay, wide, response, lift = call(
        prepare_kernel,
        [
            ((3, ROWS, channels), F32),
            ((length, channels), BF16),
            ((length, channels), F32),
            ((groups * poles, length), BF16),
            ((poles, channels), F32),
            ((groups, length), F32),
            ((length, groups * poles), BF16),
        ],
        "prepare",
        streams, conv_weight, rates, residues,
        scratch=[pltpu.VMEM((3 * tiles, ROWS + length, TILE), F32)],
        flops=10**9,
    )
    ends, sent, gated, first = call(
        states_kernel,
        [((poles, channels), F32), ((poles, channels), BF16), ((length, channels), BF16), ((ROWS, channels), F32)],
        "states",
        before, heads, conv_weight, gated, decay,
        scratch=[pltpu.VMEM((3 * tiles, 2 * ROWS, TILE), F32)],
    )
    me = lax.axis_index("ctx").astype(jnp.int32)

    def within(half):
        return call(
            functools.partial(inside_kernel, half * tiles // 2),
            [((length, channels // 2), F32)],
            "inside",
            gated, skip, response,
            scratch=[
                pltpu.VMEM((length // STRIP, channels // 2, STRIP), BF16),
                pltpu.VMEM((channels // 2, length), F32),
            ],
            flops=10**9,
        )[0]

    bases, ends, entering = [], [ends], jnp.zeros((poles, channels), F32)
    steps = (blocks - 1).bit_length()
    for bit in range(steps):
        arrived = swap(sent, 1 << bit)
        if bit < steps - 1:
            outs = [((poles, channels), BF16), ((poles, channels), F32), ((poles, channels), F32)]
            sent, entering, *ends = call(
                functools.partial(join_kernel, bit),
                outs[: 2 if bit == steps - 2 else 3],
                "join",
                arrived, ends[0], entering, wide,
            )
        if bit == steps - 2:
            bases = [within(0), within(1)]
            sent = after(sent, tuple(bases))
    if square:
        other_near = swap(after(out_weight, (entering, sent, near)), 4, 2)
    core = me % CORES
    smem = [pl.BlockSpec(memory_space=pltpu.SMEM)]

    def finished(half):
        return call(
            functools.partial(finish_kernel, steps - 1, half),
            [((length, share), BF16)],
            "finish",
            arrived, entering, wide, lift, query, first, *bases,
            flops=5 * 10**9,
            scratch=[pltpu.VMEM((poles, share), F32)],
        )[0]

    if rows == share:
        other, mine = finished(lambda core: 1 - core), finished(lambda core: core)
    else:
        mixed = jnp.concatenate([finished(lambda core, half=half: half) for half in range(CORES)], axis=1)
        by_core = mixed.reshape(length, share // rows, CORES, rows).transpose(2, 0, 1, 3)
        by_core = by_core.reshape(CORES, length, share)
        mine = lax.dynamic_index_in_dim(by_core, core, 0, keepdims=False)
        other = lax.dynamic_index_in_dim(by_core, 1 - core, 0, keepdims=False)
    block = jnp.concatenate([mine, swap(other, 1)], axis=0)
    layer = lax.axis_index("tp").astype(jnp.int32)
    beside, across = trade(block, 1), trade(block, 3)
    beyond = trade(after(across, other_near) if square else across, 1)
    if square:
        diagonal = swap(after(near, block), 4, 2)
        weight = (out_weight, near, other_near, diagonal)
    else:
        core_groups = [list(range(core, blocks, CORES)) for core in range(CORES)]
        weight = lax.all_gather(out_weight, "ctx", axis=0, axis_index_groups=core_groups)
        weight = tuple(weight.reshape(layers, share, features))
    first_row = jnp.where(core == 0, 1, 2)
    chip = me // CORES
    place = [chip, chip ^ first_row, chip ^ (3 - first_row), chip ^ 3] if square else [jnp.full_like(me, at) for at in range(4)]
    at = jnp.stack([layer] + place)
    *sooner, latest = weight
    total, last_rows, last_block = call(
        early_kernel,
        [((CORES * length, features), F32), ((share, features), BF16), (block.shape, BF16)],
        "early",
        at, block, beside, across,
        *(pltpu.with_memory_space_constraint(part, pltpu.HBM) for part in sooner),
        specs=smem + whole(3) + [pl.BlockSpec(memory_space=pltpu.HBM)] * len(sooner),
        scratch=[
            pltpu.VMEM((layers,) + block.shape, BF16),
            pltpu.VMEM((len(sooner), share, features), BF16),
            pltpu.SemaphoreType.DMA((len(sooner) + 1,)),
        ],
        flops=10**10,
    )
    anywhere = [pl.BlockSpec(memory_space=pl.ANY)]
    (last_rows,) = call(
        functools.partial(keep_kernel, square),
        [((share, features), BF16)],
        "keep",
        last_rows, latest,
        specs=anywhere * 2,
        out_specs=anywhere,
        scratch=[pltpu.SemaphoreType.DMA],
        flops=0,
        aliases={0: 0},
    )
    sides = []
    for side, kind in ((1, BF16), (0, F32)):
        sides += call(
            functools.partial(late_kernel, side * length),
            [((length, features), kind)],
            "late",
            beyond, total, last_rows, last_block, latest,
            flops=0,
        )
    other, mine = sides
    other = swap(other, 1)
    return (mine + other.astype(F32)).astype(BF16)


def solution(mesh):
    return jax.shard_map(
        local,
        mesh=mesh,
        in_specs=(
            P(None, "tp", "ctx"),
            P(None, None, "tp"),
            P("tp", None),
            P("tp", None),
            P("tp"),
            P("ctx", "tp"),
        ),
        out_specs=P("ctx", "tp"),
        check_vma=False,
    )
```
